32 devices in a mesh: group: 2 (over x), span: 4 (over y, core), tensor: 4 (over z).
Axes of the slice: x: 2, y: 2, z: 4, core: 2. Of those that a mesh axis runs over, the one named last changes fastest.
Arguments:
- queries: bfloat16 [3072, 3072], P(('group', 'span'), 'tensor'), parts along dimension 0, may hold values from -96 to 96
- keys: bfloat16 [3072, 3072], P(('group', 'span'), 'tensor'), parts along dimension 0, may hold values from -4 to 4
- values: bfloat16 [3072, 3072], P(('group', 'span'), 'tensor'), parts along dimension 0, may hold values from -6 to 6
- out_weight: bfloat16 [3072, 6144], P('tensor'), may hold values from -2 to 2
- gate_table: float32 [64, 6144], replicated, may hold values from 0.5 to 1.5
- levels: int32 [8], P('group'), parts along dimension 0, may hold values from 0 to 63
- visible: int32 [8, 4], P('group'), parts along dimension 0, may hold values from 0 to 1, as said below
Outputs:
- gated_output: bfloat16 [3072, 6144], P(('group', 'span', 'tensor')), parts along dimension 0
The draws below stay inside these ranges and needn't reach their ends.
There are 2 independent parts, one for each index of `group`. The reference program is written for one: setup_inputs(seed, part) draws one part's arguments, and reference() takes and returns one part's arrays. A program takes and returns all parts, laid end to end along the dimension named above; an argument that names none is the same for every part. Nothing has to cross between parts.
Inputs may be any that keep to these rules, and one draw needn't show every extreme that they name: visible[c, c] = 1 and visible[c, j] = 0 for j > c.
All inputs are finite; a program needn't handle non-finite values.
Results may differ from the reference program's by a relative error of at most 0.013.
Values may be sent and summed in bfloat16 or wider, within the bound.
No kernel may reach another device: no remote copies, remote signals or barrier semaphores. Data moves between devices by JAX's collectives and lax.ppermute only.
A program may use at most 64 MiB of HBM per device.

```python
import jax
import jax.numpy as jnp
from jax import lax

D = 6144
HEADS = 24
HD = 128
LEVELS = 64
CT = 384
SPANS = 4
TOKENS = 1536
HEADS_DEV = 6
N_TENSOR = 4


def shared_keys(key):
    return jax.random.truncated_normal(key, -4.0, 4.0, (TOKENS, HEADS * HD), jnp.float32)


def draw_keys(key, part):
    base = shared_keys(key)
    return base.astype(jnp.bfloat16)


def draw_queries(key, part):
    key = jax.random.fold_in(key, 3)
    fresh = 1.5 * jax.random.truncated_normal(key, -4.0, 4.0, (TOKENS, HEADS * HD), jnp.float32)
    return fresh.astype(jnp.bfloat16)


def draw_visible(key, part):
    key = jax.random.fold_in(key, 7)
    coins = jax.random.randint(key, (SPANS, SPANS), 0, 4)
    rows = jnp.arange(SPANS, dtype=jnp.int32)[:, None]
    cols = jnp.arange(SPANS, dtype=jnp.int32)[None, :]
    lower = jnp.logical_and(rows > cols, coins > 0)
    return jnp.where(jnp.logical_or(rows == cols, lower), 1, 0).astype(jnp.int32)


def set_ends(array, rng, low, high):
    index_at = [jax.random.randint(jax.random.fold_in(rng, axis), (), 0, length) for axis, length in enumerate(array.shape)]
    widest = array.shape.index(max(array.shape))
    beside = index_at[:widest] + [(index_at[widest] + 1) % array.shape[widest]] + index_at[widest + 1:]
    return array.at[tuple(index_at)].set(low).at[tuple(beside)].set(high)


def level_of(own_key, extent, shards, least, high):
    factor_of, own = 1.0, jax.random.fold_in(own_key, 6)
    for axis_at, blocks in shards:
        heights = jnp.exp(jax.random.uniform(jax.random.fold_in(own, axis_at), (blocks,), jnp.float32, least / len(shards), high / len(shards)))
        factor_of = factor_of * jnp.repeat(heights, extent[axis_at] // blocks).reshape([-1 if axis == axis_at else 1 for axis in range(len(extent))])
    return factor_of


def normal_values(key, dims, spread, limit, shards=(), held_as=jnp.bfloat16):
    loudness = level_of(key, dims, shards, -0.22, 0.18) if shards else 1.0
    drawn = jax.random.normal(key, dims, jnp.float32) * spread * loudness
    return jnp.minimum(jnp.maximum(drawn, -limit), limit).astype(held_as)


def setup_inputs(seed: int = 0, part: int = 0) -> dict:
    streams_of = jax.random.split(jax.random.key(seed), 8)
    part_keys = jax.random.split(jax.random.fold_in(streams_of[7], part), 8)
    return {
        "queries": draw_queries(jax.random.fold_in(jax.random.fold_in(streams_of[7], part), 71), part),
        "keys": draw_keys(jax.random.fold_in(jax.random.fold_in(streams_of[7], part), 71), part),
        "values": normal_values(part_keys[2], (TOKENS, HEADS * HD), 1.0, 6.0, ((0, 4), (1, 4))),
        "out_weight": normal_values(streams_of[3], (HEADS * HD, D), 8 ** -0.5, 2.0, ((0, 4),)),
        "gate_table": jnp.clip(jax.random.uniform(streams_of[4], (LEVELS, D), jnp.float32, 0.5, 1.5), 0.5, 1.5),
        "levels": set_ends(jax.random.randint(part_keys[5], (SPANS,), 0, LEVELS), jax.random.fold_in(part_keys[5], 1), 0, LEVELS - 1).astype(jnp.int32),
        "visible": draw_visible(jax.random.fold_in(jax.random.fold_in(streams_of[7], part), 71), part),
    }


def reference(queries, keys, values, out_weight, gate_table, levels, visible):
    scale = HD ** -0.5
    query_heads = queries.reshape(SPANS, CT, HEADS, HD)
    key_heads = keys.reshape(TOKENS, HEADS, HD).astype(jnp.float32)
    value_heads = values.reshape(TOKENS, HEADS, HD).astype(jnp.float32)
    key_span = jnp.arange(TOKENS, dtype=jnp.int32) // CT

    def one_span(inputs):
        block, index = inputs
        scores = jnp.einsum("qhd,khd->hqk", block.astype(jnp.float32), key_heads) * scale
        seen = visible[index][key_span] > 0
        scores = jnp.where(seen[None, None, :], scores, -jnp.inf)
        top = jnp.max(scores, axis=-1, keepdims=True)
        probs = jnp.exp(scores - top)
        total = jnp.sum(probs, axis=-1)
        weights = probs.astype(jnp.bfloat16).astype(jnp.float32)
        summed = jnp.einsum("hqk,khd->qhd", weights, value_heads)
        return (summed / jnp.transpose(total)[:, :, None]).astype(jnp.bfloat16).reshape(CT, HEADS * HD)

    attended = lax.map(one_span, (query_heads, jnp.arange(SPANS, dtype=jnp.int32)))
    attended = attended.reshape(TOKENS, HEADS * HD)
    width = HEADS_DEV * HD
    summed = jnp.zeros((TOKENS, D), jnp.float32)
    for group_index in range(N_TENSOR):
        partial_sum = jnp.dot(attended[:, group_index * width:(group_index + 1) * width],
                              out_weight[group_index * width:(group_index + 1) * width],
                              preferred_element_type=jnp.float32)
        rounded = lax.optimization_barrier(partial_sum.astype(jnp.bfloat16))
        summed = summed + rounded.astype(jnp.float32)
    gates = gate_table[levels]
    gated = summed.reshape(SPANS, CT, D) * gates[:, None, :]
    return gated.reshape(TOKENS, D).astype(jnp.bfloat16)
```

```python
import functools

import jax
import jax.numpy as jnp
from jax import lax
from jax.experimental import pallas as pl
from jax.experimental.pallas import tpu as pltpu
from jax.sharding import PartitionSpec as P

HD = 128
LANES = 128
HIDDEN = -1e30
LOG2E = 1.4426950408889634
VMEM_BYTES = 48 * 1024 * 1024
PARAMS = pltpu.CompilerParams(vmem_limit_bytes=VMEM_BYTES)
SMEM = pl.BlockSpec(memory_space=pltpu.SMEM)
VMEM = pl.BlockSpec(memory_space=pltpu.VMEM)


def cost(flops, moved, exps=0):
    return pl.CostEstimate(flops=int(flops), bytes_accessed=int(moved), transcendentals=int(exps))


def shifted(block, axis, distance):
    count = lax.axis_size(axis)
    return lax.ppermute(block, axis, [(i, i + distance) for i in range(count) if 0 <= i + distance < count])


def head_columns(head):
    return slice(head * HD, (head + 1) * HD)


def attend_head(query, keys, values, biases):
    scale = LOG2E * HD ** (-0.5)
    scores = [
        lax.dot_general(query, key, (((1,), (1,)), ((), ())), preferred_element_type=jnp.float32) * scale + bias
        for key, bias in zip(keys, biases)
    ]
    tops = [jnp.max(block, axis=-1, keepdims=True) for block in scores]
    top = functools.reduce(jnp.maximum, tops)
    probs = [jnp.exp2(block - top) for block in scores]
    total = sum(jnp.sum(block, axis=-1, keepdims=True) for block in probs)
    product = sum(
        jnp.dot(block.astype(jnp.bfloat16), value, preferred_element_type=jnp.float32)
        for block, value in zip(probs, values)
    )
    return product / total, top + jnp.log2(total)


def bias_of(flag):
    return jnp.where(flag, 0.0, HIDDEN).astype(jnp.float32)


def local_kernel(place, visible, query_outer, query_inner, key, value, key_beside, value_beside,
                 outer, outer_sum, inner, inner_sum):
    span = place[0]
    beside = span + 1 - 2 * lax.rem(span, 2)
    biases = [jnp.float32(0.0), bias_of(visible[span, beside] > 0)]
    for query, result, sums in ((query_outer, outer, outer_sum), (query_inner, inner, inner_sum)):
        rows, width = query.shape
        lane = lax.broadcasted_iota(jnp.int32, (rows, LANES), 1)
        packed = jnp.zeros((rows, LANES), jnp.float32)
        for head in range(width // HD):
            columns = head_columns(head)
            product, logsum = attend_head(
                query[:, columns],
                [key[:, columns], key_beside[:, columns]],
                [value[:, columns], value_beside[:, columns]],
                biases,
            )
            result[:, columns] = product
            packed = jnp.where(lane == head, logsum, packed)
        sums[...] = packed


def served_kernel(distance, place, visible, query, key, value, key_beside, value_beside, result):
    span = place[0]
    beside = span + 1 - 2 * lax.rem(span, 2)
    asker = jnp.minimum(span + distance, visible.shape[0] - 1)
    biases = [bias_of(visible[asker, span] > 0), bias_of(visible[asker, beside] > 0)]
    rows, width = query.shape
    lane = lax.broadcasted_iota(jnp.int32, (rows, LANES), 1)
    packed = jnp.zeros((rows, LANES), jnp.float32)
    for head in range(width // HD):
        columns = head_columns(head)
        product, logsum = attend_head(
            query[:, columns],
            [key[:, columns], key_beside[:, columns]],
            [value[:, columns], value_beside[:, columns]],
            biases,
        )
        result[:, columns] = product.astype(jnp.bfloat16)
        for piece in range(3):
            part = logsum.astype(jnp.bfloat16).astype(jnp.float32)
            packed = jnp.where(lane == 3 * head + piece, part, packed)
            logsum = logsum - part
    result[:, width:] = packed.astype(jnp.bfloat16)


def merge_kernel(distances, place, own, own_sum, *refs):
    served, result = refs[:-1], refs[-1]
    width = own.shape[1]
    span = place[0]
    logs = own_sum[...]
    away = [ref[:, width:].astype(jnp.float32) for ref in served]
    for head in range(width // HD):
        columns = head_columns(head)
        sums = [logs[:, head:head + 1]]
        for distance, pieces in zip(distances, away):
            at = 3 * head
            joined = pieces[:, at:at + 1] + pieces[:, at + 1:at + 2] + pieces[:, at + 2:at + 3]
            sums.append(jnp.where(span >= distance, joined, HIDDEN))
        top = functools.reduce(jnp.maximum, sums)
        shares = [jnp.exp2(one - top) for one in sums]
        total = sum(shares)
        merged = own[:, columns] * (shares[0] / total)
        for share, ref in zip(shares[1:], served):
            merged = merged + ref[:, columns].astype(jnp.float32) * (share / total)
        result[:, columns] = merged.astype(jnp.bfloat16)


def message_kernel(blocks, up_rows, down_rows, weight, *refs):
    ups, downs = refs[-2:]
    rows = up_rows.shape[0]
    both = jnp.concatenate([up_rows[...], down_rows[...]], axis=0)
    product = jnp.dot(both, weight[...], preferred_element_type=jnp.float32)
    up, down = product[:rows], product[rows:]
    if len(refs) == 4:
        up = up + refs[0][...].astype(jnp.float32)
        down = down + refs[1][...].astype(jnp.float32)
    ups[...] = up.astype(jnp.bfloat16)
    downs[...] = down.astype(jnp.bfloat16)


def message(blocks, attended, weight, arrived, first, columns, rows, tile):
    width = attended.shape[1]
    start = first // tile
    piece = pl.BlockSpec((rows, tile), lambda j, b: (0, j))
    return pl.pallas_call(
        message_kernel,
        grid_spec=pltpu.PrefetchScalarGridSpec(
            num_scalar_prefetch=1,
            grid=(columns // tile,),
            in_specs=[
                pl.BlockSpec((rows, width), lambda j, b: (b[0], 0)),
                pl.BlockSpec((rows, width), lambda j, b: (b[1], 0)),
                pl.BlockSpec((width, tile), lambda j, b: (0, start + j)),
            ] + [piece] * len(arrived),
            out_specs=[piece, piece],
        ),
        out_shape=[jax.ShapeDtypeStruct((rows, columns), jnp.bfloat16)] * 2,
        compiler_params=PARAMS,
        cost_estimate=cost(4 * rows * width * columns, 2 * width * columns + 8 * rows * columns),
        name="message",
    )(blocks, attended, attended, weight, *arrived)


def final_kernel(blocks, own_rows, weight, gate, up, down, result):
    product = jnp.dot(own_rows[...], weight[...], preferred_element_type=jnp.float32)
    summed = product + up[...].astype(jnp.float32) + down[...].astype(jnp.float32)
    result[...] = (summed * gate[pl.ds(lax.rem(blocks[1], 8), 1), :]).astype(jnp.bfloat16)


def final(blocks, attended, weight, gate_table, up, down, first, columns, rows, tile):
    width = attended.shape[1]
    start = first // tile
    piece = pl.BlockSpec((rows, tile), lambda j, b: (0, j))
    return pl.pallas_call(
        final_kernel,
        grid_spec=pltpu.PrefetchScalarGridSpec(
            num_scalar_prefetch=1,
            grid=(columns // tile,),
            in_specs=[
                pl.BlockSpec((rows, width), lambda j, b: (b[0], 0)),
                pl.BlockSpec((width, tile), lambda j, b: (0, start + j)),
                pl.BlockSpec((8, tile), lambda j, b: (b[1] // 8, start + j)),
                piece,
                piece,
            ],
            out_specs=piece,
        ),
        out_shape=jax.ShapeDtypeStruct((rows, columns), jnp.bfloat16),
        compiler_params=PARAMS,
        cost_estimate=cost(2 * rows * width * columns, 2 * width * columns + 10 * rows * columns),
        name="final",
    )(blocks, attended, weight, gate_table, up, down)


def body(queries, keys, values, out_weight, gate_table, levels, visible):
    rows, width = queries.shape
    model = out_weight.shape[1]
    spans = lax.axis_size("span")
    ranks = lax.axis_size("tensor")
    span = lax.axis_index("span")
    rank = lax.axis_index("tensor")
    block = rows // ranks
    quarter = rows // 4
    half = 2 * quarter
    place = jnp.stack([span, rank]).astype(jnp.int32)
    level = levels[span]

    query_outer = jnp.concatenate([queries[:quarter], queries[rows - quarter:]])
    query_inner = queries[quarter:rows - quarter]
    distances = list(range(2, spans, 2))
    asked_outer = [shifted(query_outer, "span", -distance) for distance in distances]
    swap = [(i, i + 1 - 2 * (i % 2)) for i in range(spans)]
    key_beside = lax.ppermute(keys, "span", swap)
    value_beside = lax.ppermute(values, "span", swap)
    asked_inner = [shifted(query_inner, "span", -distance) for distance in distances]

    def served(asked, distance):
        return pl.pallas_call(
            functools.partial(served_kernel, distance),
            in_specs=[SMEM, SMEM] + [VMEM] * 5,
            out_specs=VMEM,
            out_shape=jax.ShapeDtypeStruct((half, width + LANES), jnp.bfloat16),
            compiler_params=PARAMS,
            cost_estimate=cost(8 * half * rows * width, 12 * rows * width, 2 * half * rows * width // HD),
            name="served",
        )(place, visible, asked, keys, values, key_beside, value_beside)

    back_outer = [shifted(served(q, d), "span", d) for q, d in zip(asked_outer, distances)]
    local_shapes = [
        jax.ShapeDtypeStruct((half, width), jnp.float32),
        jax.ShapeDtypeStruct((half, LANES), jnp.float32),
    ] * 2
    outer, outer_sum, inner, inner_sum = pl.pallas_call(
        local_kernel,
        in_specs=[SMEM, SMEM] + [VMEM] * 6,
        out_specs=[VMEM] * 4,
        out_shape=local_shapes,
        compiler_params=PARAMS,
        cost_estimate=cost(16 * half * rows * width, 14 * rows * width, 4 * half * rows * width // HD),
        name="local",
    )(place, visible, query_outer, query_inner, keys, values, key_beside, value_beside)
    back_inner = [shifted(served(q, d), "span", d) for q, d in zip(asked_inner, distances)]

    def merge(own, own_sum, back):
        return pl.pallas_call(
            functools.partial(merge_kernel, distances),
            in_specs=[SMEM] + [VMEM] * (2 + len(back)),
            out_specs=VMEM,
            out_shape=jax.ShapeDtypeStruct((half, width), jnp.bfloat16),
            compiler_params=PARAMS,
            cost_estimate=cost(8 * half * width, 10 * half * width),
            name="merge",
        )(place, own, own_sum, *back)

    attended_outer = merge(outer, outer_sum, back_outer)
    attended_inner = merge(inner, inner_sum, back_inner)
    attended = jnp.concatenate([attended_outer[:quarter], attended_inner, attended_outer[quarter:]])

    chunks = 2
    columns = model // chunks
    tile = 512 if columns % 512 == 0 else columns
    last = ranks - 1
    arrived = [()] * chunks
    for step in range(last):
        if step == 0:
            source, blocks = attended_outer, jnp.array([half // block - 1, 0], jnp.int32)
        else:
            source = attended
            blocks = jnp.stack([jnp.minimum(last - step + rank, last), jnp.maximum(step + rank - last, 0)])
        for chunk in range(chunks):
            up, down = message(
                blocks, source, out_weight, arrived[chunk], chunk * columns, columns, block, tile
            )
            up = lax.ppermute(up, "tensor", [(i, i + 1) for i in range(step + 1)])
            down = lax.ppermute(down, "tensor", [(last - i, last - i - 1) for i in range(step + 1)])
            arrived[chunk] = (up, down)
    blocks = jnp.stack([rank, level])
    return jnp.concatenate([
        final(blocks, attended, out_weight, gate_table, *arrived[chunk], chunk * columns, columns, block, tile)
        for chunk in range(chunks)
    ], axis=1)


def solution(mesh):
    return jax.shard_map(
        body,
        mesh=mesh,
        in_specs=(
            P(("group", "span"), "tensor"),
            P(("group", "span"), "tensor"),
            P(("group", "span"), "tensor"),
            P("tensor", None),
            P(),
            P("group"),
            P("group", None),
        ),
        out_specs=P(("group", "span", "tensor"), None),
        check_vma=False,
    )
```

```python
import functools

import jax
import jax.numpy as jnp
from jax import lax
from jax.experimental import pallas as pl
from jax.experimental.pallas import tpu as pltpu
from jax.sharding import PartitionSpec as P

HD = 128
LANES = 128
HIDDEN = -1e30
LOG2E = 1.4426950408889634
PARAMS = pltpu.CompilerParams(vmem_limit_bytes=20 * 1024 * 1024)
SMEM = pl.BlockSpec(memory_space=pltpu.SMEM)
VMEM = pl.BlockSpec(memory_space=pltpu.VMEM)
PIECE_LANES = 32


def cost(flops, moved, exps=0):
    return pl.CostEstimate(flops=int(flops), bytes_accessed=int(moved), transcendentals=int(exps))


def shifted(block, axis, distance):
    count = lax.axis_size(axis)
    return lax.ppermute(block, axis, [(i, i + distance) for i in range(count) if 0 <= i + distance < count])


def head_columns(head):
    return slice(head * HD, (head + 1) * HD)


def attend(query, keys, values, flags, write):
    rows, width = query.shape
    scale = LOG2E * HD ** (-0.5)
    lane = lax.broadcasted_iota(jnp.int32, (rows, LANES), 1)
    packed = jnp.zeros((rows, LANES), jnp.float32)
    for head in range(width // HD):
        columns = head_columns(head)
        mine = query[:, columns]
        scores = [
            lax.dot_general(mine, key[:, columns], (((1,), (1,)), ((), ())), preferred_element_type=jnp.float32)
            for key in keys
        ]
        tops = [jnp.max(block, axis=-1, keepdims=True) * scale for block in scores]
        top = functools.reduce(
            jnp.maximum, [one if flag is None else jnp.where(flag, one, HIDDEN) for one, flag in zip(tops, flags)]
        )
        total, product = None, None
        for block, value, flag in zip(scores, values, flags):
            above = top if flag is None else jnp.where(flag, top, -HIDDEN)
            probs = jnp.exp2(block * scale - above)
            part = jnp.sum(probs, axis=-1, keepdims=True)
            part_product = jnp.dot(
                probs.astype(jnp.bfloat16), value[:, columns], preferred_element_type=jnp.float32
            )
            total = part if total is None else total + part
            product = part_product if product is None else product + part_product
        total = jnp.where(total > 0.0, total, 1.0)
        write(columns, product * (1.0 / total))
        packed = jnp.where(lane == head, top + jnp.log2(total), packed)
    return packed


def beside_of(span):
    return span + 1 - 2 * lax.rem(span, 2)


def local_kernel(place, visible, query, key, value, key_beside, value_beside, result, sums):
    span = place[0]

    def write(columns, block):
        result[:, columns] = block

    sums[...] = attend(
        query, [key, key_beside], [value, value_beside], [None, visible[span, beside_of(span)] > 0], write
    )


def served_kernel(distance, place, visible, query, key, value, key_beside, value_beside, result):
    span = place[0]
    asker = jnp.minimum(span + distance, visible.shape[0] - 1)
    flags = [visible[asker, span] > 0, visible[asker, beside_of(span)] > 0]

    def write(columns, block):
        result[:, columns] = block.astype(jnp.bfloat16)

    width = query.shape[1]
    rest = attend(query, [key, key_beside], [value, value_beside], flags, write)
    sent = jnp.zeros_like(rest)
    for piece in range(3):
        part = rest.astype(jnp.bfloat16).astype(jnp.float32)
        sent = sent + (part if piece == 0 else pltpu.roll(part, piece * PIECE_LANES, 1))
        rest = rest - part
    result[:, width:] = sent.astype(jnp.bfloat16)


def merge_kernel(distances, pieces, place, own, own_sum, *refs):
    served, result = refs[:-1], refs[-1]
    width = own.shape[1]
    span = place[0]
    at = 0
    for start, rows in pieces:
        there, here = slice(start, start + rows), slice(at, at + rows)
        sums = [own_sum[there, :]]
        for distance, ref in zip(distances, served):
            sent = ref[here, width:].astype(jnp.float32)
            joined = sent
            for piece in (1, 2):
                joined = joined + pltpu.roll(sent, LANES - piece * PIECE_LANES, 1)
            sums.append(jnp.where(span >= distance, joined, HIDDEN))
        top = functools.reduce(jnp.maximum, sums)
        shares = [jnp.exp2(one - top) for one in sums]
        over = 1.0 / sum(shares)
        shares = [share * over for share in shares]
        for head in range(width // HD):
            columns = head_columns(head)
            merged = own[there, columns] * shares[0][:, head:head + 1]
            for share, ref in zip(shares[1:], served):
                merged = merged + ref[here, columns].astype(jnp.float32) * share[:, head:head + 1]
            result[here, columns] = merged.astype(jnp.bfloat16)
        at += rows


def rows_at(attended, index, rows):
    return attended[pl.ds(pl.multiple_of(index * rows, rows), rows), :]


def message_kernel(first, tile, blocks, attended, weight, *refs):
    ups, downs = refs[-2:]
    rows, columns = ups.shape
    both = jnp.concatenate([rows_at(attended, blocks[0], rows), rows_at(attended, blocks[1], rows)], axis=0)
    for at in range(0, columns, tile):
        here = slice(at, at + tile)
        product = jnp.dot(both, weight[:, first + at:first + at + tile], preferred_element_type=jnp.float32)
        up, down = product[:rows], product[rows:]
        if len(refs) == 4:
            up = up + refs[0][:, here].astype(jnp.float32)
            down = down + refs[1][:, here].astype(jnp.float32)
        ups[:, here] = up.astype(jnp.bfloat16)
        downs[:, here] = down.astype(jnp.bfloat16)


def message(blocks, attended, weight, arrived, first, columns, rows, tile):
    width = attended.shape[1]
    return pl.pallas_call(
        functools.partial(message_kernel, first, tile),
        in_specs=[SMEM] + [VMEM] * (2 + len(arrived)),
        out_specs=[VMEM, VMEM],
        out_shape=[jax.ShapeDtypeStruct((rows, columns), jnp.bfloat16)] * 2,
        compiler_params=PARAMS,
        cost_estimate=cost(4 * rows * width * columns, 2 * width * columns + 8 * rows * columns),
        name="message",
    )(blocks, attended, weight, *arrived)


def own_kernel(tile, blocks, attended, weight, result):
    rows, columns = result.shape
    mine = rows_at(attended, blocks[0], rows)
    for at in range(0, columns, tile):
        here = slice(at, at + tile)
        result[:, here] = jnp.dot(mine, weight[:, here], preferred_element_type=jnp.float32)


def own_projection(blocks, attended, weight, rows, tile):
    width, columns = weight.shape
    return pl.pallas_call(
        functools.partial(own_kernel, tile),
        in_specs=[SMEM, VMEM, VMEM],
        out_specs=VMEM,
        out_shape=jax.ShapeDtypeStruct((rows, columns), jnp.float32),
        compiler_params=PARAMS,
        cost_estimate=cost(2 * rows * width * columns, 2 * width * columns + 4 * rows * columns),
        name="own",
    )(blocks, attended, weight)


def final_kernel(blocks, own, gate, up, down, *refs):
    result = refs[-1]
    summed = own[...] + up[...].astype(jnp.float32) + down[...].astype(jnp.float32)
    result[...] = (summed * gate[pl.ds(lax.rem(blocks[1], 8), 1), :]).astype(jnp.bfloat16)


def final(blocks, own, gate_table, up, down, first, tile, before):
    rows, columns = up.shape
    start = first // tile
    there = pl.BlockSpec((rows, tile), lambda j, b: (0, start + j))
    piece = pl.BlockSpec((rows, tile), lambda j, b: (0, j))
    return pl.pallas_call(
        final_kernel,
        grid_spec=pltpu.PrefetchScalarGridSpec(
            num_scalar_prefetch=1,
            grid=(columns // tile,),
            in_specs=[
                there,
                pl.BlockSpec((8, tile), lambda j, b: (b[1] // 8, start + j)),
                piece,
                piece,
            ] + [pl.BlockSpec(memory_space=pl.ANY)] * len(before),
            out_specs=there,
        ),
        out_shape=jax.ShapeDtypeStruct(own.shape, jnp.bfloat16),
        input_output_aliases={5: 0} if before else {},
        compiler_params=PARAMS,
        cost_estimate=cost(4 * rows * columns, 10 * rows * columns),
        name="final",
    )(blocks, own, gate_table, up, down, *before)


def body(queries, keys, values, out_weight, gate_table, levels, visible):
    rows, width = queries.shape
    model = out_weight.shape[1]
    spans = lax.axis_size("span")
    ranks = lax.axis_size("tensor")
    span = lax.axis_index("span")
    rank = lax.axis_index("tensor")
    block = rows // ranks
    quarter = rows // 4
    half = 2 * quarter
    place = jnp.stack([span, rank]).astype(jnp.int32)
    level = levels[span]

    query_outer = jnp.concatenate([queries[:quarter], queries[rows - quarter:]])
    query_inner = queries[quarter:rows - quarter]
    distances = list(range(2, spans, 2))
    asked_outer = [shifted(query_outer, "span", -distance) for distance in distances]
    swap = [(i, i + 1 - 2 * (i % 2)) for i in range(spans)]
    key_beside = lax.ppermute(keys, "span", swap)
    value_beside = lax.ppermute(values, "span", swap)
    asked_inner = [shifted(query_inner, "span", -distance) for distance in distances]

    own, own_sum = pl.pallas_call(
        local_kernel,
        in_specs=[SMEM, SMEM] + [VMEM] * 5,
        out_specs=[VMEM] * 2,
        out_shape=[
            jax.ShapeDtypeStruct((rows, width), jnp.float32),
            jax.ShapeDtypeStruct((rows, LANES), jnp.float32),
        ],
        compiler_params=PARAMS,
        cost_estimate=cost(8 * rows * rows * width, 14 * rows * width, 2 * rows * rows * width // HD),
        name="local",
    )(place, visible, queries, keys, values, key_beside, value_beside)

    def served(asked, distance):
        return pl.pallas_call(
            functools.partial(served_kernel, distance),
            in_specs=[SMEM, SMEM] + [VMEM] * 5,
            out_specs=VMEM,
            out_shape=jax.ShapeDtypeStruct((half, width + LANES), jnp.bfloat16),
            compiler_params=PARAMS,
            cost_estimate=cost(8 * half * rows * width, 12 * rows * width, 2 * half * rows * width // HD),
            name="served",
        )(place, visible, asked, keys, values, key_beside, value_beside)

    asked_outer, asked_inner, own_sum = lax.optimization_barrier((asked_outer, asked_inner, own_sum))
    back_outer = [shifted(served(q, d), "span", d) for q, d in zip(asked_outer, distances)]
    back_inner = [shifted(served(q, d), "span", d) for q, d in zip(asked_inner, distances)]

    def merge(back, pieces):
        return pl.pallas_call(
            functools.partial(merge_kernel, distances, pieces),
            in_specs=[SMEM] + [VMEM] * (2 + len(back)),
            out_specs=VMEM,
            out_shape=jax.ShapeDtypeStruct((half, width), jnp.bfloat16),
            compiler_params=PARAMS,
            cost_estimate=cost(8 * half * width, 10 * half * width),
            name="merge",
        )(place, own, own_sum, *back)

    attended_outer = merge(back_outer, [(0, quarter), (rows - quarter, quarter)])
    attended_inner = merge(back_inner, [(quarter, half)])
    attended = jnp.concatenate([attended_outer[:quarter], attended_inner, attended_outer[quarter:]])

    chunks = 2
    columns = model // chunks
    tile = 512 if columns % 512 == 0 else columns
    last = ranks - 1
    arrived = [()] * chunks
    for step in range(last):
        if step == 0:
            source, blocks = attended_outer, jnp.array([half // block - 1, 0], jnp.int32)
        else:
            source = attended
            blocks = jnp.stack([jnp.minimum(last - step + rank, last), jnp.maximum(step + rank - last, 0)])
        for chunk in range(chunks):
            up, down = message(
                blocks, source, out_weight, arrived[chunk], chunk * columns, columns, block, tile
            )
            up = lax.ppermute(up, "tensor", [(i, i + 1) for i in range(step + 1)])
            down = lax.ppermute(down, "tensor", [(last - i, last - i - 1) for i in range(step + 1)])
            arrived[chunk] = (up, down)
    blocks = jnp.stack([rank, level])
    projected = own_projection(blocks, attended, out_weight, block, tile)
    result = ()
    for chunk in range(chunks):
        result = (final(blocks, projected, gate_table, *arrived[chunk], chunk * columns, columns // 2, result),)
    return result[0]


def solution(mesh):
    return jax.shard_map(
        body,
        mesh=mesh,
        in_specs=(
            P(("group", "span"), "tensor"),
            P(("group", "span"), "tensor"),
            P(("group", "span"), "tensor"),
            P("tensor", None),
            P(),
            P("group"),
            P("group", None),
        ),
        out_specs=P(("group", "span", "tensor"), None),
        check_vma=False,
    )
```

```python
import functools

import jax
import jax.numpy as jnp
from jax import lax
from jax.experimental import pallas as pl
from jax.experimental.pallas import tpu as pltpu
from jax.sharding import PartitionSpec as P

HD = 128
LANES = 128
HIDDEN = -1e30
LOG2E = 1.4426950408889634
PARAMS = pltpu.CompilerParams(vmem_limit_bytes=4 * 1024 * 1024)
ATTEND_PARAMS = pltpu.CompilerParams(vmem_limit_bytes=8 * 1024 * 1024)
SMEM = pl.BlockSpec(memory_space=pltpu.SMEM)
VMEM = pl.BlockSpec(memory_space=pltpu.VMEM)
PIECE_LANES = 32


def cost(flops, moved, exps=0):
    return pl.CostEstimate(flops=int(flops), bytes_accessed=int(moved), transcendentals=int(exps))


def shifted(block, axis, distance):
    count = lax.axis_size(axis)
    return lax.ppermute(block, axis, [(i, i + distance) for i in range(count) if 0 <= i + distance < count])


def head_columns(head):
    return slice(head * HD, (head + 1) * HD)


def attend(query, keys, values, flags, write):
    rows, width = query.shape
    scale = LOG2E * HD ** (-0.5)
    lane = lax.broadcasted_iota(jnp.int32, (rows, LANES), 1)
    packed = jnp.zeros((rows, LANES), jnp.float32)
    for head in range(width // HD):
        columns = head_columns(head)
        mine = query[:, columns]
        scores = [
            lax.dot_general(mine, key[:, columns], (((1,), (1,)), ((), ())), preferred_element_type=jnp.float32)
            for key in keys
        ]
        tops = [jnp.max(block, axis=-1, keepdims=True) * scale for block in scores]
        top = functools.reduce(
            jnp.maximum, [one if flag is None else jnp.where(flag, one, HIDDEN) for one, flag in zip(tops, flags)]
        )
        total, product = None, None
        for block, value, flag in zip(scores, values, flags):
            above = top if flag is None else jnp.where(flag, top, -HIDDEN)
            probs = jnp.exp2(block * scale - above)
            part = jnp.sum(probs, axis=-1, keepdims=True)
            part_product = jnp.dot(
                probs.astype(jnp.bfloat16), value[:, columns], preferred_element_type=jnp.float32
            )
            total = part if total is None else total + part
            product = part_product if product is None else product + part_product
        total = jnp.where(total > 0.0, total, 1.0)
        write(columns, product * (1.0 / total))
        packed = jnp.where(lane == head, top + jnp.log2(total), packed)
    return packed


def beside_of(span):
    return span + 1 - 2 * lax.rem(span, 2)


def split_kernel(query, outer, inner, semaphores):
    rows = query.shape[0]
    quarter = rows // 4
    copies = [
        pltpu.make_async_copy(query.at[pl.ds(start, size)], target.at[pl.ds(at, size)], semaphores.at[index])
        for index, (start, size, target, at) in enumerate((
            (0, quarter, outer, 0),
            (rows - quarter, quarter, outer, quarter),
            (quarter, rows - 2 * quarter, inner, 0),
        ))
    ]
    for copy in copies:
        copy.start()
    for copy in copies:
        copy.wait()


def local_kernel(place, visible, query, key, value, key_beside, value_beside, result, sums):
    span = place[0]

    def write(columns, block):
        result[:, columns] = block

    sums[...] = attend(
        query, [key, key_beside], [value, value_beside], [None, visible[span, beside_of(span)] > 0], write
    )


def served_kernel(distance, place, visible, query, key, value, key_beside, value_beside, result):
    span = place[0]
    asker = jnp.minimum(span + distance, visible.shape[0] - 1)
    flags = [visible[asker, span] > 0, visible[asker, beside_of(span)] > 0]

    def write(columns, block):
        result[:, columns] = block.astype(jnp.bfloat16)

    width = query.shape[1]
    rest = attend(query, [key, key_beside], [value, value_beside], flags, write)
    sent = jnp.zeros_like(rest)
    for piece in range(3):
        part = rest.astype(jnp.bfloat16).astype(jnp.float32)
        sent = sent + (part if piece == 0 else pltpu.roll(part, piece * PIECE_LANES, 1))
        rest = rest - part
    result[:, width:] = sent.astype(jnp.bfloat16)


def merge_kernel(distances, pieces, place, own, own_sum, *refs):
    served, result = refs[:-1], refs[-1]
    width = own.shape[1]
    span = place[0]
    at = 0
    for start, rows in pieces:
        there, here = slice(start, start + rows), slice(at, at + rows)
        sums = [own_sum[there, :]]
        for distance, ref in zip(distances, served):
            sent = ref[here, width:].astype(jnp.float32)
            joined = sent
            for piece in (1, 2):
                joined = joined + pltpu.roll(sent, LANES - piece * PIECE_LANES, 1)
            sums.append(jnp.where(span >= distance, joined, HIDDEN))
        top = functools.reduce(jnp.maximum, sums)
        shares = [jnp.exp2(one - top) for one in sums]
        over = 1.0 / sum(shares)
        shares = [share * over for share in shares]
        for head in range(width // HD):
            columns = head_columns(head)
            merged = own[there, columns] * shares[0][:, head:head + 1]
            for share, ref in zip(shares[1:], served):
                merged = merged + ref[here, columns].astype(jnp.float32) * share[:, head:head + 1]
            result[here, columns] = merged.astype(jnp.bfloat16)
        at += rows


def rows_at(attended, index, rows):
    return attended[pl.ds(pl.multiple_of(index * rows, rows), rows), :]


def message_kernel(hop, first, tile, blocks, attended, weight, *refs):
    result = refs[-1]
    rows, columns = result.shape

    @pl.when(blocks[1] > 0)
    def _():
        mine = rows_at(attended, blocks[0], rows)
        for at in range(0, columns, tile):
            here = slice(at, at + tile)
            product = jnp.dot(mine, weight[:, first + at:first + at + tile], preferred_element_type=jnp.float32)
            if len(refs) == 2:
                product = product + refs[0][:, here].astype(jnp.float32)
            result[:, here] = product.astype(jnp.bfloat16)


def message(hop, blocks, attended, weight, arrived, first, columns, rows, tile):
    width = attended.shape[1]
    return pl.pallas_call(
        functools.partial(message_kernel, hop, first, tile),
        in_specs=[SMEM] + [VMEM] * (2 + len(arrived)),
        out_specs=VMEM,
        out_shape=jax.ShapeDtypeStruct((rows, columns), jnp.bfloat16),
        compiler_params=PARAMS,
        cost_estimate=cost(2 * rows * width * columns, 2 * width * columns + 4 * rows * columns),
        name="message",
    )(blocks, attended, weight, *arrived)


def own_kernel(tile, blocks, attended, weight, result):
    rows, columns = result.shape
    mine = rows_at(attended, blocks[0], rows)
    for at in range(0, columns, tile):
        here = slice(at, at + tile)
        result[:, here] = jnp.dot(mine, weight[:, here], preferred_element_type=jnp.float32)


def own_projection(blocks, attended, weight, rows, tile):
    width, columns = weight.shape
    return pl.pallas_call(
        functools.partial(own_kernel, tile),
        in_specs=[SMEM, VMEM, VMEM],
        out_specs=VMEM,
        out_shape=jax.ShapeDtypeStruct((rows, columns), jnp.float32),
        compiler_params=PARAMS,
        cost_estimate=cost(2 * rows * width * columns, 2 * width * columns + 4 * rows * columns),
        name="own",
    )(blocks, attended, weight)


def final_kernel(count, blocks, own, gate, *refs):
    result = refs[-1]
    summed = own[...] + sum(ref[...].astype(jnp.float32) for ref in refs[:count])
    result[...] = (summed * gate[pl.ds(lax.rem(blocks[1], 8), 1), :]).astype(jnp.bfloat16)


def final(blocks, own, gate_table, comes, first, tile, before):
    rows, columns = comes[0].shape
    start = first // tile
    there = pl.BlockSpec((rows, tile), lambda j, b: (0, start + j))
    piece = pl.BlockSpec((rows, tile), lambda j, b: (0, j))
    return pl.pallas_call(
        functools.partial(final_kernel, len(comes)),
        grid_spec=pltpu.PrefetchScalarGridSpec(
            num_scalar_prefetch=1,
            grid=(columns // tile,),
            in_specs=[there, pl.BlockSpec((8, tile), lambda j, b: (b[1] // 8, start + j))]
            + [piece] * len(comes)
            + [pl.BlockSpec(memory_space=pl.ANY)] * len(before),
            out_specs=there,
        ),
        out_shape=jax.ShapeDtypeStruct(own.shape, jnp.bfloat16),
        input_output_aliases={3 + len(comes): 0} if before else {},
        compiler_params=PARAMS,
        cost_estimate=cost(4 * rows * columns, 10 * rows * columns),
        name="final",
    )(blocks, own, gate_table, *comes, *before)


def body(queries, keys, values, out_weight, gate_table, levels, visible):
    rows, width = queries.shape
    model = out_weight.shape[1]
    spans = lax.axis_size("span")
    ranks = lax.axis_size("tensor")
    span = lax.axis_index("span")
    rank = lax.axis_index("tensor")
    block = rows // ranks
    quarter = rows // 4
    half = 2 * quarter
    place = jnp.stack([span, rank]).astype(jnp.int32)
    level = levels[span]

    query_outer, query_inner = pl.pallas_call(
        split_kernel,
        in_specs=[pl.BlockSpec(memory_space=pl.ANY)],
        out_specs=[VMEM, VMEM],
        out_shape=[jax.ShapeDtypeStruct((half, width), queries.dtype)] * 2,
        scratch_shapes=[pltpu.SemaphoreType.DMA((3,))],
        compiler_params=PARAMS,
        cost_estimate=cost(0, 4 * rows * width),
        name="split",
    )(queries)
    distances = list(range(2, spans, 2))
    asked_outer = [shifted(query_outer, "span", -distance) for distance in distances]
    swap = [(i, i + 1 - 2 * (i % 2)) for i in range(spans)]
    key_beside = lax.ppermute(keys, "span", swap)
    value_beside = lax.ppermute(values, "span", swap)

    own, own_sum = pl.pallas_call(
        local_kernel,
        in_specs=[SMEM, SMEM] + [VMEM] * 5,
        out_specs=[VMEM] * 2,
        out_shape=[
            jax.ShapeDtypeStruct((rows, width), jnp.float32),
            jax.ShapeDtypeStruct((rows, LANES), jnp.float32),
        ],
        compiler_params=ATTEND_PARAMS,
        cost_estimate=cost(8 * rows * rows * width, 14 * rows * width, 2 * rows * rows * width // HD),
        name="local",
    )(place, visible, queries, keys, values, key_beside, value_beside)

    def served(asked, distance):
        return pl.pallas_call(
            functools.partial(served_kernel, distance),
            in_specs=[SMEM, SMEM] + [VMEM] * 5,
            out_specs=VMEM,
            out_shape=jax.ShapeDtypeStruct((half, width + LANES), jnp.bfloat16),
            compiler_params=ATTEND_PARAMS,
            cost_estimate=cost(8 * half * rows * width, 12 * rows * width, 2 * half * rows * width // HD),
            name="served",
        )(place, visible, asked, keys, values, key_beside, value_beside)

    asked_outer, query_inner, own_sum = lax.optimization_barrier((asked_outer, query_inner, own_sum))
    asked_inner = [shifted(query_inner, "span", -distance) for distance in distances]
    out_outer = [served(q, d) for q, d in zip(asked_outer, distances)]
    back_outer = [shifted(o, "span", d) for o, d in zip(out_outer, distances)]
    asked_inner, out_outer = lax.optimization_barrier((asked_inner, out_outer))
    back_inner = [shifted(served(q, d), "span", d) for q, d in zip(asked_inner, distances)]

    def merge(back, pieces):
        return pl.pallas_call(
            functools.partial(merge_kernel, distances, pieces),
            in_specs=[SMEM] + [VMEM] * (2 + len(back)),
            out_specs=VMEM,
            out_shape=jax.ShapeDtypeStruct((half, width), jnp.bfloat16),
            compiler_params=PARAMS,
            cost_estimate=cost(8 * half * width, 10 * half * width),
            name="merge",
        )(place, own, own_sum, *back)

    attended_outer = merge(back_outer, [(0, quarter), (rows - quarter, quarter)])
    attended_inner = merge(back_inner, [(quarter, half)])
    attended = jnp.concatenate([attended_outer[:quarter], attended_inner, attended_outer[quarter:]])

    chunks = 3 if model % (3 * 512) == 0 else 1
    columns = model // chunks
    tile = 512 if columns % 512 == 0 else columns
    last = ranks - 1
    ahead = 2
    arrived = {}
    for slot in range(last * chunks):
        for hop in range(last):
            at = slot - hop * ahead
            if not 0 <= at < (last - hop) * chunks:
                continue
            target, chunk = last - at // chunks, at % chunks
            upward, downward = rank == hop, rank == last - hop
            if target == last:
                source, far, near = attended_outer, half // block - 1, 0
            else:
                source, far, near = attended, target, last - target
            blocks = jnp.stack([jnp.where(upward, far, near), jnp.logical_or(upward, downward).astype(jnp.int32)])
            before = [arrived[hop - 1, target, chunk]] if hop else []
            sent = message(hop, blocks, source, out_weight, before, chunk * columns, columns, block, tile)
            paced = slot - ahead
            if hop == 0 and paced >= 0:
                gone = (0, last - paced // chunks, paced % chunks)
                sent, arrived[gone] = lax.optimization_barrier((sent, arrived[gone]))
            arrived[hop, target, chunk] = lax.ppermute(
                sent, "tensor", [(hop, hop + 1), (last - hop, last - hop - 1)]
            )
    blocks = jnp.stack([rank, level])
    projected = own_projection(blocks, attended, out_weight, block, tile)
    result = ()
    for chunk in range(chunks):
        comes = [arrived[hop, hop + 1, chunk] for hop in range(last)]
        result = (final(blocks, projected, gate_table, comes, chunk * columns, columns // 2, result),)
    return result[0]


def solution(mesh):
    return jax.shard_map(
        body,
        mesh=mesh,
        in_specs=(
            P(("group", "span"), "tensor"),
            P(("group", "span"), "tensor"),
            P(("group", "span"), "tensor"),
            P("tensor", None),
            P(),
            P("group"),
            P("group", None),
        ),
        out_specs=P(("group", "span", "tensor"), None),
        check_vma=False,
    )
```

```python
import functools

import jax
import jax.numpy as jnp
from jax import lax
from jax.experimental import pallas as pl
from jax.experimental.pallas import tpu as pltpu
from jax.sharding import PartitionSpec as P

HD = 128
LANES = 128
HIDDEN = -1e30
LOG2E = 1.4426950408889634
PARAMS = pltpu.CompilerParams(vmem_limit_bytes=24 * 1024 * 1024)
ANY = pl.BlockSpec(memory_space=pl.ANY)
SMEM = pl.BlockSpec(memory_space=pltpu.SMEM)
VMEM = pl.BlockSpec(memory_space=pltpu.VMEM)
PIECE_LANES = 32


def cost(flops, moved, exps=0):
    return pl.CostEstimate(flops=int(flops), bytes_accessed=int(moved), transcendentals=int(exps))


def shifted(block, axis, distance):
    count = lax.axis_size(axis)
    return lax.ppermute(block, axis, [(i, i + distance) for i in range(count) if 0 <= i + distance < count])


def head_columns(head):
    return slice(head * HD, (head + 1) * HD)


def attend(query, keys, values, flags, write):
    rows, width = query.shape
    scale = LOG2E * HD ** (-0.5)
    lane = lax.broadcasted_iota(jnp.int32, (rows, LANES), 1)
    packed = jnp.zeros((rows, LANES), jnp.float32)
    for head in range(width // HD):
        columns = head_columns(head)
        mine = query[:, columns]
        scores = [
            lax.dot_general(mine, key[:, columns], (((1,), (1,)), ((), ())), preferred_element_type=jnp.float32)
            for key in keys
        ]
        tops = [jnp.max(block, axis=-1, keepdims=True) * scale for block in scores]
        top = functools.reduce(
            jnp.maximum, [one if flag is None else jnp.where(flag, one, HIDDEN) for one, flag in zip(tops, flags)]
        )
        total, product = None, None
        for block, value, flag in zip(scores, values, flags):
            above = top if flag is None else jnp.where(flag, top, -HIDDEN)
            probs = jnp.exp2(block * scale - above)
            part = jnp.sum(probs, axis=-1, keepdims=True)
            part_product = jnp.dot(
                probs.astype(jnp.bfloat16), value[:, columns], preferred_element_type=jnp.float32
            )
            total = part if total is None else total + part
            product = part_product if product is None else product + part_product
        total = jnp.where(total > 0.0, total, 1.0)
        write(columns, product * (1.0 / total))
        packed = jnp.where(lane == head, top + jnp.log2(total), packed)
    return packed


def beside_of(span):
    return span + 1 - 2 * lax.rem(span, 2)


def local_kernel(place, visible, query, key, value, key_beside, value_beside, result, sums):
    span = place[0]

    def write(columns, block):
        result[:, columns] = block

    sums[...] = attend(
        query, [key, key_beside], [value, value_beside], [None, visible[span, beside_of(span)] > 0], write
    )


def served_kernel(distance, place, visible, query, key, value, key_beside, value_beside, result):
    span = place[0]
    asker = jnp.minimum(span + distance, visible.shape[0] - 1)
    flags = [visible[asker, span] > 0, visible[asker, beside_of(span)] > 0]

    def write(columns, block):
        result[:, columns] = block.astype(jnp.bfloat16)

    width = query.shape[1]
    rest = attend(query, [key, key_beside], [value, value_beside], flags, write)
    sent = jnp.zeros_like(rest)
    for piece in range(3):
        part = rest.astype(jnp.bfloat16).astype(jnp.float32)
        sent = sent + (part if piece == 0 else pltpu.roll(part, piece * PIECE_LANES, 1))
        rest = rest - part
    result[:, width:] = sent.astype(jnp.bfloat16)


def merge_kernel(distances, pieces, place, own, own_sum, *refs):
    served, result = refs[:-1], refs[-1]
    width = own.shape[1]
    span = place[0]
    at = 0
    for start, rows in pieces:
        there, here = slice(start, start + rows), slice(at, at + rows)
        sums = [own_sum[there, :]]
        for distance, ref in zip(distances, served):
            sent = ref[here, width:].astype(jnp.float32)
            joined = sent
            for piece in (1, 2):
                joined = joined + pltpu.roll(sent, LANES - piece * PIECE_LANES, 1)
            sums.append(jnp.where(span >= distance, joined, HIDDEN))
        top = functools.reduce(jnp.maximum, sums)
        shares = [jnp.exp2(one - top) for one in sums]
        over = 1.0 / sum(shares)
        shares = [share * over for share in shares]
        for head in range(width // HD):
            columns = head_columns(head)
            merged = own[there, columns] * shares[0][:, head:head + 1]
            for share, ref in zip(shares[1:], served):
                merged = merged + ref[here, columns].astype(jnp.float32) * share[:, head:head + 1]
            result[here, columns] = merged.astype(jnp.bfloat16)
        at += rows


def project_kernel(first, attended, weight, *refs):
    result = refs[-3] if first else refs[-1]
    product = jnp.dot(attended[...], weight[...], preferred_element_type=jnp.float32).astype(jnp.bfloat16)
    result[...] = product
    if first:
        up, down = refs[-2:]
        rows = up.shape[0]
        up[...] = product[product.shape[0] - rows:]
        down[...] = product[:rows]


def project(attended, weight, chunk, columns, rows, tile, before):
    half, width = attended.shape
    start = chunk * columns // tile
    first = not before
    place = 0 if first else 1
    piece = pl.BlockSpec((rows, tile), lambda j: (0, j))
    message = jax.ShapeDtypeStruct((rows, columns), jnp.bfloat16)
    return pl.pallas_call(
        functools.partial(project_kernel, first),
        grid=(columns // tile,),
        in_specs=[
            pl.BlockSpec((half, width), lambda j: (0, 0)),
            pl.BlockSpec((width, tile), lambda j: (0, start + j)),
        ] + [ANY] * len(before),
        out_specs=[pl.BlockSpec((half, tile), lambda j: (place, j))] + [piece, piece] * first,
        out_shape=[jax.ShapeDtypeStruct((2 * half, columns), jnp.bfloat16)] + [message, message] * first,
        input_output_aliases={} if first else {2: 0},
        compiler_params=PARAMS,
        cost_estimate=cost(2 * half * width * columns, 2 * width * columns + 4 * half * columns),
        name="project",
    )(attended, weight, *before)


def message_kernel(blocks, up_block, down_block, up_arrived, down_arrived, up, down):
    up[...] = (up_block[...].astype(jnp.float32) + up_arrived[...].astype(jnp.float32)).astype(jnp.bfloat16)
    down[...] = (down_block[...].astype(jnp.float32) + down_arrived[...].astype(jnp.float32)).astype(jnp.bfloat16)


def message(blocks, projected, arrived, tile):
    rows, columns = arrived[0].shape
    piece = pl.BlockSpec((rows, tile), lambda j, b: (0, j))
    return pl.pallas_call(
        message_kernel,
        grid_spec=pltpu.PrefetchScalarGridSpec(
            num_scalar_prefetch=1,
            grid=(columns // tile,),
            in_specs=[
                pl.BlockSpec((rows, tile), lambda j, b: (b[0], j)),
                pl.BlockSpec((rows, tile), lambda j, b: (b[1], j)),
                piece,
                piece,
            ],
            out_specs=[piece, piece],
        ),
        out_shape=[jax.ShapeDtypeStruct((rows, columns), jnp.bfloat16)] * 2,
        compiler_params=PARAMS,
        cost_estimate=cost(4 * rows * columns, 12 * rows * columns),
        name="message",
    )(blocks, projected, projected, *arrived)


def final_kernel(blocks, own, gate, up, down, *refs):
    result = refs[-1]
    summed = own[...].astype(jnp.float32) + up[...].astype(jnp.float32) + down[...].astype(jnp.float32)
    result[...] = (summed * gate[pl.ds(lax.rem(blocks[1], 8), 1), :]).astype(jnp.bfloat16)


def final(blocks, projected, gate_table, arrived, first, tile, before):
    rows, columns = arrived[0].shape
    start = first // tile
    piece = pl.BlockSpec((rows, tile), lambda j, b: (0, j))
    return pl.pallas_call(
        final_kernel,
        grid_spec=pltpu.PrefetchScalarGridSpec(
            num_scalar_prefetch=1,
            grid=(columns // tile,),
            in_specs=[
                pl.BlockSpec((rows, tile), lambda j, b: (b[0], j)),
                pl.BlockSpec((8, tile), lambda j, b: (b[1] // 8, start + j)),
                piece,
                piece,
            ] + [ANY] * len(before),
            out_specs=pl.BlockSpec((rows, tile), lambda j, b: (0, start + j)),
        ),
        out_shape=jax.ShapeDtypeStruct((rows, gate_table.shape[1]), jnp.bfloat16),
        input_output_aliases={5: 0} if before else {},
        compiler_params=PARAMS,
        cost_estimate=cost(4 * rows * columns, 10 * rows * columns),
        name="final",
    )(blocks, projected, gate_table, *arrived, *before)


def body(queries, keys, values, out_weight, gate_table, levels, visible):
    rows, width = queries.shape
    model = out_weight.shape[1]
    spans = lax.axis_size("span")
    ranks = lax.axis_size("tensor")
    span = lax.axis_index("span")
    rank = lax.axis_index("tensor")
    block = rows // ranks
    quarter = rows // 4
    half = 2 * quarter
    place = jnp.stack([span, rank]).astype(jnp.int32)
    level = levels[span]

    query_outer = jnp.concatenate([queries[:quarter], queries[rows - quarter:]])
    query_inner = queries[quarter:rows - quarter]
    distances = list(range(2, spans, 2))
    asked_outer = [shifted(query_outer, "span", -distance) for distance in distances]
    swap = [(i, i + 1 - 2 * (i % 2)) for i in range(spans)]
    key_beside = lax.ppermute(keys, "span", swap)
    value_beside = lax.ppermute(values, "span", swap)

    own, own_sum = pl.pallas_call(
        local_kernel,
        in_specs=[SMEM, SMEM] + [VMEM] * 5,
        out_specs=[VMEM] * 2,
        out_shape=[
            jax.ShapeDtypeStruct((rows, width), jnp.float32),
            jax.ShapeDtypeStruct((rows, LANES), jnp.float32),
        ],
        compiler_params=PARAMS,
        cost_estimate=cost(8 * rows * rows * width, 14 * rows * width, 2 * rows * rows * width // HD),
        name="local",
    )(place, visible, queries, keys, values, key_beside, value_beside)

    def served(asked, distance):
        return pl.pallas_call(
            functools.partial(served_kernel, distance),
            in_specs=[SMEM, SMEM] + [VMEM] * 5,
            out_specs=VMEM,
            out_shape=jax.ShapeDtypeStruct((half, width + LANES), jnp.bfloat16),
            compiler_params=PARAMS,
            cost_estimate=cost(8 * half * rows * width, 12 * rows * width, 2 * half * rows * width // HD),
            name="served",
        )(place, visible, asked, keys, values, key_beside, value_beside)

    asked_outer, query_inner, own_sum = lax.optimization_barrier((asked_outer, query_inner, own_sum))
    asked_inner = [shifted(query_inner, "span", -distance) for distance in distances]
    out_outer = [served(q, d) for q, d in zip(asked_outer, distances)]
    back_outer = [shifted(o, "span", d) for o, d in zip(out_outer, distances)]
    asked_inner, out_outer = lax.optimization_barrier((asked_inner, out_outer))
    back_inner = [shifted(served(q, d), "span", d) for q, d in zip(asked_inner, distances)]

    def merge(back, pieces):
        return pl.pallas_call(
            functools.partial(merge_kernel, distances, pieces),
            in_specs=[SMEM] + [VMEM] * (2 + len(back)),
            out_specs=VMEM,
            out_shape=jax.ShapeDtypeStruct((half, width), jnp.bfloat16),
            compiler_params=PARAMS,
            cost_estimate=cost(8 * half * width, 10 * half * width),
            name="merge",
        )(place, own, own_sum, *back)

    attended_outer = merge(back_outer, [(0, quarter), (rows - quarter, quarter)])
    attended_inner = merge(back_inner, [(quarter, half)])

    chunks = 2
    columns = model // chunks
    wide = columns // 2
    last = ranks - 1
    corner = quarter // block

    def stored(target):
        late = target + 2 * corner - ranks
        return jnp.where(target < corner, target, jnp.where(late >= corner, late, target + corner))

    def exchanged(up, down, step):
        return (
            lax.ppermute(up, "tensor", [(i, i + 1) for i in range(step + 1)]),
            lax.ppermute(down, "tensor", [(last - i, last - i - 1) for i in range(step + 1)]),
        )

    projected, arrived = [], []
    for chunk in range(chunks):
        upper, up, down = project(attended_outer, out_weight, chunk, columns, block, wide, ())
        projected.append(upper)
        arrived.append(exchanged(up, down, 0))
    projected = [
        project(attended_inner, out_weight, chunk, columns, block, wide, (projected[chunk],))[0]
        for chunk in range(chunks)
    ]
    for step in range(1, last):
        blocks = jnp.stack([
            stored(jnp.minimum(last - step + rank, last)),
            stored(jnp.maximum(step + rank - last, 0)),
        ])
        for chunk in range(chunks):
            arrived[chunk] = exchanged(*message(blocks, projected[chunk], arrived[chunk], wide), step)
    blocks = jnp.stack([stored(rank), level])
    result = ()
    for chunk in range(chunks):
        result = (final(blocks, projected[chunk], gate_table, arrived[chunk], chunk * columns, wide, result),)
    return result[0]


def solution(mesh):
    return jax.shard_map(
        body,
        mesh=mesh,
        in_specs=(
            P(("group", "span"), "tensor"),
            P(("group", "span"), "tensor"),
            P(("group", "span"), "tensor"),
            P("tensor", None),
            P(),
            P("group"),
            P("group", None),
        ),
        out_specs=P(("group", "span", "tensor"), None),
        check_vma=False,
    )
```

```python
import functools

import jax
import jax.numpy as jnp
from jax import lax
from jax.experimental import pallas as pl
from jax.experimental.pallas import tpu as pltpu
from jax.sharding import PartitionSpec as P

HD = 128
LANES = 128
HIDDEN = -1e30
LOG2E = 1.4426950408889634
PARAMS = pltpu.CompilerParams(vmem_limit_bytes=24 * 1024 * 1024)
ANY = pl.BlockSpec(memory_space=pl.ANY)
HBM = pl.BlockSpec(memory_space=pltpu.HBM)
SMEM = pl.BlockSpec(memory_space=pltpu.SMEM)
VMEM = pl.BlockSpec(memory_space=pltpu.VMEM)
PIECE_LANES = 32


def cost(flops, moved, exps=0):
    return pl.CostEstimate(flops=int(flops), bytes_accessed=int(moved), transcendentals=int(exps))


def shifted(block, axis, distance):
    count = lax.axis_size(axis)
    return lax.ppermute(block, axis, [(i, i + distance) for i in range(count) if 0 <= i + distance < count])


def head_columns(head):
    return slice(head * HD, (head + 1) * HD)


def attend(query, keys, values, flags, write):
    rows, width = query.shape
    scale = LOG2E * HD ** (-0.5)
    lane = lax.broadcasted_iota(jnp.int32, (rows, LANES), 1)
    packed = jnp.zeros((rows, LANES), jnp.float32)
    for head in range(width // HD):
        columns = head_columns(head)
        mine = query[:, columns]
        scores = [
            lax.dot_general(mine, key[:, columns], (((1,), (1,)), ((), ())), preferred_element_type=jnp.float32)
            for key in keys
        ]
        tops = [jnp.max(block, axis=-1, keepdims=True) * scale for block in scores]
        top = functools.reduce(
            jnp.maximum, [one if flag is None else jnp.where(flag, one, HIDDEN) for one, flag in zip(tops, flags)]
        )
        total, product = None, None
        for block, value, flag in zip(scores, values, flags):
            above = top if flag is None else jnp.where(flag, top, -HIDDEN)
            probs = jnp.exp2(block * scale - above)
            part = jnp.sum(probs, axis=-1, keepdims=True)
            part_product = jnp.dot(
                probs.astype(jnp.bfloat16), value[:, columns], preferred_element_type=jnp.float32
            )
            total = part if total is None else total + part
            product = part_product if product is None else product + part_product
        total = jnp.where(total > 0.0, total, 1.0)
        write(columns, product * (1.0 / total))
        packed = jnp.where(lane == head, top + jnp.log2(total), packed)
    return packed


def beside_of(span):
    return span + 1 - 2 * lax.rem(span, 2)


def split_kernel(place, query, outer, semaphores):
    rows = query.shape[0]
    quarter = rows // 4

    @pl.when(place[0] > 1)
    def _():
        copies = [
            pltpu.make_async_copy(
                query.at[pl.ds(start, quarter)], outer.at[pl.ds(index * quarter, quarter)], semaphores.at[index]
            )
            for index, start in enumerate((0, rows - quarter))
        ]
        for copy in copies:
            copy.start()
        for copy in copies:
            copy.wait()


def local_kernel(place, visible, query, key, value, key_beside, value_beside, result, sums):
    span = place[0]

    def write(columns, block):
        result[:, columns] = block

    sums[...] = attend(
        query, [key, key_beside], [value, value_beside], [None, visible[span, beside_of(span)] > 0], write
    )


def served_kernel(distance, spans, place, visible, query, key, value, key_beside, value_beside, result):
    span = place[0]

    @pl.when(span + distance < spans)
    def _():
        asker = jnp.minimum(span + distance, spans - 1)
        flags = [visible[asker, span] > 0, visible[asker, beside_of(span)] > 0]

        def write(columns, block):
            result[:, columns] = block.astype(jnp.bfloat16)

        width = query.shape[1]
        rest = attend(query, [key, key_beside], [value, value_beside], flags, write)
        sent = jnp.zeros_like(rest)
        for piece in range(3):
            part = rest.astype(jnp.bfloat16).astype(jnp.float32)
            sent = sent + (part if piece == 0 else pltpu.roll(part, piece * PIECE_LANES, 1))
            rest = rest - part
        result[:, width:] = sent.astype(jnp.bfloat16)


def merge_kernel(distances, pieces, place, own, own_sum, *refs):
    served, result = refs[:-1], refs[-1]
    width = own.shape[1]
    span = place[0]
    at = 0
    for start, rows in pieces:
        there, here = slice(start, start + rows), slice(at, at + rows)
        sums = [own_sum[there, :]]
        for distance, ref in zip(distances, served):
            sent = ref[here, width:].astype(jnp.float32)
            joined = sent
            for piece in (1, 2):
                joined = joined + pltpu.roll(sent, LANES - piece * PIECE_LANES, 1)
            sums.append(jnp.where(span >= distance, joined, HIDDEN))
        top = functools.reduce(jnp.maximum, sums)
        shares = [jnp.exp2(one - top) for one in sums]
        over = 1.0 / sum(shares)
        shares = [share * over for share in shares]
        for head in range(width // HD):
            columns = head_columns(head)
            merged = own[there, columns] * shares[0][:, head:head + 1]
            for share, ref in zip(shares[1:], served):
                merged = merged + ref[here, columns].astype(jnp.float32) * share[:, head:head + 1]
            result[here, columns] = merged.astype(jnp.bfloat16)
        at += rows


def project_kernel(first, attended, weight, *refs):
    result = refs[-3] if first else refs[-1]
    product = jnp.dot(attended[...], weight[...], preferred_element_type=jnp.float32).astype(jnp.bfloat16)
    result[...] = product
    if first:
        up, down = refs[-2:]
        rows = up.shape[0]
        up[...] = product[product.shape[0] - rows:]
        down[...] = product[:rows]


def project(attended, weight, chunk, columns, rows, tile, before):
    half, width = attended.shape
    start = chunk * columns // tile
    first = not before
    place = 0 if first else 1
    piece = pl.BlockSpec((rows, tile), lambda j: (0, j))
    message = jax.ShapeDtypeStruct((rows, columns), jnp.bfloat16)
    return pl.pallas_call(
        functools.partial(project_kernel, first),
        grid=(columns // tile,),
        in_specs=[
            pl.BlockSpec((half, width), lambda j: (0, 0)),
            pl.BlockSpec((width, tile), lambda j: (0, start + j)),
        ] + [ANY] * len(before),
        out_specs=[pl.BlockSpec((half, tile), lambda j: (place, j))] + [piece, piece] * first,
        out_shape=[jax.ShapeDtypeStruct((2 * half, columns), jnp.bfloat16)] + [message, message] * first,
        input_output_aliases={} if first else {2: 0},
        compiler_params=PARAMS,
        cost_estimate=cost(2 * half * width * columns, 2 * width * columns + 4 * half * columns),
        name="project",
    )(attended, weight, *before)


def message_kernel(blocks, up_block, down_block, up_arrived, down_arrived, up, down):
    up[...] = (up_block[...].astype(jnp.float32) + up_arrived[...].astype(jnp.float32)).astype(jnp.bfloat16)
    down[...] = (down_block[...].astype(jnp.float32) + down_arrived[...].astype(jnp.float32)).astype(jnp.bfloat16)


def message(blocks, projected, arrived, tile):
    rows, columns = arrived[0].shape
    piece = pl.BlockSpec((rows, tile), lambda j, b: (0, j))
    return pl.pallas_call(
        message_kernel,
        grid_spec=pltpu.PrefetchScalarGridSpec(
            num_scalar_prefetch=1,
            grid=(columns // tile,),
            in_specs=[
                pl.BlockSpec((rows, tile), lambda j, b: (b[0], j)),
                pl.BlockSpec((rows, tile), lambda j, b: (b[1], j)),
                piece,
                piece,
            ],
            out_specs=[piece, piece],
        ),
        out_shape=[jax.ShapeDtypeStruct((rows, columns), jnp.bfloat16)] * 2,
        compiler_params=PARAMS,
        cost_estimate=cost(4 * rows * columns, 12 * rows * columns),
        name="message",
    )(blocks, projected, projected, *arrived)


def final_kernel(blocks, own, gate, up, down, *refs):
    result = refs[-1]
    summed = own[...].astype(jnp.float32) + up[...].astype(jnp.float32) + down[...].astype(jnp.float32)
    result[...] = (summed * gate[pl.ds(lax.rem(blocks[1], 8), 1), :]).astype(jnp.bfloat16)


def final(blocks, projected, gate_table, arrived, first, tile, before):
    rows, columns = arrived[0].shape
    start = first // tile
    piece = pl.BlockSpec((rows, tile), lambda j, b: (0, j))
    return pl.pallas_call(
        final_kernel,
        grid_spec=pltpu.PrefetchScalarGridSpec(
            num_scalar_prefetch=1,
            grid=(columns // tile,),
            in_specs=[
                pl.BlockSpec((rows, tile), lambda j, b: (b[0], j)),
                pl.BlockSpec((8, tile), lambda j, b: (b[1] // 8, start + j)),
                piece,
                piece,
            ] + [ANY] * len(before),
            out_specs=pl.BlockSpec((rows, tile), lambda j, b: (0, start + j)),
        ),
        out_shape=jax.ShapeDtypeStruct((rows, gate_table.shape[1]), jnp.bfloat16),
        input_output_aliases={5: 0} if before else {},
        compiler_params=PARAMS,
        cost_estimate=cost(4 * rows * columns, 10 * rows * columns),
        name="final",
    )(blocks, projected, gate_table, *arrived, *before)


def body(queries, keys, values, out_weight, gate_table, levels, visible):
    rows, width = queries.shape
    model = out_weight.shape[1]
    spans = lax.axis_size("span")
    ranks = lax.axis_size("tensor")
    span = lax.axis_index("span")
    rank = lax.axis_index("tensor")
    block = rows // ranks
    quarter = rows // 4
    half = 2 * quarter
    place = jnp.stack([span, rank]).astype(jnp.int32)
    level = levels[span]

    query_outer = pl.pallas_call(
        split_kernel,
        in_specs=[SMEM, HBM],
        out_specs=VMEM,
        out_shape=jax.ShapeDtypeStruct((half, width), queries.dtype),
        scratch_shapes=[pltpu.SemaphoreType.DMA((2,))],
        compiler_params=PARAMS,
        cost_estimate=cost(0, 2 * rows * width),
        name="split",
    )(place, pltpu.with_memory_space_constraint(queries, pltpu.HBM))
    query_inner = queries[quarter:rows - quarter]
    distances = list(range(2, spans, 2))
    asked_outer = [shifted(query_outer, "span", -distance) for distance in distances]
    swap = [(i, i + 1 - 2 * (i % 2)) for i in range(spans)]
    key_beside = lax.ppermute(keys, "span", swap)
    value_beside = lax.ppermute(values, "span", swap)

    own, own_sum = pl.pallas_call(
        local_kernel,
        in_specs=[SMEM, SMEM] + [VMEM] * 5,
        out_specs=[VMEM] * 2,
        out_shape=[
            jax.ShapeDtypeStruct((rows, width), jnp.float32),
            jax.ShapeDtypeStruct((rows, LANES), jnp.float32),
        ],
        compiler_params=PARAMS,
        cost_estimate=cost(8 * rows * rows * width, 14 * rows * width, 2 * rows * rows * width // HD),
        name="local",
    )(place, visible, queries, keys, values, key_beside, value_beside)

    def served(asked, distance):
        return pl.pallas_call(
            functools.partial(served_kernel, distance, spans),
            in_specs=[SMEM, SMEM] + [VMEM] * 5,
            out_specs=VMEM,
            out_shape=jax.ShapeDtypeStruct((half, width + LANES), jnp.bfloat16),
            compiler_params=PARAMS,
            cost_estimate=cost(8 * half * rows * width, 12 * rows * width, 2 * half * rows * width // HD),
            name="served",
        )(place, visible, asked, keys, values, key_beside, value_beside)

    asked_inner = [shifted(query_inner, "span", -distance) for distance in distances]
    asked_outer, own_sum = lax.optimization_barrier((asked_outer, own_sum))
    back_outer = [shifted(served(q, d), "span", d) for q, d in zip(asked_outer, distances)]
    out_inner = [served(q, d) for q, d in zip(asked_inner, distances)]
    back_outer, out_inner = lax.optimization_barrier((back_outer, out_inner))
    back_inner = [shifted(o, "span", d) for o, d in zip(out_inner, distances)]

    def merge(back, pieces):
        return pl.pallas_call(
            functools.partial(merge_kernel, distances, pieces),
            in_specs=[SMEM] + [VMEM] * (2 + len(back)),
            out_specs=VMEM,
            out_shape=jax.ShapeDtypeStruct((half, width), jnp.bfloat16),
            compiler_params=PARAMS,
            cost_estimate=cost(8 * half * width, 10 * half * width),
            name="merge",
        )(place, own, own_sum, *back)

    attended_outer = merge(back_outer, [(0, quarter), (rows - quarter, quarter)])
    attended_inner = merge(back_inner, [(quarter, half)])

    chunks = 2
    columns = model // chunks
    tile = columns // 4
    wide = columns // 3
    last = ranks - 1
    corner = quarter // block

    def stored(target):
        late = target + 2 * corner - ranks
        return jnp.where(target < corner, target, jnp.where(late >= corner, late, target + corner))

    def exchanged(up, down, step):
        return (
            lax.ppermute(up, "tensor", [(i, i + 1) for i in range(step + 1)]),
            lax.ppermute(down, "tensor", [(last - i, last - i - 1) for i in range(step + 1)]),
        )

    out_weight = pltpu.with_memory_space_constraint(out_weight, pltpu.HBM)
    projected, arrived = [], []
    for chunk in range(chunks):
        upper, up, down = project(attended_outer, out_weight, chunk, columns, block, tile, ())
        projected.append(upper)
        arrived.append(exchanged(up, down, 0))
    projected = [
        project(attended_inner, out_weight, chunk, columns, block, tile, (projected[chunk],))[0]
        for chunk in range(chunks)
    ]
    for step in range(1, last):
        blocks = jnp.stack([
            stored(jnp.minimum(last - step + rank, last)),
            stored(jnp.maximum(step + rank - last, 0)),
        ])
        for chunk in range(chunks):
            arrived[chunk] = exchanged(*message(blocks, projected[chunk], arrived[chunk], wide), step)
    blocks = jnp.stack([stored(rank), level])
    result = ()
    for chunk in range(chunks):
        result = (final(blocks, projected[chunk], gate_table, arrived[chunk], chunk * columns, wide, result),)
    return result[0]


def solution(mesh):
    return jax.shard_map(
        body,
        mesh=mesh,
        in_specs=(
            P(("group", "span"), "tensor"),
            P(("group", "span"), "tensor"),
            P(("group", "span"), "tensor"),
            P("tensor", None),
            P(),
            P("group"),
            P("group", None),
        ),
        out_specs=P(("group", "span", "tensor"), None),
        check_vma=False,
    )
```

```python
import functools

import jax
import jax.numpy as jnp
from jax import lax
from jax.experimental import pallas as pl
from jax.experimental.pallas import tpu as pltpu
from jax.sharding import PartitionSpec as P

HD = 128
LANES = 128
HIDDEN = -1e30
LOG2E = 1.4426950408889634
PARAMS = pltpu.CompilerParams(vmem_limit_bytes=24 * 1024 * 1024)
SMEM = pl.BlockSpec(memory_space=pltpu.SMEM)
VMEM = pl.BlockSpec(memory_space=pltpu.VMEM)
ANY = pl.BlockSpec(memory_space=pl.ANY)
HBM = pl.BlockSpec(memory_space=pltpu.HBM)
PIECE_LANES = 32
SHORT = pl.CostEstimate(flops=1, bytes_accessed=1, transcendentals=0)


def in_hbm(array):
    return pltpu.with_memory_space_constraint(array, pltpu.HBM)


def shifted(block, axis, distance):
    count = lax.axis_size(axis)
    return lax.ppermute(block, axis, [(i, i + distance) for i in range(count) if 0 <= i + distance < count])


def head_columns(head):
    return slice(head * HD, (head + 1) * HD)


def attend(query, keys, values, flags, write):
    rows, width = query.shape
    scale = LOG2E * HD ** (-0.5)
    lane = lax.broadcasted_iota(jnp.int32, (rows, LANES), 1)
    packed = jnp.zeros((rows, LANES), jnp.float32)
    for head in range(width // HD):
        columns = head_columns(head)
        mine = query[:, columns]
        scores = [
            lax.dot_general(mine, key[:, columns], (((1,), (1,)), ((), ())), preferred_element_type=jnp.float32)
            for key in keys
        ]
        tops = [jnp.max(block, axis=-1, keepdims=True) * scale for block in scores]
        top = functools.reduce(
            jnp.maximum, [one if flag is None else jnp.where(flag, one, HIDDEN) for one, flag in zip(tops, flags)]
        )
        total, product = None, None
        for block, value, flag in zip(scores, values, flags):
            above = top if flag is None else jnp.where(flag, top, -HIDDEN)
            probs = jnp.exp2(block * scale - above)
            part = jnp.sum(probs, axis=-1, keepdims=True)
            part_product = jnp.dot(
                probs.astype(jnp.bfloat16), value[:, columns], preferred_element_type=jnp.float32
            )
            total = part if total is None else total + part
            product = part_product if product is None else product + part_product
        total = jnp.where(total > 0.0, total, 1.0)
        write(columns, product * (1.0 / total))
        packed = jnp.where(lane == head, top + jnp.log2(total), packed)
    return packed


class Facts:
    def __init__(self, ref, spans):
        self.ref, self.spans = ref, spans
        self.span, self.rank = ref[spans, 0], ref[spans, 1]
        self.beside = self.span + 1 - 2 * lax.rem(self.span, 2)

    def sees(self, asker, span):
        return self.ref[asker, span] > 0

    def level(self):
        return self.ref[self.spans + 1, self.span]


def copied(source, target, semaphore):
    copy = pltpu.make_async_copy(source, target, semaphore)
    copy.start()
    return copy


def split_kernel(spans, facts, query, outer, inner, semaphores):
    rows = query.shape[0]
    quarter = rows // 4

    @pl.when(Facts(facts, spans).span > 1)
    def _():
        copies = [
            copied(query.at[pl.ds(0, quarter)], outer.at[pl.ds(0, quarter)], semaphores.at[0]),
            copied(query.at[pl.ds(rows - quarter, quarter)], outer.at[pl.ds(quarter, quarter)], semaphores.at[1]),
            copied(query.at[pl.ds(quarter, 2 * quarter)], inner, semaphores.at[2]),
        ]
        for copy in copies:
            copy.wait()


def local_kernel(spans, facts, query, key, value, key_beside, value_beside, result, sums, *scratch):
    here = Facts(facts, spans)
    query_, key_, value_, key_beside_, value_beside_, semaphores = scratch
    copies = [
        copied(source, target, semaphores.at[index])
        for index, (source, target) in enumerate((
            (query, query_), (key, key_), (key_beside, key_beside_), (value, value_), (value_beside, value_beside_),
        ))
    ]
    for copy in copies:
        copy.wait()

    def write(columns, block):
        result[:, columns] = block

    flags = [None, here.sees(here.span, here.beside)]
    sums[...] = attend(query_, [key_, key_beside_], [value_, value_beside_], flags, write)


def served_kernel(distance, spans, facts, query, key, value, key_beside, value_beside, result):
    here = Facts(facts, spans)

    @pl.when(here.span + distance < spans)
    def _():
        asker = jnp.minimum(here.span + distance, spans - 1)
        flags = [here.sees(asker, here.span), here.sees(asker, here.beside)]

        def write(columns, block):
            result[:, columns] = block.astype(jnp.bfloat16)

        width = query.shape[1]
        rest = attend(query, [key, key_beside], [value, value_beside], flags, write)
        sent = jnp.zeros_like(rest)
        for piece in range(3):
            part = rest.astype(jnp.bfloat16).astype(jnp.float32)
            sent = sent + (part if piece == 0 else pltpu.roll(part, piece * PIECE_LANES, 1))
            rest = rest - part
        result[:, width:] = sent.astype(jnp.bfloat16)


def merge(span, distances, own, own_sum, there, served, here, write):
    width = own.shape[1]
    sums = [own_sum[there, :]]
    for distance, ref in zip(distances, served):
        sent = ref[here, width:].astype(jnp.float32)
        joined = sent
        for piece in (1, 2):
            joined = joined + pltpu.roll(sent, LANES - piece * PIECE_LANES, 1)
        sums.append(jnp.where(span >= distance, joined, HIDDEN))
    top = functools.reduce(jnp.maximum, sums)
    shares = [jnp.exp2(one - top) for one in sums]
    over = 1.0 / sum(shares)
    shares = [share * over for share in shares]
    for head in range(width // HD):
        columns = head_columns(head)
        merged = own[there, columns] * shares[0][:, head:head + 1]
        for distance, share, ref in zip(distances, shares[1:], served):
            away = jnp.where(span >= distance, ref[here, columns].astype(jnp.float32), 0.0)
            merged = merged + away * share[:, head:head + 1]
        write(columns, merged.astype(jnp.bfloat16))


def opening_kernel(spans, ranks, distances, first, facts, own, own_sum, *refs):
    served = refs[:len(distances)]
    weight, result, tiles, rows, semaphores = refs[len(distances):]
    here = Facts(facts, spans)
    block, width = rows.shape
    count, _, tile = tiles.shape

    @pl.when(jnp.logical_or(here.rank == 0, here.rank == ranks - 1))
    def _():
        copies = [
            copied(weight.at[:, pl.ds(first + index * tile, tile)], tiles.at[index], semaphores.at[index])
            for index in range(count)
        ]
        lowest = here.rank == 0
        there = pl.ds(pl.multiple_of(jnp.where(lowest, own.shape[0] - block, 0), block), block)
        back = pl.ds(pl.multiple_of(jnp.where(lowest, own.shape[0] // 2 - block, 0), block), block)

        def write(columns, part):
            rows[:, columns] = part

        merge(here.span, distances, own, own_sum, there, served, back, write)
        for index, copy in enumerate(copies):
            copy.wait()
            product = jnp.dot(rows[...], tiles[index], preferred_element_type=jnp.float32)
            result[:, index * tile:(index + 1) * tile] = product.astype(jnp.bfloat16)


def project_kernel(spans, distances, facts, own, own_sum, *refs):
    count = len(distances)
    outer, inner = refs[:count], refs[count:2 * count]
    weight, result, tiles, products, attended, semaphores, out_semaphores = refs[2 * count:]
    here = Facts(facts, spans)
    total = own.shape[0]
    quarter = total // 4
    copies = [
        copied(weight.at[:, pl.ds(index * tiles.shape[2], tiles.shape[2])], tiles.at[index], semaphores.at[index])
        for index in range(tiles.shape[0])
    ]
    for served, pieces in (
        (outer, ((0, 0, quarter), (total - quarter, quarter, quarter))),
        (inner, ((quarter, 0, 2 * quarter),)),
    ):
        for start, at, size in pieces:
            there, back = slice(start, start + size), slice(at, at + size)

            def write(columns, part):
                attended[there, columns] = part

            merge(here.span, distances, own, own_sum, there, served, back, write)
    sent = []
    for index, copy in enumerate(copies):
        copy.wait()
        product = jnp.dot(attended[...], tiles[index], preferred_element_type=jnp.float32)
        products[index] = product.astype(jnp.bfloat16)
        columns = pl.ds(index * tiles.shape[2], tiles.shape[2])
        sent.append(copied(products.at[index], result.at[:, columns], out_semaphores.at[index]))
    for copy in sent:
        copy.wait()


def final_kernel(count, facts, row, own, gate, *refs):
    result = refs[-1]
    summed = own[...].astype(jnp.float32) + sum(ref[...].astype(jnp.float32) for ref in refs[:count])
    result[...] = (summed * gate[pl.ds(row[1], 1), :]).astype(jnp.bfloat16)


def final(facts, row, projected, gate_table, comes, first, tile, before):
    rows, columns = comes[0].shape
    start = first // tile
    piece = pl.BlockSpec((rows, tile), lambda j, f, r: (0, j))
    return pl.pallas_call(
        functools.partial(final_kernel, len(comes)),
        grid_spec=pltpu.PrefetchScalarGridSpec(
            num_scalar_prefetch=2,
            grid=(columns // tile,),
            in_specs=[
                pl.BlockSpec((rows, tile), lambda j, f, r: (r[2], start + j)),
                pl.BlockSpec((8, tile), lambda j, f, r: (r[0], start + j)),
            ] + [piece] * len(comes) + [ANY] * len(before),
            out_specs=pl.BlockSpec((rows, tile), lambda j, f, r: (0, start + j)),
        ),
        out_shape=jax.ShapeDtypeStruct((rows, gate_table.shape[1]), jnp.bfloat16),
        input_output_aliases={4 + len(comes): 0} if before else {},
        compiler_params=PARAMS,
        cost_estimate=SHORT,
        name="final",
    )(facts, row, in_hbm(projected), in_hbm(gate_table), *comes, *before)


def body(queries, keys, values, out_weight, gate_table, levels, visible):
    rows, width = queries.shape
    model = out_weight.shape[1]
    spans = lax.axis_size("span")
    ranks = lax.axis_size("tensor")
    span = lax.axis_index("span")
    rank = lax.axis_index("tensor")
    block = rows // ranks
    half = rows // 2
    bf16, f32 = jnp.bfloat16, jnp.float32
    numbers = jnp.arange(spans, dtype=jnp.int32)
    place = jnp.where(numbers == 0, span, jnp.where(numbers == 1, rank, 0)).astype(jnp.int32)
    facts = jnp.concatenate([visible, place[None, :], levels[None, :]], axis=0)
    level = jnp.sum(jnp.where(numbers == span, levels, 0))
    row = jnp.stack([level // 8, level % 8, rank]).astype(jnp.int32)

    query_outer, query_inner = pl.pallas_call(
        functools.partial(split_kernel, spans),
        in_specs=[SMEM, HBM],
        out_specs=[VMEM, VMEM],
        out_shape=[jax.ShapeDtypeStruct((half, width), bf16)] * 2,
        scratch_shapes=[pltpu.SemaphoreType.DMA((3,))],
        compiler_params=PARAMS,
        cost_estimate=SHORT,
        name="split",
    )(facts, in_hbm(queries))
    distances = list(range(2, spans, 2))
    asked_outer = [shifted(query_outer, "span", -distance) for distance in distances]
    swap = [(i, i + 1 - 2 * (i % 2)) for i in range(spans)]
    key_beside = lax.ppermute(keys, "span", swap)
    value_beside = lax.ppermute(values, "span", swap)

    own, own_sum = pl.pallas_call(
        functools.partial(local_kernel, spans),
        in_specs=[SMEM, HBM, HBM, HBM, ANY, ANY],
        out_specs=[VMEM] * 2,
        out_shape=[jax.ShapeDtypeStruct((rows, width), f32), jax.ShapeDtypeStruct((rows, LANES), f32)],
        scratch_shapes=[pltpu.VMEM((rows, width), bf16)] * 5 + [pltpu.SemaphoreType.DMA((5,))],
        compiler_params=PARAMS,
        cost_estimate=SHORT,
        name="local",
    )(facts, in_hbm(queries), in_hbm(keys), in_hbm(values), key_beside, value_beside)

    def served(asked, distance):
        return pl.pallas_call(
            functools.partial(served_kernel, distance, spans),
            in_specs=[SMEM] + [VMEM] * 5,
            out_specs=VMEM,
            out_shape=jax.ShapeDtypeStruct((half, width + LANES), bf16),
            compiler_params=PARAMS,
            cost_estimate=SHORT,
            name="served",
        )(facts, asked, keys, values, key_beside, value_beside)

    asked_outer, query_inner, own_sum = lax.optimization_barrier((asked_outer, query_inner, own_sum))
    asked_inner = [shifted(query_inner, "span", -distance) for distance in distances]
    out_outer = [served(q, d) for q, d in zip(asked_outer, distances)]
    back_outer = [shifted(o, "span", d) for o, d in zip(out_outer, distances)]
    asked_inner, out_outer = lax.optimization_barrier((asked_inner, out_outer))
    out_inner = [served(q, d) for q, d in zip(asked_inner, distances)]
    back_outer, out_inner = lax.optimization_barrier((back_outer, out_inner))
    back_inner = [shifted(o, "span", d) for o, d in zip(out_inner, distances)]

    chunks = 2
    columns = model // chunks
    tile = columns // 4
    last = ranks - 1
    weight = in_hbm(out_weight)

    def opening(chunk):
        return pl.pallas_call(
            functools.partial(opening_kernel, spans, ranks, distances, chunk * columns),
            in_specs=[SMEM] + [VMEM] * (2 + len(distances)) + [HBM],
            out_specs=VMEM,
            out_shape=jax.ShapeDtypeStruct((block, columns), bf16),
            scratch_shapes=[
                pltpu.VMEM((4, width, tile), bf16),
                pltpu.VMEM((block, width), bf16),
                pltpu.SemaphoreType.DMA((4,)),
            ],
            compiler_params=PARAMS,
            cost_estimate=SHORT,
            name="opening",
        )(facts, own, own_sum, *back_outer, weight)

    def hopped(sent, hop):
        return lax.ppermute(sent, "tensor", [(hop, hop + 1), (last - hop, last - hop - 1)])

    openings = [opening(chunk) for chunk in range(chunks)]
    arrived = [[hopped(sent, 0)] for sent in openings]
    back_inner, openings = lax.optimization_barrier((back_inner, openings))
    projected = pl.pallas_call(
        functools.partial(project_kernel, spans, distances),
        in_specs=[SMEM] + [VMEM] * (2 + 2 * len(distances)) + [HBM],
        out_specs=HBM,
        out_shape=jax.ShapeDtypeStruct((rows, model), bf16),
        scratch_shapes=[
            pltpu.VMEM((8, width, model // 8), bf16),
            pltpu.VMEM((8, rows, model // 8), bf16),
            pltpu.VMEM((rows, width), bf16),
            pltpu.SemaphoreType.DMA((8,)),
            pltpu.SemaphoreType.DMA((8,)),
        ],
        compiler_params=PARAMS,
        cost_estimate=SHORT,
        name="project",
    )(facts, own, own_sum, *back_outer, *back_inner, weight)

    for step in range(1, last):
        for chunk in range(chunks):
            comes = arrived[chunk]
            leaves = []
            for hop in range(step + 1):
                target = last - (step - hop)
                index = jnp.where(rank == hop, target, last - target)
                sent = lax.dynamic_slice(projected, (index * block, chunk * columns), (block, columns))
                if hop:
                    sent = (sent.astype(f32) + comes[hop - 1].astype(f32)).astype(bf16)
                else:
                    sent, comes[0] = lax.optimization_barrier((sent, comes[0]))
                leaves.append(hopped(sent, hop))
            arrived[chunk] = leaves
    result = ()
    for chunk in range(chunks):
        result = (final(facts, row, projected, gate_table, arrived[chunk], chunk * columns, columns // 2, result),)
    return result[0]


def solution(mesh):
    return jax.shard_map(
        body,
        mesh=mesh,
        in_specs=(
            P(("group", "span"), "tensor"),
            P(("group", "span"), "tensor"),
            P(("group", "span"), "tensor"),
            P("tensor", None),
            P(),
            P("group"),
            P("group", None),
        ),
        out_specs=P(("group", "span", "tensor"), None),
        check_vma=False,
    )
```

```python
import functools

import jax
import jax.numpy as jnp
from jax import lax
from jax.experimental import pallas as pl
from jax.experimental.pallas import tpu as pltpu
from jax.sharding import PartitionSpec as P

HD = 128
LANES = 128
HIDDEN = -1e30
LOG2E = 1.4426950408889634
PARAMS = pltpu.CompilerParams(vmem_limit_bytes=24 * 1024 * 1024)
SMEM = pl.BlockSpec(memory_space=pltpu.SMEM)
VMEM = pl.BlockSpec(memory_space=pltpu.VMEM)
ANY = pl.BlockSpec(memory_space=pl.ANY)
HBM = pl.BlockSpec(memory_space=pltpu.HBM)
PIECE_LANES = 32
SHORT = pl.CostEstimate(flops=1, bytes_accessed=1, transcendentals=0)


def in_hbm(array):
    return pltpu.with_memory_space_constraint(array, pltpu.HBM)


def shifted(block, axis, distance):
    count = lax.axis_size(axis)
    return lax.ppermute(block, axis, [(i, i + distance) for i in range(count) if 0 <= i + distance < count])


def head_columns(head):
    return slice(head * HD, (head + 1) * HD)


def attend(query, keys, values, flags, write):
    rows, width = query.shape
    scale = LOG2E * HD ** (-0.5)
    lane = lax.broadcasted_iota(jnp.int32, (rows, LANES), 1)
    packed = jnp.zeros((rows, LANES), jnp.float32)
    for head in range(width // HD):
        columns = head_columns(head)
        mine = query[:, columns]
        scores = [
            lax.dot_general(mine, key[:, columns], (((1,), (1,)), ((), ())), preferred_element_type=jnp.float32)
            for key in keys
        ]
        tops = [jnp.max(block, axis=-1, keepdims=True) * scale for block in scores]
        top = functools.reduce(
            jnp.maximum, [one if flag is None else jnp.where(flag, one, HIDDEN) for one, flag in zip(tops, flags)]
        )
        total, product = None, None
        for block, value, flag in zip(scores, values, flags):
            above = top if flag is None else jnp.where(flag, top, -HIDDEN)
            probs = jnp.exp2(block * scale - above)
            part = jnp.sum(probs, axis=-1, keepdims=True)
            part_product = jnp.dot(
                probs.astype(jnp.bfloat16), value[:, columns], preferred_element_type=jnp.float32
            )
            total = part if total is None else total + part
            product = part_product if product is None else product + part_product
        total = jnp.where(total > 0.0, total, 1.0)
        write(columns, product * (1.0 / total))
        packed = jnp.where(lane == head, top + jnp.log2(total), packed)
    return packed


class Facts:
    def __init__(self, ref, spans):
        self.ref, self.spans = ref, spans
        self.span, self.rank = ref[spans, 0], ref[spans, 1]
        self.beside = self.span + 1 - 2 * lax.rem(self.span, 2)

    def sees(self, asker, span):
        return self.ref[asker, span] > 0

    def level(self):
        return self.ref[self.spans + 1, self.span]


def copied(source, target, semaphore):
    copy = pltpu.make_async_copy(source, target, semaphore)
    copy.start()
    return copy


def parts_of(rank, ranks, rows):
    block = rows // ranks
    lower = rank < ranks // 2
    early = pl.multiple_of(jnp.where(lower, rows - block, 0), block)
    late = pl.multiple_of(jnp.where(lower, 0, block), block)
    return (early, block), (late, rows - block)


def split_kernel(spans, ranks, facts, query, early, late, semaphores):
    here = Facts(facts, spans)

    @pl.when(here.span > 1)
    def _():
        copies = [
            copied(query.at[pl.ds(start, size)], target, semaphores.at[index])
            for index, ((start, size), target) in enumerate(
                zip(parts_of(here.rank, ranks, query.shape[0]), (early, late))
            )
        ]
        for copy in copies:
            copy.wait()


def local_kernel(spans, facts, query, key, value, key_beside, value_beside, result, sums, *scratch):
    here = Facts(facts, spans)
    query_, key_, value_, key_beside_, value_beside_, semaphores = scratch
    copies = [
        copied(source, target, semaphores.at[index])
        for index, (source, target) in enumerate((
            (query, query_), (key, key_), (key_beside, key_beside_), (value, value_), (value_beside, value_beside_),
        ))
    ]
    for copy in copies:
        copy.wait()

    def write(columns, block):
        result[:, columns] = block

    flags = [None, here.sees(here.span, here.beside)]
    sums[...] = attend(query_, [key_, key_beside_], [value_, value_beside_], flags, write)


def served_kernel(distance, spans, facts, query, key, value, key_beside, value_beside, result):
    here = Facts(facts, spans)

    @pl.when(here.span + distance < spans)
    def _():
        asker = jnp.minimum(here.span + distance, spans - 1)
        flags = [here.sees(asker, here.span), here.sees(asker, here.beside)]

        def write(columns, block):
            result[:, columns] = block.astype(jnp.bfloat16)

        width = query.shape[1]
        rest = attend(query, [key, key_beside], [value, value_beside], flags, write)
        sent = jnp.zeros_like(rest)
        for piece in range(3):
            part = rest.astype(jnp.bfloat16).astype(jnp.float32)
            sent = sent + (part if piece == 0 else pltpu.roll(part, piece * PIECE_LANES, 1))
            rest = rest - part
        result[:, width:] = sent.astype(jnp.bfloat16)


def merge(span, distances, own, own_sum, there, served, here, write):
    width = own.shape[1]
    sums = [own_sum[there, :]]
    for distance, ref in zip(distances, served):
        sent = ref[here, width:].astype(jnp.float32)
        joined = sent
        for piece in (1, 2):
            joined = joined + pltpu.roll(sent, LANES - piece * PIECE_LANES, 1)
        sums.append(jnp.where(span >= distance, joined, HIDDEN))
    top = functools.reduce(jnp.maximum, sums)
    shares = [jnp.exp2(one - top) for one in sums]
    over = 1.0 / sum(shares)
    shares = [share * over for share in shares]
    for head in range(width // HD):
        columns = head_columns(head)
        merged = own[there, columns] * shares[0][:, head:head + 1]
        for distance, share, ref in zip(distances, shares[1:], served):
            away = jnp.where(span >= distance, ref[here, columns].astype(jnp.float32), 0.0)
            merged = merged + away * share[:, head:head + 1]
        write(columns, merged.astype(jnp.bfloat16))


def streamed(weight, first, tiles, semaphores):
    count, _, tile = tiles.shape
    return [
        copied(weight.at[:, pl.ds(first + index * tile, tile)], tiles.at[index], semaphores.at[index])
        for index in range(count)
    ]


def opening_kernel(spans, ranks, distances, first, facts, own, own_sum, *refs):
    served = refs[:len(distances)]
    weight, result, tiles, rows, semaphores = refs[len(distances):]
    here = Facts(facts, spans)
    tile = tiles.shape[2]

    @pl.when(jnp.logical_or(here.rank == 0, here.rank == ranks - 1))
    def _():
        copies = streamed(weight, first, tiles, semaphores)
        (start, size), _ = parts_of(here.rank, ranks, own.shape[0])

        def write(columns, part):
            rows[:, columns] = part

        merge(here.span, distances, own, own_sum, pl.ds(start, size), served, slice(0, size), write)
        for index, copy in enumerate(copies):
            copy.wait()
            product = jnp.dot(rows[...], tiles[index], preferred_element_type=jnp.float32)
            result[:, index * tile:(index + 1) * tile] = product.astype(jnp.bfloat16)


def project_rows(rank, ranks, first, attended, weight, result, leaving, tiles, products, semaphores, out_semaphores):
    count, width, tile = tiles.shape
    block = attended.shape[0] // ranks
    last = ranks - 1
    copies = streamed(weight, first, tiles, semaphores)
    yield
    sent = []
    for index, copy in enumerate(copies):
        copy.wait()
        product = jnp.dot(attended[...], tiles[index], preferred_element_type=jnp.float32)
        products[index] = product.astype(jnp.bfloat16)
        columns = pl.ds(index * tile, tile)
        sent.append(copied(products.at[index], result.at[:, columns], out_semaphores.at[index]))
        for step, target in enumerate(leaving, start=1):
            start = pl.multiple_of(jnp.where(rank == 0, last - step, step) * block, block)
            sent.append(copied(
                products.at[index, pl.ds(start, block)], target.at[:, columns], out_semaphores.at[step * count + index]
            ))
    for copy in sent:
        copy.wait()


def project_first_kernel(spans, ranks, distances, facts, own, own_sum, *refs):
    count = len(distances)
    early, late = refs[:count], refs[count:2 * count]
    weight, attended, result = refs[2 * count:2 * count + 3]
    leaving, scratch = refs[2 * count + 3:-4], refs[-4:]
    here = Facts(facts, spans)
    work = project_rows(here.rank, ranks, 0, attended, weight, result, leaving, *scratch)
    next(work)
    for (start, size), served in zip(parts_of(here.rank, ranks, own.shape[0]), (early, late)):
        there = pl.ds(start, size)

        def write(columns, part):
            attended[there, columns] = part

        merge(here.span, distances, own, own_sum, there, served, slice(0, size), write)
    for _ in work:
        pass


def project_next_kernel(spans, ranks, first, facts, attended, weight, result, *refs):
    leaving, scratch = refs[:-4], refs[-4:]
    here = Facts(facts, spans)
    for _ in project_rows(here.rank, ranks, first, attended, weight, result, leaving, *scratch):
        pass


def message_kernel(spans, ranks, hop, target, facts, projected, arrived, result, own, semaphores):
    here = Facts(facts, spans)
    block = result.shape[0]
    last = ranks - 1

    @pl.when(jnp.logical_or(here.rank == hop, here.rank == last - hop))
    def _():
        start = pl.multiple_of(jnp.where(here.rank == hop, target, last - target) * block, block)
        copied(projected.at[pl.ds(start, block)], own, semaphores.at[0]).wait()
        result[...] = (own[...].astype(jnp.float32) + arrived[...].astype(jnp.float32)).astype(jnp.bfloat16)


def final_kernel(spans, ranks, count, first, facts, projected, gate_table, *refs):
    comes, (result, own, gate, gated, semaphores) = refs[:count], refs[-5:]
    here = Facts(facts, spans)
    block, columns = own.shape
    pieces = gated.shape[0]
    wide = columns // pieces
    level = here.level()
    above = pl.multiple_of(level // 8 * 8, 8)
    copies = [
        copied(projected.at[pl.ds(pl.multiple_of(here.rank * block, block), block)], own, semaphores.at[0]),
        copied(gate_table.at[pl.ds(above, 8), pl.ds(first, columns)], gate, semaphores.at[1]),
    ]
    for copy in copies:
        copy.wait()
    sent = []
    for piece in range(pieces):
        there = slice(piece * wide, (piece + 1) * wide)
        summed = own[:, there].astype(jnp.float32) + sum(ref[:, there].astype(jnp.float32) for ref in comes)
        gated[piece] = (summed * gate[pl.ds(lax.rem(level, 8), 1), there]).astype(jnp.bfloat16)
        sent.append(copied(
            gated.at[piece], result.at[:, pl.ds(first + piece * wide, wide)], semaphores.at[2 + piece]
        ))
    for copy in sent:
        copy.wait()


def body(queries, keys, values, out_weight, gate_table, levels, visible):
    rows, width = queries.shape
    model = out_weight.shape[1]
    spans = lax.axis_size("span")
    ranks = lax.axis_size("tensor")
    span = lax.axis_index("span")
    rank = lax.axis_index("tensor")
    block = rows // ranks
    bf16, f32 = jnp.bfloat16, jnp.float32
    numbers = jnp.arange(spans, dtype=jnp.int32)
    place = jnp.where(numbers == 0, span, jnp.where(numbers == 1, rank, 0)).astype(jnp.int32)
    facts = jnp.concatenate([visible, place[None, :], levels[None, :]], axis=0)

    query_early, query_late = pl.pallas_call(
        functools.partial(split_kernel, spans, ranks),
        in_specs=[SMEM, HBM],
        out_specs=[VMEM, VMEM],
        out_shape=[
            jax.ShapeDtypeStruct((block, width), bf16),
            jax.ShapeDtypeStruct((rows - block, width), bf16),
        ],
        scratch_shapes=[pltpu.SemaphoreType.DMA((2,))],
        compiler_params=PARAMS,
        cost_estimate=SHORT,
        name="split",
    )(facts, in_hbm(queries))
    distances = list(range(2, spans, 2))
    asked_early = [shifted(query_early, "span", -distance) for distance in distances]
    asked_late = [shifted(query_late, "span", -distance) for distance in distances]
    swap = [(i, i + 1 - 2 * (i % 2)) for i in range(spans)]
    key_beside = lax.ppermute(keys, "span", swap)
    value_beside = lax.ppermute(values, "span", swap)

    own, own_sum = pl.pallas_call(
        functools.partial(local_kernel, spans),
        in_specs=[SMEM, HBM, HBM, HBM, ANY, ANY],
        out_specs=[VMEM] * 2,
        out_shape=[jax.ShapeDtypeStruct((rows, width), f32), jax.ShapeDtypeStruct((rows, LANES), f32)],
        scratch_shapes=[pltpu.VMEM((rows, width), bf16)] * 5 + [pltpu.SemaphoreType.DMA((5,))],
        compiler_params=PARAMS,
        cost_estimate=SHORT,
        name="local",
    )(facts, in_hbm(queries), in_hbm(keys), in_hbm(values), key_beside, value_beside)

    def served(asked, distance):
        return pl.pallas_call(
            functools.partial(served_kernel, distance, spans),
            in_specs=[SMEM] + [VMEM] * 5,
            out_specs=VMEM,
            out_shape=jax.ShapeDtypeStruct((asked.shape[0], width + LANES), bf16),
            compiler_params=PARAMS,
            cost_estimate=SHORT,
            name="served",
        )(facts, asked, keys, values, key_beside, value_beside)

    asked_early, own_sum = lax.optimization_barrier((asked_early, own_sum))
    out_early = [served(q, d) for q, d in zip(asked_early, distances)]
    back_early = [shifted(o, "span", d) for o, d in zip(out_early, distances)]
    asked_late, out_early = lax.optimization_barrier((asked_late, out_early))
    out_late = [served(q, d) for q, d in zip(asked_late, distances)]
    back_early, out_late = lax.optimization_barrier((back_early, out_late))
    back_late = [shifted(o, "span", d) for o, d in zip(out_late, distances)]

    chunks = 2
    columns = model // chunks
    tiles = 4
    tile = columns // tiles
    last = ranks - 1
    weight = in_hbm(out_weight)

    def opening(chunk):
        return pl.pallas_call(
            functools.partial(opening_kernel, spans, ranks, distances, chunk * columns),
            in_specs=[SMEM] + [VMEM] * (2 + len(distances)) + [HBM],
            out_specs=VMEM,
            out_shape=jax.ShapeDtypeStruct((block, columns), bf16),
            scratch_shapes=[
                pltpu.VMEM((tiles, width, tile), bf16),
                pltpu.VMEM((block, width), bf16),
                pltpu.SemaphoreType.DMA((tiles,)),
            ],
            compiler_params=PARAMS,
            cost_estimate=SHORT,
            name="opening",
        )(facts, own, own_sum, *back_early, weight)

    def hopped(sent, hop):
        return lax.ppermute(sent, "tensor", [(hop, hop + 1), (last - hop, last - hop - 1)])

    openings = [opening(chunk) for chunk in range(chunks)]
    arrived = [[hopped(sent, 0)] for sent in openings]
    back_late, openings = lax.optimization_barrier((back_late, openings))

    message_shape = jax.ShapeDtypeStruct((block, columns), bf16)
    stored_shape = pltpu.HBM((rows, columns), bf16)
    projection = dict(
        scratch_shapes=[
            pltpu.VMEM((tiles, width, tile), bf16),
            pltpu.VMEM((tiles, rows, tile), bf16),
            pltpu.SemaphoreType.DMA((tiles,)),
            pltpu.SemaphoreType.DMA((tiles * last,)),
        ],
        compiler_params=PARAMS,
        cost_estimate=SHORT,
        name="project",
    )
    stored = [HBM] + [HBM] * (last - 1)
    shapes = [stored_shape] + [message_shape] * (last - 1)
    attended, *first_outputs = pl.pallas_call(
        functools.partial(project_first_kernel, spans, ranks, distances),
        in_specs=[SMEM] + [VMEM] * (2 + 2 * len(distances)) + [HBM],
        out_specs=[VMEM] + stored,
        out_shape=[jax.ShapeDtypeStruct((rows, width), bf16)] + shapes,
        **projection,
    )(facts, own, own_sum, *back_early, *back_late, weight)
    projected = [first_outputs] + [
        pl.pallas_call(
            functools.partial(project_next_kernel, spans, ranks, chunk * columns),
            in_specs=[SMEM, VMEM, HBM],
            out_specs=stored,
            out_shape=shapes,
            **projection,
        )(facts, attended, weight)
        for chunk in range(1, chunks)
    ]

    def message(hop, target, chunk, comes):
        return pl.pallas_call(
            functools.partial(message_kernel, spans, ranks, hop, target),
            in_specs=[SMEM, HBM, VMEM],
            out_specs=VMEM,
            out_shape=message_shape,
            scratch_shapes=[pltpu.VMEM((block, columns), bf16), pltpu.SemaphoreType.DMA((1,))],
            compiler_params=PARAMS,
            cost_estimate=SHORT,
            name="message",
        )(facts, in_hbm(projected[chunk][0]), comes)

    before = projected[-1][0]
    for step in range(1, last):
        for chunk in range(chunks):
            comes, before = lax.optimization_barrier((arrived[chunk], before))
            sent, comes = lax.optimization_barrier((projected[chunk][step], comes))
            leaves = [hopped(sent, 0)]
            for hop in range(1, step + 1):
                before = message(hop, last - (step - hop), chunk, comes[hop - 1])
                leaves.append(hopped(before, hop))
            arrived[chunk] = leaves

    result = ()
    pieces = 2
    for chunk in range(chunks):
        result = (
            pl.pallas_call(
                functools.partial(final_kernel, spans, ranks, last, chunk * columns),
                in_specs=[SMEM, HBM, HBM] + [VMEM] * last + [ANY] * len(result),
                out_specs=HBM,
                out_shape=jax.ShapeDtypeStruct((block, model), bf16),
                input_output_aliases={3 + last: 0} if result else {},
                scratch_shapes=[
                    pltpu.VMEM((block, columns), bf16),
                    pltpu.VMEM((8, columns), f32),
                    pltpu.VMEM((pieces, block, columns // pieces), bf16),
                    pltpu.SemaphoreType.DMA((2 + pieces,)),
                ],
                compiler_params=PARAMS,
                cost_estimate=SHORT,
                name="final",
            )(facts, in_hbm(projected[chunk][0]), in_hbm(gate_table), *arrived[chunk], *result),
        )
    return result[0]


def solution(mesh):
    return jax.shard_map(
        body,
        mesh=mesh,
        in_specs=(
            P(("group", "span"), "tensor"),
            P(("group", "span"), "tensor"),
            P(("group", "span"), "tensor"),
            P("tensor", None),
            P(),
            P("group"),
            P("group", None),
        ),
        out_specs=P(("group", "span", "tensor"), None),
        check_vma=False,
    )
```

```python
import functools

import jax
import jax.numpy as jnp
from jax import lax
from jax.experimental import pallas as pl
from jax.experimental.pallas import tpu as pltpu
from jax.sharding import PartitionSpec as P

HD = 128
LANES = 128
HIDDEN = -1e30
LOG2E = 1.4426950408889634
PARAMS = pltpu.CompilerParams(vmem_limit_bytes=24 * 1024 * 1024)
SMEM = pl.BlockSpec(memory_space=pltpu.SMEM)
VMEM = pl.BlockSpec(memory_space=pltpu.VMEM)
ANY = pl.BlockSpec(memory_space=pl.ANY)
HBM = pl.BlockSpec(memory_space=pltpu.HBM)
PIECE_LANES = 32


def taking(microseconds):
    return pl.CostEstimate(flops=0, bytes_accessed=int(microseconds * 3.69e6), transcendentals=0)


def in_hbm(array):
    return pltpu.with_memory_space_constraint(array, pltpu.HBM)


def shifted(block, axis, distance):
    count = lax.axis_size(axis)
    return lax.ppermute(block, axis, [(i, i + distance) for i in range(count) if 0 <= i + distance < count])


def head_columns(head):
    return slice(head * HD, (head + 1) * HD)


def attend(query, keys, values, flags, write, lanes=0):
    rows, width = query.shape
    scale = LOG2E * HD ** (-0.5)
    lane = lax.broadcasted_iota(jnp.int32, (rows, LANES), 1)
    packed = jnp.zeros((rows, LANES), jnp.float32)
    for head in range(width // HD):
        columns = head_columns(head)
        mine = query[:, columns]
        scores = [
            lax.dot_general(mine, key[:, columns], (((1,), (1,)), ((), ())), preferred_element_type=jnp.float32)
            for key in keys
        ]
        tops = [jnp.max(block, axis=-1, keepdims=True) * scale for block in scores]
        top = functools.reduce(
            jnp.maximum, [one if flag is None else jnp.where(flag, one, HIDDEN) for one, flag in zip(tops, flags)]
        )
        total, product = None, None
        for block, value, flag in zip(scores, values, flags):
            above = top if flag is None else jnp.where(flag, top, -HIDDEN)
            probs = jnp.exp2(block * scale - above)
            part = jnp.sum(probs, axis=-1, keepdims=True)
            part_product = jnp.dot(
                probs.astype(jnp.bfloat16), value[:, columns], preferred_element_type=jnp.float32
            )
            total = part if total is None else total + part
            product = part_product if product is None else product + part_product
        total = jnp.where(total > 0.0, total, 1.0)
        write(columns, product * (1.0 / total))
        packed = jnp.where(lane == lanes + head, top + jnp.log2(total), packed)
    return packed


class Facts:
    def __init__(self, ref, spans):
        self.ref, self.spans = ref, spans
        self.span, self.rank = ref[spans, 0], ref[spans, 1]
        self.beside = self.span + 1 - 2 * lax.rem(self.span, 2)

    def sees(self, asker, span):
        return self.ref[asker, span] > 0

    def level(self):
        return self.ref[self.spans + 1, self.span]


def copied(source, target, semaphore):
    copy = pltpu.make_async_copy(source, target, semaphore)
    copy.start()
    return copy


def parts_of(rank, ranks, rows):
    block = rows // ranks
    lower = rank < ranks // 2
    early = pl.multiple_of(jnp.where(lower, rows - block, 0), block)
    late = pl.multiple_of(jnp.where(lower, 0, block), block)
    return (early, block), (late, rows - block)


def split_kernel(spans, ranks, facts, query, *refs):
    here = Facts(facts, spans)
    *targets, semaphores = refs

    @pl.when(here.span > 1)
    def _():
        (early, _), (late, rest) = parts_of(here.rank, ranks, query.shape[0])
        half = rest // 2
        copies = [
            copied(query.at[pl.ds(start, target.shape[0])], target, semaphores.at[index])
            for index, (start, target) in enumerate(zip((early, late, pl.multiple_of(late + half, 16)), targets))
        ]
        for copy in copies:
            copy.wait()


def local_kernel(spans, heads, facts, query, key, value, key_beside, value_beside, result, sums, *scratch):
    here = Facts(facts, spans)
    query_, key_, value_, key_beside_, value_beside_, semaphores = scratch
    columns = pl.ds(heads.start * HD, len(heads) * HD)
    copies = [
        copied(source.at[:, columns], target, semaphores.at[index])
        for index, (source, target) in enumerate((
            (query, query_), (key, key_), (key_beside, key_beside_), (value, value_), (value_beside, value_beside_),
        ))
    ]
    for copy in copies:
        copy.wait()

    def write(columns, block):
        result[:, columns] = block

    flags = [None, here.sees(here.span, here.beside)]
    sums[...] = attend(query_, [key_, key_beside_], [value_, value_beside_], flags, write, heads.start)


def served_kernel(distance, spans, facts, key, value, key_beside, value_beside, *refs):
    here = Facts(facts, spans)

    @pl.when(here.span + distance < spans)
    def _():
        asker = jnp.minimum(here.span + distance, spans - 1)
        flags = [here.sees(asker, here.span), here.sees(asker, here.beside)]
        *queries, result = refs
        at = 0
        for query in queries:
            rows, width = query.shape
            there = slice(at, at + rows)

            def write(columns, block):
                result[there, columns] = block.astype(jnp.bfloat16)

            rest = attend(query, [key, key_beside], [value, value_beside], flags, write)
            sent = jnp.zeros_like(rest)
            for piece in range(3):
                part = rest.astype(jnp.bfloat16).astype(jnp.float32)
                sent = sent + (part if piece == 0 else pltpu.roll(part, piece * PIECE_LANES, 1))
                rest = rest - part
            result[there, width:] = sent.astype(jnp.bfloat16)
            at += rows


def merge(span, distances, own, own_sum, there, served, here, write):
    width = served[0].shape[1] - LANES
    sums = [own_sum[0][there, :] + own_sum[1][there, :]]
    for distance, ref in zip(distances, served):
        sent = ref[here, width:].astype(jnp.float32)
        joined = sent
        for piece in (1, 2):
            joined = joined + pltpu.roll(sent, LANES - piece * PIECE_LANES, 1)
        sums.append(jnp.where(span >= distance, joined, HIDDEN))
    top = functools.reduce(jnp.maximum, sums)
    shares = [jnp.exp2(one - top) for one in sums]
    over = 1.0 / sum(shares)
    shares = [share * over for share in shares]
    for head in range(width // HD):
        columns = head_columns(head)
        split = own[0].shape[1]
        mine = own[0][there, columns] if columns.stop <= split else (
            own[1][there, columns.start - split:columns.stop - split])
        merged = mine * shares[0][:, head:head + 1]
        for distance, share, ref in zip(distances, shares[1:], served):
            away = jnp.where(span >= distance, ref[here, columns].astype(jnp.float32), 0.0)
            merged = merged + away * share[:, head:head + 1]
        write(columns, merged.astype(jnp.bfloat16))


def streamed(weight, first, tiles, semaphores):
    count, _, tile = tiles.shape
    return [
        copied(weight.at[:, pl.ds(first + index * tile, tile)], tiles.at[index], semaphores.at[index])
        for index in range(count)
    ]


def opening_kernel(spans, ranks, distances, first, facts, *refs):
    own, own_sum, served = refs[:2], refs[2:4], refs[4:4 + len(distances)]
    weight, result, tiles, rows, semaphores = refs[4 + len(distances):]
    here = Facts(facts, spans)
    tile = tiles.shape[2]

    @pl.when(jnp.logical_or(here.rank == 0, here.rank == ranks - 1))
    def _():
        copies = streamed(weight, first, tiles, semaphores)
        (start, size), _ = parts_of(here.rank, ranks, own[0].shape[0])

        def write(columns, part):
            rows[:, columns] = part

        merge(here.span, distances, own, own_sum, pl.ds(start, size), served, slice(0, size), write)
        for index, copy in enumerate(copies):
            copy.wait()
            product = jnp.dot(rows[...], tiles[index], preferred_element_type=jnp.float32)
            result[:, index * tile:(index + 1) * tile] = product.astype(jnp.bfloat16)


def project_blocks(ranks, facts, step, attended, weight, results, tiles, semaphores):
    rank = facts.rank
    last = ranks - 1
    count, _, tile = tiles.shape
    copies = streamed(weight, 0, tiles, semaphores)
    yield
    ups, downs = results[::2], results[1::2]
    block, columns = ups[0].shape
    each = columns // tile
    for index, copy in enumerate(copies):
        copy.wait()
        there = slice(index % each * tile, (index % each + 1) * tile)
        for sends, target, result in (
            (rank <= step, last - step + rank, ups[index // each]),
            (rank >= last - step, step + rank - last, downs[index // each]),
        ):

            @pl.when(sends)
            def _():
                start = pl.multiple_of(target * block, block)
                product = jnp.dot(
                    attended[pl.ds(start, block), :], tiles[index], preferred_element_type=jnp.float32
                )
                result[:, there] = product.astype(jnp.bfloat16)


def merged_blocks_kernel(spans, ranks, distances, facts, *refs):
    count = len(distances)
    own, own_sum, refs = refs[:2], refs[2:4], refs[4:]
    early, late = refs[:count], refs[count:2 * count]
    weight, attended, *results, tiles, semaphores = refs[2 * count:]
    here = Facts(facts, spans)
    work = project_blocks(ranks, here, 1, attended, weight, results, tiles, semaphores)
    next(work)
    for (start, size), served in zip(parts_of(here.rank, ranks, own[0].shape[0]), (early, late)):
        there = pl.ds(start, size)

        def write(columns, part):
            attended[there, columns] = part

        merge(here.span, distances, own, own_sum, there, served, slice(0, size), write)
    for _ in work:
        pass


def blocks_kernel(spans, ranks, step, facts, attended, weight, *refs):
    *results, tiles, semaphores = refs
    for _ in project_blocks(ranks, Facts(facts, spans), step, attended, weight, results, tiles, semaphores):
        pass


def own_kernel(spans, facts, attended, weight, result, tiles, semaphores):
    block = result.shape[0]
    count, _, tile = tiles.shape
    copies = streamed(weight, 0, tiles, semaphores)
    start = pl.multiple_of(Facts(facts, spans).rank * block, block)
    for index, copy in enumerate(copies):
        copy.wait()
        product = jnp.dot(attended[pl.ds(start, block), :], tiles[index], preferred_element_type=jnp.float32)
        result[:, index * tile:(index + 1) * tile] = product.astype(jnp.bfloat16)


def final_kernel(spans, facts, done, projected, gate_table, up, down, result, own, gate, gated, semaphores):
    here = Facts(facts, spans)
    first, (block, columns) = done.shape[1], own.shape
    pieces = gated.shape[0]
    wide = columns // pieces
    level = here.level()
    above = pl.multiple_of(level // 8 * 8, 8)
    copies = [
        copied(projected.at[:, pl.ds(first, columns)], own, semaphores.at[0]),
        copied(gate_table.at[pl.ds(above, 8), pl.ds(first, columns)], gate, semaphores.at[1]),
    ]
    sent = [copied(done, result.at[:, pl.ds(0, first)], semaphores.at[2])]
    for copy in copies:
        copy.wait()
    for piece in range(pieces):
        there = slice(piece * wide, (piece + 1) * wide)
        summed = own[:, there].astype(jnp.float32) + up[:, there].astype(jnp.float32)
        summed = summed + down[:, there].astype(jnp.float32)
        gated[piece] = (summed * gate[pl.ds(lax.rem(level, 8), 1), there]).astype(jnp.bfloat16)
        sent.append(copied(
            gated.at[piece], result.at[:, pl.ds(first + piece * wide, wide)], semaphores.at[3 + piece]
        ))
    for copy in sent:
        copy.wait()


def body(queries, keys, values, out_weight, gate_table, levels, visible):
    rows, width = queries.shape
    model = out_weight.shape[1]
    spans = lax.axis_size("span")
    ranks = lax.axis_size("tensor")
    span = lax.axis_index("span")
    rank = lax.axis_index("tensor")
    block = rows // ranks
    bf16, f32 = jnp.bfloat16, jnp.float32
    numbers = jnp.arange(spans, dtype=jnp.int32)
    place = jnp.where(numbers == 0, span, jnp.where(numbers == 1, rank, 0)).astype(jnp.int32)
    facts = jnp.concatenate([visible, place[None, :], levels[None, :]], axis=0)

    query_early, *query_late = pl.pallas_call(
        functools.partial(split_kernel, spans, ranks),
        in_specs=[SMEM, HBM],
        out_specs=[VMEM] * 3,
        out_shape=[
            jax.ShapeDtypeStruct((part, width), bf16) for part in (block, (rows - block) // 2, (rows - block) // 2)
        ],
        scratch_shapes=[pltpu.SemaphoreType.DMA((3,))],
        compiler_params=PARAMS,
        cost_estimate=taking(1.7),
        name="split",
    )(facts, in_hbm(queries))
    distances = list(range(2, spans, 2))
    asked_early = [shifted(query_early, "span", -distance) for distance in distances]
    swap = [(i, i + 1 - 2 * (i % 2)) for i in range(spans)]
    key_beside = lax.ppermute(keys, "span", swap)
    value_beside = lax.ppermute(values, "span", swap)

    def local(heads):
        wide = len(heads) * HD
        return pl.pallas_call(
            functools.partial(local_kernel, spans, heads),
            in_specs=[SMEM, HBM, HBM, HBM, ANY, ANY],
            out_specs=[VMEM] * 2,
            out_shape=[jax.ShapeDtypeStruct((rows, wide), f32), jax.ShapeDtypeStruct((rows, LANES), f32)],
            scratch_shapes=[pltpu.VMEM((rows, wide), bf16)] * 5 + [pltpu.SemaphoreType.DMA((5,))],
            compiler_params=PARAMS,
            cost_estimate=taking(1.0 + 0.8 * len(heads)),
            name="local",
        )(facts, in_hbm(queries), in_hbm(keys), in_hbm(values), key_beside, value_beside)

    heads = width // HD
    own, own_sum = local(range(heads // 3))
    query_late, own_sum = lax.optimization_barrier((query_late, own_sum))
    asked_late = [
        [shifted(query, "span", -distance) for query in query_late] for distance in distances
    ]
    own, own_sum = zip((own, own_sum), local(range(heads // 3, heads)))

    def served(asked, distance):
        return pl.pallas_call(
            functools.partial(served_kernel, distance, spans),
            in_specs=[SMEM] + [VMEM] * (4 + len(asked)),
            out_specs=VMEM,
            out_shape=jax.ShapeDtypeStruct((sum(part.shape[0] for part in asked), width + LANES), bf16),
            compiler_params=PARAMS,
            cost_estimate=taking(3.3),
            name="served",
        )(facts, keys, values, key_beside, value_beside, *asked)

    asked_early, own_sum = lax.optimization_barrier((asked_early, list(own_sum)))
    out_early = [served([q], d) for q, d in zip(asked_early, distances)]
    back_early = [shifted(o, "span", d) for o, d in zip(out_early, distances)]
    asked_late, out_early = lax.optimization_barrier((asked_late, out_early))
    out_late = [served(q, d) for q, d in zip(asked_late, distances)]
    back_early, out_late = lax.optimization_barrier((back_early, out_late))
    back_late = [shifted(o, "span", d) for o, d in zip(out_late, distances)]

    chunks = 2
    columns = model // chunks
    tiles = 4
    tile = columns // tiles
    last = ranks - 1
    weight = in_hbm(out_weight)

    def opening(chunk):
        return pl.pallas_call(
            functools.partial(opening_kernel, spans, ranks, distances, chunk * columns),
            in_specs=[SMEM] + [VMEM] * (4 + len(distances)) + [HBM],
            out_specs=VMEM,
            out_shape=jax.ShapeDtypeStruct((block, columns), bf16),
            scratch_shapes=[
                pltpu.VMEM((tiles, width, tile), bf16),
                pltpu.VMEM((block, width), bf16),
                pltpu.SemaphoreType.DMA((tiles,)),
            ],
            compiler_params=PARAMS,
            cost_estimate=taking(3.4),
            name="opening",
        )(facts, *own, *own_sum, *back_early, weight)

    openings = [opening(chunk) for chunk in range(chunks)]
    ends = [(0, 1), (last, last - 1)]
    arrived = [[lax.ppermute(sent, "tensor", ends)] for sent in openings]
    back_late, openings = lax.optimization_barrier((back_late, openings))

    streaming = dict(
        scratch_shapes=[
            pltpu.VMEM((chunks * tiles, width, tile), bf16), pltpu.SemaphoreType.DMA((chunks * tiles,))
        ],
        compiler_params=PARAMS,
    )
    attended_shape = jax.ShapeDtypeStruct((rows, width), bf16)
    block_shapes = [jax.ShapeDtypeStruct((block, columns), bf16)] * (2 * chunks)
    attended, *blocks = pl.pallas_call(
        functools.partial(merged_blocks_kernel, spans, ranks, distances),
        in_specs=[SMEM] + [VMEM] * (4 + 2 * len(distances)) + [HBM],
        out_specs=[VMEM] * (1 + 2 * chunks),
        out_shape=[attended_shape] + block_shapes,
        cost_estimate=taking(6.0),
        name="merged_blocks",
        **streaming,
    )(facts, *own, *own_sum, *back_early, *back_late, weight)

    before = attended
    for step in range(1, last):
        if step > 1:
            attended, before = lax.optimization_barrier((attended, before))
            blocks = pl.pallas_call(
                functools.partial(blocks_kernel, spans, ranks, step),
                in_specs=[SMEM, VMEM, HBM],
                out_specs=[VMEM] * (2 * chunks),
                out_shape=block_shapes,
                cost_estimate=taking(5.0),
                name="blocks",
                **streaming,
            )(facts, attended, weight)
        for chunk in range(chunks):
            comes, blocks, before = lax.optimization_barrier((arrived[chunk], blocks, before))
            up, down = [
                (mine.astype(f32) + come.astype(f32)).astype(bf16)
                for mine, come in zip(blocks[2 * chunk:2 * chunk + 2], (comes[0], comes[-1]))
            ]
            before = (up, down)
            arrived[chunk] = [
                lax.ppermute(up, "tensor", [(i, i + 1) for i in range(step + 1)]),
                lax.ppermute(down, "tensor", [(last - i, last - i - 1) for i in range(step + 1)]),
            ]
    attended, before = lax.optimization_barrier((attended, before))
    projected = pl.pallas_call(
        functools.partial(own_kernel, spans),
        in_specs=[SMEM, VMEM, HBM],
        out_specs=VMEM,
        out_shape=jax.ShapeDtypeStruct((block, model), bf16),
        cost_estimate=taking(5.0),
        name="own",
        **streaming,
    )(facts, attended, weight)
    level = jnp.sum(jnp.where(numbers == span, levels, 0))
    gate = lax.dynamic_slice(gate_table, (level, 0), (1, model))
    finished = []
    for chunk in range(chunks - 1):
        there = slice(chunk * columns, (chunk + 1) * columns)
        summed = sum(part.astype(f32) for part in (projected[:, there], *arrived[chunk]))
        finished.append((summed * gate[:, there]).astype(bf16))
    pieces = 2
    return pl.pallas_call(
        functools.partial(final_kernel, spans),
        in_specs=[SMEM, ANY, ANY, HBM, VMEM, VMEM],
        out_specs=HBM,
        out_shape=jax.ShapeDtypeStruct((block, model), bf16),
        scratch_shapes=[
            pltpu.VMEM((block, columns), bf16),
            pltpu.VMEM((8, columns), f32),
            pltpu.VMEM((pieces, block, columns // pieces), bf16),
            pltpu.SemaphoreType.DMA((3 + pieces,)),
        ],
        compiler_params=PARAMS,
        cost_estimate=taking(2.7),
        name="final",
    )(facts, jnp.concatenate(finished, axis=1), projected, in_hbm(gate_table), *arrived[-1])


def solution(mesh):
    return jax.shard_map(
        body,
        mesh=mesh,
        in_specs=(
            P(("group", "span"), "tensor"),
            P(("group", "span"), "tensor"),
            P(("group", "span"), "tensor"),
            P("tensor", None),
            P(),
            P("group"),
            P("group", None),
        ),
        out_specs=P(("group", "span", "tensor"), None),
        check_vma=False,
    )
```

```python
import functools

import jax
import jax.numpy as jnp
from jax import lax
from jax.experimental import pallas as pl
from jax.experimental.pallas import tpu as pltpu
from jax.sharding import PartitionSpec as P

HD = 128
LANES = 128
HIDDEN = -1e30
LOG2E = 1.4426950408889634
PARAMS = pltpu.CompilerParams(vmem_limit_bytes=24 * 1024 * 1024)
SMEM = pl.BlockSpec(memory_space=pltpu.SMEM)
VMEM = pl.BlockSpec(memory_space=pltpu.VMEM)
ANY = pl.BlockSpec(memory_space=pl.ANY)
HBM = pl.BlockSpec(memory_space=pltpu.HBM)
PIECE_LANES = 32


def taking(microseconds):
    return pl.CostEstimate(flops=0, bytes_accessed=int(microseconds * 3.69e6), transcendentals=0)


def in_hbm(array):
    return pltpu.with_memory_space_constraint(array, pltpu.HBM)


def shifted(block, axis, distance):
    count = lax.axis_size(axis)
    return lax.ppermute(block, axis, [(i, i + distance) for i in range(count) if 0 <= i + distance < count])


def head_columns(head):
    return slice(head * HD, (head + 1) * HD)


def attend(query, keys, values, flags, write):
    rows, width = query.shape
    scale = LOG2E * HD ** (-0.5)
    lane = lax.broadcasted_iota(jnp.int32, (rows, LANES), 1)
    packed = jnp.zeros((rows, LANES), jnp.float32)
    for head in range(width // HD):
        columns = head_columns(head)
        mine = query[:, columns]
        scores = [
            lax.dot_general(mine, key[:, columns], (((1,), (1,)), ((), ())), preferred_element_type=jnp.float32)
            for key in keys
        ]
        tops = [jnp.max(block, axis=-1, keepdims=True) * scale for block in scores]
        top = functools.reduce(
            jnp.maximum, [one if flag is None else jnp.where(flag, one, HIDDEN) for one, flag in zip(tops, flags)]
        )
        total, product = None, None
        for block, value, flag in zip(scores, values, flags):
            above = top if flag is None else jnp.where(flag, top, -HIDDEN)
            probs = jnp.exp2(block * scale - above)
            part = jnp.sum(probs, axis=-1, keepdims=True)
            part_product = jnp.dot(
                probs.astype(jnp.bfloat16), value[:, columns], preferred_element_type=jnp.float32
            )
            total = part if total is None else total + part
            product = part_product if product is None else product + part_product
        total = jnp.where(total > 0.0, total, 1.0)
        write(columns, product * (1.0 / total))
        packed = jnp.where(lane == head, top + jnp.log2(total), packed)
    return packed


class Facts:
    def __init__(self, ref, spans):
        self.ref, self.spans = ref, spans
        self.span, self.rank = ref[spans, 0], ref[spans, 1]
        self.beside = self.span + 1 - 2 * lax.rem(self.span, 2)

    def sees(self, asker, span):
        return self.ref[asker, span] > 0

    def level(self):
        return self.ref[self.spans + 1, self.span]


def copied(source, target, semaphore):
    copy = pltpu.make_async_copy(source, target, semaphore)
    copy.start()
    return copy


def parts_of(rank, ranks, rows):
    block = rows // ranks
    lower = rank < ranks // 2
    early = pl.multiple_of(jnp.where(lower, rows - block, 0), block)
    late = pl.multiple_of(jnp.where(lower, 0, block), block)
    return (early, block), (late, rows - block)


def split_kernel(spans, ranks, facts, query, *refs):
    here = Facts(facts, spans)
    *targets, semaphores = refs

    @pl.when(here.span > 1)
    def _():
        (early, _), (late, _) = parts_of(here.rank, ranks, query.shape[0])
        starts = (early, late, pl.multiple_of(late + targets[1].shape[0], 16))
        copies = [
            copied(query.at[pl.ds(start, target.shape[0])], target, semaphores.at[index])
            for index, (start, target) in enumerate(zip(starts, targets))
        ]
        for copy in copies:
            copy.wait()


def local_kernel(spans, ranks, part, facts, query, key, value, key_beside, value_beside, result, sums, *scratch):
    here = Facts(facts, spans)
    query_, key_, value_, key_beside_, value_beside_, semaphores = scratch
    start, size = parts_of(here.rank, ranks, query.shape[0])[part]
    copies = [
        copied(source, target, semaphores.at[index])
        for index, (source, target) in enumerate((
            (query.at[pl.ds(start, size)], query_),
            (key, key_), (key_beside, key_beside_), (value, value_), (value_beside, value_beside_),
        ))
    ]
    for copy in copies:
        copy.wait()

    def write(columns, block):
        result[:, columns] = block

    flags = [None, here.sees(here.span, here.beside)]
    sums[...] = attend(query_, [key_, key_beside_], [value_, value_beside_], flags, write)


def served_kernel(distance, spans, facts, key, value, key_beside, value_beside, *refs):
    here = Facts(facts, spans)

    @pl.when(here.span + distance < spans)
    def _():
        asker = jnp.minimum(here.span + distance, spans - 1)
        flags = [here.sees(asker, here.span), here.sees(asker, here.beside)]
        *queries, result, query = refs
        at = 0
        for part in queries:
            query[at:at + part.shape[0], :] = part[...]
            at += part.shape[0]

        def write(columns, block):
            result[:, columns] = block.astype(jnp.bfloat16)

        rest = attend(query, [key, key_beside], [value, value_beside], flags, write)
        sent = jnp.zeros_like(rest)
        for piece in range(3):
            part = rest.astype(jnp.bfloat16).astype(jnp.float32)
            sent = sent + (part if piece == 0 else pltpu.roll(part, piece * PIECE_LANES, 1))
            rest = rest - part
        result[:, query.shape[1]:] = sent.astype(jnp.bfloat16)


def merge(span, distances, own, own_sum, served, write):
    width = own.shape[1]
    sums = [own_sum[...]]
    for distance, ref in zip(distances, served):
        sent = ref[:, width:].astype(jnp.float32)
        joined = sent
        for piece in (1, 2):
            joined = joined + pltpu.roll(sent, LANES - piece * PIECE_LANES, 1)
        sums.append(jnp.where(span >= distance, joined, HIDDEN))
    top = functools.reduce(jnp.maximum, sums)
    shares = [jnp.exp2(one - top) for one in sums]
    over = 1.0 / sum(shares)
    shares = [share * over for share in shares]
    for head in range(width // HD):
        columns = head_columns(head)
        merged = own[:, columns] * shares[0][:, head:head + 1]
        for distance, share, ref in zip(distances, shares[1:], served):
            away = jnp.where(span >= distance, ref[:, columns].astype(jnp.float32), 0.0)
            merged = merged + away * share[:, head:head + 1]
        write(columns, merged.astype(jnp.bfloat16))


def streamed(weight, first, tiles, semaphores):
    count, _, tile = tiles.shape
    return [
        copied(weight.at[:, pl.ds(first + index * tile, tile)], tiles.at[index], semaphores.at[index])
        for index in range(count)
    ]


def opening_kernel(spans, ranks, distances, first, facts, *refs):
    own, own_sum, *served = refs[:2 + len(distances)]
    weight, result, tiles, rows, semaphores = refs[2 + len(distances):]
    here = Facts(facts, spans)
    tile = tiles.shape[2]

    @pl.when(jnp.logical_or(here.rank == 0, here.rank == ranks - 1))
    def _():
        copies = streamed(weight, first, tiles, semaphores)

        def write(columns, part):
            rows[:, columns] = part

        merge(here.span, distances, own, own_sum, served, write)
        for index, copy in enumerate(copies):
            copy.wait()
            product = jnp.dot(rows[...], tiles[index], preferred_element_type=jnp.float32)
            result[:, index * tile:(index + 1) * tile] = product.astype(jnp.bfloat16)


def project_blocks(ranks, facts, step, attended, weight, results, tiles, semaphores):
    rank = facts.rank
    last = ranks - 1
    count, _, tile = tiles.shape
    copies = streamed(weight, 0, tiles, semaphores)
    yield
    ups, downs = results[::2], results[1::2]
    block, columns = ups[0].shape
    each = columns // tile
    for index, copy in enumerate(copies):
        copy.wait()
        there = slice(index % each * tile, (index % each + 1) * tile)
        for sends, target, result in (
            (rank <= step, last - step + rank, ups[index // each]),
            (rank >= last - step, step + rank - last, downs[index // each]),
        ):

            @pl.when(sends)
            def _():
                start = pl.multiple_of(target * block, block)
                product = jnp.dot(
                    attended[pl.ds(start, block), :], tiles[index], preferred_element_type=jnp.float32
                )
                result[:, there] = product.astype(jnp.bfloat16)


def merged_blocks_kernel(spans, ranks, distances, facts, *refs):
    each = 2 + len(distances)
    parts, (weight, attended, *results, tiles, semaphores) = (refs[:each], refs[each:2 * each]), refs[2 * each:]
    here = Facts(facts, spans)
    work = project_blocks(ranks, here, 1, attended, weight, results, tiles, semaphores)
    next(work)
    for (start, size), (own, own_sum, *served) in zip(parts_of(here.rank, ranks, attended.shape[0]), parts):
        there = pl.ds(start, size)

        def write(columns, part):
            attended[there, columns] = part

        merge(here.span, distances, own, own_sum, served, write)
    for _ in work:
        pass


def blocks_kernel(spans, ranks, step, facts, attended, weight, *refs):
    *results, tiles, semaphores = refs
    for _ in project_blocks(ranks, Facts(facts, spans), step, attended, weight, results, tiles, semaphores):
        pass


def own_kernel(spans, facts, attended, weight, result, tiles, semaphores):
    block = result.shape[0]
    count, _, tile = tiles.shape
    copies = streamed(weight, 0, tiles, semaphores)
    start = pl.multiple_of(Facts(facts, spans).rank * block, block)
    for index, copy in enumerate(copies):
        copy.wait()
        product = jnp.dot(attended[pl.ds(start, block), :], tiles[index], preferred_element_type=jnp.float32)
        result[:, index * tile:(index + 1) * tile] = product.astype(jnp.bfloat16)


def final_kernel(spans, facts, done, projected, gate_table, up, down, result, own, gate, gated, semaphores):
    here = Facts(facts, spans)
    first, (block, columns) = done.shape[1], own.shape
    pieces = gated.shape[0]
    wide = columns // pieces
    level = here.level()
    above = pl.multiple_of(level // 8 * 8, 8)
    copies = [
        copied(projected.at[:, pl.ds(first, columns)], own, semaphores.at[0]),
        copied(gate_table.at[pl.ds(above, 8), pl.ds(first, columns)], gate, semaphores.at[1]),
    ]
    sent = [copied(done, result.at[:, pl.ds(0, first)], semaphores.at[2])]
    for copy in copies:
        copy.wait()
    for piece in range(pieces):
        there = slice(piece * wide, (piece + 1) * wide)
        summed = own[:, there].astype(jnp.float32) + up[:, there].astype(jnp.float32)
        summed = summed + down[:, there].astype(jnp.float32)
        gated[piece] = (summed * gate[pl.ds(lax.rem(level, 8), 1), there]).astype(jnp.bfloat16)
        sent.append(copied(
            gated.at[piece], result.at[:, pl.ds(first + piece * wide, wide)], semaphores.at[3 + piece]
        ))
    for copy in sent:
        copy.wait()


def body(queries, keys, values, out_weight, gate_table, levels, visible):
    rows, width = queries.shape
    model = out_weight.shape[1]
    spans = lax.axis_size("span")
    ranks = lax.axis_size("tensor")
    span = lax.axis_index("span")
    rank = lax.axis_index("tensor")
    block = rows // ranks
    bf16, f32 = jnp.bfloat16, jnp.float32
    numbers = jnp.arange(spans, dtype=jnp.int32)
    place = jnp.where(numbers == 0, span, jnp.where(numbers == 1, rank, 0)).astype(jnp.int32)
    facts = jnp.concatenate([visible, place[None, :], levels[None, :]], axis=0)

    third = (rows - block) // 48 * 16
    query_early, *query_late = pl.pallas_call(
        functools.partial(split_kernel, spans, ranks),
        in_specs=[SMEM, HBM],
        out_specs=[VMEM] * 3,
        out_shape=[jax.ShapeDtypeStruct((part, width), bf16) for part in (block, rows - block - third, third)],
        scratch_shapes=[pltpu.SemaphoreType.DMA((3,))],
        compiler_params=PARAMS,
        cost_estimate=taking(1.7),
        name="split",
    )(facts, in_hbm(queries))
    distances = list(range(2, spans, 2))
    asked_early = [shifted(query_early, "span", -distance) for distance in distances]
    swap = [(i, i + 1 - 2 * (i % 2)) for i in range(spans)]
    key_beside = lax.ppermute(keys, "span", swap)
    value_beside = lax.ppermute(values, "span", swap)

    def after(value, *others):
        return lax.optimization_barrier((value, others))[0]

    def local(part, facts):
        size = (block, rows - block)[part]
        return pl.pallas_call(
            functools.partial(local_kernel, spans, ranks, part),
            in_specs=[SMEM, HBM, HBM, HBM, ANY, ANY],
            out_specs=[VMEM] * 2,
            out_shape=[jax.ShapeDtypeStruct((size, width), f32), jax.ShapeDtypeStruct((size, LANES), f32)],
            scratch_shapes=[pltpu.VMEM((size, width), bf16)] + [pltpu.VMEM((rows, width), bf16)] * 4
            + [pltpu.SemaphoreType.DMA((5,))],
            compiler_params=PARAMS,
            cost_estimate=taking(4.0),
            name="local",
        )(facts, in_hbm(queries), in_hbm(keys), in_hbm(values), key_beside, value_beside)

    def served(asked, distance):
        return pl.pallas_call(
            functools.partial(served_kernel, distance, spans),
            in_specs=[SMEM] + [VMEM] * (4 + len(asked)),
            out_specs=VMEM,
            out_shape=jax.ShapeDtypeStruct((sum(part.shape[0] for part in asked), width + LANES), bf16),
            scratch_shapes=[pltpu.VMEM((sum(part.shape[0] for part in asked), width), bf16)],
            compiler_params=PARAMS,
            cost_estimate=taking(3.3),
            name="served",
        )(facts, keys, values, key_beside, value_beside, *asked)

    early = list(local(0, facts))
    query_late = after(query_late, early)
    asked_early = after(asked_early, early)
    asked_late = [[shifted(query, "span", -distance) for query in query_late] for distance in distances]
    early += [shifted(served([q], d), "span", d) for q, d in zip(asked_early, distances)]

    chunks = 2
    columns = model // chunks
    tiles = 4
    tile = columns // tiles
    last = ranks - 1
    weight = in_hbm(out_weight)

    def opening(chunk, facts):
        return pl.pallas_call(
            functools.partial(opening_kernel, spans, ranks, distances, chunk * columns),
            in_specs=[SMEM] + [VMEM] * (2 + len(distances)) + [HBM],
            out_specs=VMEM,
            out_shape=jax.ShapeDtypeStruct((block, columns), bf16),
            scratch_shapes=[
                pltpu.VMEM((tiles, width, tile), bf16),
                pltpu.VMEM((block, width), bf16),
                pltpu.SemaphoreType.DMA((tiles,)),
            ],
            compiler_params=PARAMS,
            cost_estimate=taking(3.4),
            name="opening",
        )(facts, *early, weight)

    ends = [(0, 1), (last, last - 1)]
    sent = opening(0, facts)
    arrived = [[lax.ppermute(sent, "tensor", ends)]]
    out_late = [served(q, d) for q, d in zip(after(asked_late, sent), distances)]
    late = list(local(1, after(facts, out_late)))
    for chunk in range(1, chunks):
        sent = opening(chunk, after(facts, late))
        arrived.append([lax.ppermute(sent, "tensor", ends)])
    late += after([shifted(o, "span", d) for o, d in zip(out_late, distances)], sent)

    streaming = dict(
        scratch_shapes=[
            pltpu.VMEM((chunks * tiles, width, tile), bf16), pltpu.SemaphoreType.DMA((chunks * tiles,))
        ],
        compiler_params=PARAMS,
    )
    attended_shape = jax.ShapeDtypeStruct((rows, width), bf16)
    block_shapes = [jax.ShapeDtypeStruct((block, columns), bf16)] * (2 * chunks)
    attended, *blocks = pl.pallas_call(
        functools.partial(merged_blocks_kernel, spans, ranks, distances),
        in_specs=[SMEM] + [VMEM] * (4 + 2 * len(distances)) + [HBM],
        out_specs=[VMEM] * (1 + 2 * chunks),
        out_shape=[attended_shape] + block_shapes,
        cost_estimate=taking(6.0),
        name="merged_blocks",
        **streaming,
    )(facts, *early, *late, weight)

    before = attended
    for step in range(1, last):
        if step > 1:
            attended, before = lax.optimization_barrier((attended, before))
            blocks = pl.pallas_call(
                functools.partial(blocks_kernel, spans, ranks, step),
                in_specs=[SMEM, VMEM, HBM],
                out_specs=[VMEM] * (2 * chunks),
                out_shape=block_shapes,
                cost_estimate=taking(5.0),
                name="blocks",
                **streaming,
            )(facts, attended, weight)
        for chunk in range(chunks):
            comes, blocks, before = lax.optimization_barrier((arrived[chunk], blocks, before))
            up, down = [
                (mine.astype(f32) + come.astype(f32)).astype(bf16)
                for mine, come in zip(blocks[2 * chunk:2 * chunk + 2], (comes[0], comes[-1]))
            ]
            before = (up, down)
            arrived[chunk] = [
                lax.ppermute(up, "tensor", [(i, i + 1) for i in range(step + 1)]),
                lax.ppermute(down, "tensor", [(last - i, last - i - 1) for i in range(step + 1)]),
            ]
    attended, before = lax.optimization_barrier((attended, before))
    projected = pl.pallas_call(
        functools.partial(own_kernel, spans),
        in_specs=[SMEM, VMEM, HBM],
        out_specs=VMEM,
        out_shape=jax.ShapeDtypeStruct((block, model), bf16),
        cost_estimate=taking(5.0),
        name="own",
        **streaming,
    )(facts, attended, weight)
    level = jnp.sum(jnp.where(numbers == span, levels, 0))
    gate = lax.dynamic_slice(gate_table, (level, 0), (1, model))
    finished = []
    for chunk in range(chunks - 1):
        there = slice(chunk * columns, (chunk + 1) * columns)
        summed = sum(part.astype(f32) for part in (projected[:, there], *arrived[chunk]))
        finished.append((summed * gate[:, there]).astype(bf16))
    pieces = 2
    return pl.pallas_call(
        functools.partial(final_kernel, spans),
        in_specs=[SMEM, ANY, ANY, HBM, VMEM, VMEM],
        out_specs=HBM,
        out_shape=jax.ShapeDtypeStruct((block, model), bf16),
        scratch_shapes=[
            pltpu.VMEM((block, columns), bf16),
            pltpu.VMEM((8, columns), f32),
            pltpu.VMEM((pieces, block, columns // pieces), bf16),
            pltpu.SemaphoreType.DMA((3 + pieces,)),
        ],
        compiler_params=PARAMS,
        cost_estimate=taking(2.7),
        name="final",
    )(facts, jnp.concatenate(finished, axis=1), projected, in_hbm(gate_table), *arrived[-1])


def solution(mesh):
    return jax.shard_map(
        body,
        mesh=mesh,
        in_specs=(
            P(("group", "span"), "tensor"),
            P(("group", "span"), "tensor"),
            P(("group", "span"), "tensor"),
            P("tensor", None),
            P(),
            P("group"),
            P("group", None),
        ),
        out_specs=P(("group", "span", "tensor"), None),
        check_vma=False,
    )
```

```python
import functools

import jax
import jax.numpy as jnp
from jax import lax
from jax.experimental import pallas as pl
from jax.experimental.pallas import tpu as pltpu
from jax.sharding import PartitionSpec as P

HD = 128
LANES = 128
HIDDEN = -1e30
LOG2E = 1.4426950408889634
PARAMS = pltpu.CompilerParams(vmem_limit_bytes=24 * 1024 * 1024)
SMEM = pl.BlockSpec(memory_space=pltpu.SMEM)
VMEM = pl.BlockSpec(memory_space=pltpu.VMEM)
ANY = pl.BlockSpec(memory_space=pl.ANY)
HBM = pl.BlockSpec(memory_space=pltpu.HBM)
PIECE_LANES = 32


def taking(microseconds):
    return pl.CostEstimate(flops=0, bytes_accessed=int(microseconds * 3.69e6), transcendentals=0)


def in_hbm(array):
    return pltpu.with_memory_space_constraint(array, pltpu.HBM)


def shifted(block, axis, distance):
    count = lax.axis_size(axis)
    return lax.ppermute(block, axis, [(i, i + distance) for i in range(count) if 0 <= i + distance < count])


def head_columns(head):
    return slice(head * HD, (head + 1) * HD)


def attend(query, keys, values, flags, write):
    rows, width = query.shape
    scale = LOG2E * HD ** (-0.5)
    lane = lax.broadcasted_iota(jnp.int32, (rows, LANES), 1)
    packed = jnp.zeros((rows, LANES), jnp.float32)
    for head in range(width // HD):
        columns = head_columns(head)
        mine = query[:, columns]
        scores = [
            lax.dot_general(mine, key[:, columns], (((1,), (1,)), ((), ())), preferred_element_type=jnp.float32)
            for key in keys
        ]
        tops = [jnp.max(block, axis=-1, keepdims=True) * scale for block in scores]
        top = functools.reduce(
            jnp.maximum, [one if flag is None else jnp.where(flag, one, HIDDEN) for one, flag in zip(tops, flags)]
        )
        joined = None
        for block, value, flag in zip(scores, values, flags):
            above = top if flag is None else jnp.where(flag, top, -HIDDEN)
            probs = jnp.exp2(block * scale - above).astype(jnp.bfloat16)
            beside = jnp.concatenate([value[:, columns], jnp.ones((value.shape[0], HD), jnp.bfloat16)], axis=1)
            part = jnp.dot(probs, beside, preferred_element_type=jnp.float32)
            joined = part if joined is None else joined + part
        product, total = joined[:, :HD], jnp.where(joined[:, HD:] > 0.0, joined[:, HD:], 1.0)
        write(columns, product / total)
        packed = jnp.where(lane == head, top + jnp.log2(total), packed)
    return packed


class Facts:
    def __init__(self, ref, spans):
        self.ref, self.spans = ref, spans
        self.span, self.rank = ref[spans, 0], ref[spans, 1]
        self.beside = self.span + 1 - 2 * lax.rem(self.span, 2)

    def sees(self, asker, span):
        return self.ref[asker, span] > 0

    def level(self):
        return self.ref[self.spans + 1, self.span]


def copied(source, target, semaphore):
    copy = pltpu.make_async_copy(source, target, semaphore)
    copy.start()
    return copy


def parts_of(rank, ranks, rows):
    block = rows // ranks
    lower = rank < ranks // 2
    early = pl.multiple_of(jnp.where(lower, rows - block, 0), block)
    late = pl.multiple_of(jnp.where(lower, 0, block), block)
    return (early, block), (late, rows - block)


def split_kernel(spans, ranks, facts, query, *refs):
    here = Facts(facts, spans)
    *targets, semaphores = refs

    @pl.when(here.span > 1)
    def _():
        (early, _), (late, _) = parts_of(here.rank, ranks, query.shape[0])
        starts = (early, late, pl.multiple_of(late + targets[1].shape[0], 16))
        copies = [
            copied(query.at[pl.ds(start, target.shape[0])], target, semaphores.at[index])
            for index, (start, target) in enumerate(zip(starts, targets))
        ]
        for copy in copies:
            copy.wait()


def local_kernel(spans, ranks, part, facts, query, key, value, key_beside, value_beside, result, sums, *scratch):
    here = Facts(facts, spans)
    query_, key_, value_, key_beside_, value_beside_, semaphores = scratch
    start, size = parts_of(here.rank, ranks, query.shape[0])[part]
    copies = [
        copied(source, target, semaphores.at[index])
        for index, (source, target) in enumerate((
            (query.at[pl.ds(start, size)], query_),
            (key, key_), (key_beside, key_beside_), (value, value_), (value_beside, value_beside_),
        ))
    ]
    for copy in copies:
        copy.wait()

    def write(columns, block):
        result[:, columns] = block

    flags = [None, here.sees(here.span, here.beside)]
    sums[...] = attend(query_, [key_, key_beside_], [value_, value_beside_], flags, write)


def served_kernel(distance, spans, facts, key, value, key_beside, value_beside, *refs):
    here = Facts(facts, spans)

    @pl.when(here.span + distance < spans)
    def _():
        asker = jnp.minimum(here.span + distance, spans - 1)
        flags = [here.sees(asker, here.span), here.sees(asker, here.beside)]
        *queries, result, query = refs
        at = 0
        for part in queries:
            query[at:at + part.shape[0], :] = part[...]
            at += part.shape[0]

        def write(columns, block):
            result[:, columns] = block.astype(jnp.bfloat16)

        rest = attend(query, [key, key_beside], [value, value_beside], flags, write)
        sent = jnp.zeros_like(rest)
        for piece in range(3):
            part = rest.astype(jnp.bfloat16).astype(jnp.float32)
            sent = sent + (part if piece == 0 else pltpu.roll(part, piece * PIECE_LANES, 1))
            rest = rest - part
        result[:, query.shape[1]:] = sent.astype(jnp.bfloat16)


def merge(span, distances, own, own_sum, served, write):
    width = own.shape[1]
    sums = [own_sum[...]]
    for distance, ref in zip(distances, served):
        sent = ref[:, width:].astype(jnp.float32)
        joined = sent
        for piece in (1, 2):
            joined = joined + pltpu.roll(sent, LANES - piece * PIECE_LANES, 1)
        sums.append(jnp.where(span >= distance, joined, HIDDEN))
    top = functools.reduce(jnp.maximum, sums)
    shares = [jnp.exp2(one - top) for one in sums]
    over = 1.0 / sum(shares)
    shares = [share * over for share in shares]
    for head in range(width // HD):
        columns = head_columns(head)
        merged = own[:, columns] * shares[0][:, head:head + 1]
        for distance, share, ref in zip(distances, shares[1:], served):
            away = jnp.where(span >= distance, ref[:, columns].astype(jnp.float32), 0.0)
            merged = merged + away * share[:, head:head + 1]
        write(columns, merged.astype(jnp.bfloat16))


def streamed(weight, first, tiles, semaphores):
    count, _, tile = tiles.shape
    return [
        copied(weight.at[:, pl.ds(first + index * tile, tile)], tiles.at[index], semaphores.at[index])
        for index in range(count)
    ]


def opening_kernel(spans, ranks, distances, first, facts, *refs):
    own, own_sum, *served = refs[:2 + len(distances)]
    weight, result, tiles, rows, semaphores = refs[2 + len(distances):]
    here = Facts(facts, spans)
    tile = tiles.shape[2]

    @pl.when(jnp.logical_or(here.rank == 0, here.rank == ranks - 1))
    def _():
        copies = streamed(weight, first, tiles, semaphores)

        def write(columns, part):
            rows[:, columns] = part

        merge(here.span, distances, own, own_sum, served, write)
        for index, copy in enumerate(copies):
            copy.wait()
            product = jnp.dot(rows[...], tiles[index], preferred_element_type=jnp.float32)
            result[:, index * tile:(index + 1) * tile] = product.astype(jnp.bfloat16)


def project_blocks(ranks, first, facts, step, attended, weight, up, down, tiles, semaphores):
    rank = facts.rank
    last = ranks - 1
    tile = tiles.shape[2]
    block = up.shape[0]
    copies = streamed(weight, first, tiles, semaphores)
    yield
    sends = rank <= step, rank >= last - step
    starts = [
        pl.multiple_of(jnp.clip(target, 0, last) * block, block) for target in (last - step + rank, step + rank - last)
    ]
    rows = [attended[pl.ds(start, block), :] for start in starts]
    for index, copy in enumerate(copies):
        copy.wait()
        there = slice(index * tile, (index + 1) * tile)

        @pl.when(jnp.logical_and(*sends))
        def _():
            both = jnp.dot(jnp.concatenate(rows, axis=0), tiles[index], preferred_element_type=jnp.float32)
            up[:, there] = both[:block].astype(jnp.bfloat16)
            down[:, there] = both[block:].astype(jnp.bfloat16)

        @pl.when(jnp.logical_not(jnp.logical_and(*sends)))
        def _():
            one = jnp.dot(
                jnp.where(sends[0], rows[0], rows[1]), tiles[index], preferred_element_type=jnp.float32
            ).astype(jnp.bfloat16)
            up[:, there] = one
            down[:, there] = one


def merged_blocks_kernel(spans, ranks, distances, facts, *refs):
    each = 2 + len(distances)
    parts, (weight, attended, *results) = (refs[:each], refs[each:2 * each]), refs[2 * each:]
    here = Facts(facts, spans)
    work = project_blocks(ranks, 0, here, 1, attended, weight, *results)
    next(work)
    for (start, size), (own, own_sum, *served) in zip(parts_of(here.rank, ranks, attended.shape[0]), parts):
        there = pl.ds(start, size)

        def write(columns, part):
            attended[there, columns] = part

        merge(here.span, distances, own, own_sum, served, write)
    for _ in work:
        pass


def blocks_kernel(spans, ranks, first, step, facts, attended, weight, *results):
    for _ in project_blocks(ranks, first, Facts(facts, spans), step, attended, weight, *results):
        pass


def own_kernel(spans, facts, attended, weight, gate_table, result, gate, tiles, gates, semaphores):
    here = Facts(facts, spans)
    block = result.shape[0]
    count, _, tile = tiles.shape
    level = here.level()
    above = pl.multiple_of(level // 8 * 8, 8)
    gate_copy = copied(gate_table.at[pl.ds(above, 8)], gates, semaphores.at[count])
    copies = streamed(weight, 0, tiles, semaphores)
    start = pl.multiple_of(here.rank * block, block)
    for index, copy in enumerate(copies):
        copy.wait()
        product = jnp.dot(attended[pl.ds(start, block), :], tiles[index], preferred_element_type=jnp.float32)
        result[:, index * tile:(index + 1) * tile] = product.astype(jnp.bfloat16)
    gate_copy.wait()
    gate[...] = gates[pl.ds(lax.rem(level, 8), 1), :]


def final_kernel(done, projected, gate, up, down, result, own, gated, semaphores):
    first, (block, columns) = done.shape[1], own.shape
    pieces = gated.shape[0]
    wide = columns // pieces
    own_copy = copied(projected.at[:, pl.ds(first, columns)], own, semaphores.at[0])
    sent = [copied(done, result.at[:, pl.ds(0, first)], semaphores.at[1])]
    own_copy.wait()
    for piece in range(pieces):
        there = slice(piece * wide, (piece + 1) * wide)
        summed = own[:, there].astype(jnp.float32) + up[:, there].astype(jnp.float32)
        summed = summed + down[:, there].astype(jnp.float32)
        gated[piece] = (summed * gate[:, first + piece * wide:first + (piece + 1) * wide]).astype(jnp.bfloat16)
        sent.append(copied(
            gated.at[piece], result.at[:, pl.ds(first + piece * wide, wide)], semaphores.at[2 + piece]
        ))
    for copy in sent:
        copy.wait()


def body(queries, keys, values, out_weight, gate_table, levels, visible):
    rows, width = queries.shape
    model = out_weight.shape[1]
    spans = lax.axis_size("span")
    ranks = lax.axis_size("tensor")
    span = lax.axis_index("span")
    rank = lax.axis_index("tensor")
    block = rows // ranks
    bf16, f32 = jnp.bfloat16, jnp.float32
    numbers = jnp.arange(spans, dtype=jnp.int32)
    place = jnp.where(numbers == 0, span, jnp.where(numbers == 1, rank, 0)).astype(jnp.int32)
    facts = jnp.concatenate([visible, place[None, :], levels[None, :]], axis=0)

    third = (rows - block) // 48 * 16
    query_early, *query_late = pl.pallas_call(
        functools.partial(split_kernel, spans, ranks),
        in_specs=[SMEM, HBM],
        out_specs=[VMEM] * 3,
        out_shape=[jax.ShapeDtypeStruct((part, width), bf16) for part in (block, rows - block - third, third)],
        scratch_shapes=[pltpu.SemaphoreType.DMA((3,))],
        compiler_params=PARAMS,
        cost_estimate=taking(1.7),
        name="split",
    )(facts, in_hbm(queries))
    distances = list(range(2, spans, 2))
    asked_early = [shifted(query_early, "span", -distance) for distance in distances]
    swap = [(i, i + 1 - 2 * (i % 2)) for i in range(spans)]
    key_beside = lax.ppermute(keys, "span", swap)
    value_beside = lax.ppermute(values, "span", swap)

    def after(value, *others):
        return lax.optimization_barrier((value, others))[0]

    def local(part, facts):
        size = (block, rows - block)[part]
        return pl.pallas_call(
            functools.partial(local_kernel, spans, ranks, part),
            in_specs=[SMEM, HBM, HBM, HBM, ANY, ANY],
            out_specs=[VMEM] * 2,
            out_shape=[jax.ShapeDtypeStruct((size, width), f32), jax.ShapeDtypeStruct((size, LANES), f32)],
            scratch_shapes=[pltpu.VMEM((size, width), bf16)] + [pltpu.VMEM((rows, width), bf16)] * 4
            + [pltpu.SemaphoreType.DMA((5,))],
            compiler_params=PARAMS,
            cost_estimate=taking(4.0),
            name="local",
        )(facts, in_hbm(queries), in_hbm(keys), in_hbm(values), key_beside, value_beside)

    def served(asked, distance):
        return pl.pallas_call(
            functools.partial(served_kernel, distance, spans),
            in_specs=[SMEM] + [VMEM] * (4 + len(asked)),
            out_specs=VMEM,
            out_shape=jax.ShapeDtypeStruct((sum(part.shape[0] for part in asked), width + LANES), bf16),
            scratch_shapes=[pltpu.VMEM((sum(part.shape[0] for part in asked), width), bf16)],
            compiler_params=PARAMS,
            cost_estimate=taking(3.3),
            name="served",
        )(facts, keys, values, key_beside, value_beside, *asked)

    early = list(local(0, facts))
    query_late = after(query_late, early)
    asked_early = after(asked_early, early)
    asked_late = [[shifted(query, "span", -distance) for query in query_late] for distance in distances]
    early += [shifted(served([q], d), "span", d) for q, d in zip(asked_early, distances)]

    chunks = 2
    columns = model // chunks
    tiles = 4
    tile = columns // tiles
    last = ranks - 1
    weight = in_hbm(out_weight)

    def opening(chunk, facts):
        return pl.pallas_call(
            functools.partial(opening_kernel, spans, ranks, distances, chunk * columns),
            in_specs=[SMEM] + [VMEM] * (2 + len(distances)) + [HBM],
            out_specs=VMEM,
            out_shape=jax.ShapeDtypeStruct((block, columns), bf16),
            scratch_shapes=[
                pltpu.VMEM((tiles, width, tile), bf16),
                pltpu.VMEM((block, width), bf16),
                pltpu.SemaphoreType.DMA((tiles,)),
            ],
            compiler_params=PARAMS,
            cost_estimate=taking(3.4),
            name="opening",
        )(facts, *early, weight)

    ends = [(0, 1), (last, last - 1)]
    sent = opening(0, facts)
    arrived = [[lax.ppermute(sent, "tensor", ends)]]
    out_late = [served(q, d) for q, d in zip(after(asked_late, sent), distances)]
    for chunk in range(1, chunks):
        sent = opening(chunk, after(facts, out_late))
        arrived.append([lax.ppermute(sent, "tensor", ends)])
    late = list(local(1, after(facts, sent)))
    late += [shifted(o, "span", d) for o, d in zip(out_late, distances)]

    streaming = dict(
        scratch_shapes=[pltpu.VMEM((tiles, width, tile), bf16), pltpu.SemaphoreType.DMA((tiles,))],
        compiler_params=PARAMS,
        cost_estimate=taking(3.0),
    )
    attended_shape = jax.ShapeDtypeStruct((rows, width), bf16)
    block_shapes = [jax.ShapeDtypeStruct((block, columns), bf16)] * 2
    attended, *merged = pl.pallas_call(
        functools.partial(merged_blocks_kernel, spans, ranks, distances),
        in_specs=[SMEM] + [VMEM] * (4 + 2 * len(distances)) + [HBM],
        out_specs=[VMEM] * 3,
        out_shape=[attended_shape] + block_shapes,
        name="merged_blocks",
        **streaming,
    )(facts, *early, *late, weight)

    def blocks_of(step, chunk, attended):
        return pl.pallas_call(
            functools.partial(blocks_kernel, spans, ranks, chunk * columns, step),
            in_specs=[SMEM, VMEM, HBM],
            out_specs=[VMEM] * 2,
            out_shape=block_shapes,
            name="blocks",
            **streaming,
        )(facts, attended, weight)

    before = attended
    for step in range(1, last):
        for chunk in range(chunks):
            if step == 1 and chunk == 0:
                blocks = merged
            else:
                blocks = blocks_of(step, chunk, after(attended, before))
            comes, blocks = lax.optimization_barrier((arrived[chunk], blocks))
            up, down = [
                (mine.astype(f32) + come.astype(f32)).astype(bf16)
                for mine, come in zip(blocks, (comes[0], comes[-1]))
            ]
            before = (up, down)
            arrived[chunk] = [
                lax.ppermute(up, "tensor", [(i, i + 1) for i in range(step + 1)]),
                lax.ppermute(down, "tensor", [(last - i, last - i - 1) for i in range(step + 1)]),
            ]
    everything = chunks * tiles
    projected, gate = pl.pallas_call(
        functools.partial(own_kernel, spans),
        in_specs=[SMEM, VMEM, HBM, HBM],
        out_specs=[VMEM, VMEM],
        out_shape=[jax.ShapeDtypeStruct((block, model), bf16), jax.ShapeDtypeStruct((1, model), f32)],
        scratch_shapes=[
            pltpu.VMEM((everything, width, tile), bf16),
            pltpu.VMEM((8, model), f32),
            pltpu.SemaphoreType.DMA((everything + 1,)),
        ],
        compiler_params=PARAMS,
        cost_estimate=taking(5.0),
        name="own",
    )(facts, after(attended, before), weight, in_hbm(gate_table))

    finished = []
    for chunk in range(chunks - 1):
        there = slice(chunk * columns, (chunk + 1) * columns)
        summed = sum(part.astype(f32) for part in (projected[:, there], *arrived[chunk]))
        finished.append((summed * gate[:, there]).astype(bf16))
    pieces = 2
    return pl.pallas_call(
        final_kernel,
        in_specs=[ANY, ANY, VMEM, VMEM, VMEM],
        out_specs=HBM,
        out_shape=jax.ShapeDtypeStruct((block, model), bf16),
        scratch_shapes=[
            pltpu.VMEM((block, columns), bf16),
            pltpu.VMEM((pieces, block, columns // pieces), bf16),
            pltpu.SemaphoreType.DMA((2 + pieces,)),
        ],
        compiler_params=PARAMS,
        cost_estimate=taking(2.7),
        name="final",
    )(jnp.concatenate(finished, axis=1), projected, gate, *arrived[-1])


def solution(mesh):
    return jax.shard_map(
        body,
        mesh=mesh,
        in_specs=(
            P(("group", "span"), "tensor"),
            P(("group", "span"), "tensor"),
            P(("group", "span"), "tensor"),
            P("tensor", None),
            P(),
            P("group"),
            P("group", None),
        ),
        out_specs=P(("group", "span", "tensor"), None),
        check_vma=False,
    )
```

```python
import functools

import jax
import jax.numpy as jnp
from jax import lax
from jax.experimental import pallas as pl
from jax.experimental.pallas import tpu as pltpu
from jax.sharding import PartitionSpec as P

HD = 128
LANES = 128
HIDDEN = -1e30
LOG2E = 1.4426950408889634
PARAMS = pltpu.CompilerParams(vmem_limit_bytes=24 * 1024 * 1024)
SMEM = pl.BlockSpec(memory_space=pltpu.SMEM)
VMEM = pl.BlockSpec(memory_space=pltpu.VMEM)
ANY = pl.BlockSpec(memory_space=pl.ANY)
HBM = pl.BlockSpec(memory_space=pltpu.HBM)
PIECE_LANES = 32


def taking(microseconds):
    return pl.CostEstimate(flops=0, bytes_accessed=int(microseconds * 3.69e6), transcendentals=0)


def in_hbm(array):
    return pltpu.with_memory_space_constraint(array, pltpu.HBM)


def shifted(block, axis, distance):
    count = lax.axis_size(axis)
    return lax.ppermute(block, axis, [(i, i + distance) for i in range(count) if 0 <= i + distance < count])


def head_columns(head):
    return slice(head * HD, (head + 1) * HD)


def attend(query, keys, values, flags, write):
    rows, width = query.shape
    scale = LOG2E * HD ** (-0.5)
    lane = lax.broadcasted_iota(jnp.int32, (rows, LANES), 1)
    packed = jnp.zeros((rows, LANES), jnp.float32)
    for head in range(width // HD):
        columns = head_columns(head)
        mine = query[:, columns]
        scores = [
            lax.dot_general(mine, key[:, columns], (((1,), (1,)), ((), ())), preferred_element_type=jnp.float32)
            for key in keys
        ]
        tops = [jnp.max(block, axis=-1, keepdims=True) * scale for block in scores]
        top = functools.reduce(
            jnp.maximum, [one if flag is None else jnp.where(flag, one, HIDDEN) for one, flag in zip(tops, flags)]
        )
        joined = None
        for block, value, flag in zip(scores, values, flags):
            above = top if flag is None else jnp.where(flag, top, -HIDDEN)
            probs = jnp.exp2(block * scale - above).astype(jnp.bfloat16)
            beside = jnp.concatenate([value[:, columns], jnp.ones((value.shape[0], HD), jnp.bfloat16)], axis=1)
            part = jnp.dot(probs, beside, preferred_element_type=jnp.float32)
            joined = part if joined is None else joined + part
        product, total = joined[:, :HD], jnp.where(joined[:, HD:] > 0.0, joined[:, HD:], 1.0)
        write(columns, product / total)
        packed = jnp.where(lane == head, top + jnp.log2(total), packed)
    return packed


class Facts:
    def __init__(self, ref, spans):
        self.ref, self.spans = ref, spans
        self.span, self.rank = ref[spans, 0], ref[spans, 1]
        self.beside = self.span + 1 - 2 * lax.rem(self.span, 2)

    def sees(self, asker, span):
        return self.ref[asker, span] > 0

    def level(self):
        return self.ref[self.spans + 1, self.span]


def copied(source, target, semaphore):
    copy = pltpu.make_async_copy(source, target, semaphore)
    copy.start()
    return copy


def parts_of(rank, ranks, rows):
    block = rows // ranks
    lower = rank < ranks // 2
    early = pl.multiple_of(jnp.where(lower, rows - block, 0), block)
    late = pl.multiple_of(jnp.where(lower, 0, block), block)
    return (early, block), (late, rows - block)


def split_kernel(spans, ranks, facts, query, weight, *refs):
    here = Facts(facts, spans)
    *targets, piece, semaphores = refs
    (early, _), (late, _) = parts_of(here.rank, ranks, query.shape[0])
    starts = (early, late, late + targets[1].shape[0])
    copies = [
        pltpu.make_async_copy(
            query.at[pl.ds(pl.multiple_of(start, 16), target.shape[0])], target, semaphores.at[index]
        )
        for index, (start, target) in enumerate(zip(starts, targets))
    ]
    size, columns = piece.shape
    first = pl.multiple_of(jnp.minimum(facts[spans, 2] * size, weight.shape[0] - size), 16)
    taken = copied(
        weight.at[pl.ds(first, size), pl.ds(weight.shape[1] - columns, columns)], piece, semaphores.at[len(copies)]
    )

    @pl.when(here.span > 1)
    def _():
        for copy in copies:
            copy.start()
        for copy in copies:
            copy.wait()

    taken.wait()


def local_kernel(spans, ranks, part, facts, query, key, value, key_beside, value_beside, result, sums, *scratch):
    here = Facts(facts, spans)
    query_, key_, value_, key_beside_, value_beside_, semaphores = scratch
    start, size = parts_of(here.rank, ranks, query.shape[0])[part]
    copies = [
        copied(source, target, semaphores.at[index])
        for index, (source, target) in enumerate((
            (query.at[pl.ds(start, size)], query_),
            (key, key_), (key_beside, key_beside_), (value, value_), (value_beside, value_beside_),
        ))
    ]
    for copy in copies:
        copy.wait()

    def write(columns, block):
        result[:, columns] = block

    flags = [None, here.sees(here.span, here.beside)]
    sums[...] = attend(query_, [key_, key_beside_], [value_, value_beside_], flags, write)


def served_kernel(distance, spans, facts, key, value, key_beside, value_beside, *refs):
    here = Facts(facts, spans)

    @pl.when(here.span + distance < spans)
    def _():
        asker = jnp.minimum(here.span + distance, spans - 1)
        flags = [here.sees(asker, here.span), here.sees(asker, here.beside)]
        *queries, result, query = refs
        at = 0
        for part in queries:
            query[at:at + part.shape[0], :] = part[...]
            at += part.shape[0]

        def write(columns, block):
            result[:, columns] = block.astype(jnp.bfloat16)

        rest = attend(query, [key, key_beside], [value, value_beside], flags, write)
        sent = jnp.zeros_like(rest)
        for piece in range(3):
            part = rest.astype(jnp.bfloat16).astype(jnp.float32)
            sent = sent + (part if piece == 0 else pltpu.roll(part, piece * PIECE_LANES, 1))
            rest = rest - part
        result[:, query.shape[1]:] = sent.astype(jnp.bfloat16)


def merge(span, distances, own, own_sum, served, write):
    width = own.shape[1]
    sums = [own_sum[...]]
    for distance, ref in zip(distances, served):
        sent = ref[:, width:].astype(jnp.float32)
        joined = sent
        for piece in (1, 2):
            joined = joined + pltpu.roll(sent, LANES - piece * PIECE_LANES, 1)
        sums.append(jnp.where(span >= distance, joined, HIDDEN))
    top = functools.reduce(jnp.maximum, sums)
    shares = [jnp.exp2(one - top) for one in sums]
    over = 1.0 / sum(shares)
    shares = [share * over for share in shares]
    for head in range(width // HD):
        columns = head_columns(head)
        merged = own[:, columns] * shares[0][:, head:head + 1]
        for distance, share, ref in zip(distances, shares[1:], served):
            away = jnp.where(span >= distance, ref[:, columns].astype(jnp.float32), 0.0)
            merged = merged + away * share[:, head:head + 1]
        write(columns, merged.astype(jnp.bfloat16))


def streamed(weight, first, tiles, semaphores):
    count, _, tile = tiles.shape
    return [
        copied(weight.at[:, pl.ds(first + index * tile, tile)], tiles.at[index], semaphores.at[index])
        for index in range(count)
    ]


def opening_kernel(spans, ranks, distances, facts, *refs):
    own, own_sum, *served = refs[:2 + len(distances)]
    weight, rows, result, tiles, semaphores = refs[2 + len(distances):]
    here = Facts(facts, spans)
    tile = tiles.shape[2]
    is_end = jnp.logical_or(here.rank == 0, here.rank == ranks - 1)

    def merged():
        def write(columns, part):
            rows[:, columns] = part

        merge(here.span, distances, own, own_sum, served, write)

    @pl.when(is_end)
    def _():
        copies = streamed(weight, 0, tiles, semaphores)
        merged()
        for index, copy in enumerate(copies):
            copy.wait()
            product = jnp.dot(rows[...], tiles[index], preferred_element_type=jnp.float32)
            result[:, index * tile:(index + 1) * tile] = product.astype(jnp.bfloat16)

    @pl.when(jnp.logical_not(is_end))
    def _():
        merged()


def project_blocks(ranks, first, facts, step, attended, weight, up, down, tiles, semaphores):
    rank = facts.rank
    last = ranks - 1
    tile = tiles.shape[2]
    block = up.shape[0]
    copies = streamed(weight, first, tiles, semaphores)
    yield
    sends = rank <= step, rank >= last - step
    starts = [
        pl.multiple_of(jnp.clip(target, 0, last) * block, block) for target in (last - step + rank, step + rank - last)
    ]
    rows = [attended[pl.ds(start, block), :] for start in starts]
    for index, copy in enumerate(copies):
        copy.wait()
        there = slice(index * tile, (index + 1) * tile)

        @pl.when(jnp.logical_and(*sends))
        def _():
            both = jnp.dot(jnp.concatenate(rows, axis=0), tiles[index], preferred_element_type=jnp.float32)
            up[:, there] = both[:block].astype(jnp.bfloat16)
            down[:, there] = both[block:].astype(jnp.bfloat16)

        @pl.when(jnp.logical_not(jnp.logical_and(*sends)))
        def _():
            one = jnp.dot(
                jnp.where(sends[0], rows[0], rows[1]), tiles[index], preferred_element_type=jnp.float32
            ).astype(jnp.bfloat16)
            up[:, there] = one
            down[:, there] = one


def merged_blocks_kernel(spans, ranks, distances, facts, *refs):
    each = 2 + len(distances)
    parts, (weight, attended, *results) = (refs[:each], refs[each:2 * each]), refs[2 * each:]
    here = Facts(facts, spans)
    work = project_blocks(ranks, 0, here, 1, attended, weight, *results)
    next(work)
    for (start, size), (own, own_sum, *served) in zip(parts_of(here.rank, ranks, attended.shape[0]), parts):
        there = pl.ds(start, size)

        def write(columns, part):
            attended[there, columns] = part

        merge(here.span, distances, own, own_sum, served, write)
    for _ in work:
        pass


def blocks_kernel(spans, ranks, first, step, facts, attended, weight, *results):
    for _ in project_blocks(ranks, first, Facts(facts, spans), step, attended, weight, *results):
        pass


def is_inner(rank, ranks):
    return jnp.logical_or(rank == 1, rank == ranks - 2)


def streamed_pairs(weight, first, end_weight, tiles, semaphores):
    count, depth, tile = tiles.shape
    width = depth // 2
    copies = []
    for index in range(count):
        columns = pl.ds(first + index * tile, tile)
        copies.append((
            copied(weight.at[:, columns], tiles.at[index, pl.ds(0, width)], semaphores.at[2 * index]),
            copied(
                end_weight.at[:, pl.ds(index * tile, tile)], tiles.at[index, pl.ds(width, width)],
                semaphores.at[2 * index + 1],
            ),
        ))
    return copies


def joint_opening_kernel(spans, ranks, first, facts, rows, end_rows, weight, end_weight, result, tiles, semaphores):
    tile = tiles.shape[2]

    @pl.when(is_inner(Facts(facts, spans).rank, ranks))
    def _():
        copies = streamed_pairs(weight, first, end_weight, tiles, semaphores)
        both = jnp.concatenate([rows[...], end_rows[...]], axis=1)
        for index, pair in enumerate(copies):
            for copy in pair:
                copy.wait()
            product = jnp.dot(both, tiles[index], preferred_element_type=jnp.float32)
            result[:, index * tile:(index + 1) * tile] = product.astype(jnp.bfloat16)


def joint_blocks_kernel(spans, ranks, first, step, facts, attended, end_rows, weight, end_weight,
                        up, down, tiles, semaphores):
    rank = Facts(facts, spans).rank
    last = ranks - 1
    block, tile = up.shape[0], tiles.shape[2]
    width = attended.shape[1]
    copies = streamed_pairs(weight, first, end_weight, tiles, semaphores)

    def block_of(array, target, count):
        return array[pl.ds(pl.multiple_of(jnp.clip(target, 0, count - 1) * block, block), block), :]

    up_target, down_target = last - step + rank - 1, step - last + rank + 1
    rows = jnp.concatenate([block_of(attended, target, ranks) for target in (up_target, down_target)], axis=0)
    others = jnp.concatenate([
        jnp.where(takes, block_of(end_rows, target - 1, ranks - 2), jnp.zeros((block, width), jnp.bfloat16))
        for takes, target in ((rank == 1, up_target), (rank == last - 1, down_target))
    ], axis=0)
    for index, pair in enumerate(copies):
        for copy in pair:
            copy.wait()
        there = slice(index * tile, (index + 1) * tile)

        def write(product):
            up[:, there] = product[:block].astype(jnp.bfloat16)
            down[:, there] = product[block:].astype(jnp.bfloat16)

        @pl.when(is_inner(rank, ranks))
        def _():
            both = jnp.concatenate([rows, others], axis=1)
            write(jnp.dot(both, tiles[index], preferred_element_type=jnp.float32))

        @pl.when(jnp.logical_not(is_inner(rank, ranks)))
        def _():
            write(jnp.dot(rows, tiles[index, :width], preferred_element_type=jnp.float32))


def own_kernel(spans, ranks, facts, attended, end_rows, weight, end_weight, gate_table, result, gate,
               tiles, pairs, gates, semaphores, pair_semaphores):
    here = Facts(facts, spans)
    block, width = result.shape[0], attended.shape[1]
    count, _, tile = tiles.shape
    columns = count * tile
    level = here.level()
    above = pl.multiple_of(level // 8 * 8, 8)
    gate_copy = copied(gate_table.at[pl.ds(above, 8)], gates, semaphores.at[count])
    copies = streamed(weight, 0, tiles, semaphores)
    pair_copies = streamed_pairs(weight, columns, end_weight, pairs, pair_semaphores)
    mine = attended[pl.ds(pl.multiple_of(here.rank * block, block), block), :]
    target = jnp.clip(here.rank - 1, 0, ranks - 3)
    other = end_rows[pl.ds(pl.multiple_of(target * block, block), block), :]
    other = jnp.where(is_inner(here.rank, ranks), other, jnp.zeros((block, width), jnp.bfloat16))
    for index, copy in enumerate(copies):
        copy.wait()
        product = jnp.dot(mine, tiles[index], preferred_element_type=jnp.float32)
        result[:, index * tile:(index + 1) * tile] = product.astype(jnp.bfloat16)
    both = jnp.concatenate([mine, other], axis=1)
    for index, pair in enumerate(pair_copies):
        for copy in pair:
            copy.wait()
        product = jnp.dot(both, pairs[index], preferred_element_type=jnp.float32)
        result[:, columns + index * tile:columns + (index + 1) * tile] = product.astype(jnp.bfloat16)
    gate_copy.wait()
    gate[...] = gates[pl.ds(lax.rem(level, 8), 1), :]


def final_kernel(done, projected, gate, up, down, result, own, gated, semaphores):
    first, (block, columns) = done.shape[1], own.shape
    pieces = gated.shape[0]
    wide = columns // pieces
    own_copy = copied(projected.at[:, pl.ds(first, columns)], own, semaphores.at[0])
    sent = [copied(done, result.at[:, pl.ds(0, first)], semaphores.at[1])]
    own_copy.wait()
    for piece in range(pieces):
        there = slice(piece * wide, (piece + 1) * wide)
        summed = own[:, there].astype(jnp.float32) + up[:, there].astype(jnp.float32)
        summed = summed + down[:, there].astype(jnp.float32)
        gated[piece] = (summed * gate[:, first + piece * wide:first + (piece + 1) * wide]).astype(jnp.bfloat16)
        sent.append(copied(
            gated.at[piece], result.at[:, pl.ds(first + piece * wide, wide)], semaphores.at[2 + piece]
        ))
    for copy in sent:
        copy.wait()


def body(queries, keys, values, out_weight, gate_table, levels, visible):
    rows, width = queries.shape
    model = out_weight.shape[1]
    spans = lax.axis_size("span")
    ranks = lax.axis_size("tensor")
    span = lax.axis_index("span")
    rank = lax.axis_index("tensor")
    block = rows // ranks
    bf16, f32 = jnp.bfloat16, jnp.float32
    numbers = jnp.arange(spans, dtype=jnp.int32)
    member = lax.axis_index("group") * spans + span
    place = jnp.where(numbers == 0, span, jnp.where(numbers == 1, rank, member)).astype(jnp.int32)
    facts = jnp.concatenate([visible, place[None, :], levels[None, :]], axis=0)

    third = (rows - block) // 48 * 16
    columns = model // 2
    pieces = -(-width // (16 * lax.axis_size("group") * spans)) * 16
    query_early, *query_late, piece = pl.pallas_call(
        functools.partial(split_kernel, spans, ranks),
        in_specs=[SMEM, HBM, HBM],
        out_specs=[VMEM] * 3 + [HBM],
        out_shape=[jax.ShapeDtypeStruct((part, width), bf16) for part in (block, rows - block - third, third)]
        + [pltpu.HBM((pieces, columns), bf16)],
        scratch_shapes=[pltpu.SemaphoreType.DMA((4,))],
        compiler_params=PARAMS,
        cost_estimate=taking(1.7),
        name="split",
    )(facts, in_hbm(queries), in_hbm(out_weight))
    distances = list(range(2, spans, 2))
    asked_early = [shifted(query_early, "span", -distance) for distance in distances]
    swap = [(i, i + 1 - 2 * (i % 2)) for i in range(spans)]
    key_beside = lax.ppermute(keys, "span", swap)
    value_beside = lax.ppermute(values, "span", swap)

    def after(value, *others):
        return lax.optimization_barrier((value, others))[0]

    def local(part, facts):
        size = (block, rows - block)[part]
        return pl.pallas_call(
            functools.partial(local_kernel, spans, ranks, part),
            in_specs=[SMEM, HBM, HBM, HBM, ANY, ANY],
            out_specs=[VMEM] * 2,
            out_shape=[jax.ShapeDtypeStruct((size, width), f32), jax.ShapeDtypeStruct((size, LANES), f32)],
            scratch_shapes=[pltpu.VMEM((size, width), bf16)] + [pltpu.VMEM((rows, width), bf16)] * 4
            + [pltpu.SemaphoreType.DMA((5,))],
            compiler_params=PARAMS,
            cost_estimate=taking(4.0),
            name="local",
        )(facts, in_hbm(queries), in_hbm(keys), in_hbm(values), key_beside, value_beside)

    def served(asked, distance):
        return pl.pallas_call(
            functools.partial(served_kernel, distance, spans),
            in_specs=[SMEM] + [VMEM] * (4 + len(asked)),
            out_specs=VMEM,
            out_shape=jax.ShapeDtypeStruct((sum(part.shape[0] for part in asked), width + LANES), bf16),
            scratch_shapes=[pltpu.VMEM((sum(part.shape[0] for part in asked), width), bf16)],
            compiler_params=PARAMS,
            cost_estimate=taking(3.3),
            name="served",
        )(facts, keys, values, key_beside, value_beside, *asked)

    ends = [(0, 1), (ranks - 1, ranks - 2)]
    end_piece = lax.ppermute(after(piece, key_beside), "tensor", ends)

    query_late = after(query_late, value_beside)
    asked_late = [[shifted(query, "span", -distance) for query in query_late] for distance in distances]
    out_early = [served([q], d) for q, d in zip(asked_early, distances)]
    early = list(local(0, after(facts, out_early)))
    early += [shifted(o, "span", d) for o, d in zip(out_early, distances)]

    tiles = 4
    tile = columns // tiles
    last = ranks - 1
    weight = in_hbm(out_weight)
    message_shape = jax.ShapeDtypeStruct((block, columns), bf16)
    streaming = dict(
        scratch_shapes=[pltpu.VMEM((tiles, width, tile), bf16), pltpu.SemaphoreType.DMA((tiles,))],
        compiler_params=PARAMS,
        cost_estimate=taking(3.0),
    )
    pair_streaming = dict(streaming, scratch_shapes=[
        pltpu.VMEM((tiles, 2 * width, tile), bf16), pltpu.SemaphoreType.DMA((2 * tiles,))
    ])

    early_rows, sent = pl.pallas_call(
        functools.partial(opening_kernel, spans, ranks, distances),
        in_specs=[SMEM] + [VMEM] * (2 + len(distances)) + [HBM],
        out_specs=[VMEM, VMEM],
        out_shape=[jax.ShapeDtypeStruct((block, width), bf16), message_shape],
        name="opening",
        **streaming,
    )(after(facts, asked_late), *early, weight)
    arrived = [lax.ppermute(sent, "tensor", ends)]
    end_early = lax.ppermute(early_rows, "tensor", ends)
    end_weight = lax.all_gather(after(end_piece, sent), ("group", "span"), axis=0, tiled=True)[:width]
    out_late = [served(q, d) for q, d in zip(after(asked_late, sent), distances)]
    late = list(local(1, after(facts, out_late)))
    late += [shifted(o, "span", d) for o, d in zip(out_late, distances)]

    attended_shape = jax.ShapeDtypeStruct((rows, width), bf16)
    block_shapes = [message_shape] * 2
    attended, *merged = pl.pallas_call(
        functools.partial(merged_blocks_kernel, spans, ranks, distances),
        in_specs=[SMEM] + [VMEM] * (4 + 2 * len(distances)) + [HBM],
        out_specs=[VMEM] * 3,
        out_shape=[attended_shape] + block_shapes,
        name="merged_blocks",
        **streaming,
    )(after(facts, end_early), *early, *late, weight)

    def exchanged(up, down, base, step):
        reached = range(base, step + 1)
        return [
            lax.ppermute(up, "tensor", [(i, i + 1) for i in reached]),
            lax.ppermute(down, "tensor", [(last - i, last - i - 1) for i in reached]),
        ]

    def added(blocks, comes):
        return [
            (mine.astype(f32) + come.astype(f32)).astype(bf16) for mine, come in zip(blocks, (comes[0], comes[-1]))
        ]

    before = attended
    for step in range(1, last):
        if step == 1:
            blocks = merged
        else:
            blocks = pl.pallas_call(
                functools.partial(blocks_kernel, spans, ranks, 0, step),
                in_specs=[SMEM, VMEM, HBM],
                out_specs=[VMEM] * 2,
                out_shape=block_shapes,
                name="blocks",
                **streaming,
            )(facts, after(attended, before), weight)
        comes, blocks = lax.optimization_barrier((arrived, blocks))
        before = up, down = added(blocks, comes)
        arrived = exchanged(up, down, 0, step)
        if step == 1:
            end_rows = lax.ppermute(attended[block:rows - block], "tensor", ends)
            before = joint = pl.pallas_call(
                functools.partial(joint_opening_kernel, spans, ranks, columns),
                in_specs=[SMEM, VMEM, VMEM, HBM, HBM],
                out_specs=VMEM,
                out_shape=message_shape,
                name="joint_opening",
                **pair_streaming,
            )(facts, after(early_rows, before), end_early, weight, in_hbm(end_weight))
            come = lax.ppermute(joint, "tensor", [(1, 2), (last - 1, last - 2)])
            joint_arrived = [jnp.where(rank == to, come, jnp.zeros_like(come)) for to in (2, last - 2)]
        else:
            blocks = pl.pallas_call(
                functools.partial(joint_blocks_kernel, spans, ranks, columns, step - 1),
                in_specs=[SMEM, VMEM, VMEM, HBM, HBM],
                out_specs=[VMEM] * 2,
                out_shape=block_shapes,
                name="joint_blocks",
                **pair_streaming,
            )(facts, after(attended, before), end_rows, weight, in_hbm(end_weight))
            comes, blocks = lax.optimization_barrier((joint_arrived, blocks))
            before = up, down = added(blocks, comes)
            joint_arrived = exchanged(up, down, 1, step)
    arrived = [arrived, joint_arrived]
    projected, gate = pl.pallas_call(
        functools.partial(own_kernel, spans, ranks),
        in_specs=[SMEM, VMEM, VMEM, HBM, HBM, HBM],
        out_specs=[VMEM, VMEM],
        out_shape=[jax.ShapeDtypeStruct((block, model), bf16), jax.ShapeDtypeStruct((1, model), f32)],
        scratch_shapes=[
            pltpu.VMEM((tiles, width, tile), bf16),
            pltpu.VMEM((tiles, 2 * width, tile), bf16),
            pltpu.VMEM((8, model), f32),
            pltpu.SemaphoreType.DMA((tiles + 1,)),
            pltpu.SemaphoreType.DMA((2 * tiles,)),
        ],
        compiler_params=PARAMS,
        cost_estimate=taking(7.0),
        name="own",
    )(facts, after(attended, before), end_rows, weight, in_hbm(end_weight), in_hbm(gate_table))

    summed = sum(part.astype(f32) for part in (projected[:, :columns], *arrived[0]))
    finished = (summed * gate[:, :columns]).astype(bf16)
    pieces = 2
    return pl.pallas_call(
        final_kernel,
        in_specs=[ANY, ANY, VMEM, VMEM, VMEM],
        out_specs=HBM,
        out_shape=jax.ShapeDtypeStruct((block, model), bf16),
        scratch_shapes=[
            pltpu.VMEM((block, columns), bf16),
            pltpu.VMEM((pieces, block, columns // pieces), bf16),
            pltpu.SemaphoreType.DMA((2 + pieces,)),
        ],
        compiler_params=PARAMS,
        cost_estimate=taking(2.7),
        name="final",
    )(finished, projected, gate, *arrived[1])


def solution(mesh):
    return jax.shard_map(
        body,
        mesh=mesh,
        in_specs=(
            P(("group", "span"), "tensor"),
            P(("group", "span"), "tensor"),
            P(("group", "span"), "tensor"),
            P("tensor", None),
            P(),
            P("group"),
            P("group", None),
        ),
        out_specs=P(("group", "span", "tensor"), None),
        check_vma=False,
    )
```

```python
import functools

import jax
import jax.numpy as jnp
from jax import lax
from jax.experimental import pallas as pl
from jax.experimental.pallas import tpu as pltpu
from jax.sharding import PartitionSpec as P

HD = 128
LANES = 128
HIDDEN = -1e30
LOG2E = 1.4426950408889634
PARAMS = pltpu.CompilerParams(vmem_limit_bytes=24 * 1024 * 1024)
SMEM = pl.BlockSpec(memory_space=pltpu.SMEM)
VMEM = pl.BlockSpec(memory_space=pltpu.VMEM)
ANY = pl.BlockSpec(memory_space=pl.ANY)
HBM = pl.BlockSpec(memory_space=pltpu.HBM)
PIECE_LANES = 32


def taking(microseconds):
    return pl.CostEstimate(flops=0, bytes_accessed=int(microseconds * 3.69e6), transcendentals=0)


def in_hbm(array):
    return pltpu.with_memory_space_constraint(array, pltpu.HBM)


def shifted(block, axis, distance):
    count = lax.axis_size(axis)
    return lax.ppermute(block, axis, [(i, i + distance) for i in range(count) if 0 <= i + distance < count])


def head_columns(head):
    return slice(head * HD, (head + 1) * HD)


def attend(query, keys, values, flags, write):
    rows, width = query.shape
    scale = LOG2E * HD ** (-0.5)
    lane = lax.broadcasted_iota(jnp.int32, (rows, LANES), 1)
    packed = jnp.zeros((rows, LANES), jnp.float32)

    def scored(head):
        columns = head_columns(head)
        return [
            lax.dot_general(
                query[:, columns], key[:, columns], (((1,), (1,)), ((), ())), preferred_element_type=jnp.float32
            )
            for key in keys
        ]

    heads = width // HD
    later = scored(0)
    for head in range(heads):
        columns = head_columns(head)
        scores, later = later, scored(head + 1) if head + 1 < heads else None
        tops = [jnp.max(block, axis=-1, keepdims=True) * scale for block in scores]
        top = functools.reduce(
            jnp.maximum, [one if flag is None else jnp.where(flag, one, HIDDEN) for one, flag in zip(tops, flags)]
        )
        joined = None
        for block, value, flag in zip(scores, values, flags):
            above = top if flag is None else jnp.where(flag, top, -HIDDEN)
            probs = jnp.exp2(block * scale - above).astype(jnp.bfloat16)
            beside = jnp.concatenate([value[:, columns], jnp.ones((value.shape[0], HD), jnp.bfloat16)], axis=1)
            part = jnp.dot(probs, beside, preferred_element_type=jnp.float32)
            joined = part if joined is None else joined + part
        product, total = joined[:, :HD], jnp.where(joined[:, HD:] > 0.0, joined[:, HD:], 1.0)
        write(columns, product / total)
        packed = jnp.where(lane == head, top + jnp.log2(total), packed)
    return packed


class Facts:
    def __init__(self, ref, spans):
        self.ref, self.spans = ref, spans
        self.span, self.rank = ref[spans, 0], ref[spans, 1]
        self.beside = self.span + 1 - 2 * lax.rem(self.span, 2)

    def sees(self, asker, span):
        return self.ref[asker, span] > 0

    def level(self):
        return self.ref[self.spans + 1, self.span]


def copied(source, target, semaphore):
    copy = pltpu.make_async_copy(source, target, semaphore)
    copy.start()
    return copy


def parts_of(rank, ranks, rows):
    block = rows // ranks
    lower = rank < ranks // 2
    early = pl.multiple_of(jnp.where(lower, rows - block, 0), block)
    late = pl.multiple_of(jnp.where(lower, 0, block), block)
    return (early, block), (late, rows - block)


def split_kernel(ranks, part, place, query, *refs):
    *targets, semaphores = refs

    @pl.when(place[0] > 1)
    def _():
        start, _ = parts_of(place[1], ranks, query.shape[0])[part]
        copies = []
        for index, target in enumerate(targets):
            size = target.shape[0]
            copies.append(copied(query.at[pl.ds(pl.multiple_of(start, 16), size)], target, semaphores.at[index]))
            start = start + size
        for copy in copies:
            copy.wait()


def local_kernel(spans, ranks, part, who, facts, query, key, value, key_beside, value_beside, *refs):
    here = Facts(facts, spans)
    if who is None:
        attend_here(here, ranks, part, query, key, value, key_beside, value_beside, *refs)
        return

    mine = here.span > 1 if who == "askers" else here.span < 2

    @pl.when(mine)
    def _():
        attend_here(here, ranks, part, query, key, value, key_beside, value_beside, *refs)

    *before, result, sums = refs[:-6]
    if before:

        @pl.when(jnp.logical_not(mine))
        def _():
            result[...] = before[0][...]
            sums[...] = before[1][...]


def attend_here(here, ranks, part, query, key, value, key_beside, value_beside, *refs):
    result, sums, query_, key_, value_, key_beside_, value_beside_, semaphores = refs[-8:]
    start, size = parts_of(here.rank, ranks, query.shape[0])[part]
    copies = [
        copied(source, target, semaphores.at[index])
        for index, (source, target) in enumerate((
            (query.at[pl.ds(start, size)], query_),
            (key, key_), (key_beside, key_beside_), (value, value_), (value_beside, value_beside_),
        ))
    ]
    for copy in copies:
        copy.wait()

    def write(columns, block):
        result[:, columns] = block

    flags = [None, here.sees(here.span, here.beside)]
    sums[...] = attend(query_, [key_, key_beside_], [value_, value_beside_], flags, write)


def served_kernel(distance, spans, facts, key, value, key_beside, value_beside, *refs):
    here = Facts(facts, spans)

    @pl.when(here.span + distance < spans)
    def _():
        asker = jnp.minimum(here.span + distance, spans - 1)
        flags = [here.sees(asker, here.span), here.sees(asker, here.beside)]
        *queries, result, query = refs
        at = 0
        for part in queries:
            query[at:at + part.shape[0], :] = part[...]
            at += part.shape[0]

        def write(columns, block):
            result[:, columns] = block.astype(jnp.bfloat16)

        rest = attend(query, [key, key_beside], [value, value_beside], flags, write)
        sent = jnp.zeros_like(rest)
        for piece in range(3):
            part = rest.astype(jnp.bfloat16).astype(jnp.float32)
            sent = sent + (part if piece == 0 else pltpu.roll(part, piece * PIECE_LANES, 1))
            rest = rest - part
        result[:, query.shape[1]:] = sent.astype(jnp.bfloat16)


def merge(span, distances, own, own_sum, served, write):
    width = own.shape[1]
    sums = [own_sum[...]]
    for distance, ref in zip(distances, served):
        sent = ref[:, width:].astype(jnp.float32)
        joined = sent
        for piece in (1, 2):
            joined = joined + pltpu.roll(sent, LANES - piece * PIECE_LANES, 1)
        sums.append(jnp.where(span >= distance, joined, HIDDEN))
    top = functools.reduce(jnp.maximum, sums)
    shares = [jnp.exp2(one - top) for one in sums]
    over = 1.0 / sum(shares)
    shares = [share * over for share in shares]
    for head in range(width // HD):
        columns = head_columns(head)
        merged = own[:, columns] * shares[0][:, head:head + 1]
        for distance, share, ref in zip(distances, shares[1:], served):
            away = jnp.where(span >= distance, ref[:, columns].astype(jnp.float32), 0.0)
            merged = merged + away * share[:, head:head + 1]
        write(columns, merged.astype(jnp.bfloat16))


def streamed(weight, first, tiles, semaphores):
    count, _, tile = tiles.shape
    return [
        copied(weight.at[:, pl.ds(first + index * tile, tile)], tiles.at[index], semaphores.at[index])
        for index in range(count)
    ]


def opening_kernel(spans, ranks, distances, first, facts, *refs):
    own, own_sum, *served = refs[:2 + len(distances)]
    weight, result, tiles, rows, semaphores = refs[2 + len(distances):]
    here = Facts(facts, spans)
    tile = tiles.shape[2]

    @pl.when(jnp.logical_or(here.rank == 0, here.rank == ranks - 1))
    def _():
        copies = streamed(weight, first, tiles, semaphores)

        def write(columns, part):
            rows[:, columns] = part

        merge(here.span, distances, own, own_sum, served, write)
        for index, copy in enumerate(copies):
            copy.wait()
            product = jnp.dot(rows[...], tiles[index], preferred_element_type=jnp.float32)
            result[:, index * tile:(index + 1) * tile] = product.astype(jnp.bfloat16)


def project_blocks(ranks, first, facts, step, attended, weight, up, down, tiles, semaphores):
    rank = facts.rank
    last = ranks - 1
    tile = tiles.shape[2]
    block = up.shape[0]
    copies = streamed(weight, first, tiles, semaphores)
    yield
    sends = rank <= step, rank >= last - step
    starts = [
        pl.multiple_of(jnp.clip(target, 0, last) * block, block) for target in (last - step + rank, step + rank - last)
    ]
    rows = [attended[pl.ds(start, block), :] for start in starts]
    for index, copy in enumerate(copies):
        copy.wait()
        there = slice(index * tile, (index + 1) * tile)

        @pl.when(jnp.logical_and(*sends))
        def _():
            both = jnp.dot(jnp.concatenate(rows, axis=0), tiles[index], preferred_element_type=jnp.float32)
            up[:, there] = both[:block].astype(jnp.bfloat16)
            down[:, there] = both[block:].astype(jnp.bfloat16)

        @pl.when(jnp.logical_not(jnp.logical_and(*sends)))
        def _():
            one = jnp.dot(
                jnp.where(sends[0], rows[0], rows[1]), tiles[index], preferred_element_type=jnp.float32
            ).astype(jnp.bfloat16)
            up[:, there] = one
            down[:, there] = one


def merged_blocks_kernel(spans, ranks, distances, facts, *refs):
    each = 2 + len(distances)
    parts, (weight, attended, *results) = (refs[:each], refs[each:2 * each]), refs[2 * each:]
    here = Facts(facts, spans)
    work = project_blocks(ranks, 0, here, 1, attended, weight, *results)
    next(work)
    for (start, size), (own, own_sum, *served) in zip(parts_of(here.rank, ranks, attended.shape[0]), parts):
        there = pl.ds(start, size)

        def write(columns, part):
            attended[there, columns] = part

        merge(here.span, distances, own, own_sum, served, write)
    for _ in work:
        pass


def blocks_kernel(spans, ranks, first, step, facts, attended, weight, *results):
    for _ in project_blocks(ranks, first, Facts(facts, spans), step, attended, weight, *results):
        pass


def own_kernel(spans, facts, attended, weight, gate_table, result, gate, tiles, gates, semaphores):
    here = Facts(facts, spans)
    block = result.shape[0]
    count, _, tile = tiles.shape
    level = here.level()
    above = pl.multiple_of(level // 8 * 8, 8)
    gate_copy = copied(gate_table.at[pl.ds(above, 8)], gates, semaphores.at[count])
    copies = streamed(weight, 0, tiles, semaphores)
    start = pl.multiple_of(here.rank * block, block)
    for index, copy in enumerate(copies):
        copy.wait()
        product = jnp.dot(attended[pl.ds(start, block), :], tiles[index], preferred_element_type=jnp.float32)
        result[:, index * tile:(index + 1) * tile] = product.astype(jnp.bfloat16)
    gate_copy.wait()
    gate[...] = gates[pl.ds(lax.rem(level, 8), 1), :]


def final_kernel(done, projected, gate, up, down, result, own, gated, semaphores):
    first, (block, columns) = done.shape[1], own.shape
    pieces = gated.shape[0]
    wide = columns // pieces
    own_copy = copied(projected.at[:, pl.ds(first, columns)], own, semaphores.at[0])
    sent = [copied(done, result.at[:, pl.ds(0, first)], semaphores.at[1])]
    own_copy.wait()
    for piece in range(pieces):
        there = slice(piece * wide, (piece + 1) * wide)
        summed = own[:, there].astype(jnp.float32) + up[:, there].astype(jnp.float32)
        summed = summed + down[:, there].astype(jnp.float32)
        gated[piece] = (summed * gate[:, first + piece * wide:first + (piece + 1) * wide]).astype(jnp.bfloat16)
        sent.append(copied(
            gated.at[piece], result.at[:, pl.ds(first + piece * wide, wide)], semaphores.at[2 + piece]
        ))
    for copy in sent:
        copy.wait()


def body(queries, keys, values, out_weight, gate_table, levels, visible):
    rows, width = queries.shape
    model = out_weight.shape[1]
    spans = lax.axis_size("span")
    ranks = lax.axis_size("tensor")
    span = lax.axis_index("span")
    rank = lax.axis_index("tensor")
    block = rows // ranks
    bf16, f32 = jnp.bfloat16, jnp.float32
    numbers = jnp.arange(spans, dtype=jnp.int32)
    place = jnp.where(numbers == 0, span, jnp.where(numbers == 1, rank, 0)).astype(jnp.int32)
    facts = jnp.concatenate([visible, place[None, :], levels[None, :]], axis=0)

    third = (rows - block) // 48 * 16
    here = jnp.stack([span, rank]).astype(jnp.int32)

    def split(part, place, sizes):
        return pl.pallas_call(
            functools.partial(split_kernel, ranks, part),
            in_specs=[SMEM, HBM],
            out_specs=[VMEM] * len(sizes),
            out_shape=[jax.ShapeDtypeStruct((size, width), bf16) for size in sizes],
            scratch_shapes=[pltpu.SemaphoreType.DMA((len(sizes),))],
            compiler_params=PARAMS,
            cost_estimate=taking(1.0),
            name="split",
        )(place, in_hbm(queries))

    query_early, = split(0, here, [block])
    distances = list(range(2, spans, 2))
    asked_early = [shifted(query_early, "span", -distance) for distance in distances]
    swap = [(i, i + 1 - 2 * (i % 2)) for i in range(spans)]
    key_beside = lax.ppermute(keys, "span", swap)
    value_beside = lax.ppermute(values, "span", swap)

    def after(value, *others):
        return lax.optimization_barrier((value, others))[0]

    def local(part, facts, who=None, before=()):
        size = (block, rows - block)[part]
        return list(pl.pallas_call(
            functools.partial(local_kernel, spans, ranks, part, who),
            in_specs=[SMEM, HBM, HBM, HBM, ANY, ANY] + [VMEM] * len(before),
            out_specs=[VMEM] * 2,
            out_shape=[jax.ShapeDtypeStruct((size, width), f32), jax.ShapeDtypeStruct((size, LANES), f32)],
            scratch_shapes=[pltpu.VMEM((size, width), bf16)] + [pltpu.VMEM((rows, width), bf16)] * 4
            + [pltpu.SemaphoreType.DMA((5,))],
            compiler_params=PARAMS,
            cost_estimate=taking(4.0),
            name="local",
        )(facts, in_hbm(queries), in_hbm(keys), in_hbm(values), key_beside, value_beside, *before))

    def served(asked, distance):
        return pl.pallas_call(
            functools.partial(served_kernel, distance, spans),
            in_specs=[SMEM] + [VMEM] * (4 + len(asked)),
            out_specs=VMEM,
            out_shape=jax.ShapeDtypeStruct((sum(part.shape[0] for part in asked), width + LANES), bf16),
            scratch_shapes=[pltpu.VMEM((sum(part.shape[0] for part in asked), width), bf16)],
            compiler_params=PARAMS,
            cost_estimate=taking(3.3),
            name="served",
        )(facts, keys, values, key_beside, value_beside, *asked)

    early = local(0, facts, "others")
    query_late = split(1, after(here, early), [rows - block - third, third])
    asked_late = [[shifted(query, "span", -distance) for query in query_late] for distance in distances]
    out_early = [served([q], d) for q, d in zip(after(asked_early, early), distances)]
    early = local(0, after(facts, out_early), "askers", early)
    early += [shifted(o, "span", d) for o, d in zip(out_early, distances)]

    chunks = 2
    columns = model // chunks
    tiles = 4
    tile = columns // tiles
    last = ranks - 1
    weight = in_hbm(out_weight)

    def opening(chunk, facts):
        return pl.pallas_call(
            functools.partial(opening_kernel, spans, ranks, distances, chunk * columns),
            in_specs=[SMEM] + [VMEM] * (2 + len(distances)) + [HBM],
            out_specs=VMEM,
            out_shape=jax.ShapeDtypeStruct((block, columns), bf16),
            scratch_shapes=[
                pltpu.VMEM((2 * tiles, width, tile // 2), bf16),
                pltpu.VMEM((block, width), bf16),
                pltpu.SemaphoreType.DMA((2 * tiles,)),
            ],
            compiler_params=PARAMS,
            cost_estimate=taking(3.4),
            name="opening",
        )(facts, *early, weight)

    ends = [(0, 1), (last, last - 1)]
    sent = opening(0, facts)
    arrived = [[lax.ppermute(sent, "tensor", ends)]]
    out_late = [served(q, d) for q, d in zip(after(asked_late, sent), distances)]
    for chunk in range(1, chunks):
        sent = opening(chunk, after(facts, out_late))
        arrived.append([lax.ppermute(sent, "tensor", ends)])
    late = local(1, after(facts, sent))
    late += [shifted(o, "span", d) for o, d in zip(out_late, distances)]

    streaming = dict(
        scratch_shapes=[pltpu.VMEM((tiles, width, tile), bf16), pltpu.SemaphoreType.DMA((tiles,))],
        compiler_params=PARAMS,
        cost_estimate=taking(3.0),
    )
    attended_shape = jax.ShapeDtypeStruct((rows, width), bf16)
    block_shapes = [jax.ShapeDtypeStruct((block, columns), bf16)] * 2
    attended, *merged = pl.pallas_call(
        functools.partial(merged_blocks_kernel, spans, ranks, distances),
        in_specs=[SMEM] + [VMEM] * (4 + 2 * len(distances)) + [HBM],
        out_specs=[VMEM] * 3,
        out_shape=[attended_shape] + block_shapes,
        name="merged_blocks",
        **streaming,
    )(facts, *early, *late, weight)

    def blocks_of(step, chunk, attended):
        return pl.pallas_call(
            functools.partial(blocks_kernel, spans, ranks, chunk * columns, step),
            in_specs=[SMEM, VMEM, HBM],
            out_specs=[VMEM] * 2,
            out_shape=block_shapes,
            name="blocks",
            **streaming,
        )(facts, attended, weight)

    before = attended
    for step in range(1, last):
        for chunk in range(chunks):
            if step == 1 and chunk == 0:
                blocks = merged
            else:
                blocks = blocks_of(step, chunk, after(attended, before))
            comes, blocks = lax.optimization_barrier((arrived[chunk], blocks))
            up, down = [
                (mine.astype(f32) + come.astype(f32)).astype(bf16)
                for mine, come in zip(blocks, (comes[0], comes[-1]))
            ]
            before = (up, down)
            arrived[chunk] = [
                lax.ppermute(up, "tensor", [(i, i + 1) for i in range(step + 1)]),
                lax.ppermute(down, "tensor", [(last - i, last - i - 1) for i in range(step + 1)]),
            ]
    everything = chunks * tiles
    projected, gate = pl.pallas_call(
        functools.partial(own_kernel, spans),
        in_specs=[SMEM, VMEM, HBM, HBM],
        out_specs=[VMEM, VMEM],
        out_shape=[jax.ShapeDtypeStruct((block, model), bf16), jax.ShapeDtypeStruct((1, model), f32)],
        scratch_shapes=[
            pltpu.VMEM((everything, width, tile), bf16),
            pltpu.VMEM((8, model), f32),
            pltpu.SemaphoreType.DMA((everything + 1,)),
        ],
        compiler_params=PARAMS,
        cost_estimate=taking(5.0),
        name="own",
    )(facts, after(attended, before), weight, in_hbm(gate_table))

    finished = []
    for chunk in range(chunks - 1):
        there = slice(chunk * columns, (chunk + 1) * columns)
        summed = sum(part.astype(f32) for part in (projected[:, there], *arrived[chunk]))
        finished.append((summed * gate[:, there]).astype(bf16))
    pieces = 2
    return pl.pallas_call(
        final_kernel,
        in_specs=[ANY, ANY, VMEM, VMEM, VMEM],
        out_specs=HBM,
        out_shape=jax.ShapeDtypeStruct((block, model), bf16),
        scratch_shapes=[
            pltpu.VMEM((block, columns), bf16),
            pltpu.VMEM((pieces, block, columns // pieces), bf16),
            pltpu.SemaphoreType.DMA((2 + pieces,)),
        ],
        compiler_params=PARAMS,
        cost_estimate=taking(2.7),
        name="final",
    )(jnp.concatenate(finished, axis=1), projected, gate, *arrived[-1])


def solution(mesh):
    return jax.shard_map(
        body,
        mesh=mesh,
        in_specs=(
            P(("group", "span"), "tensor"),
            P(("group", "span"), "tensor"),
            P(("group", "span"), "tensor"),
            P("tensor", None),
            P(),
            P("group"),
            P("group", None),
        ),
        out_specs=P(("group", "span", "tensor"), None),
        check_vma=False,
    )
```

```python
import functools

import jax
import jax.numpy as jnp
from jax import lax
from jax.experimental import pallas as pl
from jax.experimental.pallas import tpu as pltpu
from jax.sharding import PartitionSpec as P

HD = 128
LANES = 128
HIDDEN = -1e30
LOG2E = 1.4426950408889634
PARAMS = pltpu.CompilerParams(vmem_limit_bytes=24 * 1024 * 1024)
SMEM = pl.BlockSpec(memory_space=pltpu.SMEM)
VMEM = pl.BlockSpec(memory_space=pltpu.VMEM)
ANY = pl.BlockSpec(memory_space=pl.ANY)
HBM = pl.BlockSpec(memory_space=pltpu.HBM)
PIECE_LANES = 32


def taking(microseconds):
    return pl.CostEstimate(flops=0, bytes_accessed=int(microseconds * 3.69e6), transcendentals=0)


def in_hbm(array):
    return pltpu.with_memory_space_constraint(array, pltpu.HBM)


def shifted(block, axis, distance):
    count = lax.axis_size(axis)
    return lax.ppermute(block, axis, [(i, i + distance) for i in range(count) if 0 <= i + distance < count])


def head_columns(head):
    return slice(head * HD, (head + 1) * HD)


def attend(query, keys, values, flags, write):
    rows, width = query.shape
    scale = LOG2E * HD ** (-0.5)
    lane = lax.broadcasted_iota(jnp.int32, (rows, LANES), 1)
    packed = jnp.zeros((rows, LANES), jnp.float32)

    def scored(head):
        columns = head_columns(head)
        return [
            lax.dot_general(
                query[:, columns], key[:, columns], (((1,), (1,)), ((), ())), preferred_element_type=jnp.float32
            )
            for key in keys
        ]

    heads = width // HD
    later = scored(0)
    for head in range(heads):
        columns = head_columns(head)
        scores, later = later, scored(head + 1) if head + 1 < heads else None
        tops = [jnp.max(block, axis=-1, keepdims=True) * scale for block in scores]
        top = functools.reduce(
            jnp.maximum, [one if flag is None else jnp.where(flag, one, HIDDEN) for one, flag in zip(tops, flags)]
        )
        joined = None
        for block, value, flag in zip(scores, values, flags):
            above = top if flag is None else jnp.where(flag, top, -HIDDEN)
            probs = jnp.exp2(block * scale - above).astype(jnp.bfloat16)
            beside = jnp.concatenate([value[:, columns], jnp.ones((value.shape[0], HD), jnp.bfloat16)], axis=1)
            part = jnp.dot(probs, beside, preferred_element_type=jnp.float32)
            joined = part if joined is None else joined + part
        product, total = joined[:, :HD], jnp.where(joined[:, HD:] > 0.0, joined[:, HD:], 1.0)
        write(columns, product / total)
        packed = jnp.where(lane == head, top + jnp.log2(total), packed)
    return packed


class Facts:
    def __init__(self, ref, spans):
        self.ref, self.spans = ref, spans
        self.span, self.rank = ref[spans, 0], ref[spans, 1]
        self.beside = self.span + 1 - 2 * lax.rem(self.span, 2)

    def sees(self, asker, span):
        return self.ref[asker, span] > 0

    def level(self):
        return self.ref[self.spans + 1, self.span]


def copied(source, target, semaphore):
    copy = pltpu.make_async_copy(source, target, semaphore)
    copy.start()
    return copy


def parts_of(rank, ranks, rows):
    block = rows // ranks
    lower = rank < ranks // 2
    early = pl.multiple_of(jnp.where(lower, rows - block, 0), block)
    late = pl.multiple_of(jnp.where(lower, 0, block), block)
    return (early, block), (late, rows - block)


def split_kernel(ranks, place, query, *refs):
    *targets, semaphores = refs

    @pl.when(place[0] > 1)
    def _():
        (early, _), (late, _) = parts_of(place[1], ranks, query.shape[0])
        starts = (early, late, pl.multiple_of(late + targets[1].shape[0], 16))
        copies = [
            copied(query.at[pl.ds(start, target.shape[0])], target, semaphores.at[index])
            for index, (start, target) in enumerate(zip(starts, targets))
        ]
        for copy in copies:
            copy.wait()


def local_kernel(spans, ranks, part, facts, query, key, value, key_beside, value_beside, result, sums, *scratch):
    here = Facts(facts, spans)
    query_, key_, value_, key_beside_, value_beside_, semaphores = scratch
    start, size = parts_of(here.rank, ranks, query.shape[0])[part]
    copies = [
        copied(source, target, semaphores.at[index])
        for index, (source, target) in enumerate((
            (query.at[pl.ds(start, size)], query_),
            (key, key_), (key_beside, key_beside_), (value, value_), (value_beside, value_beside_),
        ))
    ]
    for copy in copies:
        copy.wait()

    def write(columns, block):
        result[:, columns] = block

    flags = [None, here.sees(here.span, here.beside)]
    sums[...] = attend(query_, [key_, key_beside_], [value_, value_beside_], flags, write)


def served_kernel(distance, spans, facts, key, value, key_beside, value_beside, *refs):
    here = Facts(facts, spans)

    @pl.when(here.span + distance < spans)
    def _():
        asker = jnp.minimum(here.span + distance, spans - 1)
        flags = [here.sees(asker, here.span), here.sees(asker, here.beside)]
        *queries, result, query = refs
        at = 0
        for part in queries:
            query[at:at + part.shape[0], :] = part[...]
            at += part.shape[0]

        def write(columns, block):
            result[:, columns] = block.astype(jnp.bfloat16)

        rest = attend(query, [key, key_beside], [value, value_beside], flags, write)
        sent = jnp.zeros_like(rest)
        for piece in range(3):
            part = rest.astype(jnp.bfloat16).astype(jnp.float32)
            sent = sent + (part if piece == 0 else pltpu.roll(part, piece * PIECE_LANES, 1))
            rest = rest - part
        result[:, query.shape[1]:] = sent.astype(jnp.bfloat16)


def merge(span, distances, own, own_sum, served, write):
    width = own.shape[1]
    sums = [own_sum[...]]
    for distance, ref in zip(distances, served):
        sent = ref[:, width:].astype(jnp.float32)
        joined = sent
        for piece in (1, 2):
            joined = joined + pltpu.roll(sent, LANES - piece * PIECE_LANES, 1)
        sums.append(jnp.where(span >= distance, joined, HIDDEN))
    top = functools.reduce(jnp.maximum, sums)
    shares = [jnp.exp2(one - top) for one in sums]
    over = 1.0 / sum(shares)
    shares = [share * over for share in shares]
    for head in range(width // HD):
        columns = head_columns(head)
        merged = own[:, columns] * shares[0][:, head:head + 1]
        for distance, share, ref in zip(distances, shares[1:], served):
            away = jnp.where(span >= distance, ref[:, columns].astype(jnp.float32), 0.0)
            merged = merged + away * share[:, head:head + 1]
        write(columns, merged.astype(jnp.bfloat16))


def streamed(weight, first, tiles, semaphores):
    count, _, tile = tiles.shape
    return [
        copied(weight.at[:, pl.ds(first + index * tile, tile)], tiles.at[index], semaphores.at[index])
        for index in range(count)
    ]


def opening_kernel(spans, ranks, distances, first, facts, *refs):
    own, own_sum, *served = refs[:2 + len(distances)]
    weight, result, tiles, rows, semaphores = refs[2 + len(distances):]
    here = Facts(facts, spans)
    tile = tiles.shape[2]

    @pl.when(jnp.logical_or(here.rank == 0, here.rank == ranks - 1))
    def _():
        copies = streamed(weight, first, tiles, semaphores)

        def write(columns, part):
            rows[:, columns] = part

        merge(here.span, distances, own, own_sum, served, write)
        for index, copy in enumerate(copies):
            copy.wait()
            product = jnp.dot(rows[...], tiles[index], preferred_element_type=jnp.float32)
            result[:, index * tile:(index + 1) * tile] = product.astype(jnp.bfloat16)


def project_blocks(ranks, first, facts, step, attended, weight, up, down, tiles, semaphores):
    rank = facts.rank
    last = ranks - 1
    tile = tiles.shape[2]
    block = up.shape[0]
    copies = streamed(weight, first, tiles, semaphores)
    yield
    sends = rank <= step, rank >= last - step
    starts = [
        pl.multiple_of(jnp.clip(target, 0, last) * block, block) for target in (last - step + rank, step + rank - last)
    ]
    rows = [attended[pl.ds(start, block), :] for start in starts]
    for index, copy in enumerate(copies):
        copy.wait()
        there = slice(index * tile, (index + 1) * tile)

        @pl.when(jnp.logical_and(*sends))
        def _():
            both = jnp.dot(jnp.concatenate(rows, axis=0), tiles[index], preferred_element_type=jnp.float32)
            up[:, there] = both[:block].astype(jnp.bfloat16)
            down[:, there] = both[block:].astype(jnp.bfloat16)

        @pl.when(jnp.logical_not(jnp.logical_and(*sends)))
        def _():
            one = jnp.dot(
                jnp.where(sends[0], rows[0], rows[1]), tiles[index], preferred_element_type=jnp.float32
            ).astype(jnp.bfloat16)
            up[:, there] = one
            down[:, there] = one


def merged_blocks_kernel(spans, ranks, distances, facts, *refs):
    each = 2 + len(distances)
    parts, (weight, attended, *results) = (refs[:each], refs[each:2 * each]), refs[2 * each:]
    here = Facts(facts, spans)
    work = project_blocks(ranks, 0, here, 1, attended, weight, *results)
    next(work)
    for (start, size), (own, own_sum, *served) in zip(parts_of(here.rank, ranks, attended.shape[0]), parts):
        there = pl.ds(start, size)

        def write(columns, part):
            attended[there, columns] = part

        merge(here.span, distances, own, own_sum, served, write)
    for _ in work:
        pass


def blocks_kernel(spans, ranks, first, step, facts, attended, weight, *results):
    for _ in project_blocks(ranks, first, Facts(facts, spans), step, attended, weight, *results):
        pass


def own_kernel(spans, facts, attended, weight, gate_table, result, gate, tiles, gates, semaphores):
    here = Facts(facts, spans)
    block = result.shape[0]
    count, _, tile = tiles.shape
    level = here.level()
    above = pl.multiple_of(level // 8 * 8, 8)
    gate_copy = copied(gate_table.at[pl.ds(above, 8)], gates, semaphores.at[count])
    copies = streamed(weight, 0, tiles, semaphores)
    start = pl.multiple_of(here.rank * block, block)
    for index, copy in enumerate(copies):
        copy.wait()
        product = jnp.dot(attended[pl.ds(start, block), :], tiles[index], preferred_element_type=jnp.float32)
        result[:, index * tile:(index + 1) * tile] = product.astype(jnp.bfloat16)
    gate_copy.wait()
    gate[...] = gates[pl.ds(lax.rem(level, 8), 1), :]


def final_kernel(done, projected, gate, up, down, result, own, gated, semaphores):
    first, (block, columns) = done.shape[1], own.shape
    pieces = gated.shape[0]
    wide = columns // pieces
    own_copy = copied(projected.at[:, pl.ds(first, columns)], own, semaphores.at[0])
    sent = [copied(done, result.at[:, pl.ds(0, first)], semaphores.at[1])]
    own_copy.wait()
    for piece in range(pieces):
        there = slice(piece * wide, (piece + 1) * wide)
        summed = own[:, there].astype(jnp.float32) + up[:, there].astype(jnp.float32)
        summed = summed + down[:, there].astype(jnp.float32)
        gated[piece] = (summed * gate[:, first + piece * wide:first + (piece + 1) * wide]).astype(jnp.bfloat16)
        sent.append(copied(
            gated.at[piece], result.at[:, pl.ds(first + piece * wide, wide)], semaphores.at[2 + piece]
        ))
    for copy in sent:
        copy.wait()


def body(queries, keys, values, out_weight, gate_table, levels, visible):
    rows, width = queries.shape
    model = out_weight.shape[1]
    spans = lax.axis_size("span")
    ranks = lax.axis_size("tensor")
    span = lax.axis_index("span")
    rank = lax.axis_index("tensor")
    block = rows // ranks
    bf16, f32 = jnp.bfloat16, jnp.float32
    numbers = jnp.arange(spans, dtype=jnp.int32)
    place = jnp.where(numbers == 0, span, jnp.where(numbers == 1, rank, 0)).astype(jnp.int32)
    facts = jnp.concatenate([visible, place[None, :], levels[None, :]], axis=0)

    third = (rows - block) // 48 * 16
    query_early, *query_late = pl.pallas_call(
        functools.partial(split_kernel, ranks),
        in_specs=[SMEM, HBM],
        out_specs=[VMEM] * 3,
        out_shape=[jax.ShapeDtypeStruct((part, width), bf16) for part in (block, rows - block - third, third)],
        scratch_shapes=[pltpu.SemaphoreType.DMA((3,))],
        compiler_params=PARAMS,
        cost_estimate=taking(1.7),
        name="split",
    )(jnp.stack([span, rank]).astype(jnp.int32), in_hbm(queries))
    distances = list(range(2, spans, 2))
    asked_early = [shifted(query_early, "span", -distance) for distance in distances]
    swap = [(i, i + 1 - 2 * (i % 2)) for i in range(spans)]
    key_beside = lax.ppermute(keys, "span", swap)
    value_beside = lax.ppermute(values, "span", swap)

    def after(value, *others):
        return lax.optimization_barrier((value, others))[0]

    def local(part, facts):
        size = (block, rows - block)[part]
        return pl.pallas_call(
            functools.partial(local_kernel, spans, ranks, part),
            in_specs=[SMEM, HBM, HBM, HBM, ANY, ANY],
            out_specs=[VMEM] * 2,
            out_shape=[jax.ShapeDtypeStruct((size, width), f32), jax.ShapeDtypeStruct((size, LANES), f32)],
            scratch_shapes=[pltpu.VMEM((size, width), bf16)] + [pltpu.VMEM((rows, width), bf16)] * 4
            + [pltpu.SemaphoreType.DMA((5,))],
            compiler_params=PARAMS,
            cost_estimate=taking(4.0),
            name="local",
        )(facts, in_hbm(queries), in_hbm(keys), in_hbm(values), key_beside, value_beside)

    def served(asked, distance):
        return pl.pallas_call(
            functools.partial(served_kernel, distance, spans),
            in_specs=[SMEM] + [VMEM] * (4 + len(asked)),
            out_specs=VMEM,
            out_shape=jax.ShapeDtypeStruct((sum(part.shape[0] for part in asked), width + LANES), bf16),
            scratch_shapes=[pltpu.VMEM((sum(part.shape[0] for part in asked), width), bf16)],
            compiler_params=PARAMS,
            cost_estimate=taking(3.3),
            name="served",
        )(facts, keys, values, key_beside, value_beside, *asked)

    early = list(local(0, facts))
    query_late = after(query_late, early)
    asked_early = after(asked_early, early)
    asked_late = [[shifted(query, "span", -distance) for query in query_late] for distance in distances]
    early += [shifted(served([q], d), "span", d) for q, d in zip(asked_early, distances)]

    chunks = 2
    columns = model // chunks
    tiles = 4
    tile = columns // tiles
    last = ranks - 1
    weight = in_hbm(out_weight)

    def opening(chunk, facts):
        return pl.pallas_call(
            functools.partial(opening_kernel, spans, ranks, distances, chunk * columns),
            in_specs=[SMEM] + [VMEM] * (2 + len(distances)) + [HBM],
            out_specs=VMEM,
            out_shape=jax.ShapeDtypeStruct((block, columns), bf16),
            scratch_shapes=[
                pltpu.VMEM((2, width, columns // 2), bf16),
                pltpu.VMEM((block, width), bf16),
                pltpu.SemaphoreType.DMA((2,)),
            ],
            compiler_params=PARAMS,
            cost_estimate=taking(3.4),
            name="opening",
        )(facts, *early, weight)

    ends = [(0, 1), (last, last - 1)]
    sent = opening(0, facts)
    arrived = [[lax.ppermute(sent, "tensor", ends)]]
    out_late = [served(q, d) for q, d in zip(after(asked_late, sent), distances)]
    for chunk in range(1, chunks):
        sent = opening(chunk, after(facts, out_late))
        arrived.append([lax.ppermute(sent, "tensor", ends)])
    late = list(local(1, after(facts, sent)))
    late += [shifted(o, "span", d) for o, d in zip(out_late, distances)]

    streaming = dict(
        scratch_shapes=[pltpu.VMEM((tiles, width, tile), bf16), pltpu.SemaphoreType.DMA((tiles,))],
        compiler_params=PARAMS,
        cost_estimate=taking(3.0),
    )
    attended_shape = jax.ShapeDtypeStruct((rows, width), bf16)
    block_shapes = [jax.ShapeDtypeStruct((block, columns), bf16)] * 2
    attended, *merged = pl.pallas_call(
        functools.partial(merged_blocks_kernel, spans, ranks, distances),
        in_specs=[SMEM] + [VMEM] * (4 + 2 * len(distances)) + [HBM],
        out_specs=[VMEM] * 3,
        out_shape=[attended_shape] + block_shapes,
        name="merged_blocks",
        **streaming,
    )(facts, *early, *late, weight)

    def blocks_of(step, chunk, attended):
        return pl.pallas_call(
            functools.partial(blocks_kernel, spans, ranks, chunk * columns, step),
            in_specs=[SMEM, VMEM, HBM],
            out_specs=[VMEM] * 2,
            out_shape=block_shapes,
            name="blocks",
            **streaming,
        )(facts, attended, weight)

    before = attended
    for step in range(1, last):
        for chunk in range(chunks):
            if step == 1 and chunk == 0:
                blocks = merged
            else:
                blocks = blocks_of(step, chunk, after(attended, before))
            comes, blocks = lax.optimization_barrier((arrived[chunk], blocks))
            up, down = [
                (mine.astype(f32) + come.astype(f32)).astype(bf16)
                for mine, come in zip(blocks, (comes[0], comes[-1]))
            ]
            before = (up, down)
            arrived[chunk] = [
                lax.ppermute(up, "tensor", [(i, i + 1) for i in range(step + 1)]),
                lax.ppermute(down, "tensor", [(last - i, last - i - 1) for i in range(step + 1)]),
            ]
    everything = chunks * tiles
    projected, gate = pl.pallas_call(
        functools.partial(own_kernel, spans),
        in_specs=[SMEM, VMEM, HBM, HBM],
        out_specs=[VMEM, VMEM],
        out_shape=[jax.ShapeDtypeStruct((block, model), bf16), jax.ShapeDtypeStruct((1, model), f32)],
        scratch_shapes=[
            pltpu.VMEM((everything, width, tile), bf16),
            pltpu.VMEM((8, model), f32),
            pltpu.SemaphoreType.DMA((everything + 1,)),
        ],
        compiler_params=PARAMS,
        cost_estimate=taking(5.0),
        name="own",
    )(facts, after(attended, before), weight, in_hbm(gate_table))

    finished = []
    for chunk in range(chunks - 1):
        there = slice(chunk * columns, (chunk + 1) * columns)
        summed = sum(part.astype(f32) for part in (projected[:, there], *arrived[chunk]))
        finished.append((summed * gate[:, there]).astype(bf16))
    pieces = 2
    return pl.pallas_call(
        final_kernel,
        in_specs=[ANY, ANY, VMEM, VMEM, VMEM],
        out_specs=HBM,
        out_shape=jax.ShapeDtypeStruct((block, model), bf16),
        scratch_shapes=[
            pltpu.VMEM((block, columns), bf16),
            pltpu.VMEM((pieces, block, columns // pieces), bf16),
            pltpu.SemaphoreType.DMA((2 + pieces,)),
        ],
        compiler_params=PARAMS,
        cost_estimate=taking(2.7),
        name="final",
    )(jnp.concatenate(finished, axis=1), projected, gate, *arrived[-1])


def solution(mesh):
    return jax.shard_map(
        body,
        mesh=mesh,
        in_specs=(
            P(("group", "span"), "tensor"),
            P(("group", "span"), "tensor"),
            P(("group", "span"), "tensor"),
            P("tensor", None),
            P(),
            P("group"),
            P("group", None),
        ),
        out_specs=P(("group", "span", "tensor"), None),
        check_vma=False,
    )
```

```python
import functools

import jax
import jax.numpy as jnp
from jax import lax
from jax.experimental import pallas as pl
from jax.experimental.pallas import tpu as pltpu
from jax.sharding import PartitionSpec as P

HD = 128
LANES = 128
HIDDEN = -1e30
LOG2E = 1.4426950408889634
PARAMS = pltpu.CompilerParams(vmem_limit_bytes=24 * 1024 * 1024)
SMEM = pl.BlockSpec(memory_space=pltpu.SMEM)
VMEM = pl.BlockSpec(memory_space=pltpu.VMEM)
ANY = pl.BlockSpec(memory_space=pl.ANY)
HBM = pl.BlockSpec(memory_space=pltpu.HBM)
PIECE_LANES = 32


def taking(microseconds):
    return pl.CostEstimate(flops=0, bytes_accessed=int(microseconds * 3.69e6), transcendentals=0)


def in_hbm(array):
    return pltpu.with_memory_space_constraint(array, pltpu.HBM)


def shifted(block, axis, distance):
    count = lax.axis_size(axis)
    return lax.ppermute(block, axis, [(i, i + distance) for i in range(count) if 0 <= i + distance < count])


def head_columns(head):
    return slice(head * HD, (head + 1) * HD)


def attend(query, keys, values, flags, write):
    rows, width = query.shape
    scale = LOG2E * HD ** (-0.5)
    lane = lax.broadcasted_iota(jnp.int32, (rows, LANES), 1)
    packed = jnp.zeros((rows, LANES), jnp.float32)

    def scored(head):
        columns = head_columns(head)
        return [
            lax.dot_general(
                query[:, columns], key[:, columns], (((1,), (1,)), ((), ())), preferred_element_type=jnp.float32
            )
            for key in keys
        ]

    heads = width // HD
    later = scored(0)
    for head in range(heads):
        columns = head_columns(head)
        scores, later = later, scored(head + 1) if head + 1 < heads else None
        tops = [jnp.max(block, axis=-1, keepdims=True) * scale for block in scores]
        top = functools.reduce(
            jnp.maximum, [one if flag is None else jnp.where(flag, one, HIDDEN) for one, flag in zip(tops, flags)]
        )
        joined = None
        for block, value, flag in zip(scores, values, flags):
            above = top if flag is None else jnp.where(flag, top, -HIDDEN)
            probs = jnp.exp2(block * scale - above).astype(jnp.bfloat16)
            beside = jnp.concatenate([value[:, columns], jnp.ones((value.shape[0], HD), jnp.bfloat16)], axis=1)
            part = jnp.dot(probs, beside, preferred_element_type=jnp.float32)
            joined = part if joined is None else joined + part
        product, total = joined[:, :HD], jnp.where(joined[:, HD:] > 0.0, joined[:, HD:], 1.0)
        write(columns, product / total)
        packed = jnp.where(lane == head, top + jnp.log2(total), packed)
    return packed


class Facts:
    def __init__(self, ref, spans):
        self.ref, self.spans = ref, spans
        self.span, self.rank = ref[spans, 0], ref[spans, 1]
        self.beside = self.span + 1 - 2 * lax.rem(self.span, 2)

    def sees(self, asker, span):
        return self.ref[asker, span] > 0

    def level(self):
        return self.ref[self.spans + 1, self.span]


def copied(source, target, semaphore):
    copy = pltpu.make_async_copy(source, target, semaphore)
    copy.start()
    return copy


def parts_of(rank, ranks, rows):
    block = rows // ranks
    lower = rank < ranks // 2
    early = pl.multiple_of(jnp.where(lower, rows - block, 0), block)
    late = pl.multiple_of(jnp.where(lower, 0, block), block)
    return (early, block), (late, rows - block)


def split_kernel(ranks, place, query, weight, *refs):
    *targets, piece, semaphores = refs
    (early, _), (late, _) = parts_of(place[1], ranks, query.shape[0])
    starts = (early, late, late + targets[1].shape[0])
    size, columns = piece.shape
    first = pl.multiple_of(jnp.minimum(place[2] * size, weight.shape[0] - size), 16)
    taken = copied(
        weight.at[pl.ds(first, size), pl.ds(weight.shape[1] - columns, columns)], piece, semaphores.at[len(targets)]
    )

    @pl.when(place[0] > 1)
    def _():
        copies = [
            copied(
                query.at[pl.ds(pl.multiple_of(start, 16), target.shape[0])], target, semaphores.at[index]
            )
            for index, (start, target) in enumerate(zip(starts, targets))
        ]
        for copy in copies:
            copy.wait()

    taken.wait()


def local_kernel(spans, ranks, part, facts, query, key, value, key_beside, value_beside, result, sums, *scratch):
    here = Facts(facts, spans)
    query_, key_, value_, key_beside_, value_beside_, semaphores = scratch
    start, size = parts_of(here.rank, ranks, query.shape[0])[part]
    copies = [
        copied(source, target, semaphores.at[index])
        for index, (source, target) in enumerate((
            (query.at[pl.ds(start, size)], query_),
            (key, key_), (key_beside, key_beside_), (value, value_), (value_beside, value_beside_),
        ))
    ]
    for copy in copies:
        copy.wait()

    def write(columns, block):
        result[:, columns] = block

    flags = [None, here.sees(here.span, here.beside)]
    sums[...] = attend(query_, [key_, key_beside_], [value_, value_beside_], flags, write)


def served_kernel(distance, spans, facts, key, value, key_beside, value_beside, *refs):
    here = Facts(facts, spans)

    @pl.when(here.span + distance < spans)
    def _():
        asker = jnp.minimum(here.span + distance, spans - 1)
        flags = [here.sees(asker, here.span), here.sees(asker, here.beside)]
        *queries, result, query = refs
        at = 0
        for part in queries:
            query[at:at + part.shape[0], :] = part[...]
            at += part.shape[0]

        def write(columns, block):
            result[:, columns] = block.astype(jnp.bfloat16)

        rest = attend(query, [key, key_beside], [value, value_beside], flags, write)
        sent = jnp.zeros_like(rest)
        for piece in range(3):
            part = rest.astype(jnp.bfloat16).astype(jnp.float32)
            sent = sent + (part if piece == 0 else pltpu.roll(part, piece * PIECE_LANES, 1))
            rest = rest - part
        result[:, query.shape[1]:] = sent.astype(jnp.bfloat16)


def merge(span, distances, own, own_sum, served, write):
    width = own.shape[1]
    sums = [own_sum[...]]
    for distance, ref in zip(distances, served):
        sent = ref[:, width:].astype(jnp.float32)
        joined = sent
        for piece in (1, 2):
            joined = joined + pltpu.roll(sent, LANES - piece * PIECE_LANES, 1)
        sums.append(jnp.where(span >= distance, joined, HIDDEN))
    top = functools.reduce(jnp.maximum, sums)
    shares = [jnp.exp2(one - top) for one in sums]
    over = 1.0 / sum(shares)
    shares = [share * over for share in shares]
    for head in range(width // HD):
        columns = head_columns(head)
        merged = own[:, columns] * shares[0][:, head:head + 1]
        for distance, share, ref in zip(distances, shares[1:], served):
            away = jnp.where(span >= distance, ref[:, columns].astype(jnp.float32), 0.0)
            merged = merged + away * share[:, head:head + 1]
        write(columns, merged.astype(jnp.bfloat16))


def streamed(weight, first, tiles, semaphores):
    count, _, tile = tiles.shape
    return [
        copied(weight.at[:, pl.ds(first + index * tile, tile)], tiles.at[index], semaphores.at[index])
        for index in range(count)
    ]


def opening_kernel(spans, ranks, distances, first, facts, *refs):
    own, own_sum, *served = refs[:2 + len(distances)]
    weight, result, tiles, rows, semaphores = refs[2 + len(distances):]
    here = Facts(facts, spans)
    tile = tiles.shape[2]

    @pl.when(jnp.logical_or(here.rank == 0, here.rank == ranks - 1))
    def _():
        copies = streamed(weight, first, tiles, semaphores)

        def write(columns, part):
            rows[:, columns] = part

        merge(here.span, distances, own, own_sum, served, write)
        for index, copy in enumerate(copies):
            copy.wait()
            product = jnp.dot(rows[...], tiles[index], preferred_element_type=jnp.float32)
            result[:, index * tile:(index + 1) * tile] = product.astype(jnp.bfloat16)


def project_blocks(ranks, first, facts, step, attended, weight, up, down, tiles, semaphores):
    rank = facts.rank
    last = ranks - 1
    tile = tiles.shape[2]
    block = up.shape[0]
    copies = streamed(weight, first, tiles, semaphores)
    yield
    sends = rank <= step, rank >= last - step
    starts = [
        pl.multiple_of(jnp.clip(target, 0, last) * block, block) for target in (last - step + rank, step + rank - last)
    ]
    rows = [attended[pl.ds(start, block), :] for start in starts]
    for index, copy in enumerate(copies):
        copy.wait()
        there = slice(index * tile, (index + 1) * tile)

        @pl.when(jnp.logical_and(*sends))
        def _():
            both = jnp.dot(jnp.concatenate(rows, axis=0), tiles[index], preferred_element_type=jnp.float32)
            up[:, there] = both[:block].astype(jnp.bfloat16)
            down[:, there] = both[block:].astype(jnp.bfloat16)

        @pl.when(jnp.logical_not(jnp.logical_and(*sends)))
        def _():
            one = jnp.dot(
                jnp.where(sends[0], rows[0], rows[1]), tiles[index], preferred_element_type=jnp.float32
            ).astype(jnp.bfloat16)
            up[:, there] = one
            down[:, there] = one


def merged_blocks_kernel(spans, ranks, distances, facts, *refs):
    each = 2 + len(distances)
    parts, (weight, attended, end_rows, *results) = (refs[:each], refs[each:2 * each]), refs[2 * each:]
    here = Facts(facts, spans)
    block = end_rows.shape[0]
    work = project_blocks(ranks, 0, here, 1, attended, weight, *results)
    next(work)
    for (start, size), (own, own_sum, *served) in zip(parts_of(here.rank, ranks, attended.shape[0]), parts):
        there = pl.ds(start, size)

        def write(columns, part):
            attended[there, columns] = part

        merge(here.span, distances, own, own_sum, served, write)
    inward = jnp.where(here.rank == 0, 1, ranks - 2)
    end_rows[...] = attended[pl.ds(pl.multiple_of(inward * block, block), block), :]
    for _ in work:
        pass


def blocks_kernel(spans, ranks, first, step, facts, attended, weight, *results):
    for _ in project_blocks(ranks, first, Facts(facts, spans), step, attended, weight, *results):
        pass


def is_inner(rank, ranks):
    return jnp.logical_or(rank == 1, rank == ranks - 2)


def streamed_pairs(weight, first, end_weight, tiles, semaphores):
    count, depth, tile = tiles.shape
    width = depth // 2
    copies = []
    for index in range(count):
        columns = pl.ds(first + index * tile, tile)
        copies.append((
            copied(weight.at[:, columns], tiles.at[index, pl.ds(0, width)], semaphores.at[2 * index]),
            copied(
                end_weight.at[:, pl.ds(index * tile, tile)], tiles.at[index, pl.ds(width, width)],
                semaphores.at[2 * index + 1],
            ),
        ))
    return copies


def own_kernel(spans, ranks, facts, attended, end_rows, weight, end_weight, gate_table, result, gate,
               tiles, pairs, gates, semaphores, pair_semaphores):
    here = Facts(facts, spans)
    block, width = result.shape[0], attended.shape[1]
    count, _, tile = tiles.shape
    columns = count * tile
    level = here.level()
    above = pl.multiple_of(level // 8 * 8, 8)
    gate_copy = copied(gate_table.at[pl.ds(above, 8)], gates, semaphores.at[count])
    copies = streamed(weight, 0, tiles, semaphores)
    pair_copies = streamed_pairs(weight, columns, end_weight, pairs, pair_semaphores)
    mine = attended[pl.ds(pl.multiple_of(here.rank * block, block), block), :]
    other = jnp.where(is_inner(here.rank, ranks), end_rows[...], jnp.zeros((block, width), jnp.bfloat16))
    for index, copy in enumerate(copies):
        copy.wait()
        product = jnp.dot(mine, tiles[index], preferred_element_type=jnp.float32)
        result[:, index * tile:(index + 1) * tile] = product.astype(jnp.bfloat16)
    both = jnp.concatenate([mine, other], axis=1)
    for index, pair in enumerate(pair_copies):
        for copy in pair:
            copy.wait()
        product = jnp.dot(both, pairs[index], preferred_element_type=jnp.float32)
        result[:, columns + index * tile:columns + (index + 1) * tile] = product.astype(jnp.bfloat16)
    gate_copy.wait()
    gate[...] = gates[pl.ds(lax.rem(level, 8), 1), :]


def final_kernel(done, projected, gate, up, down, result, own, gated, semaphores):
    first, (block, columns) = done.shape[1], own.shape
    pieces = gated.shape[0]
    wide = columns // pieces
    own_copy = copied(projected.at[:, pl.ds(first, columns)], own, semaphores.at[0])
    sent = [copied(done, result.at[:, pl.ds(0, first)], semaphores.at[1])]
    own_copy.wait()
    for piece in range(pieces):
        there = slice(piece * wide, (piece + 1) * wide)
        summed = own[:, there].astype(jnp.float32) + up[:, there].astype(jnp.float32)
        summed = summed + down[:, there].astype(jnp.float32)
        gated[piece] = (summed * gate[:, first + piece * wide:first + (piece + 1) * wide]).astype(jnp.bfloat16)
        sent.append(copied(
            gated.at[piece], result.at[:, pl.ds(first + piece * wide, wide)], semaphores.at[2 + piece]
        ))
    for copy in sent:
        copy.wait()


def body(queries, keys, values, out_weight, gate_table, levels, visible):
    rows, width = queries.shape
    model = out_weight.shape[1]
    spans = lax.axis_size("span")
    ranks = lax.axis_size("tensor")
    span = lax.axis_index("span")
    rank = lax.axis_index("tensor")
    block = rows // ranks
    bf16, f32 = jnp.bfloat16, jnp.float32
    numbers = jnp.arange(spans, dtype=jnp.int32)
    place = jnp.where(numbers == 0, span, jnp.where(numbers == 1, rank, 0)).astype(jnp.int32)
    facts = jnp.concatenate([visible, place[None, :], levels[None, :]], axis=0)

    third = (rows - block) // 48 * 16
    columns = model // 2
    plane = lax.axis_size("group") * spans
    pieces = -(-width // (16 * plane)) * 16
    here = jnp.stack([span, rank, lax.axis_index("group") * spans + span]).astype(jnp.int32)
    query_early, *query_late, piece = pl.pallas_call(
        functools.partial(split_kernel, ranks),
        in_specs=[SMEM, HBM, HBM],
        out_specs=[VMEM] * 4,
        out_shape=[jax.ShapeDtypeStruct((part, width), bf16) for part in (block, rows - block - third, third)]
        + [jax.ShapeDtypeStruct((pieces, columns), bf16)],
        scratch_shapes=[pltpu.SemaphoreType.DMA((4,))],
        compiler_params=PARAMS,
        cost_estimate=taking(1.7),
        name="split",
    )(here, in_hbm(queries), in_hbm(out_weight))
    distances = list(range(2, spans, 2))
    asked_early = [shifted(query_early, "span", -distance) for distance in distances]
    swap = [(i, i + 1 - 2 * (i % 2)) for i in range(spans)]
    key_beside = lax.ppermute(keys, "span", swap)
    value_beside = lax.ppermute(values, "span", swap)

    def after(value, *others):
        return lax.optimization_barrier((value, others))[0]

    def local(part, facts):
        size = (block, rows - block)[part]
        return pl.pallas_call(
            functools.partial(local_kernel, spans, ranks, part),
            in_specs=[SMEM, HBM, HBM, HBM, ANY, ANY],
            out_specs=[VMEM] * 2,
            out_shape=[jax.ShapeDtypeStruct((size, width), f32), jax.ShapeDtypeStruct((size, LANES), f32)],
            scratch_shapes=[pltpu.VMEM((size, width), bf16)] + [pltpu.VMEM((rows, width), bf16)] * 4
            + [pltpu.SemaphoreType.DMA((5,))],
            compiler_params=PARAMS,
            cost_estimate=taking(4.0),
            name="local",
        )(facts, in_hbm(queries), in_hbm(keys), in_hbm(values), key_beside, value_beside)

    def served(asked, distance):
        return pl.pallas_call(
            functools.partial(served_kernel, distance, spans),
            in_specs=[SMEM] + [VMEM] * (4 + len(asked)),
            out_specs=VMEM,
            out_shape=jax.ShapeDtypeStruct((sum(part.shape[0] for part in asked), width + LANES), bf16),
            scratch_shapes=[pltpu.VMEM((sum(part.shape[0] for part in asked), width), bf16)],
            compiler_params=PARAMS,
            cost_estimate=taking(3.3),
            name="served",
        )(facts, keys, values, key_beside, value_beside, *asked)

    early = list(local(0, facts))
    query_late = after(query_late, early)
    end_piece = lax.ppermute(after(piece, key_beside), "tensor", [(0, 1), (ranks - 1, ranks - 2)])
    asked_early = after(asked_early, early)
    asked_late = [[shifted(query, "span", -distance) for query in query_late] for distance in distances]
    early += [shifted(served([q], d), "span", d) for q, d in zip(asked_early, distances)]

    chunks = 2
    tiles = 4
    tile = columns // tiles
    last = ranks - 1
    weight = in_hbm(out_weight)

    def opening(chunk, facts):
        return pl.pallas_call(
            functools.partial(opening_kernel, spans, ranks, distances, chunk * columns),
            in_specs=[SMEM] + [VMEM] * (2 + len(distances)) + [HBM],
            out_specs=VMEM,
            out_shape=jax.ShapeDtypeStruct((block, columns), bf16),
            scratch_shapes=[
                pltpu.VMEM((2, width, columns // 2), bf16),
                pltpu.VMEM((block, width), bf16),
                pltpu.SemaphoreType.DMA((2,)),
            ],
            compiler_params=PARAMS,
            cost_estimate=taking(3.4),
            name="opening",
        )(facts, *early, weight)

    ends = [(0, 1), (last, last - 1)]
    sent = opening(0, facts)
    arrived = [[lax.ppermute(sent, "tensor", ends)]]
    out_late = [served(q, d) for q, d in zip(after(asked_late, sent, end_piece), distances)]
    for chunk in range(1, chunks):
        sent = opening(chunk, after(facts, out_late))
        arrived.append([lax.ppermute(sent, "tensor", ends)])
    late = list(local(1, after(facts, sent)))
    late += [shifted(o, "span", d) for o, d in zip(out_late, distances)]

    streaming = dict(
        scratch_shapes=[pltpu.VMEM((tiles, width, tile), bf16), pltpu.SemaphoreType.DMA((tiles,))],
        compiler_params=PARAMS,
        cost_estimate=taking(3.0),
    )
    attended_shape = jax.ShapeDtypeStruct((rows, width), bf16)
    block_shapes = [jax.ShapeDtypeStruct((block, columns), bf16)] * 2
    attended, end_rows, *merged = pl.pallas_call(
        functools.partial(merged_blocks_kernel, spans, ranks, distances),
        in_specs=[SMEM] + [VMEM] * (4 + 2 * len(distances)) + [HBM],
        out_specs=[VMEM] * 4,
        out_shape=[attended_shape, jax.ShapeDtypeStruct((block, width), bf16)] + block_shapes,
        name="merged_blocks",
        **streaming,
    )(facts, *early, *late, weight)

    end_rows = lax.ppermute(end_rows, "tensor", ends)
    end_weight = lax.all_gather(after(end_piece, attended), ("group", "span"), axis=0, tiled=True)[:width]

    def blocks_of(step, chunk, attended):
        return pl.pallas_call(
            functools.partial(blocks_kernel, spans, ranks, chunk * columns, step),
            in_specs=[SMEM, VMEM, HBM],
            out_specs=[VMEM] * 2,
            out_shape=block_shapes,
            name="blocks",
            **streaming,
        )(facts, attended, weight)

    before = attended
    for step in range(1, last):
        for chunk in range(chunks):
            if step == 1 and chunk == 0:
                blocks = merged
            else:
                blocks = blocks_of(step, chunk, after(attended, before, *[end_rows] * (step > 1)))
            comes, blocks = lax.optimization_barrier((arrived[chunk], blocks))
            up, down = [
                (mine.astype(f32) + come.astype(f32)).astype(bf16)
                for mine, come in zip(blocks, (comes[0], comes[-1]))
            ]
            before = (up, down)
            senders = range(1 if (step, chunk) == (last - 1, 1) else 0, step + 1)
            arrived[chunk] = [
                lax.ppermute(up, "tensor", [(i, i + 1) for i in senders]),
                lax.ppermute(down, "tensor", [(last - i, last - i - 1) for i in senders]),
            ]
    projected, gate = pl.pallas_call(
        functools.partial(own_kernel, spans, ranks),
        in_specs=[SMEM, VMEM, VMEM, HBM, HBM, HBM],
        out_specs=[VMEM, VMEM],
        out_shape=[jax.ShapeDtypeStruct((block, model), bf16), jax.ShapeDtypeStruct((1, model), f32)],
        scratch_shapes=[
            pltpu.VMEM((tiles, width, tile), bf16),
            pltpu.VMEM((tiles, 2 * width, tile), bf16),
            pltpu.VMEM((8, model), f32),
            pltpu.SemaphoreType.DMA((tiles + 1,)),
            pltpu.SemaphoreType.DMA((2 * tiles,)),
        ],
        compiler_params=PARAMS,
        cost_estimate=taking(7.0),
        name="own",
    )(facts, after(attended, before), end_rows, weight, in_hbm(end_weight), in_hbm(gate_table))

    finished = []
    for chunk in range(chunks - 1):
        there = slice(chunk * columns, (chunk + 1) * columns)
        summed = sum(part.astype(f32) for part in (projected[:, there], *arrived[chunk]))
        finished.append((summed * gate[:, there]).astype(bf16))
    pieces = 2
    return pl.pallas_call(
        final_kernel,
        in_specs=[ANY, ANY, VMEM, VMEM, VMEM],
        out_specs=HBM,
        out_shape=jax.ShapeDtypeStruct((block, model), bf16),
        scratch_shapes=[
            pltpu.VMEM((block, columns), bf16),
            pltpu.VMEM((pieces, block, columns // pieces), bf16),
            pltpu.SemaphoreType.DMA((2 + pieces,)),
        ],
        compiler_params=PARAMS,
        cost_estimate=taking(2.7),
        name="final",
    )(jnp.concatenate(finished, axis=1), projected, gate, *arrived[-1])


def solution(mesh):
    return jax.shard_map(
        body,
        mesh=mesh,
        in_specs=(
            P(("group", "span"), "tensor"),
            P(("group", "span"), "tensor"),
            P(("group", "span"), "tensor"),
            P("tensor", None),
            P(),
            P("group"),
            P("group", None),
        ),
        out_specs=P(("group", "span", "tensor"), None),
        check_vma=False,
    )
```

```python
import functools

import jax
import jax.numpy as jnp
from jax import lax
from jax.experimental import pallas as pl
from jax.experimental.pallas import tpu as pltpu
from jax.sharding import PartitionSpec as P

HD = 128
LANES = 128
HIDDEN = -1e30
LOG2E = 1.4426950408889634
PARAMS = pltpu.CompilerParams(vmem_limit_bytes=24 * 1024 * 1024)
SMEM = pl.BlockSpec(memory_space=pltpu.SMEM)
VMEM = pl.BlockSpec(memory_space=pltpu.VMEM)
ANY = pl.BlockSpec(memory_space=pl.ANY)
HBM = pl.BlockSpec(memory_space=pltpu.HBM)
PIECE_LANES = 32


def taking(microseconds):
    return pl.CostEstimate(flops=0, bytes_accessed=int(microseconds * 3.69e6), transcendentals=0)


def in_hbm(array):
    return pltpu.with_memory_space_constraint(array, pltpu.HBM)


def shifted(block, axis, distance):
    count = lax.axis_size(axis)
    return lax.ppermute(block, axis, [(i, i + distance) for i in range(count) if 0 <= i + distance < count])


def head_columns(head):
    return slice(head * HD, (head + 1) * HD)


def attend(query, keys, values, flags, write):
    rows, width = query.shape
    scale = LOG2E * HD ** (-0.5)
    lane = lax.broadcasted_iota(jnp.int32, (rows, LANES), 1)
    packed = jnp.zeros((rows, LANES), jnp.float32)

    def scored(head):
        columns = head_columns(head)
        return [
            lax.dot_general(
                query[:, columns], key[:, columns], (((1,), (1,)), ((), ())), preferred_element_type=jnp.float32
            )
            for key in keys
        ]

    heads = width // HD
    later = scored(0)
    for head in range(heads):
        columns = head_columns(head)
        scores, later = later, scored(head + 1) if head + 1 < heads else None
        tops = [jnp.max(block, axis=-1, keepdims=True) * scale for block in scores]
        top = functools.reduce(
            jnp.maximum, [one if flag is None else jnp.where(flag, one, HIDDEN) for one, flag in zip(tops, flags)]
        )
        joined = None
        for block, value, flag in zip(scores, values, flags):
            above = top if flag is None else jnp.where(flag, top, -HIDDEN)
            probs = jnp.exp2(block * scale - above).astype(jnp.bfloat16)
            beside = jnp.concatenate([value[:, columns], jnp.ones((value.shape[0], HD), jnp.bfloat16)], axis=1)
            part = jnp.dot(probs, beside, preferred_element_type=jnp.float32)
            joined = part if joined is None else joined + part
        product, total = joined[:, :HD], jnp.where(joined[:, HD:] > 0.0, joined[:, HD:], 1.0)
        write(columns, product / total)
        packed = jnp.where(lane == head, top + jnp.log2(total), packed)
    return packed


class Facts:
    def __init__(self, ref, spans):
        self.ref, self.spans = ref, spans
        self.span, self.rank = ref[spans, 0], ref[spans, 1]
        self.beside = self.span + 1 - 2 * lax.rem(self.span, 2)

    def sees(self, asker, span):
        return self.ref[asker, span] > 0

    def level(self):
        return self.ref[self.spans + 1, self.span]


def copied(source, target, semaphore):
    copy = pltpu.make_async_copy(source, target, semaphore)
    copy.start()
    return copy


def parts_of(rank, ranks, rows):
    block = rows // ranks
    lower = rank < ranks // 2
    early = pl.multiple_of(jnp.where(lower, rows - block, 0), block)
    late = pl.multiple_of(jnp.where(lower, 0, block), block)
    return (early, block), (late, rows - block)


def split_kernel(ranks, place, query, *refs):
    *targets, semaphores = refs

    @pl.when(place[0] > 1)
    def _():
        (early, _), (late, _) = parts_of(place[1], ranks, query.shape[0])
        starts = (early, late, pl.multiple_of(late + targets[1].shape[0], 16))
        copies = [
            copied(query.at[pl.ds(start, target.shape[0])], target, semaphores.at[index])
            for index, (start, target) in enumerate(zip(starts, targets))
        ]
        for copy in copies:
            copy.wait()


def local_kernel(spans, ranks, part, facts, query, key, value, key_beside, value_beside, result, sums, *scratch):
    here = Facts(facts, spans)
    query_, key_, value_, key_beside_, value_beside_, semaphores = scratch
    start, size = parts_of(here.rank, ranks, query.shape[0])[part]
    copies = [
        copied(source, target, semaphores.at[index])
        for index, (source, target) in enumerate((
            (query.at[pl.ds(start, size)], query_),
            (key, key_), (key_beside, key_beside_), (value, value_), (value_beside, value_beside_),
        ))
    ]
    for copy in copies:
        copy.wait()

    def write(columns, block):
        result[:, columns] = block

    flags = [None, here.sees(here.span, here.beside)]
    sums[...] = attend(query_, [key_, key_beside_], [value_, value_beside_], flags, write)


def served_kernel(distance, spans, facts, key, value, key_beside, value_beside, *refs):
    here = Facts(facts, spans)

    @pl.when(here.span + distance < spans)
    def _():
        asker = jnp.minimum(here.span + distance, spans - 1)
        flags = [here.sees(asker, here.span), here.sees(asker, here.beside)]
        *queries, result, query = refs
        at = 0
        for part in queries:
            query[at:at + part.shape[0], :] = part[...]
            at += part.shape[0]

        def write(columns, block):
            result[:, columns] = block.astype(jnp.bfloat16)

        rest = attend(query, [key, key_beside], [value, value_beside], flags, write)
        sent = jnp.zeros_like(rest)
        for piece in range(3):
            part = rest.astype(jnp.bfloat16).astype(jnp.float32)
            sent = sent + (part if piece == 0 else pltpu.roll(part, piece * PIECE_LANES, 1))
            rest = rest - part
        result[:, query.shape[1]:] = sent.astype(jnp.bfloat16)


def merge(span, distances, own, own_sum, served, write):
    width = own.shape[1]
    sums = [own_sum[...]]
    for distance, ref in zip(distances, served):
        sent = ref[:, width:].astype(jnp.float32)
        joined = sent
        for piece in (1, 2):
            joined = joined + pltpu.roll(sent, LANES - piece * PIECE_LANES, 1)
        sums.append(jnp.where(span >= distance, joined, HIDDEN))
    top = functools.reduce(jnp.maximum, sums)
    shares = [jnp.exp2(one - top) for one in sums]
    over = 1.0 / sum(shares)
    shares = [share * over for share in shares]
    for head in range(width // HD):
        columns = head_columns(head)
        merged = own[:, columns] * shares[0][:, head:head + 1]
        for distance, share, ref in zip(distances, shares[1:], served):
            away = jnp.where(span >= distance, ref[:, columns].astype(jnp.float32), 0.0)
            merged = merged + away * share[:, head:head + 1]
        write(columns, merged.astype(jnp.bfloat16))


def streamed(weight, first, tiles, semaphores):
    count, _, tile = tiles.shape
    return [
        copied(weight.at[:, pl.ds(first + index * tile, tile)], tiles.at[index], semaphores.at[index])
        for index in range(count)
    ]


def fetch_kernel(weight, tiles, semaphores):
    for copy in streamed(weight, 0, tiles, semaphores):
        copy.wait()


def opening_kernel(ranks, distances, spans, first, facts, *refs):
    own, own_sum, *served = refs[:2 + len(distances)]
    weight, result, *scratch = refs[2 + len(distances):]
    rows = scratch[-1]
    here = Facts(facts, spans)

    @pl.when(jnp.logical_or(here.rank == 0, here.rank == ranks - 1))
    def _():
        tiles, copies = weight, [None] * weight.shape[0]
        if first:
            tiles, semaphores, _ = scratch
            copies = streamed(weight, first, tiles, semaphores)

        def write(columns, part):
            rows[:, columns] = part

        merge(here.span, distances, own, own_sum, served, write)
        tile = tiles.shape[2]
        for index, copy in enumerate(copies):
            if copy is not None:
                copy.wait()
            product = jnp.dot(rows[...], tiles[index], preferred_element_type=jnp.float32)
            result[:, index * tile:(index + 1) * tile] = product.astype(jnp.bfloat16)


def project_blocks(ranks, first, facts, step, attended, weight, up, down, tiles, semaphores):
    rank = facts.rank
    last = ranks - 1
    tile = tiles.shape[2]
    block = up.shape[0]
    copies = streamed(weight, first, tiles, semaphores)
    yield
    sends = rank <= step, rank >= last - step
    starts = [
        pl.multiple_of(jnp.clip(target, 0, last) * block, block) for target in (last - step + rank, step + rank - last)
    ]
    rows = [attended[pl.ds(start, block), :] for start in starts]
    for index, copy in enumerate(copies):
        copy.wait()
        there = slice(index * tile, (index + 1) * tile)

        @pl.when(jnp.logical_and(*sends))
        def _():
            both = jnp.dot(jnp.concatenate(rows, axis=0), tiles[index], preferred_element_type=jnp.float32)
            up[:, there] = both[:block].astype(jnp.bfloat16)
            down[:, there] = both[block:].astype(jnp.bfloat16)

        @pl.when(jnp.logical_not(jnp.logical_and(*sends)))
        def _():
            one = jnp.dot(
                jnp.where(sends[0], rows[0], rows[1]), tiles[index], preferred_element_type=jnp.float32
            ).astype(jnp.bfloat16)
            up[:, there] = one
            down[:, there] = one


def merged_blocks_kernel(spans, ranks, distances, facts, *refs):
    each = 2 + len(distances)
    parts, (weight, attended, *results) = (refs[:each], refs[each:2 * each]), refs[2 * each:]
    here = Facts(facts, spans)
    work = project_blocks(ranks, 0, here, 1, attended, weight, *results)
    next(work)
    for (start, size), (own, own_sum, *served) in zip(parts_of(here.rank, ranks, attended.shape[0]), parts):
        there = pl.ds(start, size)

        def write(columns, part):
            attended[there, columns] = part

        merge(here.span, distances, own, own_sum, served, write)
    for _ in work:
        pass


def blocks_kernel(spans, ranks, first, step, facts, attended, weight, *results):
    for _ in project_blocks(ranks, first, Facts(facts, spans), step, attended, weight, *results):
        pass


def own_kernel(spans, facts, attended, weight, gate_table, result, gate, tiles, gates, semaphores):
    here = Facts(facts, spans)
    block = result.shape[0]
    count, _, tile = tiles.shape
    level = here.level()
    above = pl.multiple_of(level // 8 * 8, 8)
    gate_copy = copied(gate_table.at[pl.ds(above, 8)], gates, semaphores.at[count])
    copies = streamed(weight, 0, tiles, semaphores)
    start = pl.multiple_of(here.rank * block, block)
    for index, copy in enumerate(copies):
        copy.wait()
        product = jnp.dot(attended[pl.ds(start, block), :], tiles[index], preferred_element_type=jnp.float32)
        result[:, index * tile:(index + 1) * tile] = product.astype(jnp.bfloat16)
    gate_copy.wait()
    gate[...] = gates[pl.ds(lax.rem(level, 8), 1), :]


def final_kernel(done, projected, gate, up, down, result, own, gated, semaphores):
    first, (block, columns) = done.shape[1], own.shape
    pieces = gated.shape[0]
    wide = columns // pieces
    own_copy = copied(projected.at[:, pl.ds(first, columns)], own, semaphores.at[0])
    sent = [copied(done, result.at[:, pl.ds(0, first)], semaphores.at[1])]
    own_copy.wait()
    for piece in range(pieces):
        there = slice(piece * wide, (piece + 1) * wide)
        summed = own[:, there].astype(jnp.float32) + up[:, there].astype(jnp.float32)
        summed = summed + down[:, there].astype(jnp.float32)
        gated[piece] = (summed * gate[:, first + piece * wide:first + (piece + 1) * wide]).astype(jnp.bfloat16)
        sent.append(copied(
            gated.at[piece], result.at[:, pl.ds(first + piece * wide, wide)], semaphores.at[2 + piece]
        ))
    for copy in sent:
        copy.wait()


def body(queries, keys, values, out_weight, gate_table, levels, visible):
    rows, width = queries.shape
    model = out_weight.shape[1]
    spans = lax.axis_size("span")
    ranks = lax.axis_size("tensor")
    span = lax.axis_index("span")
    rank = lax.axis_index("tensor")
    block = rows // ranks
    bf16, f32 = jnp.bfloat16, jnp.float32
    numbers = jnp.arange(spans, dtype=jnp.int32)
    place = jnp.where(numbers == 0, span, jnp.where(numbers == 1, rank, 0)).astype(jnp.int32)
    facts = jnp.concatenate([visible, place[None, :], levels[None, :]], axis=0)

    third = (rows - block) // 48 * 16
    query_early, *query_late = pl.pallas_call(
        functools.partial(split_kernel, ranks),
        in_specs=[SMEM, HBM],
        out_specs=[VMEM] * 3,
        out_shape=[jax.ShapeDtypeStruct((part, width), bf16) for part in (block, rows - block - third, third)],
        scratch_shapes=[pltpu.SemaphoreType.DMA((3,))],
        compiler_params=PARAMS,
        cost_estimate=taking(1.7),
        name="split",
    )(jnp.stack([span, rank]).astype(jnp.int32), in_hbm(queries))
    distances = list(range(2, spans, 2))
    asked_early = [shifted(query_early, "span", -distance) for distance in distances]
    swap = [(i, i + 1 - 2 * (i % 2)) for i in range(spans)]
    key_beside = lax.ppermute(keys, "span", swap)
    value_beside = lax.ppermute(values, "span", swap)

    def after(value, *others):
        return lax.optimization_barrier((value, others))[0]

    def local(part, facts):
        size = (block, rows - block)[part]
        return pl.pallas_call(
            functools.partial(local_kernel, spans, ranks, part),
            in_specs=[SMEM, HBM, HBM, HBM, ANY, ANY],
            out_specs=[VMEM] * 2,
            out_shape=[jax.ShapeDtypeStruct((size, width), f32), jax.ShapeDtypeStruct((size, LANES), f32)],
            scratch_shapes=[pltpu.VMEM((size, width), bf16)] + [pltpu.VMEM((rows, width), bf16)] * 4
            + [pltpu.SemaphoreType.DMA((5,))],
            compiler_params=PARAMS,
            cost_estimate=taking(4.0),
            name="local",
        )(facts, in_hbm(queries), in_hbm(keys), in_hbm(values), key_beside, value_beside)

    def served(asked, distance):
        return pl.pallas_call(
            functools.partial(served_kernel, distance, spans),
            in_specs=[SMEM] + [VMEM] * (4 + len(asked)),
            out_specs=VMEM,
            out_shape=jax.ShapeDtypeStruct((sum(part.shape[0] for part in asked), width + LANES), bf16),
            scratch_shapes=[pltpu.VMEM((sum(part.shape[0] for part in asked), width), bf16)],
            compiler_params=PARAMS,
            cost_estimate=taking(3.3),
            name="served",
        )(facts, keys, values, key_beside, value_beside, *asked)

    early = list(local(0, facts))
    query_late = after(query_late, early)
    asked_early = after(asked_early, early)
    asked_late = [[shifted(query, "span", -distance) for query in query_late] for distance in distances]
    out_early = [served([q], d) for q, d in zip(asked_early, distances)]
    early += [shifted(o, "span", d) for o, d in zip(out_early, distances)]

    chunks = 2
    columns = model // chunks
    tiles = 4
    tile = columns // tiles
    last = ranks - 1
    weight = in_hbm(out_weight)

    tile_shape = (tiles, width, tile)
    streaming = dict(
        scratch_shapes=[pltpu.VMEM(tile_shape, bf16), pltpu.SemaphoreType.DMA((tiles,))],
        compiler_params=PARAMS,
        cost_estimate=taking(3.0),
    )
    fetched = pl.pallas_call(
        fetch_kernel,
        in_specs=[HBM],
        out_specs=VMEM,
        out_shape=jax.ShapeDtypeStruct(tile_shape, bf16),
        scratch_shapes=[pltpu.SemaphoreType.DMA((tiles,))],
        compiler_params=PARAMS,
        cost_estimate=taking(2.4),
        name="fetch",
    )(in_hbm(after(out_weight, out_early)))

    def opening(chunk, facts):
        scratch = streaming["scratch_shapes"] if chunk else []
        return pl.pallas_call(
            functools.partial(opening_kernel, ranks, distances, spans, chunk * columns),
            in_specs=[SMEM] + [VMEM] * (2 + len(distances)) + [HBM if chunk else VMEM],
            out_specs=VMEM,
            out_shape=jax.ShapeDtypeStruct((block, columns), bf16),
            scratch_shapes=scratch + [pltpu.VMEM((block, width), bf16)],
            compiler_params=PARAMS,
            cost_estimate=taking(3.4),
            name="opening",
        )(facts, *early, weight if chunk else fetched)

    ends = [(0, 1), (last, last - 1)]
    sent = opening(0, facts)
    arrived = [[lax.ppermute(sent, "tensor", ends)]]
    out_late = [served(q, d) for q, d in zip(after(asked_late, sent), distances)]
    for chunk in range(1, chunks):
        sent = opening(chunk, after(facts, out_late))
        arrived.append([lax.ppermute(sent, "tensor", ends)])
    late = list(local(1, after(facts, sent)))
    late += [shifted(o, "span", d) for o, d in zip(out_late, distances)]

    attended_shape = jax.ShapeDtypeStruct((rows, width), bf16)
    block_shapes = [jax.ShapeDtypeStruct((block, columns), bf16)] * 2
    attended, *merged = pl.pallas_call(
        functools.partial(merged_blocks_kernel, spans, ranks, distances),
        in_specs=[SMEM] + [VMEM] * (4 + 2 * len(distances)) + [HBM],
        out_specs=[VMEM] * 3,
        out_shape=[attended_shape] + block_shapes,
        name="merged_blocks",
        **streaming,
    )(facts, *early, *late, weight)

    def blocks_of(step, chunk, attended):
        return pl.pallas_call(
            functools.partial(blocks_kernel, spans, ranks, chunk * columns, step),
            in_specs=[SMEM, VMEM, HBM],
            out_specs=[VMEM] * 2,
            out_shape=block_shapes,
            name="blocks",
            **streaming,
        )(facts, attended, weight)

    before = attended
    for step in range(1, last):
        for chunk in range(chunks):
            if step == 1 and chunk == 0:
                blocks = merged
            else:
                blocks = blocks_of(step, chunk, after(attended, before))
            comes, blocks = lax.optimization_barrier((arrived[chunk], blocks))
            up, down = [
                (mine.astype(f32) + come.astype(f32)).astype(bf16)
                for mine, come in zip(blocks, (comes[0], comes[-1]))
            ]
            before = (up, down)
            arrived[chunk] = [
                lax.ppermute(up, "tensor", [(i, i + 1) for i in range(step + 1)]),
                lax.ppermute(down, "tensor", [(last - i, last - i - 1) for i in range(step + 1)]),
            ]
    everything = chunks * tiles
    projected, gate = pl.pallas_call(
        functools.partial(own_kernel, spans),
        in_specs=[SMEM, VMEM, HBM, HBM],
        out_specs=[VMEM, VMEM],
        out_shape=[jax.ShapeDtypeStruct((block, model), bf16), jax.ShapeDtypeStruct((1, model), f32)],
        scratch_shapes=[
            pltpu.VMEM((everything, width, tile), bf16),
            pltpu.VMEM((8, model), f32),
            pltpu.SemaphoreType.DMA((everything + 1,)),
        ],
        compiler_params=PARAMS,
        cost_estimate=taking(5.0),
        name="own",
    )(facts, after(attended, before), weight, in_hbm(gate_table))

    finished = []
    for chunk in range(chunks - 1):
        there = slice(chunk * columns, (chunk + 1) * columns)
        summed = sum(part.astype(f32) for part in (projected[:, there], *arrived[chunk]))
        finished.append((summed * gate[:, there]).astype(bf16))
    pieces = 2
    return pl.pallas_call(
        final_kernel,
        in_specs=[ANY, ANY, VMEM, VMEM, VMEM],
        out_specs=HBM,
        out_shape=jax.ShapeDtypeStruct((block, model), bf16),
        scratch_shapes=[
            pltpu.VMEM((block, columns), bf16),
            pltpu.VMEM((pieces, block, columns // pieces), bf16),
            pltpu.SemaphoreType.DMA((2 + pieces,)),
        ],
        compiler_params=PARAMS,
        cost_estimate=taking(2.7),
        name="final",
    )(jnp.concatenate(finished, axis=1), projected, gate, *arrived[-1])


def solution(mesh):
    return jax.shard_map(
        body,
        mesh=mesh,
        in_specs=(
            P(("group", "span"), "tensor"),
            P(("group", "span"), "tensor"),
            P(("group", "span"), "tensor"),
            P("tensor", None),
            P(),
            P("group"),
            P("group", None),
        ),
        out_specs=P(("group", "span", "tensor"), None),
        check_vma=False,
    )
```

```python
import functools

import jax
import jax.numpy as jnp
from jax import lax
from jax.experimental import pallas as pl
from jax.experimental.pallas import tpu as pltpu
from jax.sharding import PartitionSpec as P

HD = 128
LANES = 128
HIDDEN = -1e30
LOG2E = 1.4426950408889634
PARAMS = pltpu.CompilerParams(vmem_limit_bytes=24 * 1024 * 1024)
SMEM = pl.BlockSpec(memory_space=pltpu.SMEM)
VMEM = pl.BlockSpec(memory_space=pltpu.VMEM)
ANY = pl.BlockSpec(memory_space=pl.ANY)
HBM = pl.BlockSpec(memory_space=pltpu.HBM)
PIECE_LANES = 32


def taking(microseconds):
    return pl.CostEstimate(flops=0, bytes_accessed=int(microseconds * 3.69e6), transcendentals=0)


def in_hbm(array):
    return pltpu.with_memory_space_constraint(array, pltpu.HBM)


def shifted(block, axis, distance):
    count = lax.axis_size(axis)
    return lax.ppermute(block, axis, [(i, i + distance) for i in range(count) if 0 <= i + distance < count])


def head_columns(head):
    return slice(head * HD, (head + 1) * HD)


def attend(query, keys, values, flags, write):
    rows, width = query.shape
    scale = LOG2E * HD ** (-0.5)
    lane = lax.broadcasted_iota(jnp.int32, (rows, LANES), 1)
    packed = jnp.zeros((rows, LANES), jnp.float32)

    def scored(head):
        columns = head_columns(head)
        return [
            lax.dot_general(
                query[:, columns], key[:, columns], (((1,), (1,)), ((), ())), preferred_element_type=jnp.float32
            )
            for key in keys
        ]

    heads = width // HD
    later = scored(0)
    for head in range(heads):
        columns = head_columns(head)
        scores, later = later, scored(head + 1) if head + 1 < heads else None
        tops = [jnp.max(block, axis=-1, keepdims=True) * scale for block in scores]
        top = functools.reduce(
            jnp.maximum, [one if flag is None else jnp.where(flag, one, HIDDEN) for one, flag in zip(tops, flags)]
        )
        joined = None
        for block, value, flag in zip(scores, values, flags):
            above = top if flag is None else jnp.where(flag, top, -HIDDEN)
            probs = jnp.exp2(block * scale - above).astype(jnp.bfloat16)
            beside = jnp.concatenate([value[:, columns], jnp.ones((value.shape[0], HD), jnp.bfloat16)], axis=1)
            part = jnp.dot(probs, beside, preferred_element_type=jnp.float32)
            joined = part if joined is None else joined + part
        product, total = joined[:, :HD], jnp.where(joined[:, HD:] > 0.0, joined[:, HD:], 1.0)
        write(columns, product / total)
        packed = jnp.where(lane == head, top + jnp.log2(total), packed)
    return packed


class Facts:
    def __init__(self, place, visible):
        self.span, self.rank, self.visible = place[0], place[1], visible
        self.beside = self.span + 1 - 2 * lax.rem(self.span, 2)

    def sees(self, asker, span):
        return self.visible[asker, span] > 0


def copied(source, target, semaphore):
    copy = pltpu.make_async_copy(source, target, semaphore)
    copy.start()
    return copy


def parts_of(rank, ranks, rows):
    block = rows // ranks
    lower = rank < ranks // 2
    early = pl.multiple_of(jnp.where(lower, rows - block, 0), block)
    late = pl.multiple_of(jnp.where(lower, 0, block), block)
    return (early, block), (late, rows - block)


def split_kernel(ranks, place, query, *refs):
    *targets, semaphores = refs

    @pl.when(place[0] > 1)
    def _():
        (early, _), (late, _) = parts_of(place[1], ranks, query.shape[0])
        starts = (early, late, pl.multiple_of(late + targets[1].shape[0], 16))
        copies = [
            copied(query.at[pl.ds(start, target.shape[0])], target, semaphores.at[index])
            for index, (start, target) in enumerate(zip(starts, targets))
        ]
        for copy in copies:
            copy.wait()


def local_kernel(ranks, part, place, visible, query, key, value, key_beside, value_beside, result, sums, *scratch):
    here = Facts(place, visible)
    query_, key_, value_, key_beside_, value_beside_, semaphores = scratch
    start, size = parts_of(here.rank, ranks, query.shape[0])[part]
    copies = [
        copied(source, target, semaphores.at[index])
        for index, (source, target) in enumerate((
            (query.at[pl.ds(start, size)], query_),
            (key, key_), (key_beside, key_beside_), (value, value_), (value_beside, value_beside_),
        ))
    ]
    for copy in copies:
        copy.wait()

    def write(columns, block):
        result[:, columns] = block

    flags = [None, here.sees(here.span, here.beside)]
    sums[...] = attend(query_, [key_, key_beside_], [value_, value_beside_], flags, write)


def served_kernel(distance, spans, place, visible, key, value, key_beside, value_beside, *refs):
    here = Facts(place, visible)

    @pl.when(here.span + distance < spans)
    def _():
        asker = jnp.minimum(here.span + distance, spans - 1)
        flags = [here.sees(asker, here.span), here.sees(asker, here.beside)]
        *queries, result, query = refs
        at = 0
        for part in queries:
            query[at:at + part.shape[0], :] = part[...]
            at += part.shape[0]

        def write(columns, block):
            result[:, columns] = block.astype(jnp.bfloat16)

        rest = attend(query, [key, key_beside], [value, value_beside], flags, write)
        sent = jnp.zeros_like(rest)
        for piece in range(3):
            part = rest.astype(jnp.bfloat16).astype(jnp.float32)
            sent = sent + (part if piece == 0 else pltpu.roll(part, piece * PIECE_LANES, 1))
            rest = rest - part
        result[:, query.shape[1]:] = sent.astype(jnp.bfloat16)


def merge(span, distances, own, own_sum, served, write):
    width = own.shape[1]
    sums = [own_sum[...]]
    for distance, ref in zip(distances, served):
        sent = ref[:, width:].astype(jnp.float32)
        joined = sent
        for piece in (1, 2):
            joined = joined + pltpu.roll(sent, LANES - piece * PIECE_LANES, 1)
        sums.append(jnp.where(span >= distance, joined, HIDDEN))
    top = functools.reduce(jnp.maximum, sums)
    shares = [jnp.exp2(one - top) for one in sums]
    over = 1.0 / sum(shares)
    shares = [share * over for share in shares]
    for head in range(width // HD):
        columns = head_columns(head)
        merged = own[:, columns] * shares[0][:, head:head + 1]
        for distance, share, ref in zip(distances, shares[1:], served):
            away = jnp.where(span >= distance, ref[:, columns].astype(jnp.float32), 0.0)
            merged = merged + away * share[:, head:head + 1]
        write(columns, merged.astype(jnp.bfloat16))


def streamed(weight, first, tiles, semaphores):
    count, _, tile = tiles.shape
    return [
        copied(weight.at[:, pl.ds(first + index * tile, tile)], tiles.at[index], semaphores.at[index])
        for index in range(count)
    ]


def fetch_kernel(ranks, place, weight, tiles, semaphores):
    @pl.when(jnp.logical_or(place[1] == 0, place[1] == ranks - 1))
    def _():
        for copy in streamed(weight, 0, tiles, semaphores):
            copy.wait()


def opening_kernel(ranks, distances, first, place, *refs):
    own, own_sum, *served = refs[:2 + len(distances)]
    weight, result, *scratch = refs[2 + len(distances):]
    rows = scratch[-1]

    @pl.when(jnp.logical_or(place[1] == 0, place[1] == ranks - 1))
    def _():
        tiles, copies = weight, [None] * weight.shape[0]
        if first:
            tiles, semaphores, _ = scratch
            copies = streamed(weight, first, tiles, semaphores)

        def write(columns, part):
            rows[:, columns] = part

        merge(place[0], distances, own, own_sum, served, write)
        tile = tiles.shape[2]
        for index, copy in enumerate(copies):
            if copy is not None:
                copy.wait()
            product = jnp.dot(rows[...], tiles[index], preferred_element_type=jnp.float32)
            result[:, index * tile:(index + 1) * tile] = product.astype(jnp.bfloat16)


def project_blocks(ranks, first, rank, step, attended, weight, up, down, tiles, semaphores):
    last = ranks - 1
    tile = tiles.shape[2]
    block = up.shape[0]
    copies = streamed(weight, first, tiles, semaphores)
    yield
    sends = rank <= step, rank >= last - step
    starts = [
        pl.multiple_of(jnp.clip(target, 0, last) * block, block) for target in (last - step + rank, step + rank - last)
    ]
    rows = [attended[pl.ds(start, block), :] for start in starts]
    for index, copy in enumerate(copies):
        copy.wait()
        there = slice(index * tile, (index + 1) * tile)

        @pl.when(jnp.logical_and(*sends))
        def _():
            both = jnp.dot(jnp.concatenate(rows, axis=0), tiles[index], preferred_element_type=jnp.float32)
            up[:, there] = both[:block].astype(jnp.bfloat16)
            down[:, there] = both[block:].astype(jnp.bfloat16)

        @pl.when(jnp.logical_not(jnp.logical_and(*sends)))
        def _():
            one = jnp.dot(
                jnp.where(sends[0], rows[0], rows[1]), tiles[index], preferred_element_type=jnp.float32
            ).astype(jnp.bfloat16)
            up[:, there] = one
            down[:, there] = one


def merged_blocks_kernel(ranks, distances, place, *refs):
    each = 2 + len(distances)
    parts, (weight, attended, *results) = (refs[:each], refs[each:2 * each]), refs[2 * each:]
    work = project_blocks(ranks, 0, place[1], 1, attended, weight, *results)
    next(work)
    for (start, size), (own, own_sum, *served) in zip(parts_of(place[1], ranks, attended.shape[0]), parts):
        there = pl.ds(start, size)

        def write(columns, part):
            attended[there, columns] = part

        merge(place[0], distances, own, own_sum, served, write)
    for _ in work:
        pass


def blocks_kernel(ranks, first, step, place, attended, weight, *results):
    for _ in project_blocks(ranks, first, place[1], step, attended, weight, *results):
        pass


def own_kernel(place, levels, attended, weight, gate_table, result, gate, tiles, gates, semaphores):
    block = result.shape[0]
    count, _, tile = tiles.shape
    level = levels[place[0]]
    above = pl.multiple_of(level // 8 * 8, 8)
    gate_copy = copied(gate_table.at[pl.ds(above, 8)], gates, semaphores.at[count])
    copies = streamed(weight, 0, tiles, semaphores)
    start = pl.multiple_of(place[1] * block, block)
    for index, copy in enumerate(copies):
        copy.wait()
        product = jnp.dot(attended[pl.ds(start, block), :], tiles[index], preferred_element_type=jnp.float32)
        result[:, index * tile:(index + 1) * tile] = product.astype(jnp.bfloat16)
    gate_copy.wait()
    gate[...] = gates[pl.ds(lax.rem(level, 8), 1), :]


def final_kernel(done, projected, gate, up, down, result, own, gated, semaphores):
    first, (block, columns) = done.shape[1], own.shape
    pieces = gated.shape[0]
    wide = columns // pieces
    own_copy = copied(projected.at[:, pl.ds(first, columns)], own, semaphores.at[0])
    sent = [copied(done, result.at[:, pl.ds(0, first)], semaphores.at[1])]
    own_copy.wait()
    for piece in range(pieces):
        there = slice(piece * wide, (piece + 1) * wide)
        summed = own[:, there].astype(jnp.float32) + up[:, there].astype(jnp.float32)
        summed = summed + down[:, there].astype(jnp.float32)
        gated[piece] = (summed * gate[:, first + piece * wide:first + (piece + 1) * wide]).astype(jnp.bfloat16)
        sent.append(copied(
            gated.at[piece], result.at[:, pl.ds(first + piece * wide, wide)], semaphores.at[2 + piece]
        ))
    for copy in sent:
        copy.wait()


def body(queries, keys, values, out_weight, gate_table, levels, visible):
    rows, width = queries.shape
    model = out_weight.shape[1]
    spans = lax.axis_size("span")
    ranks = lax.axis_size("tensor")
    span = lax.axis_index("span")
    rank = lax.axis_index("tensor")
    block = rows // ranks
    bf16, f32 = jnp.bfloat16, jnp.float32
    place = jnp.stack([span, rank]).astype(jnp.int32)
    third = (rows - block) // 48 * 16
    query_early, *query_late = pl.pallas_call(
        functools.partial(split_kernel, ranks),
        in_specs=[SMEM, HBM],
        out_specs=[VMEM] * 3,
        out_shape=[jax.ShapeDtypeStruct((part, width), bf16) for part in (block, rows - block - third, third)],
        scratch_shapes=[pltpu.SemaphoreType.DMA((3,))],
        compiler_params=PARAMS,
        cost_estimate=taking(1.7),
        name="split",
    )(place, in_hbm(queries))
    distances = list(range(2, spans, 2))
    asked_early = [shifted(query_early, "span", -distance) for distance in distances]
    swap = [(i, i + 1 - 2 * (i % 2)) for i in range(spans)]
    key_beside = lax.ppermute(keys, "span", swap)
    value_beside = lax.ppermute(values, "span", swap)

    def after(value, *others):
        return lax.optimization_barrier((value, others))[0]

    def local(part, place):
        size = (block, rows - block)[part]
        return pl.pallas_call(
            functools.partial(local_kernel, ranks, part),
            in_specs=[SMEM, SMEM, HBM, HBM, HBM, ANY, ANY],
            out_specs=[VMEM] * 2,
            out_shape=[jax.ShapeDtypeStruct((size, width), f32), jax.ShapeDtypeStruct((size, LANES), f32)],
            scratch_shapes=[pltpu.VMEM((size, width), bf16)] + [pltpu.VMEM((rows, width), bf16)] * 4
            + [pltpu.SemaphoreType.DMA((5,))],
            compiler_params=PARAMS,
            cost_estimate=taking(4.0),
            name="local",
        )(place, visible, in_hbm(queries), in_hbm(keys), in_hbm(values), key_beside, value_beside)

    def served(asked, distance):
        return pl.pallas_call(
            functools.partial(served_kernel, distance, spans),
            in_specs=[SMEM, SMEM] + [VMEM] * (4 + len(asked)),
            out_specs=VMEM,
            out_shape=jax.ShapeDtypeStruct((sum(part.shape[0] for part in asked), width + LANES), bf16),
            scratch_shapes=[pltpu.VMEM((sum(part.shape[0] for part in asked), width), bf16)],
            compiler_params=PARAMS,
            cost_estimate=taking(3.3),
            name="served",
        )(place, visible, keys, values, key_beside, value_beside, *asked)

    early = list(local(0, place))
    query_late = after(query_late, early)
    asked_early = after(asked_early, early)
    asked_late = [[shifted(query, "span", -distance) for query in query_late] for distance in distances]
    out_early = [served([q], d) for q, d in zip(asked_early, distances)]
    early += [shifted(o, "span", d) for o, d in zip(out_early, distances)]

    chunks = 2
    columns = model // chunks
    tiles = 4
    tile = columns // tiles
    last = ranks - 1
    weight = in_hbm(out_weight)

    tile_shape = (tiles, width, tile)
    streaming = dict(
        scratch_shapes=[pltpu.VMEM(tile_shape, bf16), pltpu.SemaphoreType.DMA((tiles,))],
        compiler_params=PARAMS,
        cost_estimate=taking(3.0),
    )
    fetched = pl.pallas_call(
        functools.partial(fetch_kernel, ranks),
        in_specs=[SMEM, HBM],
        out_specs=VMEM,
        out_shape=jax.ShapeDtypeStruct(tile_shape, bf16),
        scratch_shapes=[pltpu.SemaphoreType.DMA((tiles,))],
        compiler_params=PARAMS,
        cost_estimate=taking(2.4),
        name="fetch",
    )(after(place, out_early), weight)

    def opening(chunk, place):
        scratch = streaming["scratch_shapes"] if chunk else []
        return pl.pallas_call(
            functools.partial(opening_kernel, ranks, distances, chunk * columns),
            in_specs=[SMEM] + [VMEM] * (2 + len(distances)) + [HBM if chunk else VMEM],
            out_specs=VMEM,
            out_shape=jax.ShapeDtypeStruct((block, columns), bf16),
            scratch_shapes=scratch + [pltpu.VMEM((block, width), bf16)],
            compiler_params=PARAMS,
            cost_estimate=taking(3.4),
            name="opening",
        )(place, *early, weight if chunk else fetched)

    ends = [(0, 1), (last, last - 1)]
    sent = opening(0, place)
    arrived = [[lax.ppermute(sent, "tensor", ends)]]
    out_late = [served(q, d) for q, d in zip(after(asked_late, sent), distances)]
    for chunk in range(1, chunks):
        sent = opening(chunk, after(place, out_late))
        arrived.append([lax.ppermute(sent, "tensor", ends)])
    late = list(local(1, after(place, sent)))
    late += [shifted(o, "span", d) for o, d in zip(out_late, distances)]

    attended_shape = jax.ShapeDtypeStruct((rows, width), bf16)
    block_shapes = [jax.ShapeDtypeStruct((block, columns), bf16)] * 2
    attended, *merged = pl.pallas_call(
        functools.partial(merged_blocks_kernel, ranks, distances),
        in_specs=[SMEM] + [VMEM] * (4 + 2 * len(distances)) + [HBM],
        out_specs=[VMEM] * 3,
        out_shape=[attended_shape] + block_shapes,
        name="merged_blocks",
        **streaming,
    )(place, *early, *late, weight)

    def blocks_of(step, chunk, attended):
        return pl.pallas_call(
            functools.partial(blocks_kernel, ranks, chunk * columns, step),
            in_specs=[SMEM, VMEM, HBM],
            out_specs=[VMEM] * 2,
            out_shape=block_shapes,
            name="blocks",
            **streaming,
        )(place, attended, weight)

    before = attended
    for step in range(1, last):
        for chunk in range(chunks):
            if step == 1 and chunk == 0:
                blocks = merged
            else:
                blocks = blocks_of(step, chunk, after(attended, before))
            comes, blocks = lax.optimization_barrier((arrived[chunk], blocks))
            up, down = [
                (mine.astype(f32) + come.astype(f32)).astype(bf16)
                for mine, come in zip(blocks, (comes[0], comes[-1]))
            ]
            before = (up, down)
            arrived[chunk] = [
                lax.ppermute(up, "tensor", [(i, i + 1) for i in range(step + 1)]),
                lax.ppermute(down, "tensor", [(last - i, last - i - 1) for i in range(step + 1)]),
            ]
    everything = chunks * tiles
    projected, gate = pl.pallas_call(
        own_kernel,
        in_specs=[SMEM, SMEM, VMEM, HBM, HBM],
        out_specs=[VMEM, VMEM],
        out_shape=[jax.ShapeDtypeStruct((block, model), bf16), jax.ShapeDtypeStruct((1, model), f32)],
        scratch_shapes=[
            pltpu.VMEM((everything, width, tile), bf16),
            pltpu.VMEM((8, model), f32),
            pltpu.SemaphoreType.DMA((everything + 1,)),
        ],
        compiler_params=PARAMS,
        cost_estimate=taking(5.0),
        name="own",
    )(place, levels, after(attended, before), weight, in_hbm(gate_table))

    finished = []
    for chunk in range(chunks - 1):
        there = slice(chunk * columns, (chunk + 1) * columns)
        summed = sum(part.astype(f32) for part in (projected[:, there], *arrived[chunk]))
        finished.append((summed * gate[:, there]).astype(bf16))
    pieces = 2
    return pl.pallas_call(
        final_kernel,
        in_specs=[ANY, ANY, VMEM, VMEM, VMEM],
        out_specs=HBM,
        out_shape=jax.ShapeDtypeStruct((block, model), bf16),
        scratch_shapes=[
            pltpu.VMEM((block, columns), bf16),
            pltpu.VMEM((pieces, block, columns // pieces), bf16),
            pltpu.SemaphoreType.DMA((2 + pieces,)),
        ],
        compiler_params=PARAMS,
        cost_estimate=taking(2.7),
        name="final",
    )(jnp.concatenate(finished, axis=1), projected, gate, *arrived[-1])


def solution(mesh):
    return jax.shard_map(
        body,
        mesh=mesh,
        in_specs=(
            P(("group", "span"), "tensor"),
            P(("group", "span"), "tensor"),
            P(("group", "span"), "tensor"),
            P("tensor", None),
            P(),
            P("group"),
            P("group", None),
        ),
        out_specs=P(("group", "span", "tensor"), None),
        check_vma=False,
    )
```

```python
import functools

import jax
import jax.numpy as jnp
from jax import lax
from jax.experimental import pallas as pl
from jax.experimental.pallas import tpu as pltpu
from jax.sharding import PartitionSpec as P

HD = 128
LANES = 128
HIDDEN = -1e30
LOG2E = 1.4426950408889634
PARAMS = pltpu.CompilerParams(vmem_limit_bytes=24 * 1024 * 1024)
SMEM = pl.BlockSpec(memory_space=pltpu.SMEM)
VMEM = pl.BlockSpec(memory_space=pltpu.VMEM)
ANY = pl.BlockSpec(memory_space=pl.ANY)
HBM = pl.BlockSpec(memory_space=pltpu.HBM)
PIECE_LANES = 32


def taking(microseconds):
    return pl.CostEstimate(flops=0, bytes_accessed=int(microseconds * 3.69e6), transcendentals=0)


def in_hbm(array):
    return pltpu.with_memory_space_constraint(array, pltpu.HBM)


def shifted(block, axis, distance):
    count = lax.axis_size(axis)
    return lax.ppermute(block, axis, [(i, i + distance) for i in range(count) if 0 <= i + distance < count])


def head_columns(head):
    return slice(head * HD, (head + 1) * HD)


def attend(query, keys, values, flags, write):
    rows, width = query.shape
    scale = LOG2E * HD ** (-0.5)
    lane = lax.broadcasted_iota(jnp.int32, (rows, LANES), 1)
    packed = jnp.zeros((rows, LANES), jnp.float32)

    def scored(head):
        columns = head_columns(head)
        return [
            lax.dot_general(
                query[:, columns], key[:, columns], (((1,), (1,)), ((), ())), preferred_element_type=jnp.float32
            )
            for key in keys
        ]

    heads = width // HD
    later = scored(0)
    for head in range(heads):
        columns = head_columns(head)
        scores, later = later, scored(head + 1) if head + 1 < heads else None
        tops = [jnp.max(block, axis=-1, keepdims=True) * scale for block in scores]
        top = functools.reduce(
            jnp.maximum, [one if flag is None else jnp.where(flag, one, HIDDEN) for one, flag in zip(tops, flags)]
        )
        joined = None
        for block, value, flag in zip(scores, values, flags):
            above = top if flag is None else jnp.where(flag, top, -HIDDEN)
            probs = jnp.exp2(block * scale - above).astype(jnp.bfloat16)
            beside = jnp.concatenate([value[:, columns], jnp.ones((value.shape[0], HD), jnp.bfloat16)], axis=1)
            part = jnp.dot(probs, beside, preferred_element_type=jnp.float32)
            joined = part if joined is None else joined + part
        product, total = joined[:, :HD], jnp.where(joined[:, HD:] > 0.0, joined[:, HD:], 1.0)
        write(columns, product / total)
        packed = jnp.where(lane == head, top + jnp.log2(total), packed)
    return packed


class Facts:
    def __init__(self, ref, spans):
        self.ref, self.spans = ref, spans
        self.span, self.rank = ref[spans, 0], ref[spans, 1]
        self.beside = self.span + 1 - 2 * lax.rem(self.span, 2)

    def sees(self, asker, span):
        return self.ref[asker, span] > 0

    def level(self):
        return self.ref[self.spans + 1, self.span]


def copied(source, target, semaphore):
    copy = pltpu.make_async_copy(source, target, semaphore)
    copy.start()
    return copy


def parts_of(rank, ranks, rows):
    block = rows // ranks
    lower = rank < ranks // 2
    early = pl.multiple_of(jnp.where(lower, rows - block, 0), block)
    late = pl.multiple_of(jnp.where(lower, 0, block), block)
    return (early, block), (late, rows - block)


def split_kernel(ranks, place, query, *refs):
    *targets, semaphores = refs

    @pl.when(place[0] > 1)
    def _():
        (early, _), (late, _) = parts_of(place[1], ranks, query.shape[0])
        starts = (early, late, pl.multiple_of(late + targets[1].shape[0], 16))
        copies = [
            copied(query.at[pl.ds(start, target.shape[0])], target, semaphores.at[index])
            for index, (start, target) in enumerate(zip(starts, targets))
        ]
        for copy in copies:
            copy.wait()


def local_kernel(spans, ranks, part, who, facts, query, key, value, key_beside, value_beside, *refs):
    here = Facts(facts, spans)
    if who is None:
        attend_here(here, ranks, part, query, key, value, key_beside, value_beside, *refs)
        return
    mine = here.span > 1 if who == "askers" else here.span < 2

    @pl.when(mine)
    def _():
        attend_here(here, ranks, part, query, key, value, key_beside, value_beside, *refs)

    *before, result, sums = refs[:-6]
    if before:

        @pl.when(jnp.logical_not(mine))
        def _():
            result[...] = before[0][...]
            sums[...] = before[1][...]


def attend_here(here, ranks, part, query, key, value, key_beside, value_beside, *refs):
    result, sums, query_, key_, value_, key_beside_, value_beside_, semaphores = refs[-8:]
    start, size = parts_of(here.rank, ranks, query.shape[0])[part]
    copies = [
        copied(source, target, semaphores.at[index])
        for index, (source, target) in enumerate((
            (query.at[pl.ds(start, size)], query_),
            (key, key_), (key_beside, key_beside_), (value, value_), (value_beside, value_beside_),
        ))
    ]
    for copy in copies:
        copy.wait()

    def write(columns, block):
        result[:, columns] = block

    flags = [None, here.sees(here.span, here.beside)]
    sums[...] = attend(query_, [key_, key_beside_], [value_, value_beside_], flags, write)


def served_kernel(distance, spans, facts, key, value, key_beside, value_beside, *refs):
    here = Facts(facts, spans)

    @pl.when(here.span + distance < spans)
    def _():
        asker = jnp.minimum(here.span + distance, spans - 1)
        flags = [here.sees(asker, here.span), here.sees(asker, here.beside)]
        *queries, result, query = refs
        at = 0
        for part in queries:
            query[at:at + part.shape[0], :] = part[...]
            at += part.shape[0]

        def write(columns, block):
            result[:, columns] = block.astype(jnp.bfloat16)

        rest = attend(query, [key, key_beside], [value, value_beside], flags, write)
        sent = jnp.zeros_like(rest)
        for piece in range(3):
            part = rest.astype(jnp.bfloat16).astype(jnp.float32)
            sent = sent + (part if piece == 0 else pltpu.roll(part, piece * PIECE_LANES, 1))
            rest = rest - part
        result[:, query.shape[1]:] = sent.astype(jnp.bfloat16)


def merge(span, distances, own, own_sum, served, write):
    width = own.shape[1]
    sums = [own_sum[...]]
    for distance, ref in zip(distances, served):
        sent = ref[:, width:].astype(jnp.float32)
        joined = sent
        for piece in (1, 2):
            joined = joined + pltpu.roll(sent, LANES - piece * PIECE_LANES, 1)
        sums.append(jnp.where(span >= distance, joined, HIDDEN))
    top = functools.reduce(jnp.maximum, sums)
    shares = [jnp.exp2(one - top) for one in sums]
    over = 1.0 / sum(shares)
    shares = [share * over for share in shares]
    for head in range(width // HD):
        columns = head_columns(head)
        merged = own[:, columns] * shares[0][:, head:head + 1]
        for distance, share, ref in zip(distances, shares[1:], served):
            away = jnp.where(span >= distance, ref[:, columns].astype(jnp.float32), 0.0)
            merged = merged + away * share[:, head:head + 1]
        write(columns, merged.astype(jnp.bfloat16))


def streamed(weight, first, tiles, semaphores):
    count, _, tile = tiles.shape
    return [
        copied(weight.at[:, pl.ds(first + index * tile, tile)], tiles.at[index], semaphores.at[index])
        for index in range(count)
    ]


def fetch_kernel(weight, tiles, semaphores):
    for copy in streamed(weight, 0, tiles, semaphores):
        copy.wait()


def opening_kernel(ranks, distances, spans, first, facts, *refs):
    own, own_sum, *served = refs[:2 + len(distances)]
    weight, *fetched, result = refs[2 + len(distances):-3]
    scratch = refs[-3:]
    fetched = fetched[0] if fetched else None
    rows = scratch[-1]
    here = Facts(facts, spans)

    @pl.when(jnp.logical_or(here.rank == 0, here.rank == ranks - 1))
    def _():
        tiles, semaphores, _ = scratch
        tile = tiles.shape[2]
        parts = [] if fetched is None else [(None, fetched, index) for index in range(fetched.shape[0])]
        copies = streamed(weight, first + len(parts) * tile, tiles, semaphores)
        parts += [(copy, tiles, index) for index, copy in enumerate(copies)]

        def write(columns, part):
            rows[:, columns] = part

        merge(here.span, distances, own, own_sum, served, write)
        for at, (copy, held, index) in enumerate(parts):
            if copy is not None:
                copy.wait()
            product = jnp.dot(rows[...], held[index], preferred_element_type=jnp.float32)
            result[:, at * tile:(at + 1) * tile] = product.astype(jnp.bfloat16)


def project_blocks(ranks, first, facts, step, attended, weight, up, down, tiles, semaphores):
    rank = facts.rank
    last = ranks - 1
    tile = tiles.shape[2]
    block = up.shape[0]
    copies = streamed(weight, first, tiles, semaphores)
    yield
    sends = rank <= step, rank >= last - step
    starts = [
        pl.multiple_of(jnp.clip(target, 0, last) * block, block) for target in (last - step + rank, step + rank - last)
    ]
    rows = [attended[pl.ds(start, block), :] for start in starts]
    for index, copy in enumerate(copies):
        copy.wait()
        there = slice(index * tile, (index + 1) * tile)

        @pl.when(jnp.logical_and(*sends))
        def _():
            both = jnp.dot(jnp.concatenate(rows, axis=0), tiles[index], preferred_element_type=jnp.float32)
            up[:, there] = both[:block].astype(jnp.bfloat16)
            down[:, there] = both[block:].astype(jnp.bfloat16)

        @pl.when(jnp.logical_not(jnp.logical_and(*sends)))
        def _():
            one = jnp.dot(
                jnp.where(sends[0], rows[0], rows[1]), tiles[index], preferred_element_type=jnp.float32
            ).astype(jnp.bfloat16)
            up[:, there] = one
            down[:, there] = one


def merged_blocks_kernel(spans, ranks, distances, facts, *refs):
    each = 2 + len(distances)
    parts, (weight, attended, *results) = (refs[:each], refs[each:2 * each]), refs[2 * each:]
    here = Facts(facts, spans)
    work = project_blocks(ranks, 0, here, 1, attended, weight, *results)
    next(work)
    for (start, size), (own, own_sum, *served) in zip(parts_of(here.rank, ranks, attended.shape[0]), parts):
        there = pl.ds(start, size)

        def write(columns, part):
            attended[there, columns] = part

        merge(here.span, distances, own, own_sum, served, write)
    for _ in work:
        pass


def blocks_kernel(spans, ranks, first, step, facts, attended, weight, *results):
    for _ in project_blocks(ranks, first, Facts(facts, spans), step, attended, weight, *results):
        pass


def own_kernel(spans, facts, attended, weight, gate_table, result, gate, tiles, gates, semaphores):
    here = Facts(facts, spans)
    block = result.shape[0]
    count, _, tile = tiles.shape
    level = here.level()
    above = pl.multiple_of(level // 8 * 8, 8)
    gate_copy = copied(gate_table.at[pl.ds(above, 8)], gates, semaphores.at[count])
    copies = streamed(weight, 0, tiles, semaphores)
    start = pl.multiple_of(here.rank * block, block)
    for index, copy in enumerate(copies):
        copy.wait()
        product = jnp.dot(attended[pl.ds(start, block), :], tiles[index], preferred_element_type=jnp.float32)
        result[:, index * tile:(index + 1) * tile] = product.astype(jnp.bfloat16)
    gate_copy.wait()
    gate[...] = gates[pl.ds(lax.rem(level, 8), 1), :]


def final_kernel(done, projected, gate, up, down, result, own, gated, semaphores):
    first, (block, columns) = done.shape[1], own.shape
    pieces = gated.shape[0]
    wide = columns // pieces
    own_copy = copied(projected.at[:, pl.ds(first, columns)], own, semaphores.at[0])
    sent = [copied(done, result.at[:, pl.ds(0, first)], semaphores.at[1])]
    own_copy.wait()
    for piece in range(pieces):
        there = slice(piece * wide, (piece + 1) * wide)
        summed = own[:, there].astype(jnp.float32) + up[:, there].astype(jnp.float32)
        summed = summed + down[:, there].astype(jnp.float32)
        gated[piece] = (summed * gate[:, first + piece * wide:first + (piece + 1) * wide]).astype(jnp.bfloat16)
        sent.append(copied(
            gated.at[piece], result.at[:, pl.ds(first + piece * wide, wide)], semaphores.at[2 + piece]
        ))
    for copy in sent:
        copy.wait()


def body(queries, keys, values, out_weight, gate_table, levels, visible):
    rows, width = queries.shape
    model = out_weight.shape[1]
    spans = lax.axis_size("span")
    ranks = lax.axis_size("tensor")
    span = lax.axis_index("span")
    rank = lax.axis_index("tensor")
    block = rows // ranks
    bf16, f32 = jnp.bfloat16, jnp.float32
    numbers = jnp.arange(spans, dtype=jnp.int32)
    place = jnp.where(numbers == 0, span, jnp.where(numbers == 1, rank, 0)).astype(jnp.int32)
    facts = jnp.concatenate([visible, place[None, :], levels[None, :]], axis=0)

    third = (rows - block) // 48 * 16
    query_early, *query_late = pl.pallas_call(
        functools.partial(split_kernel, ranks),
        in_specs=[SMEM, HBM],
        out_specs=[VMEM] * 3,
        out_shape=[jax.ShapeDtypeStruct((part, width), bf16) for part in (block, rows - block - third, third)],
        scratch_shapes=[pltpu.SemaphoreType.DMA((3,))],
        compiler_params=PARAMS,
        cost_estimate=taking(1.7),
        name="split",
    )(jnp.stack([span, rank]).astype(jnp.int32), in_hbm(queries))
    query_late = list(query_late)
    distances = list(range(2, spans, 2))
    asked_early = [shifted(query_early, "span", -distance) for distance in distances]
    swap = [(i, i + 1 - 2 * (i % 2)) for i in range(spans)]
    key_beside = lax.ppermute(keys, "span", swap)
    value_beside = lax.ppermute(values, "span", swap)

    def after(value, *others):
        return lax.optimization_barrier((value, others))[0]

    def local(part, facts, who=None, before=()):
        size = (block, rows - block)[part]
        return list(pl.pallas_call(
            functools.partial(local_kernel, spans, ranks, part, who),
            in_specs=[SMEM, HBM, HBM, HBM, ANY, ANY] + [VMEM] * len(before),
            out_specs=[VMEM] * 2,
            out_shape=[jax.ShapeDtypeStruct((size, width), f32), jax.ShapeDtypeStruct((size, LANES), f32)],
            scratch_shapes=[pltpu.VMEM((size, width), bf16)] + [pltpu.VMEM((rows, width), bf16)] * 4
            + [pltpu.SemaphoreType.DMA((5,))],
            compiler_params=PARAMS,
            cost_estimate=taking(4.0),
            name="local",
        )(facts, in_hbm(queries), in_hbm(keys), in_hbm(values), key_beside, value_beside, *before))

    def served(asked, distance):
        return pl.pallas_call(
            functools.partial(served_kernel, distance, spans),
            in_specs=[SMEM] + [VMEM] * (4 + len(asked)),
            out_specs=VMEM,
            out_shape=jax.ShapeDtypeStruct((sum(part.shape[0] for part in asked), width + LANES), bf16),
            scratch_shapes=[pltpu.VMEM((sum(part.shape[0] for part in asked), width), bf16)],
            compiler_params=PARAMS,
            cost_estimate=taking(3.3),
            name="served",
        )(facts, keys, values, key_beside, value_beside, *asked)

    early = local(0, facts, "others")
    query_late[0] = after(query_late[0], early)
    asked_early = after(asked_early, early)
    out_early = [served([q], d) for q, d in zip(asked_early, distances)]
    early = local(0, after(facts, out_early), "askers", early)
    query_late[1] = after(query_late[1], early)
    asked_late = [[shifted(query, "span", -distance) for query in query_late] for distance in distances]
    early += [shifted(o, "span", d) for o, d in zip(out_early, distances)]

    chunks = 2
    columns = model // chunks
    tiles = 4
    tile = columns // tiles
    last = ranks - 1
    weight = in_hbm(out_weight)

    tile_shape = (tiles, width, tile)
    streaming = dict(
        scratch_shapes=[pltpu.VMEM(tile_shape, bf16), pltpu.SemaphoreType.DMA((tiles,))],
        compiler_params=PARAMS,
        cost_estimate=taking(3.0),
    )
    fetched = pl.pallas_call(
        fetch_kernel,
        in_specs=[HBM],
        out_specs=VMEM,
        out_shape=jax.ShapeDtypeStruct((tiles // 2, width, tile), bf16),
        scratch_shapes=[pltpu.SemaphoreType.DMA((tiles // 2,))],
        compiler_params=PARAMS,
        cost_estimate=taking(1.5),
        name="fetch",
    )(in_hbm(after(out_weight, early[:2])))

    def opening(chunk, facts):
        fetches = [] if chunk else [fetched]
        streams = tiles if chunk else tiles - tiles // 2
        return pl.pallas_call(
            functools.partial(opening_kernel, ranks, distances, spans, chunk * columns),
            in_specs=[SMEM] + [VMEM] * (2 + len(distances)) + [HBM] + [VMEM] * len(fetches),
            out_specs=VMEM,
            out_shape=jax.ShapeDtypeStruct((block, columns), bf16),
            scratch_shapes=[
                pltpu.VMEM((streams, width, tile), bf16),
                pltpu.SemaphoreType.DMA((streams,)),
                pltpu.VMEM((block, width), bf16),
            ],
            compiler_params=PARAMS,
            cost_estimate=taking(3.4),
            name="opening",
        )(facts, *early, weight, *fetches)

    ends = [(0, 1), (last, last - 1)]
    sent = opening(0, facts)
    arrived = [[lax.ppermute(sent, "tensor", ends)]]
    out_late = [served(q, d) for q, d in zip(after(asked_late, sent), distances)]
    for chunk in range(1, chunks):
        sent = opening(chunk, after(facts, out_late))
        arrived.append([lax.ppermute(sent, "tensor", ends)])
    late = local(1, after(facts, sent))
    late += [shifted(o, "span", d) for o, d in zip(out_late, distances)]

    attended_shape = jax.ShapeDtypeStruct((rows, width), bf16)
    block_shapes = [jax.ShapeDtypeStruct((block, columns), bf16)] * 2
    attended, *merged = pl.pallas_call(
        functools.partial(merged_blocks_kernel, spans, ranks, distances),
        in_specs=[SMEM] + [VMEM] * (4 + 2 * len(distances)) + [HBM],
        out_specs=[VMEM] * 3,
        out_shape=[attended_shape] + block_shapes,
        name="merged_blocks",
        **streaming,
    )(facts, *early, *late, weight)

    def blocks_of(step, chunk, attended):
        return pl.pallas_call(
            functools.partial(blocks_kernel, spans, ranks, chunk * columns, step),
            in_specs=[SMEM, VMEM, HBM],
            out_specs=[VMEM] * 2,
            out_shape=block_shapes,
            name="blocks",
            **streaming,
        )(facts, attended, weight)

    before = attended
    for step in range(1, last):
        for chunk in range(chunks):
            if step == 1 and chunk == 0:
                blocks = merged
            else:
                blocks = blocks_of(step, chunk, after(attended, before))
            comes, blocks = lax.optimization_barrier((arrived[chunk], blocks))
            up, down = [
                (mine.astype(f32) + come.astype(f32)).astype(bf16)
                for mine, come in zip(blocks, (comes[0], comes[-1]))
            ]
            before = (up, down)
            arrived[chunk] = [
                lax.ppermute(up, "tensor", [(i, i + 1) for i in range(step + 1)]),
                lax.ppermute(down, "tensor", [(last - i, last - i - 1) for i in range(step + 1)]),
            ]
    everything = chunks * tiles
    projected, gate = pl.pallas_call(
        functools.partial(own_kernel, spans),
        in_specs=[SMEM, VMEM, HBM, HBM],
        out_specs=[VMEM, VMEM],
        out_shape=[jax.ShapeDtypeStruct((block, model), bf16), jax.ShapeDtypeStruct((1, model), f32)],
        scratch_shapes=[
            pltpu.VMEM((everything, width, tile), bf16),
            pltpu.VMEM((8, model), f32),
            pltpu.SemaphoreType.DMA((everything + 1,)),
        ],
        compiler_params=PARAMS,
        cost_estimate=taking(5.0),
        name="own",
    )(facts, after(attended, before), weight, in_hbm(gate_table))

    finished = []
    for chunk in range(chunks - 1):
        there = slice(chunk * columns, (chunk + 1) * columns)
        summed = sum(part.astype(f32) for part in (projected[:, there], *arrived[chunk]))
        finished.append((summed * gate[:, there]).astype(bf16))
    pieces = 2
    return pl.pallas_call(
        final_kernel,
        in_specs=[ANY, ANY, VMEM, VMEM, VMEM],
        out_specs=HBM,
        out_shape=jax.ShapeDtypeStruct((block, model), bf16),
        scratch_shapes=[
            pltpu.VMEM((block, columns), bf16),
            pltpu.VMEM((pieces, block, columns // pieces), bf16),
            pltpu.SemaphoreType.DMA((2 + pieces,)),
        ],
        compiler_params=PARAMS,
        cost_estimate=taking(2.7),
        name="final",
    )(jnp.concatenate(finished, axis=1), projected, gate, *arrived[-1])


def solution(mesh):
    return jax.shard_map(
        body,
        mesh=mesh,
        in_specs=(
            P(("group", "span"), "tensor"),
            P(("group", "span"), "tensor"),
            P(("group", "span"), "tensor"),
            P("tensor", None),
            P(),
            P("group"),
            P("group", None),
        ),
        out_specs=P(("group", "span", "tensor"), None),
        check_vma=False,
    )
```

```python
import functools

import jax
import jax.numpy as jnp
from jax import lax
from jax.experimental import pallas as pl
from jax.experimental.pallas import tpu as pltpu
from jax.sharding import PartitionSpec as P

HD = 128
LANES = 128
HIDDEN = -1e30
LOG2E = 1.4426950408889634
PARAMS = pltpu.CompilerParams(vmem_limit_bytes=24 * 1024 * 1024)
SMEM = pl.BlockSpec(memory_space=pltpu.SMEM)
VMEM = pl.BlockSpec(memory_space=pltpu.VMEM)
ANY = pl.BlockSpec(memory_space=pl.ANY)
HBM = pl.BlockSpec(memory_space=pltpu.HBM)
PIECE_LANES = 32


def taking(microseconds):
    return pl.CostEstimate(flops=0, bytes_accessed=int(microseconds * 3.69e6), transcendentals=0)


def in_hbm(array):
    return pltpu.with_memory_space_constraint(array, pltpu.HBM)


def shifted(block, axis, distance):
    count = lax.axis_size(axis)
    return lax.ppermute(block, axis, [(i, i + distance) for i in range(count) if 0 <= i + distance < count])


def head_columns(head):
    return slice(head * HD, (head + 1) * HD)


def attend(query, keys, values, flags, write):
    rows, width = query.shape
    scale = LOG2E * HD ** (-0.5)
    lane = lax.broadcasted_iota(jnp.int32, (rows, LANES), 1)
    packed = jnp.zeros((rows, LANES), jnp.float32)

    def scored(head):
        columns = head_columns(head)
        return [
            lax.dot_general(
                query[:, columns], key[:, columns], (((1,), (1,)), ((), ())), preferred_element_type=jnp.float32
            )
            for key in keys
        ]

    heads = width // HD
    later = scored(0)
    for head in range(heads):
        columns = head_columns(head)
        scores, later = later, scored(head + 1) if head + 1 < heads else None
        tops = [jnp.max(block, axis=-1, keepdims=True) * scale for block in scores]
        top = functools.reduce(
            jnp.maximum, [one if flag is None else jnp.where(flag, one, HIDDEN) for one, flag in zip(tops, flags)]
        )
        joined = None
        for block, value, flag in zip(scores, values, flags):
            above = top if flag is None else jnp.where(flag, top, -HIDDEN)
            probs = jnp.exp2(block * scale - above).astype(jnp.bfloat16)
            beside = jnp.concatenate([value[:, columns], jnp.ones((value.shape[0], HD), jnp.bfloat16)], axis=1)
            part = jnp.dot(probs, beside, preferred_element_type=jnp.float32)
            joined = part if joined is None else joined + part
        product, total = joined[:, :HD], jnp.where(joined[:, HD:] > 0.0, joined[:, HD:], 1.0)
        write(columns, product / total)
        packed = jnp.where(lane == head, top + jnp.log2(total), packed)
    return packed


class Facts:
    def __init__(self, place, visible):
        self.span, self.rank, self.visible = place[0], place[1], visible
        self.beside = self.span + 1 - 2 * lax.rem(self.span, 2)

    def sees(self, asker, span):
        return self.visible[asker, span] > 0


def copied(source, target, semaphore):
    copy = pltpu.make_async_copy(source, target, semaphore)
    copy.start()
    return copy


def parts_of(rank, ranks, rows):
    block = rows // ranks
    lower = rank < ranks // 2
    early = pl.multiple_of(jnp.where(lower, rows - block, 0), block)
    late = pl.multiple_of(jnp.where(lower, 0, block), block)
    return (early, block), (late, rows - block)


def split_kernel(ranks, place, query, visible, *refs):
    *targets, seen, semaphores = refs
    scalars = copied(visible, seen, semaphores.at[len(targets)])

    @pl.when(place[0] > 1)
    def _():
        (early, _), (late, _) = parts_of(place[1], ranks, query.shape[0])
        starts = (early, late, pl.multiple_of(late + targets[1].shape[0], 16))
        copies = [
            copied(query.at[pl.ds(start, target.shape[0])], target, semaphores.at[index])
            for index, (start, target) in enumerate(zip(starts, targets))
        ]
        for copy in copies:
            copy.wait()

    scalars.wait()


def local_kernel(ranks, part, place, visible, query, key, value, key_beside, value_beside, result, sums, *scratch):
    here = Facts(place, visible)
    query_, key_, value_, key_beside_, value_beside_, semaphores = scratch
    start, size = parts_of(here.rank, ranks, query.shape[0])[part]
    copies = [
        copied(source, target, semaphores.at[index])
        for index, (source, target) in enumerate((
            (query.at[pl.ds(start, size)], query_),
            (key, key_), (key_beside, key_beside_), (value, value_), (value_beside, value_beside_),
        ))
    ]
    for copy in copies:
        copy.wait()

    def write(columns, block):
        result[:, columns] = block

    flags = [None, here.sees(here.span, here.beside)]
    sums[...] = attend(query_, [key_, key_beside_], [value_, value_beside_], flags, write)


def served_kernel(distance, spans, place, visible, key, value, key_beside, value_beside, *refs):
    here = Facts(place, visible)

    @pl.when(here.span + distance < spans)
    def _():
        asker = jnp.minimum(here.span + distance, spans - 1)
        flags = [here.sees(asker, here.span), here.sees(asker, here.beside)]
        *queries, result, query = refs
        at = 0
        for part in queries:
            query[at:at + part.shape[0], :] = part[...]
            at += part.shape[0]

        def write(columns, block):
            result[:, columns] = block.astype(jnp.bfloat16)

        rest = attend(query, [key, key_beside], [value, value_beside], flags, write)
        sent = jnp.zeros_like(rest)
        for piece in range(3):
            part = rest.astype(jnp.bfloat16).astype(jnp.float32)
            sent = sent + (part if piece == 0 else pltpu.roll(part, piece * PIECE_LANES, 1))
            rest = rest - part
        result[:, query.shape[1]:] = sent.astype(jnp.bfloat16)


def merge(span, distances, own, own_sum, served, write):
    width = own.shape[1]
    sums = [own_sum[...]]
    for distance, ref in zip(distances, served):
        sent = ref[:, width:].astype(jnp.float32)
        joined = sent
        for piece in (1, 2):
            joined = joined + pltpu.roll(sent, LANES - piece * PIECE_LANES, 1)
        sums.append(jnp.where(span >= distance, joined, HIDDEN))
    top = functools.reduce(jnp.maximum, sums)
    shares = [jnp.exp2(one - top) for one in sums]
    over = 1.0 / sum(shares)
    shares = [share * over for share in shares]
    for head in range(width // HD):
        columns = head_columns(head)
        merged = own[:, columns] * shares[0][:, head:head + 1]
        for distance, share, ref in zip(distances, shares[1:], served):
            away = jnp.where(span >= distance, ref[:, columns].astype(jnp.float32), 0.0)
            merged = merged + away * share[:, head:head + 1]
        write(columns, merged.astype(jnp.bfloat16))


def streamed(weight, first, tiles, semaphores):
    count, _, tile = tiles.shape
    return [
        copied(weight.at[:, pl.ds(first + index * tile, tile)], tiles.at[index], semaphores.at[index])
        for index in range(count)
    ]


def fetch_kernel(weight, tiles, semaphores):
    for copy in streamed(weight, 0, tiles, semaphores):
        copy.wait()


def opening_kernel(ranks, distances, first, place, *refs):
    own, own_sum, *served = refs[:2 + len(distances)]
    weight, result, *scratch = refs[2 + len(distances):]
    rows = scratch[-1]

    @pl.when(jnp.logical_or(place[1] == 0, place[1] == ranks - 1))
    def _():
        tiles, copies = weight, [None] * weight.shape[0]
        if first:
            tiles, semaphores, _ = scratch
            copies = streamed(weight, first, tiles, semaphores)

        def write(columns, part):
            rows[:, columns] = part

        merge(place[0], distances, own, own_sum, served, write)
        tile = tiles.shape[2]
        for index, copy in enumerate(copies):
            if copy is not None:
                copy.wait()
            product = jnp.dot(rows[...], tiles[index], preferred_element_type=jnp.float32)
            result[:, index * tile:(index + 1) * tile] = product.astype(jnp.bfloat16)


def project_blocks(ranks, first, rank, step, attended, weight, up, down, tiles, semaphores):
    last = ranks - 1
    tile = tiles.shape[2]
    block = up.shape[0]
    copies = streamed(weight, first, tiles, semaphores)
    yield
    sends = rank <= step, rank >= last - step
    starts = [
        pl.multiple_of(jnp.clip(target, 0, last) * block, block) for target in (last - step + rank, step + rank - last)
    ]
    rows = [attended[pl.ds(start, block), :] for start in starts]
    for index, copy in enumerate(copies):
        copy.wait()
        there = slice(index * tile, (index + 1) * tile)

        @pl.when(jnp.logical_and(*sends))
        def _():
            both = jnp.dot(jnp.concatenate(rows, axis=0), tiles[index], preferred_element_type=jnp.float32)
            up[:, there] = both[:block].astype(jnp.bfloat16)
            down[:, there] = both[block:].astype(jnp.bfloat16)

        @pl.when(jnp.logical_not(jnp.logical_and(*sends)))
        def _():
            one = jnp.dot(
                jnp.where(sends[0], rows[0], rows[1]), tiles[index], preferred_element_type=jnp.float32
            ).astype(jnp.bfloat16)
            up[:, there] = one
            down[:, there] = one


def merged_blocks_kernel(ranks, distances, place, *refs):
    each = 2 + len(distances)
    parts, (weight, attended, *results) = (refs[:each], refs[each:2 * each]), refs[2 * each:]
    work = project_blocks(ranks, 0, place[1], 1, attended, weight, *results)
    next(work)
    for (start, size), (own, own_sum, *served) in zip(parts_of(place[1], ranks, attended.shape[0]), parts):
        there = pl.ds(start, size)

        def write(columns, part):
            attended[there, columns] = part

        merge(place[0], distances, own, own_sum, served, write)
    for _ in work:
        pass


def blocks_kernel(ranks, first, step, place, attended, weight, *results):
    for _ in project_blocks(ranks, first, place[1], step, attended, weight, *results):
        pass


def own_kernel(place, levels, attended, weight, gate_table, result, gate, tiles, gates, semaphores):
    block = result.shape[0]
    count, _, tile = tiles.shape
    level = levels[place[0]]
    above = pl.multiple_of(level // 8 * 8, 8)
    gate_copy = copied(gate_table.at[pl.ds(above, 8)], gates, semaphores.at[count])
    copies = streamed(weight, 0, tiles, semaphores)
    start = pl.multiple_of(place[1] * block, block)
    for index, copy in enumerate(copies):
        copy.wait()
        product = jnp.dot(attended[pl.ds(start, block), :], tiles[index], preferred_element_type=jnp.float32)
        result[:, index * tile:(index + 1) * tile] = product.astype(jnp.bfloat16)
    gate_copy.wait()
    gate[...] = gates[pl.ds(lax.rem(level, 8), 1), :]


def final_kernel(done, projected, gate, up, down, result, own, gated, semaphores):
    first, (block, columns) = done.shape[1], own.shape
    pieces = gated.shape[0]
    wide = columns // pieces
    own_copy = copied(projected.at[:, pl.ds(first, columns)], own, semaphores.at[0])
    sent = [copied(done, result.at[:, pl.ds(0, first)], semaphores.at[1])]
    own_copy.wait()
    for piece in range(pieces):
        there = slice(piece * wide, (piece + 1) * wide)
        summed = own[:, there].astype(jnp.float32) + up[:, there].astype(jnp.float32)
        summed = summed + down[:, there].astype(jnp.float32)
        gated[piece] = (summed * gate[:, first + piece * wide:first + (piece + 1) * wide]).astype(jnp.bfloat16)
        sent.append(copied(
            gated.at[piece], result.at[:, pl.ds(first + piece * wide, wide)], semaphores.at[2 + piece]
        ))
    for copy in sent:
        copy.wait()


def body(queries, keys, values, out_weight, gate_table, levels, visible):
    rows, width = queries.shape
    model = out_weight.shape[1]
    spans = lax.axis_size("span")
    ranks = lax.axis_size("tensor")
    span = lax.axis_index("span")
    rank = lax.axis_index("tensor")
    block = rows // ranks
    bf16, f32 = jnp.bfloat16, jnp.float32
    place = jnp.stack([span, rank]).astype(jnp.int32)
    third = (rows - block) // 48 * 16
    query_early, *query_late, seen = pl.pallas_call(
        functools.partial(split_kernel, ranks),
        in_specs=[SMEM, HBM, HBM],
        out_specs=[VMEM] * 3 + [SMEM],
        out_shape=[jax.ShapeDtypeStruct((part, width), bf16) for part in (block, rows - block - third, third)]
        + [jax.ShapeDtypeStruct(visible.shape, visible.dtype)],
        scratch_shapes=[pltpu.SemaphoreType.DMA((4,))],
        compiler_params=PARAMS,
        cost_estimate=taking(1.7),
        name="split",
    )(place, in_hbm(queries), in_hbm(visible))
    distances = list(range(2, spans, 2))
    asked_early = [shifted(query_early, "span", -distance) for distance in distances]
    swap = [(i, i + 1 - 2 * (i % 2)) for i in range(spans)]
    key_beside = lax.ppermute(keys, "span", swap)
    value_beside = lax.ppermute(values, "span", swap)

    def after(value, *others):
        return lax.optimization_barrier((value, others))[0]

    def local(part, place):
        size = (block, rows - block)[part]
        return pl.pallas_call(
            functools.partial(local_kernel, ranks, part),
            in_specs=[SMEM, SMEM, HBM, HBM, HBM, ANY, ANY],
            out_specs=[VMEM] * 2,
            out_shape=[jax.ShapeDtypeStruct((size, width), f32), jax.ShapeDtypeStruct((size, LANES), f32)],
            scratch_shapes=[pltpu.VMEM((size, width), bf16)] + [pltpu.VMEM((rows, width), bf16)] * 4
            + [pltpu.SemaphoreType.DMA((5,))],
            compiler_params=PARAMS,
            cost_estimate=taking(4.0),
            name="local",
        )(place, seen, in_hbm(queries), in_hbm(keys), in_hbm(values), key_beside, value_beside)

    def served(asked, distance):
        return pl.pallas_call(
            functools.partial(served_kernel, distance, spans),
            in_specs=[SMEM, SMEM] + [VMEM] * (4 + len(asked)),
            out_specs=VMEM,
            out_shape=jax.ShapeDtypeStruct((sum(part.shape[0] for part in asked), width + LANES), bf16),
            scratch_shapes=[pltpu.VMEM((sum(part.shape[0] for part in asked), width), bf16)],
            compiler_params=PARAMS,
            cost_estimate=taking(3.3),
            name="served",
        )(place, seen, keys, values, key_beside, value_beside, *asked)

    early = list(local(0, place))
    query_late = after(query_late, early)
    asked_early = after(asked_early, early)
    asked_late = [[shifted(query, "span", -distance) for query in query_late] for distance in distances]
    out_early = [served([q], d) for q, d in zip(asked_early, distances)]
    early += [shifted(o, "span", d) for o, d in zip(out_early, distances)]

    chunks = 2
    columns = model // chunks
    tiles = 4
    tile = columns // tiles
    last = ranks - 1
    weight = in_hbm(out_weight)

    tile_shape = (tiles, width, tile)
    streaming = dict(
        scratch_shapes=[pltpu.VMEM(tile_shape, bf16), pltpu.SemaphoreType.DMA((tiles,))],
        compiler_params=PARAMS,
        cost_estimate=taking(3.0),
    )
    fetched = pl.pallas_call(
        fetch_kernel,
        in_specs=[HBM],
        out_specs=VMEM,
        out_shape=jax.ShapeDtypeStruct(tile_shape, bf16),
        scratch_shapes=[pltpu.SemaphoreType.DMA((tiles,))],
        compiler_params=PARAMS,
        cost_estimate=taking(2.4),
        name="fetch",
    )(in_hbm(after(out_weight, out_early)))

    def opening(chunk, place):
        scratch = streaming["scratch_shapes"] if chunk else []
        return pl.pallas_call(
            functools.partial(opening_kernel, ranks, distances, chunk * columns),
            in_specs=[SMEM] + [VMEM] * (2 + len(distances)) + [HBM if chunk else VMEM],
            out_specs=VMEM,
            out_shape=jax.ShapeDtypeStruct((block, columns), bf16),
            scratch_shapes=scratch + [pltpu.VMEM((block, width), bf16)],
            compiler_params=PARAMS,
            cost_estimate=taking(3.4),
            name="opening",
        )(place, *early, weight if chunk else fetched)

    ends = [(0, 1), (last, last - 1)]
    sent = opening(0, place)
    arrived = [[lax.ppermute(sent, "tensor", ends)]]
    out_late = [served(q, d) for q, d in zip(after(asked_late, sent), distances)]
    for chunk in range(1, chunks):
        sent = opening(chunk, after(place, out_late))
        arrived.append([lax.ppermute(sent, "tensor", ends)])
    late = list(local(1, after(place, sent)))
    late += [shifted(o, "span", d) for o, d in zip(out_late, distances)]

    attended_shape = jax.ShapeDtypeStruct((rows, width), bf16)
    block_shapes = [jax.ShapeDtypeStruct((block, columns), bf16)] * 2
    attended, *merged = pl.pallas_call(
        functools.partial(merged_blocks_kernel, ranks, distances),
        in_specs=[SMEM] + [VMEM] * (4 + 2 * len(distances)) + [HBM],
        out_specs=[VMEM] * 3,
        out_shape=[attended_shape] + block_shapes,
        name="merged_blocks",
        **streaming,
    )(place, *early, *late, weight)

    def blocks_of(step, chunk, attended):
        return pl.pallas_call(
            functools.partial(blocks_kernel, ranks, chunk * columns, step),
            in_specs=[SMEM, VMEM, HBM],
            out_specs=[VMEM] * 2,
            out_shape=block_shapes,
            name="blocks",
            **streaming,
        )(place, attended, weight)

    before = attended
    for step in range(1, last):
        for chunk in range(chunks):
            if step == 1 and chunk == 0:
                blocks = merged
            else:
                blocks = blocks_of(step, chunk, after(attended, before))
            comes, blocks = lax.optimization_barrier((arrived[chunk], blocks))
            up, down = [
                (mine.astype(f32) + come.astype(f32)).astype(bf16)
                for mine, come in zip(blocks, (comes[0], comes[-1]))
            ]
            before = (up, down)
            arrived[chunk] = [
                lax.ppermute(up, "tensor", [(i, i + 1) for i in range(step + 1)]),
                lax.ppermute(down, "tensor", [(last - i, last - i - 1) for i in range(step + 1)]),
            ]
    everything = chunks * tiles
    projected, gate = pl.pallas_call(
        own_kernel,
        in_specs=[SMEM, SMEM, VMEM, HBM, HBM],
        out_specs=[VMEM, VMEM],
        out_shape=[jax.ShapeDtypeStruct((block, model), bf16), jax.ShapeDtypeStruct((1, model), f32)],
        scratch_shapes=[
            pltpu.VMEM((everything, width, tile), bf16),
            pltpu.VMEM((8, model), f32),
            pltpu.SemaphoreType.DMA((everything + 1,)),
        ],
        compiler_params=PARAMS,
        cost_estimate=taking(5.0),
        name="own",
    )(place, levels, after(attended, before), weight, in_hbm(gate_table))

    finished = []
    for chunk in range(chunks - 1):
        there = slice(chunk * columns, (chunk + 1) * columns)
        summed = sum(part.astype(f32) for part in (projected[:, there], *arrived[chunk]))
        finished.append((summed * gate[:, there]).astype(bf16))
    pieces = 2
    return pl.pallas_call(
        final_kernel,
        in_specs=[ANY, ANY, VMEM, VMEM, VMEM],
        out_specs=HBM,
        out_shape=jax.ShapeDtypeStruct((block, model), bf16),
        scratch_shapes=[
            pltpu.VMEM((block, columns), bf16),
            pltpu.VMEM((pieces, block, columns // pieces), bf16),
            pltpu.SemaphoreType.DMA((2 + pieces,)),
        ],
        compiler_params=PARAMS,
        cost_estimate=taking(2.7),
        name="final",
    )(jnp.concatenate(finished, axis=1), projected, gate, *arrived[-1])


def solution(mesh):
    return jax.shard_map(
        body,
        mesh=mesh,
        in_specs=(
            P(("group", "span"), "tensor"),
            P(("group", "span"), "tensor"),
            P(("group", "span"), "tensor"),
            P("tensor", None),
            P(),
            P("group"),
            P("group", None),
        ),
        out_specs=P(("group", "span", "tensor"), None),
        check_vma=False,
    )
```

```python
import functools

import jax
import jax.numpy as jnp
from jax import lax
from jax.experimental import pallas as pl
from jax.experimental.pallas import tpu as pltpu
from jax.sharding import PartitionSpec as P

HD = 128
LANES = 128
HIDDEN = -1e30
LOG2E = 1.4426950408889634
PARAMS = pltpu.CompilerParams(vmem_limit_bytes=24 * 1024 * 1024)
SMEM = pl.BlockSpec(memory_space=pltpu.SMEM)
VMEM = pl.BlockSpec(memory_space=pltpu.VMEM)
ANY = pl.BlockSpec(memory_space=pl.ANY)
HBM = pl.BlockSpec(memory_space=pltpu.HBM)
PIECE_LANES = 32


def taking(microseconds):
    return pl.CostEstimate(flops=0, bytes_accessed=int(microseconds * 3.69e6), transcendentals=0)


def in_hbm(array):
    return pltpu.with_memory_space_constraint(array, pltpu.HBM)


def shifted(block, axis, distance):
    count = lax.axis_size(axis)
    return lax.ppermute(block, axis, [(i, i + distance) for i in range(count) if 0 <= i + distance < count])


def head_columns(head):
    return slice(head * HD, (head + 1) * HD)


def attend(query, keys, values, flags, write, arrive=None):
    rows, width = query.shape
    scale = LOG2E * HD ** (-0.5)
    lane = lax.broadcasted_iota(jnp.int32, (rows, LANES), 1)
    packed = jnp.zeros((rows, LANES), jnp.float32)

    def scored(head):
        columns = head_columns(head)
        return [
            lax.dot_general(
                query[:, columns], key[:, columns], (((1,), (1,)), ((), ())), preferred_element_type=jnp.float32
            )
            for key in keys
        ]

    heads = width // HD
    later = scored(0)
    if arrive is not None:
        arrive()
    for head in range(heads):
        columns = head_columns(head)
        scores, later = later, scored(head + 1) if head + 1 < heads else None
        tops = [jnp.max(block, axis=-1, keepdims=True) * scale for block in scores]
        top = functools.reduce(
            jnp.maximum, [one if flag is None else jnp.where(flag, one, HIDDEN) for one, flag in zip(tops, flags)]
        )
        joined = None
        for block, value, flag in zip(scores, values, flags):
            above = top if flag is None else jnp.where(flag, top, -HIDDEN)
            probs = jnp.exp2(block * scale - above).astype(jnp.bfloat16)
            beside = jnp.concatenate([value[:, columns], jnp.ones((value.shape[0], HD), jnp.bfloat16)], axis=1)
            part = jnp.dot(probs, beside, preferred_element_type=jnp.float32)
            joined = part if joined is None else joined + part
        product, total = joined[:, :HD], jnp.where(joined[:, HD:] > 0.0, joined[:, HD:], 1.0)
        write(columns, product / total)
        packed = jnp.where(lane == head, top + jnp.log2(total), packed)
    return packed


def seen_by(visible, asker, span):
    table = visible[...]
    row, column = (lax.broadcasted_iota(jnp.int32, table.shape, axis) for axis in (0, 1))
    here = jnp.logical_and(row == asker, column == span)
    return jnp.max(jnp.where(here, table, 0).astype(jnp.float32), axis=(0, 1), keepdims=True) > 0.0


def beside_of(span):
    return span + 1 - 2 * lax.rem(span, 2)


def copied(source, target, semaphore):
    copy = pltpu.make_async_copy(source, target, semaphore)
    copy.start()
    return copy


def parts_of(rank, ranks, rows):
    block = rows // ranks
    lower = rank < ranks // 2
    early = pl.multiple_of(jnp.where(lower, rows - block, 0), block)
    late = pl.multiple_of(jnp.where(lower, 0, block), block)
    return (early, block), (late, rows - block)


def split_kernel(ranks, place, query, *refs):
    *targets, semaphores = refs

    @pl.when(place[0] > 1)
    def _():
        (early, _), (late, _) = parts_of(place[1], ranks, query.shape[0])
        starts = (early, late, pl.multiple_of(late + targets[1].shape[0], 16))
        copies = [
            copied(query.at[pl.ds(start, target.shape[0])], target, semaphores.at[index])
            for index, (start, target) in enumerate(zip(starts, targets))
        ]
        for copy in copies:
            copy.wait()


def local_kernel(ranks, part, place, visible, query, key, value, key_beside, value_beside,
                 result, sums, seen, *scratch):
    query_, key_, value_, key_beside_, value_beside_, semaphores = scratch
    start, size = parts_of(place[1], ranks, query.shape[0])[part]
    copies = [
        copied(source, target, semaphores.at[index])
        for index, (source, target) in enumerate((
            (visible, seen), (query.at[pl.ds(start, size)], query_),
            (key, key_), (key_beside, key_beside_), (value, value_), (value_beside, value_beside_),
        ))
    ]
    for copy in copies[:4]:
        copy.wait()

    def arrive():
        for copy in copies[4:]:
            copy.wait()

    def write(columns, block):
        result[:, columns] = block

    flags = [None, seen_by(seen, place[0], beside_of(place[0]))]
    sums[...] = attend(query_, [key_, key_beside_], [value_, value_beside_], flags, write, arrive)


def served_kernel(distance, spans, place, visible, key, value, key_beside, value_beside, *refs):
    span = place[0]

    @pl.when(span + distance < spans)
    def _():
        asker = jnp.minimum(span + distance, spans - 1)
        flags = [seen_by(visible, asker, span), seen_by(visible, asker, beside_of(span))]
        *queries, result, query = refs
        at = 0
        for part in queries:
            query[at:at + part.shape[0], :] = part[...]
            at += part.shape[0]

        def write(columns, block):
            result[:, columns] = block.astype(jnp.bfloat16)

        rest = attend(query, [key, key_beside], [value, value_beside], flags, write)
        sent = jnp.zeros_like(rest)
        for piece in range(3):
            part = rest.astype(jnp.bfloat16).astype(jnp.float32)
            sent = sent + (part if piece == 0 else pltpu.roll(part, piece * PIECE_LANES, 1))
            rest = rest - part
        result[:, query.shape[1]:] = sent.astype(jnp.bfloat16)


def merge(span, distances, own, own_sum, served, write):
    width = own.shape[1]
    sums = [own_sum[...]]
    for distance, ref in zip(distances, served):
        sent = ref[:, width:].astype(jnp.float32)
        joined = sent
        for piece in (1, 2):
            joined = joined + pltpu.roll(sent, LANES - piece * PIECE_LANES, 1)
        sums.append(jnp.where(span >= distance, joined, HIDDEN))
    top = functools.reduce(jnp.maximum, sums)
    shares = [jnp.exp2(one - top) for one in sums]
    over = 1.0 / sum(shares)
    shares = [share * over for share in shares]
    for head in range(width // HD):
        columns = head_columns(head)
        merged = own[:, columns] * shares[0][:, head:head + 1]
        for distance, share, ref in zip(distances, shares[1:], served):
            away = jnp.where(span >= distance, ref[:, columns].astype(jnp.float32), 0.0)
            merged = merged + away * share[:, head:head + 1]
        write(columns, merged.astype(jnp.bfloat16))


def streamed(weight, first, tiles, semaphores):
    count, _, tile = tiles.shape
    return [
        copied(weight.at[:, pl.ds(first + index * tile, tile)], tiles.at[index], semaphores.at[index])
        for index in range(count)
    ]


def fetch_kernel(weight, tiles, semaphores):
    for copy in streamed(weight, 0, tiles, semaphores):
        copy.wait()


def opening_kernel(ranks, distances, first, place, *refs):
    own, own_sum, *served = refs[:2 + len(distances)]
    weight, result, *scratch = refs[2 + len(distances):]
    rows = scratch[-1]

    @pl.when(jnp.logical_or(place[1] == 0, place[1] == ranks - 1))
    def _():
        tiles, copies = weight, [None] * weight.shape[0]
        if first:
            tiles, semaphores, _ = scratch
            copies = streamed(weight, first, tiles, semaphores)

        def write(columns, part):
            rows[:, columns] = part

        merge(place[0], distances, own, own_sum, served, write)
        tile = tiles.shape[2]
        for index, copy in enumerate(copies):
            if copy is not None:
                copy.wait()
            product = jnp.dot(rows[...], tiles[index], preferred_element_type=jnp.float32)
            result[:, index * tile:(index + 1) * tile] = product.astype(jnp.bfloat16)


def project_blocks(ranks, first, rank, step, attended, weight, up, down, tiles, semaphores):
    last = ranks - 1
    tile = tiles.shape[2]
    block = up.shape[0]
    copies = streamed(weight, first, tiles, semaphores)
    yield
    sends = rank <= step, rank >= last - step
    starts = [
        pl.multiple_of(jnp.clip(target, 0, last) * block, block) for target in (last - step + rank, step + rank - last)
    ]
    rows = [attended[pl.ds(start, block), :] for start in starts]
    for index, copy in enumerate(copies):
        copy.wait()
        there = slice(index * tile, (index + 1) * tile)

        @pl.when(jnp.logical_and(*sends))
        def _():
            both = jnp.dot(jnp.concatenate(rows, axis=0), tiles[index], preferred_element_type=jnp.float32)
            up[:, there] = both[:block].astype(jnp.bfloat16)
            down[:, there] = both[block:].astype(jnp.bfloat16)

        @pl.when(jnp.logical_not(jnp.logical_and(*sends)))
        def _():
            one = jnp.dot(
                jnp.where(sends[0], rows[0], rows[1]), tiles[index], preferred_element_type=jnp.float32
            ).astype(jnp.bfloat16)
            up[:, there] = one
            down[:, there] = one


def merged_blocks_kernel(ranks, distances, place, *refs):
    each = 2 + len(distances)
    parts, (weight, attended, *results) = (refs[:each], refs[each:2 * each]), refs[2 * each:]
    work = project_blocks(ranks, 0, place[1], 1, attended, weight, *results)
    next(work)
    for (start, size), (own, own_sum, *served) in zip(parts_of(place[1], ranks, attended.shape[0]), parts):
        there = pl.ds(start, size)

        def write(columns, part):
            attended[there, columns] = part

        merge(place[0], distances, own, own_sum, served, write)
    for _ in work:
        pass


def blocks_kernel(ranks, first, step, place, attended, weight, *results):
    for _ in project_blocks(ranks, first, place[1], step, attended, weight, *results):
        pass


def own_kernel(place, levels, attended, weight, gate_table, result, gate, tiles, gates, semaphores):
    block = result.shape[0]
    count, _, tile = tiles.shape
    level = levels[place[0]]
    above = pl.multiple_of(level // 8 * 8, 8)
    gate_copy = copied(gate_table.at[pl.ds(above, 8)], gates, semaphores.at[count])
    copies = streamed(weight, 0, tiles, semaphores)
    start = pl.multiple_of(place[1] * block, block)
    for index, copy in enumerate(copies):
        copy.wait()
        product = jnp.dot(attended[pl.ds(start, block), :], tiles[index], preferred_element_type=jnp.float32)
        result[:, index * tile:(index + 1) * tile] = product.astype(jnp.bfloat16)
    gate_copy.wait()
    gate[...] = gates[pl.ds(lax.rem(level, 8), 1), :]


def final_kernel(done, projected, gate, up, down, result, own, gated, semaphores):
    first, (block, columns) = done.shape[1], own.shape
    pieces = gated.shape[0]
    wide = columns // pieces
    own_copy = copied(projected.at[:, pl.ds(first, columns)], own, semaphores.at[0])
    sent = [copied(done, result.at[:, pl.ds(0, first)], semaphores.at[1])]
    own_copy.wait()
    for piece in range(pieces):
        there = slice(piece * wide, (piece + 1) * wide)
        summed = own[:, there].astype(jnp.float32) + up[:, there].astype(jnp.float32)
        summed = summed + down[:, there].astype(jnp.float32)
        gated[piece] = (summed * gate[:, first + piece * wide:first + (piece + 1) * wide]).astype(jnp.bfloat16)
        sent.append(copied(
            gated.at[piece], result.at[:, pl.ds(first + piece * wide, wide)], semaphores.at[2 + piece]
        ))
    for copy in sent:
        copy.wait()


def body(queries, keys, values, out_weight, gate_table, levels, visible):
    rows, width = queries.shape
    model = out_weight.shape[1]
    spans = lax.axis_size("span")
    ranks = lax.axis_size("tensor")
    span = lax.axis_index("span")
    rank = lax.axis_index("tensor")
    block = rows // ranks
    bf16, f32 = jnp.bfloat16, jnp.float32
    place = jnp.stack([span, rank]).astype(jnp.int32)
    third = (rows - block) // 48 * 16
    query_early, *query_late = pl.pallas_call(
        functools.partial(split_kernel, ranks),
        in_specs=[SMEM, HBM],
        out_specs=[VMEM] * 3,
        out_shape=[jax.ShapeDtypeStruct((part, width), bf16) for part in (block, rows - block - third, third)],
        scratch_shapes=[pltpu.SemaphoreType.DMA((3,))],
        compiler_params=PARAMS,
        cost_estimate=taking(1.7),
        name="split",
    )(place, in_hbm(queries))
    distances = list(range(2, spans, 2))
    asked_early = [shifted(query_early, "span", -distance) for distance in distances]
    swap = [(i, i + 1 - 2 * (i % 2)) for i in range(spans)]
    key_beside = lax.ppermute(keys, "span", swap)
    value_beside = lax.ppermute(values, "span", swap)

    def after(value, *others):
        return lax.optimization_barrier((value, others))[0]

    def local(part, place):
        size = (block, rows - block)[part]
        return pl.pallas_call(
            functools.partial(local_kernel, ranks, part),
            in_specs=[SMEM, HBM, HBM, HBM, HBM, ANY, ANY],
            out_specs=[VMEM] * 3,
            out_shape=[
                jax.ShapeDtypeStruct((size, width), f32),
                jax.ShapeDtypeStruct((size, LANES), f32),
                jax.ShapeDtypeStruct(visible.shape, visible.dtype),
            ],
            scratch_shapes=[pltpu.VMEM((size, width), bf16)] + [pltpu.VMEM((rows, width), bf16)] * 4
            + [pltpu.SemaphoreType.DMA((6,))],
            compiler_params=PARAMS,
            cost_estimate=taking(4.0),
            name="local",
        )(place, in_hbm(visible), in_hbm(queries), in_hbm(keys), in_hbm(values), key_beside, value_beside)

    def served(asked, distance):
        return pl.pallas_call(
            functools.partial(served_kernel, distance, spans),
            in_specs=[SMEM] + [VMEM] * (5 + len(asked)),
            out_specs=VMEM,
            out_shape=jax.ShapeDtypeStruct((sum(part.shape[0] for part in asked), width + LANES), bf16),
            scratch_shapes=[pltpu.VMEM((sum(part.shape[0] for part in asked), width), bf16)],
            compiler_params=PARAMS,
            cost_estimate=taking(3.3),
            name="served",
        )(place, seen, keys, values, key_beside, value_beside, *asked)

    *early, seen = local(0, place)
    query_late = after(query_late, early)
    asked_early = after(asked_early, early)
    asked_late = [[shifted(query, "span", -distance) for query in query_late] for distance in distances]
    out_early = [served([q], d) for q, d in zip(asked_early, distances)]
    early += [shifted(o, "span", d) for o, d in zip(out_early, distances)]

    chunks = 2
    columns = model // chunks
    tiles = 4
    tile = columns // tiles
    last = ranks - 1
    weight = in_hbm(out_weight)

    tile_shape = (tiles, width, tile)
    streaming = dict(
        scratch_shapes=[pltpu.VMEM(tile_shape, bf16), pltpu.SemaphoreType.DMA((tiles,))],
        compiler_params=PARAMS,
        cost_estimate=taking(3.0),
    )
    fetched = pl.pallas_call(
        fetch_kernel,
        in_specs=[HBM],
        out_specs=VMEM,
        out_shape=jax.ShapeDtypeStruct(tile_shape, bf16),
        scratch_shapes=[pltpu.SemaphoreType.DMA((tiles,))],
        compiler_params=PARAMS,
        cost_estimate=taking(2.4),
        name="fetch",
    )(in_hbm(after(out_weight, out_early)))

    def opening(chunk, place):
        scratch = streaming["scratch_shapes"] if chunk else []
        return pl.pallas_call(
            functools.partial(opening_kernel, ranks, distances, chunk * columns),
            in_specs=[SMEM] + [VMEM] * (2 + len(distances)) + [HBM if chunk else VMEM],
            out_specs=VMEM,
            out_shape=jax.ShapeDtypeStruct((block, columns), bf16),
            scratch_shapes=scratch + [pltpu.VMEM((block, width), bf16)],
            compiler_params=PARAMS,
            cost_estimate=taking(3.4),
            name="opening",
        )(place, *early, weight if chunk else fetched)

    ends = [(0, 1), (last, last - 1)]
    sent = opening(0, place)
    arrived = [[lax.ppermute(sent, "tensor", ends)]]
    out_late = [served(q, d) for q, d in zip(after(asked_late, sent), distances)]
    for chunk in range(1, chunks):
        sent = opening(chunk, after(place, out_late))
        arrived.append([lax.ppermute(sent, "tensor", ends)])
    *late, _ = local(1, after(place, sent))
    late += [shifted(o, "span", d) for o, d in zip(out_late, distances)]

    attended_shape = jax.ShapeDtypeStruct((rows, width), bf16)
    block_shapes = [jax.ShapeDtypeStruct((block, columns), bf16)] * 2
    attended, *merged = pl.pallas_call(
        functools.partial(merged_blocks_kernel, ranks, distances),
        in_specs=[SMEM] + [VMEM] * (4 + 2 * len(distances)) + [HBM],
        out_specs=[VMEM] * 3,
        out_shape=[attended_shape] + block_shapes,
        name="merged_blocks",
        **streaming,
    )(place, *early, *late, weight)

    def blocks_of(step, chunk, attended):
        return pl.pallas_call(
            functools.partial(blocks_kernel, ranks, chunk * columns, step),
            in_specs=[SMEM, VMEM, HBM],
            out_specs=[VMEM] * 2,
            out_shape=block_shapes,
            name="blocks",
            **streaming,
        )(place, attended, weight)

    before = attended
    for step in range(1, last):
        for chunk in range(chunks):
            if step == 1 and chunk == 0:
                blocks = merged
            else:
                blocks = blocks_of(step, chunk, after(attended, before))
            comes, blocks = lax.optimization_barrier((arrived[chunk], blocks))
            up, down = [
                (mine.astype(f32) + come.astype(f32)).astype(bf16)
                for mine, come in zip(blocks, (comes[0], comes[-1]))
            ]
            before = (up, down)
            arrived[chunk] = [
                lax.ppermute(up, "tensor", [(i, i + 1) for i in range(step + 1)]),
                lax.ppermute(down, "tensor", [(last - i, last - i - 1) for i in range(step + 1)]),
            ]
    everything = chunks * tiles
    projected, gate = pl.pallas_call(
        own_kernel,
        in_specs=[SMEM, SMEM, VMEM, HBM, HBM],
        out_specs=[VMEM, VMEM],
        out_shape=[jax.ShapeDtypeStruct((block, model), bf16), jax.ShapeDtypeStruct((1, model), f32)],
        scratch_shapes=[
            pltpu.VMEM((everything, width, tile), bf16),
            pltpu.VMEM((8, model), f32),
            pltpu.SemaphoreType.DMA((everything + 1,)),
        ],
        compiler_params=PARAMS,
        cost_estimate=taking(5.0),
        name="own",
    )(place, levels, after(attended, before), weight, in_hbm(gate_table))

    finished = []
    for chunk in range(chunks - 1):
        there = slice(chunk * columns, (chunk + 1) * columns)
        summed = sum(part.astype(f32) for part in (projected[:, there], *arrived[chunk]))
        finished.append((summed * gate[:, there]).astype(bf16))
    pieces = 2
    return pl.pallas_call(
        final_kernel,
        in_specs=[ANY, ANY, VMEM, VMEM, VMEM],
        out_specs=HBM,
        out_shape=jax.ShapeDtypeStruct((block, model), bf16),
        scratch_shapes=[
            pltpu.VMEM((block, columns), bf16),
            pltpu.VMEM((pieces, block, columns // pieces), bf16),
            pltpu.SemaphoreType.DMA((2 + pieces,)),
        ],
        compiler_params=PARAMS,
        cost_estimate=taking(2.7),
        name="final",
    )(jnp.concatenate(finished, axis=1), projected, gate, *arrived[-1])


def solution(mesh):
    return jax.shard_map(
        body,
        mesh=mesh,
        in_specs=(
            P(("group", "span"), "tensor"),
            P(("group", "span"), "tensor"),
            P(("group", "span"), "tensor"),
            P("tensor", None),
            P(),
            P("group"),
            P("group", None),
        ),
        out_specs=P(("group", "span", "tensor"), None),
        check_vma=False,
    )
```

```python
import functools

import jax
import jax.numpy as jnp
from jax import lax
from jax.experimental import pallas as pl
from jax.experimental.pallas import tpu as pltpu
from jax.sharding import PartitionSpec as P

HD = 128
LANES = 128
HIDDEN = -1e30
LOG2E = 1.4426950408889634
PARAMS = pltpu.CompilerParams(vmem_limit_bytes=24 * 1024 * 1024)
SMEM = pl.BlockSpec(memory_space=pltpu.SMEM)
VMEM = pl.BlockSpec(memory_space=pltpu.VMEM)
ANY = pl.BlockSpec(memory_space=pl.ANY)
HBM = pl.BlockSpec(memory_space=pltpu.HBM)
PIECE_LANES = 32


def taking(microseconds):
    return pl.CostEstimate(flops=0, bytes_accessed=int(microseconds * 3.69e6), transcendentals=0)


def in_hbm(array):
    return pltpu.with_memory_space_constraint(array, pltpu.HBM)


def shifted(block, axis, distance):
    count = lax.axis_size(axis)
    return lax.ppermute(block, axis, [(i, i + distance) for i in range(count) if 0 <= i + distance < count])


def head_columns(head):
    return slice(head * HD, (head + 1) * HD)


def attend(query, keys, values, flags, write, arrive=None):
    rows, width = query.shape
    scale = LOG2E * HD ** (-0.5)
    lane = lax.broadcasted_iota(jnp.int32, (rows, LANES), 1)
    packed = jnp.zeros((rows, LANES), jnp.float32)

    def scored(head):
        columns = head_columns(head)
        return [
            lax.dot_general(
                query[:, columns], key[:, columns], (((1,), (1,)), ((), ())), preferred_element_type=jnp.float32
            )
            for key in keys
        ]

    heads = width // HD
    later = scored(0)
    if arrive is not None:
        arrive()
    for head in range(heads):
        columns = head_columns(head)
        scores, later = later, scored(head + 1) if head + 1 < heads else None
        tops = [jnp.max(block, axis=-1, keepdims=True) * scale for block in scores]
        top = functools.reduce(
            jnp.maximum, [one if flag is None else jnp.where(flag, one, HIDDEN) for one, flag in zip(tops, flags)]
        )
        joined = None
        for block, value, flag in zip(scores, values, flags):
            above = top if flag is None else jnp.where(flag, top, -HIDDEN)
            probs = jnp.exp2(block * scale - above).astype(jnp.bfloat16)
            beside = jnp.concatenate([value[:, columns], jnp.ones((value.shape[0], HD), jnp.bfloat16)], axis=1)
            part = jnp.dot(probs, beside, preferred_element_type=jnp.float32)
            joined = part if joined is None else joined + part
        product, total = joined[:, :HD], jnp.where(joined[:, HD:] > 0.0, joined[:, HD:], 1.0)
        write(columns, product / total)
        packed = jnp.where(lane == head, top + jnp.log2(total), packed)
    return packed


def seen_by(visible, asker, span):
    table = visible[...]
    row, column = (lax.broadcasted_iota(jnp.int32, table.shape, axis) for axis in (0, 1))
    here = jnp.logical_and(row == asker, column == span)
    return jnp.max(jnp.where(here, table, 0).astype(jnp.float32), axis=(0, 1), keepdims=True) > 0.0


def beside_of(span):
    return span + 1 - 2 * lax.rem(span, 2)


def copied(source, target, semaphore):
    copy = pltpu.make_async_copy(source, target, semaphore)
    copy.start()
    return copy


def parts_of(rank, ranks, rows):
    block = rows // ranks
    lower = rank < ranks // 2
    early = pl.multiple_of(jnp.where(lower, rows - block, 0), block)
    late = pl.multiple_of(jnp.where(lower, 0, block), block)
    return (early, block), (late, rows - block)


def split_kernel(ranks, place, query, *refs):
    *targets, semaphores = refs

    @pl.when(place[0] > 1)
    def _():
        (early, _), (late, _) = parts_of(place[1], ranks, query.shape[0])
        starts = (early, late, pl.multiple_of(late + targets[1].shape[0], 16))
        copies = [
            copied(query.at[pl.ds(start, target.shape[0])], target, semaphores.at[index])
            for index, (start, target) in enumerate(zip(starts, targets))
        ]
        for copy in copies:
            copy.wait()


def local_kernel(ranks, part, place, visible, query, key, value, key_beside, value_beside,
                 result, sums, seen, *scratch):
    query_, key_, value_, key_beside_, value_beside_, semaphores = scratch
    start, size = parts_of(place[1], ranks, query.shape[0])[part]
    copies = [
        copied(source, target, semaphores.at[index])
        for index, (source, target) in enumerate((
            (visible, seen), (query.at[pl.ds(start, size)], query_),
            (key, key_), (key_beside, key_beside_), (value, value_), (value_beside, value_beside_),
        ))
    ]
    for copy in copies[:4]:
        copy.wait()

    def arrive():
        for copy in copies[4:]:
            copy.wait()

    def write(columns, block):
        result[:, columns] = block

    flags = [None, seen_by(seen, place[0], beside_of(place[0]))]
    sums[...] = attend(query_, [key_, key_beside_], [value_, value_beside_], flags, write, arrive)


def served_kernel(distance, spans, place, visible, key, value, key_beside, value_beside, *refs):
    span = place[0]

    @pl.when(span + distance < spans)
    def _():
        asker = jnp.minimum(span + distance, spans - 1)
        flags = [seen_by(visible, asker, span), seen_by(visible, asker, beside_of(span))]
        *queries, result, query = refs
        at = 0
        for part in queries:
            query[at:at + part.shape[0], :] = part[...]
            at += part.shape[0]

        def write(columns, block):
            result[:, columns] = block.astype(jnp.bfloat16)

        rest = attend(query, [key, key_beside], [value, value_beside], flags, write)
        sent = jnp.zeros_like(rest)
        for piece in range(3):
            part = rest.astype(jnp.bfloat16).astype(jnp.float32)
            sent = sent + (part if piece == 0 else pltpu.roll(part, piece * PIECE_LANES, 1))
            rest = rest - part
        result[:, query.shape[1]:] = sent.astype(jnp.bfloat16)


def merge(span, distances, own, own_sum, served, write):
    width = own.shape[1]
    sums = [own_sum[...]]
    for distance, ref in zip(distances, served):
        sent = ref[:, width:].astype(jnp.float32)
        joined = sent
        for piece in (1, 2):
            joined = joined + pltpu.roll(sent, LANES - piece * PIECE_LANES, 1)
        sums.append(jnp.where(span >= distance, joined, HIDDEN))
    top = functools.reduce(jnp.maximum, sums)
    shares = [jnp.exp2(one - top) for one in sums]
    over = 1.0 / sum(shares)
    shares = [share * over for share in shares]
    for head in range(width // HD):
        columns = head_columns(head)
        merged = own[:, columns] * shares[0][:, head:head + 1]
        for distance, share, ref in zip(distances, shares[1:], served):
            away = jnp.where(span >= distance, ref[:, columns].astype(jnp.float32), 0.0)
            merged = merged + away * share[:, head:head + 1]
        write(columns, merged.astype(jnp.bfloat16))


def streamed(weight, first, tiles, semaphores):
    count, _, tile = tiles.shape
    return [
        copied(weight.at[:, pl.ds(first + index * tile, tile)], tiles.at[index], semaphores.at[index])
        for index in range(count)
    ]


def fetch_kernel(askers, place, weight, *refs):
    tiles, semaphores = refs[-2:]

    @pl.when(place[0] > 1 if askers else place[0] < 2)
    def _():
        for copy in streamed(weight, 0, tiles, semaphores):
            copy.wait()


def opening_kernel(ranks, distances, first, place, *refs):
    own, own_sum, *served = refs[:2 + len(distances)]
    weight, result, *scratch = refs[2 + len(distances):]
    rows = scratch[-1]

    @pl.when(jnp.logical_or(place[1] == 0, place[1] == ranks - 1))
    def _():
        tiles, copies = weight, [None] * weight.shape[0]
        if first:
            tiles, semaphores, _ = scratch
            copies = streamed(weight, first, tiles, semaphores)

        def write(columns, part):
            rows[:, columns] = part

        merge(place[0], distances, own, own_sum, served, write)
        tile = tiles.shape[2]
        for index, copy in enumerate(copies):
            if copy is not None:
                copy.wait()
            product = jnp.dot(rows[...], tiles[index], preferred_element_type=jnp.float32)
            result[:, index * tile:(index + 1) * tile] = product.astype(jnp.bfloat16)


def project_blocks(ranks, first, rank, step, attended, weight, up, down, tiles, semaphores):
    last = ranks - 1
    tile = tiles.shape[2]
    block = up.shape[0]
    copies = streamed(weight, first, tiles, semaphores)
    yield
    sends = rank <= step, rank >= last - step
    starts = [
        pl.multiple_of(jnp.clip(target, 0, last) * block, block) for target in (last - step + rank, step + rank - last)
    ]
    rows = [attended[pl.ds(start, block), :] for start in starts]
    for index, copy in enumerate(copies):
        copy.wait()
        there = slice(index * tile, (index + 1) * tile)

        @pl.when(jnp.logical_and(*sends))
        def _():
            both = jnp.dot(jnp.concatenate(rows, axis=0), tiles[index], preferred_element_type=jnp.float32)
            up[:, there] = both[:block].astype(jnp.bfloat16)
            down[:, there] = both[block:].astype(jnp.bfloat16)

        @pl.when(jnp.logical_not(jnp.logical_and(*sends)))
        def _():
            one = jnp.dot(
                jnp.where(sends[0], rows[0], rows[1]), tiles[index], preferred_element_type=jnp.float32
            ).astype(jnp.bfloat16)
            up[:, there] = one
            down[:, there] = one


def merged_blocks_kernel(ranks, distances, place, *refs):
    each = 2 + len(distances)
    parts, (weight, attended, *results) = (refs[:each], refs[each:2 * each]), refs[2 * each:]
    work = project_blocks(ranks, 0, place[1], 1, attended, weight, *results)
    next(work)
    for (start, size), (own, own_sum, *served) in zip(parts_of(place[1], ranks, attended.shape[0]), parts):
        there = pl.ds(start, size)

        def write(columns, part):
            attended[there, columns] = part

        merge(place[0], distances, own, own_sum, served, write)
    for _ in work:
        pass


def blocks_kernel(ranks, first, step, place, attended, weight, *results):
    for _ in project_blocks(ranks, first, place[1], step, attended, weight, *results):
        pass


def own_kernel(place, levels, attended, weight, gate_table, result, gate, tiles, gates, semaphores):
    block = result.shape[0]
    count, _, tile = tiles.shape
    level = levels[place[0]]
    above = pl.multiple_of(level // 8 * 8, 8)
    gate_copy = copied(gate_table.at[pl.ds(above, 8)], gates, semaphores.at[count])
    copies = streamed(weight, 0, tiles, semaphores)
    start = pl.multiple_of(place[1] * block, block)
    for index, copy in enumerate(copies):
        copy.wait()
        product = jnp.dot(attended[pl.ds(start, block), :], tiles[index], preferred_element_type=jnp.float32)
        result[:, index * tile:(index + 1) * tile] = product.astype(jnp.bfloat16)
    gate_copy.wait()
    gate[...] = gates[pl.ds(lax.rem(level, 8), 1), :]


def final_kernel(done, projected, gate, up, down, result, own, gated, semaphores):
    first, (block, columns) = done.shape[1], own.shape
    pieces = gated.shape[0]
    wide = columns // pieces
    own_copy = copied(projected.at[:, pl.ds(first, columns)], own, semaphores.at[0])
    sent = [copied(done, result.at[:, pl.ds(0, first)], semaphores.at[1])]
    own_copy.wait()
    for piece in range(pieces):
        there = slice(piece * wide, (piece + 1) * wide)
        summed = own[:, there].astype(jnp.float32) + up[:, there].astype(jnp.float32)
        summed = summed + down[:, there].astype(jnp.float32)
        gated[piece] = (summed * gate[:, first + piece * wide:first + (piece + 1) * wide]).astype(jnp.bfloat16)
        sent.append(copied(
            gated.at[piece], result.at[:, pl.ds(first + piece * wide, wide)], semaphores.at[2 + piece]
        ))
    for copy in sent:
        copy.wait()


def body(queries, keys, values, out_weight, gate_table, levels, visible):
    rows, width = queries.shape
    model = out_weight.shape[1]
    spans = lax.axis_size("span")
    ranks = lax.axis_size("tensor")
    span = lax.axis_index("span")
    rank = lax.axis_index("tensor")
    block = rows // ranks
    bf16, f32 = jnp.bfloat16, jnp.float32
    place = jnp.stack([span, rank]).astype(jnp.int32)
    third = (rows - block) // 48 * 16
    query_early, *query_late = pl.pallas_call(
        functools.partial(split_kernel, ranks),
        in_specs=[SMEM, HBM],
        out_specs=[VMEM] * 3,
        out_shape=[jax.ShapeDtypeStruct((part, width), bf16) for part in (block, rows - block - third, third)],
        scratch_shapes=[pltpu.SemaphoreType.DMA((3,))],
        compiler_params=PARAMS,
        cost_estimate=taking(1.7),
        name="split",
    )(place, in_hbm(queries))
    distances = list(range(2, spans, 2))
    asked_early = [shifted(query_early, "span", -distance) for distance in distances]
    swap = [(i, i + 1 - 2 * (i % 2)) for i in range(spans)]
    key_beside = lax.ppermute(keys, "span", swap)
    value_beside = lax.ppermute(values, "span", swap)

    def after(value, *others):
        return lax.optimization_barrier((value, others))[0]

    def local(part, place):
        size = (block, rows - block)[part]
        return pl.pallas_call(
            functools.partial(local_kernel, ranks, part),
            in_specs=[SMEM, HBM, HBM, HBM, HBM, ANY, ANY],
            out_specs=[VMEM] * 3,
            out_shape=[
                jax.ShapeDtypeStruct((size, width), f32),
                jax.ShapeDtypeStruct((size, LANES), f32),
                jax.ShapeDtypeStruct(visible.shape, visible.dtype),
            ],
            scratch_shapes=[pltpu.VMEM((size, width), bf16)] + [pltpu.VMEM((rows, width), bf16)] * 4
            + [pltpu.SemaphoreType.DMA((6,))],
            compiler_params=PARAMS,
            cost_estimate=taking(4.0),
            name="local",
        )(place, in_hbm(visible), in_hbm(queries), in_hbm(keys), in_hbm(values), key_beside, value_beside)

    def served(asked, distance):
        return pl.pallas_call(
            functools.partial(served_kernel, distance, spans),
            in_specs=[SMEM] + [VMEM] * (5 + len(asked)),
            out_specs=VMEM,
            out_shape=jax.ShapeDtypeStruct((sum(part.shape[0] for part in asked), width + LANES), bf16),
            scratch_shapes=[pltpu.VMEM((sum(part.shape[0] for part in asked), width), bf16)],
            compiler_params=PARAMS,
            cost_estimate=taking(3.3),
            name="served",
        )(place, seen, keys, values, key_beside, value_beside, *asked)

    *early, seen = local(0, place)
    query_late = after(query_late, early)
    asked_early = after(asked_early, early)
    chunks = 2
    columns = model // chunks
    tiles = 4
    tile = columns // tiles
    last = ranks - 1
    weight = in_hbm(out_weight)

    tile_shape = (tiles, width, tile)
    streaming = dict(
        scratch_shapes=[pltpu.VMEM(tile_shape, bf16), pltpu.SemaphoreType.DMA((tiles,))],
        compiler_params=PARAMS,
        cost_estimate=taking(3.0),
    )

    def fetch(askers, place, *before):
        return pl.pallas_call(
            functools.partial(fetch_kernel, askers),
            in_specs=[SMEM, HBM] + [VMEM] * len(before),
            out_specs=VMEM,
            out_shape=jax.ShapeDtypeStruct(tile_shape, bf16),
            input_output_aliases={2: 0} if before else {},
            scratch_shapes=[pltpu.SemaphoreType.DMA((tiles,))],
            compiler_params=PARAMS,
            cost_estimate=taking(2.4),
            name="fetch",
        )(place, weight, *before)

    out_early = [served([q], d) for q, d in zip(asked_early, distances)]
    early += [shifted(o, "span", d) for o, d in zip(out_early, distances)]
    fetched = fetch(True, after(place, out_early))
    query_late = [query_late[0], after(query_late[1], fetched)]
    asked_late = [[shifted(query, "span", -distance) for query in query_late] for distance in distances]
    fetched = fetch(False, place, fetched)

    def opening(chunk, place):
        scratch = streaming["scratch_shapes"] if chunk else []
        return pl.pallas_call(
            functools.partial(opening_kernel, ranks, distances, chunk * columns),
            in_specs=[SMEM] + [VMEM] * (2 + len(distances)) + [HBM if chunk else VMEM],
            out_specs=VMEM,
            out_shape=jax.ShapeDtypeStruct((block, columns), bf16),
            scratch_shapes=scratch + [pltpu.VMEM((block, width), bf16)],
            compiler_params=PARAMS,
            cost_estimate=taking(3.4),
            name="opening",
        )(place, *early, weight if chunk else fetched)

    ends = [(0, 1), (last, last - 1)]
    sent = opening(0, place)
    arrived = [[lax.ppermute(sent, "tensor", ends)]]
    out_late = [served(q, d) for q, d in zip(after(asked_late, sent), distances)]
    for chunk in range(1, chunks):
        sent = opening(chunk, after(place, out_late))
        arrived.append([lax.ppermute(sent, "tensor", ends)])
    *late, _ = local(1, after(place, sent))
    late += [shifted(o, "span", d) for o, d in zip(out_late, distances)]

    attended_shape = jax.ShapeDtypeStruct((rows, width), bf16)
    block_shapes = [jax.ShapeDtypeStruct((block, columns), bf16)] * 2
    attended, *merged = pl.pallas_call(
        functools.partial(merged_blocks_kernel, ranks, distances),
        in_specs=[SMEM] + [VMEM] * (4 + 2 * len(distances)) + [HBM],
        out_specs=[VMEM] * 3,
        out_shape=[attended_shape] + block_shapes,
        name="merged_blocks",
        **streaming,
    )(place, *early, *late, weight)

    def blocks_of(step, chunk, attended):
        return pl.pallas_call(
            functools.partial(blocks_kernel, ranks, chunk * columns, step),
            in_specs=[SMEM, VMEM, HBM],
            out_specs=[VMEM] * 2,
            out_shape=block_shapes,
            name="blocks",
            **streaming,
        )(place, attended, weight)

    before = attended
    for step in range(1, last):
        for chunk in range(chunks):
            if step == 1 and chunk == 0:
                blocks = merged
            else:
                blocks = blocks_of(step, chunk, after(attended, before))
            comes, blocks = lax.optimization_barrier((arrived[chunk], blocks))
            up, down = [
                (mine.astype(f32) + come.astype(f32)).astype(bf16)
                for mine, come in zip(blocks, (comes[0], comes[-1]))
            ]
            before = (up, down)
            arrived[chunk] = [
                lax.ppermute(up, "tensor", [(i, i + 1) for i in range(step + 1)]),
                lax.ppermute(down, "tensor", [(last - i, last - i - 1) for i in range(step + 1)]),
            ]
    everything = chunks * tiles
    projected, gate = pl.pallas_call(
        own_kernel,
        in_specs=[SMEM, SMEM, VMEM, HBM, HBM],
        out_specs=[VMEM, VMEM],
        out_shape=[jax.ShapeDtypeStruct((block, model), bf16), jax.ShapeDtypeStruct((1, model), f32)],
        scratch_shapes=[
            pltpu.VMEM((everything, width, tile), bf16),
            pltpu.VMEM((8, model), f32),
            pltpu.SemaphoreType.DMA((everything + 1,)),
        ],
        compiler_params=PARAMS,
        cost_estimate=taking(5.0),
        name="own",
    )(place, levels, after(attended, before), weight, in_hbm(gate_table))

    finished = []
    for chunk in range(chunks - 1):
        there = slice(chunk * columns, (chunk + 1) * columns)
        summed = sum(part.astype(f32) for part in (projected[:, there], *arrived[chunk]))
        finished.append((summed * gate[:, there]).astype(bf16))
    pieces = 2
    return pl.pallas_call(
        final_kernel,
        in_specs=[ANY, ANY, VMEM, VMEM, VMEM],
        out_specs=HBM,
        out_shape=jax.ShapeDtypeStruct((block, model), bf16),
        scratch_shapes=[
            pltpu.VMEM((block, columns), bf16),
            pltpu.VMEM((pieces, block, columns // pieces), bf16),
            pltpu.SemaphoreType.DMA((2 + pieces,)),
        ],
        compiler_params=PARAMS,
        cost_estimate=taking(2.7),
        name="final",
    )(jnp.concatenate(finished, axis=1), projected, gate, *arrived[-1])


def solution(mesh):
    return jax.shard_map(
        body,
        mesh=mesh,
        in_specs=(
            P(("group", "span"), "tensor"),
            P(("group", "span"), "tensor"),
            P(("group", "span"), "tensor"),
            P("tensor", None),
            P(),
            P("group"),
            P("group", None),
        ),
        out_specs=P(("group", "span", "tensor"), None),
        check_vma=False,
    )
```

```python
import functools

import jax
import jax.numpy as jnp
from jax import lax
from jax.experimental import pallas as pl
from jax.experimental.pallas import tpu as pltpu
from jax.sharding import PartitionSpec as P

HD = 128
LANES = 128
HIDDEN = -1e30
LOG2E = 1.4426950408889634
PARAMS = pltpu.CompilerParams(vmem_limit_bytes=24 * 1024 * 1024)
SMEM = pl.BlockSpec(memory_space=pltpu.SMEM)
VMEM = pl.BlockSpec(memory_space=pltpu.VMEM)
ANY = pl.BlockSpec(memory_space=pl.ANY)
HBM = pl.BlockSpec(memory_space=pltpu.HBM)
PIECE_LANES = 32


def taking(microseconds):
    return pl.CostEstimate(flops=0, bytes_accessed=int(microseconds * 3.69e6), transcendentals=0)


def in_hbm(array):
    return pltpu.with_memory_space_constraint(array, pltpu.HBM)


def shifted(block, axis, distance):
    count = lax.axis_size(axis)
    return lax.ppermute(block, axis, [(i, i + distance) for i in range(count) if 0 <= i + distance < count])


def head_columns(head):
    return slice(head * HD, (head + 1) * HD)


def attend(query, keys, values, flags, write, arrive=None):
    rows, width = query.shape
    scale = LOG2E * HD ** (-0.5)
    lane = lax.broadcasted_iota(jnp.int32, (rows, LANES), 1)
    packed = jnp.zeros((rows, LANES), jnp.float32)

    def scored(head):
        columns = head_columns(head)
        return [
            lax.dot_general(
                query[:, columns], key[:, columns], (((1,), (1,)), ((), ())), preferred_element_type=jnp.float32
            )
            for key in keys
        ]

    heads = width // HD
    later = scored(0)
    if arrive is not None:
        arrive()
    for head in range(heads):
        columns = head_columns(head)
        scores, later = later, scored(head + 1) if head + 1 < heads else None
        tops = [jnp.max(block, axis=-1, keepdims=True) * scale for block in scores]
        top = functools.reduce(
            jnp.maximum, [one if flag is None else jnp.where(flag, one, HIDDEN) for one, flag in zip(tops, flags)]
        )
        joined = None
        for block, value, flag in zip(scores, values, flags):
            above = top if flag is None else jnp.where(flag, top, -HIDDEN)
            probs = jnp.exp2(block * scale - above).astype(jnp.bfloat16)
            beside = jnp.concatenate([value[:, columns], jnp.ones((value.shape[0], HD), jnp.bfloat16)], axis=1)
            part = jnp.dot(probs, beside, preferred_element_type=jnp.float32)
            joined = part if joined is None else joined + part
        product, total = joined[:, :HD], jnp.where(joined[:, HD:] > 0.0, joined[:, HD:], 1.0)
        write(columns, product / total)
        packed = jnp.where(lane == head, top + jnp.log2(total), packed)
    return packed


def seen_by(visible, asker, span):
    table = visible[...]
    row, column = (lax.broadcasted_iota(jnp.int32, table.shape, axis) for axis in (0, 1))
    here = jnp.logical_and(row == asker, column == span)
    return jnp.max(jnp.where(here, table, 0).astype(jnp.float32), axis=(0, 1), keepdims=True) > 0.0


def beside_of(span):
    return span + 1 - 2 * lax.rem(span, 2)


def place_here():
    return lax.axis_index("span"), lax.axis_index("tensor")


def copied(source, target, semaphore):
    copy = pltpu.make_async_copy(source, target, semaphore)
    copy.start()
    return copy


def parts_of(rank, ranks, rows):
    block = rows // ranks
    lower = rank < ranks // 2
    early = pl.multiple_of(jnp.where(lower, rows - block, 0), block)
    late = pl.multiple_of(jnp.where(lower, 0, block), block)
    return (early, block), (late, rows - block)


def split_kernel(ranks, query, *refs):
    *targets, semaphores = refs
    place = place_here()

    @pl.when(place[0] > 1)
    def _():
        (early, _), (late, _) = parts_of(place[1], ranks, query.shape[0])
        starts = (early, late, pl.multiple_of(late + targets[1].shape[0], 16))
        copies = [
            copied(query.at[pl.ds(start, target.shape[0])], target, semaphores.at[index])
            for index, (start, target) in enumerate(zip(starts, targets))
        ]
        for copy in copies:
            copy.wait()


def local_kernel(ranks, part, visible, query, key, value, key_beside, value_beside,
                 result, sums, seen, *scratch):
    query_, key_, value_, key_beside_, value_beside_, semaphores = scratch
    place = place_here()
    start, size = parts_of(place[1], ranks, query.shape[0])[part]
    copies = [
        copied(source, target, semaphores.at[index])
        for index, (source, target) in enumerate((
            (visible, seen), (query.at[pl.ds(start, size)], query_),
            (key, key_), (key_beside, key_beside_), (value, value_), (value_beside, value_beside_),
        ))
    ]
    for copy in copies[:4]:
        copy.wait()

    def arrive():
        for copy in copies[4:]:
            copy.wait()

    def write(columns, block):
        result[:, columns] = block

    flags = [None, seen_by(seen, place[0], beside_of(place[0]))]
    sums[...] = attend(query_, [key_, key_beside_], [value_, value_beside_], flags, write, arrive)


def served_kernel(distance, spans, visible, key, value, key_beside, value_beside, *refs):
    span, _ = place_here()

    @pl.when(span + distance < spans)
    def _():
        asker = jnp.minimum(span + distance, spans - 1)
        flags = [seen_by(visible, asker, span), seen_by(visible, asker, beside_of(span))]
        *queries, result, query = refs
        at = 0
        for part in queries:
            query[at:at + part.shape[0], :] = part[...]
            at += part.shape[0]

        def write(columns, block):
            result[:, columns] = block.astype(jnp.bfloat16)

        rest = attend(query, [key, key_beside], [value, value_beside], flags, write)
        sent = jnp.zeros_like(rest)
        for piece in range(3):
            part = rest.astype(jnp.bfloat16).astype(jnp.float32)
            sent = sent + (part if piece == 0 else pltpu.roll(part, piece * PIECE_LANES, 1))
            rest = rest - part
        result[:, query.shape[1]:] = sent.astype(jnp.bfloat16)


def merge(span, distances, own, own_sum, served, write):
    width = own.shape[1]
    sums = [own_sum[...]]
    for distance, ref in zip(distances, served):
        sent = ref[:, width:].astype(jnp.float32)
        joined = sent
        for piece in (1, 2):
            joined = joined + pltpu.roll(sent, LANES - piece * PIECE_LANES, 1)
        sums.append(jnp.where(span >= distance, joined, HIDDEN))
    top = functools.reduce(jnp.maximum, sums)
    shares = [jnp.exp2(one - top) for one in sums]
    over = 1.0 / sum(shares)
    shares = [share * over for share in shares]
    for head in range(width // HD):
        columns = head_columns(head)
        merged = own[:, columns] * shares[0][:, head:head + 1]
        for distance, share, ref in zip(distances, shares[1:], served):
            away = jnp.where(span >= distance, ref[:, columns].astype(jnp.float32), 0.0)
            merged = merged + away * share[:, head:head + 1]
        write(columns, merged.astype(jnp.bfloat16))


def streamed(weight, first, tiles, semaphores):
    count, _, tile = tiles.shape
    return [
        copied(weight.at[:, pl.ds(first + index * tile, tile)], tiles.at[index], semaphores.at[index])
        for index in range(count)
    ]


def fetch_kernel(askers, weight, *refs):
    tiles, semaphores = refs[-2:]
    span, _ = place_here()

    @pl.when(span > 1 if askers else span < 2)
    def _():
        for copy in streamed(weight, 0, tiles, semaphores):
            copy.wait()


def opening_kernel(ranks, distances, first, *refs):
    own, own_sum, *served = refs[:2 + len(distances)]
    weight, result, *scratch = refs[2 + len(distances):]
    rows = scratch[-1]
    place = place_here()

    @pl.when(jnp.logical_or(place[1] == 0, place[1] == ranks - 1))
    def _():
        tiles, copies = weight, [None] * weight.shape[0]
        if first:
            tiles, semaphores, _ = scratch
            copies = streamed(weight, first, tiles, semaphores)

        def write(columns, part):
            rows[:, columns] = part

        merge(place[0], distances, own, own_sum, served, write)
        tile = tiles.shape[2]
        for index, copy in enumerate(copies):
            if copy is not None:
                copy.wait()
            product = jnp.dot(rows[...], tiles[index], preferred_element_type=jnp.float32)
            result[:, index * tile:(index + 1) * tile] = product.astype(jnp.bfloat16)


def project_blocks(ranks, first, rank, step, attended, weight, up, down, tiles, semaphores):
    last = ranks - 1
    tile = tiles.shape[2]
    block = up.shape[0]
    copies = streamed(weight, first, tiles, semaphores)
    yield
    sends = rank <= step, rank >= last - step
    starts = [
        pl.multiple_of(jnp.clip(target, 0, last) * block, block) for target in (last - step + rank, step + rank - last)
    ]
    rows = [attended[pl.ds(start, block), :] for start in starts]
    for index, copy in enumerate(copies):
        copy.wait()
        there = slice(index * tile, (index + 1) * tile)

        @pl.when(jnp.logical_and(*sends))
        def _():
            both = jnp.dot(jnp.concatenate(rows, axis=0), tiles[index], preferred_element_type=jnp.float32)
            up[:, there] = both[:block].astype(jnp.bfloat16)
            down[:, there] = both[block:].astype(jnp.bfloat16)

        @pl.when(jnp.logical_not(jnp.logical_and(*sends)))
        def _():
            one = jnp.dot(
                jnp.where(sends[0], rows[0], rows[1]), tiles[index], preferred_element_type=jnp.float32
            ).astype(jnp.bfloat16)
            up[:, there] = one
            down[:, there] = one


def merged_blocks_kernel(ranks, distances, place, *refs):
    each = 2 + len(distances)
    parts, (weight, attended, *results) = (refs[:each], refs[each:2 * each]), refs[2 * each:]
    work = project_blocks(ranks, 0, place[1], 1, attended, weight, *results)
    next(work)
    for (start, size), (own, own_sum, *served) in zip(parts_of(place[1], ranks, attended.shape[0]), parts):
        there = pl.ds(start, size)

        def write(columns, part):
            attended[there, columns] = part

        merge(place[0], distances, own, own_sum, served, write)
    for _ in work:
        pass


def blocks_kernel(ranks, first, step, place, attended, weight, *results):
    for _ in project_blocks(ranks, first, place[1], step, attended, weight, *results):
        pass


def own_kernel(place, levels, attended, weight, gate_table, result, gate, tiles, gates, semaphores):
    block = result.shape[0]
    count, _, tile = tiles.shape
    level = levels[place[0]]
    above = pl.multiple_of(level // 8 * 8, 8)
    gate_copy = copied(gate_table.at[pl.ds(above, 8)], gates, semaphores.at[count])
    copies = streamed(weight, 0, tiles, semaphores)
    start = pl.multiple_of(place[1] * block, block)
    for index, copy in enumerate(copies):
        copy.wait()
        product = jnp.dot(attended[pl.ds(start, block), :], tiles[index], preferred_element_type=jnp.float32)
        result[:, index * tile:(index + 1) * tile] = product.astype(jnp.bfloat16)
    gate_copy.wait()
    gate[...] = gates[pl.ds(lax.rem(level, 8), 1), :]


def final_kernel(done, projected, gate, up, down, result, own, gated, semaphores):
    first, (block, columns) = done.shape[1], own.shape
    pieces = gated.shape[0]
    wide = columns // pieces
    own_copy = copied(projected.at[:, pl.ds(first, columns)], own, semaphores.at[0])
    sent = [copied(done, result.at[:, pl.ds(0, first)], semaphores.at[1])]
    own_copy.wait()
    for piece in range(pieces):
        there = slice(piece * wide, (piece + 1) * wide)
        summed = own[:, there].astype(jnp.float32) + up[:, there].astype(jnp.float32)
        summed = summed + down[:, there].astype(jnp.float32)
        gated[piece] = (summed * gate[:, first + piece * wide:first + (piece + 1) * wide]).astype(jnp.bfloat16)
        sent.append(copied(
            gated.at[piece], result.at[:, pl.ds(first + piece * wide, wide)], semaphores.at[2 + piece]
        ))
    for copy in sent:
        copy.wait()


def body(queries, keys, values, out_weight, gate_table, levels, visible):
    rows, width = queries.shape
    model = out_weight.shape[1]
    spans = lax.axis_size("span")
    ranks = lax.axis_size("tensor")
    span = lax.axis_index("span")
    rank = lax.axis_index("tensor")
    block = rows // ranks
    bf16, f32 = jnp.bfloat16, jnp.float32
    place = jnp.stack([span, rank]).astype(jnp.int32)
    third = (rows - block) // 48 * 16
    query_early, *query_late = pl.pallas_call(
        functools.partial(split_kernel, ranks),
        in_specs=[HBM],
        out_specs=[VMEM] * 3,
        out_shape=[jax.ShapeDtypeStruct((part, width), bf16) for part in (block, rows - block - third, third)],
        scratch_shapes=[pltpu.SemaphoreType.DMA((3,))],
        compiler_params=PARAMS,
        cost_estimate=taking(1.7),
        name="split",
    )(in_hbm(queries))
    distances = list(range(2, spans, 2))
    asked_early = [shifted(query_early, "span", -distance) for distance in distances]
    swap = [(i, i + 1 - 2 * (i % 2)) for i in range(spans)]
    key_beside = lax.ppermute(keys, "span", swap)
    value_beside = lax.ppermute(values, "span", swap)

    def after(value, *others):
        return lax.optimization_barrier((value, others))[0]

    def local(part, queries):
        size = (block, rows - block)[part]
        return pl.pallas_call(
            functools.partial(local_kernel, ranks, part),
            in_specs=[HBM, HBM, HBM, HBM, ANY, ANY],
            out_specs=[VMEM] * 3,
            out_shape=[
                jax.ShapeDtypeStruct((size, width), f32),
                jax.ShapeDtypeStruct((size, LANES), f32),
                jax.ShapeDtypeStruct(visible.shape, visible.dtype),
            ],
            scratch_shapes=[pltpu.VMEM((size, width), bf16)] + [pltpu.VMEM((rows, width), bf16)] * 4
            + [pltpu.SemaphoreType.DMA((6,))],
            compiler_params=PARAMS,
            cost_estimate=taking(4.0),
            name="local",
        )(in_hbm(visible), in_hbm(queries), in_hbm(keys), in_hbm(values), key_beside, value_beside)

    def served(asked, distance):
        return pl.pallas_call(
            functools.partial(served_kernel, distance, spans),
            in_specs=[VMEM] * (5 + len(asked)),
            out_specs=VMEM,
            out_shape=jax.ShapeDtypeStruct((sum(part.shape[0] for part in asked), width + LANES), bf16),
            scratch_shapes=[pltpu.VMEM((sum(part.shape[0] for part in asked), width), bf16)],
            compiler_params=PARAMS,
            cost_estimate=taking(3.3),
            name="served",
        )(seen, keys, values, key_beside, value_beside, *asked)

    *early, seen = local(0, queries)
    query_late = after(query_late, early)
    asked_early = after(asked_early, early)
    chunks = 2
    columns = model // chunks
    tiles = 4
    tile = columns // tiles
    last = ranks - 1
    weight = in_hbm(out_weight)

    tile_shape = (tiles, width, tile)
    streaming = dict(
        scratch_shapes=[pltpu.VMEM(tile_shape, bf16), pltpu.SemaphoreType.DMA((tiles,))],
        compiler_params=PARAMS,
        cost_estimate=taking(3.0),
    )

    def fetch(askers, weight, *before):
        return pl.pallas_call(
            functools.partial(fetch_kernel, askers),
            in_specs=[HBM] + [VMEM] * len(before),
            out_specs=VMEM,
            out_shape=jax.ShapeDtypeStruct(tile_shape, bf16),
            input_output_aliases={1: 0} if before else {},
            scratch_shapes=[pltpu.SemaphoreType.DMA((tiles,))],
            compiler_params=PARAMS,
            cost_estimate=taking(2.4),
            name="fetch",
        )(in_hbm(weight), *before)

    out_early = [served([q], d) for q, d in zip(asked_early, distances)]
    early += [shifted(o, "span", d) for o, d in zip(out_early, distances)]
    fetched = fetch(True, after(out_weight, out_early))
    query_late = [query_late[0], after(query_late[1], fetched)]
    asked_late = [[shifted(query, "span", -distance) for query in query_late] for distance in distances]
    fetched = fetch(False, out_weight, fetched)

    def opening(chunk, weight):
        scratch = streaming["scratch_shapes"] if chunk else []
        return pl.pallas_call(
            functools.partial(opening_kernel, ranks, distances, chunk * columns),
            in_specs=[VMEM] * (2 + len(distances)) + [HBM if chunk else VMEM],
            out_specs=VMEM,
            out_shape=jax.ShapeDtypeStruct((block, columns), bf16),
            scratch_shapes=scratch + [pltpu.VMEM((block, width), bf16)],
            compiler_params=PARAMS,
            cost_estimate=taking(3.4),
            name="opening",
        )(*early, in_hbm(weight) if chunk else fetched)

    ends = [(0, 1), (last, last - 1)]
    sent = opening(0, out_weight)
    arrived = [[lax.ppermute(sent, "tensor", ends)]]
    out_late = [served(q, d) for q, d in zip(after(asked_late, sent), distances)]
    for chunk in range(1, chunks):
        sent = opening(chunk, after(out_weight, out_late))
        arrived.append([lax.ppermute(sent, "tensor", ends)])
    *late, _ = local(1, after(queries, sent))
    late += [shifted(o, "span", d) for o, d in zip(out_late, distances)]

    attended_shape = jax.ShapeDtypeStruct((rows, width), bf16)
    block_shapes = [jax.ShapeDtypeStruct((block, columns), bf16)] * 2
    attended, *merged = pl.pallas_call(
        functools.partial(merged_blocks_kernel, ranks, distances),
        in_specs=[SMEM] + [VMEM] * (4 + 2 * len(distances)) + [HBM],
        out_specs=[VMEM] * 3,
        out_shape=[attended_shape] + block_shapes,
        name="merged_blocks",
        **streaming,
    )(place, *early, *late, weight)

    def blocks_of(step, chunk, attended):
        return pl.pallas_call(
            functools.partial(blocks_kernel, ranks, chunk * columns, step),
            in_specs=[SMEM, VMEM, HBM],
            out_specs=[VMEM] * 2,
            out_shape=block_shapes,
            name="blocks",
            **streaming,
        )(place, attended, weight)

    before = attended
    for step in range(1, last):
        for chunk in range(chunks):
            if step == 1 and chunk == 0:
                blocks = merged
            else:
                blocks = blocks_of(step, chunk, after(attended, before))
            comes, blocks = lax.optimization_barrier((arrived[chunk], blocks))
            up, down = [
                (mine.astype(f32) + come.astype(f32)).astype(bf16)
                for mine, come in zip(blocks, (comes[0], comes[-1]))
            ]
            before = (up, down)
            arrived[chunk] = [
                lax.ppermute(up, "tensor", [(i, i + 1) for i in range(step + 1)]),
                lax.ppermute(down, "tensor", [(last - i, last - i - 1) for i in range(step + 1)]),
            ]
    everything = chunks * tiles
    projected, gate = pl.pallas_call(
        own_kernel,
        in_specs=[SMEM, SMEM, VMEM, HBM, HBM],
        out_specs=[VMEM, VMEM],
        out_shape=[jax.ShapeDtypeStruct((block, model), bf16), jax.ShapeDtypeStruct((1, model), f32)],
        scratch_shapes=[
            pltpu.VMEM((everything, width, tile), bf16),
            pltpu.VMEM((8, model), f32),
            pltpu.SemaphoreType.DMA((everything + 1,)),
        ],
        compiler_params=PARAMS,
        cost_estimate=taking(5.0),
        name="own",
    )(place, levels, after(attended, before), weight, in_hbm(gate_table))

    finished = []
    for chunk in range(chunks - 1):
        there = slice(chunk * columns, (chunk + 1) * columns)
        summed = sum(part.astype(f32) for part in (projected[:, there], *arrived[chunk]))
        finished.append((summed * gate[:, there]).astype(bf16))
    pieces = 2
    return pl.pallas_call(
        final_kernel,
        in_specs=[ANY, ANY, VMEM, VMEM, VMEM],
        out_specs=HBM,
        out_shape=jax.ShapeDtypeStruct((block, model), bf16),
        scratch_shapes=[
            pltpu.VMEM((block, columns), bf16),
            pltpu.VMEM((pieces, block, columns // pieces), bf16),
            pltpu.SemaphoreType.DMA((2 + pieces,)),
        ],
        compiler_params=PARAMS,
        cost_estimate=taking(2.7),
        name="final",
    )(jnp.concatenate(finished, axis=1), projected, gate, *arrived[-1])


def solution(mesh):
    return jax.shard_map(
        body,
        mesh=mesh,
        in_specs=(
            P(("group", "span"), "tensor"),
            P(("group", "span"), "tensor"),
            P(("group", "span"), "tensor"),
            P("tensor", None),
            P(),
            P("group"),
            P("group", None),
        ),
        out_specs=P(("group", "span", "tensor"), None),
        check_vma=False,
    )
```

```python
import functools

import jax
import jax.numpy as jnp
from jax import lax
from jax.experimental import pallas as pl
from jax.experimental.pallas import tpu as pltpu
from jax.sharding import PartitionSpec as P

HD = 128
LANES = 128
HIDDEN = -1e30
LOG2E = 1.4426950408889634
PARAMS = pltpu.CompilerParams(vmem_limit_bytes=24 * 1024 * 1024)
SMEM = pl.BlockSpec(memory_space=pltpu.SMEM)
VMEM = pl.BlockSpec(memory_space=pltpu.VMEM)
ANY = pl.BlockSpec(memory_space=pl.ANY)
HBM = pl.BlockSpec(memory_space=pltpu.HBM)
PIECE_LANES = 32


def taking(microseconds):
    return pl.CostEstimate(flops=0, bytes_accessed=int(microseconds * 3.69e6), transcendentals=0)


def in_hbm(array):
    return pltpu.with_memory_space_constraint(array, pltpu.HBM)


def shifted(block, axis, distance):
    count = lax.axis_size(axis)
    return lax.ppermute(block, axis, [(i, i + distance) for i in range(count) if 0 <= i + distance < count])


def head_columns(head):
    return slice(head * HD, (head + 1) * HD)


def attend(query, keys, values, flags, write, arrive=None):
    rows, width = query.shape
    scale = LOG2E * HD ** (-0.5)
    lane = lax.broadcasted_iota(jnp.int32, (rows, LANES), 1)
    packed = jnp.zeros((rows, LANES), jnp.float32)

    def scored(head):
        columns = head_columns(head)
        return [
            lax.dot_general(
                query[:, columns], key[:, columns], (((1,), (1,)), ((), ())), preferred_element_type=jnp.float32
            )
            for key in keys
        ]

    heads = width // HD
    later = scored(0)
    if arrive is not None:
        arrive()
    for head in range(heads):
        columns = head_columns(head)
        scores, later = later, scored(head + 1) if head + 1 < heads else None
        tops = [jnp.max(block, axis=-1, keepdims=True) * scale for block in scores]
        top = functools.reduce(
            jnp.maximum, [one if flag is None else jnp.where(flag, one, HIDDEN) for one, flag in zip(tops, flags)]
        )
        joined = None
        for block, value, flag in zip(scores, values, flags):
            above = top if flag is None else jnp.where(flag, top, -HIDDEN)
            probs = jnp.exp2(block * scale - above).astype(jnp.bfloat16)
            beside = jnp.concatenate([value[:, columns], jnp.ones((value.shape[0], HD), jnp.bfloat16)], axis=1)
            part = jnp.dot(probs, beside, preferred_element_type=jnp.float32)
            joined = part if joined is None else joined + part
        product, total = joined[:, :HD], jnp.where(joined[:, HD:] > 0.0, joined[:, HD:], 1.0)
        write(columns, product / total)
        packed = jnp.where(lane == head, top + jnp.log2(total), packed)
    return packed


def seen_by(visible, asker, span):
    table = visible[...]
    row, column = (lax.broadcasted_iota(jnp.int32, table.shape, axis) for axis in (0, 1))
    here = jnp.logical_and(row == asker, column == span)
    return jnp.max(jnp.where(here, table, 0).astype(jnp.float32), axis=(0, 1), keepdims=True) > 0.0


def beside_of(span):
    return span + 1 - 2 * lax.rem(span, 2)


def place_here():
    return lax.axis_index("span"), lax.axis_index("tensor")


def copied(source, target, semaphore):
    copy = pltpu.make_async_copy(source, target, semaphore)
    copy.start()
    return copy


def parts_of(rank, ranks, rows):
    block = rows // ranks
    lower = rank < ranks // 2
    early = pl.multiple_of(jnp.where(lower, rows - block, 0), block)
    late = pl.multiple_of(jnp.where(lower, 0, block), block)
    return (early, block), (late, rows - block)


def split_kernel(ranks, query, *refs):
    *targets, semaphores = refs
    place = place_here()

    @pl.when(place[0] > 1)
    def _():
        (early, _), (late, _) = parts_of(place[1], ranks, query.shape[0])
        starts = (early, late, pl.multiple_of(late + targets[1].shape[0], 16))
        copies = [
            copied(query.at[pl.ds(start, target.shape[0])], target, semaphores.at[index])
            for index, (start, target) in enumerate(zip(starts, targets))
        ]
        for copy in copies:
            copy.wait()


def local_kernel(ranks, part, visible, query, key, value, key_beside, value_beside,
                 result, sums, seen, *scratch):
    query_, key_, value_, key_beside_, value_beside_, semaphores = scratch
    place = place_here()
    start, size = parts_of(place[1], ranks, query.shape[0])[part]
    copies = [
        copied(source, target, semaphores.at[index])
        for index, (source, target) in enumerate((
            (visible, seen), (query.at[pl.ds(start, size)], query_),
            (key, key_), (key_beside, key_beside_), (value, value_), (value_beside, value_beside_),
        ))
    ]
    for copy in copies[:4]:
        copy.wait()

    def arrive():
        for copy in copies[4:]:
            copy.wait()

    def write(columns, block):
        result[:, columns] = block

    flags = [None, seen_by(seen, place[0], beside_of(place[0]))]
    sums[...] = attend(query_, [key_, key_beside_], [value_, value_beside_], flags, write, arrive)


def served_kernel(distance, spans, visible, key, value, key_beside, value_beside, *refs):
    span, _ = place_here()

    @pl.when(span + distance < spans)
    def _():
        asker = jnp.minimum(span + distance, spans - 1)
        flags = [seen_by(visible, asker, span), seen_by(visible, asker, beside_of(span))]
        *queries, result, query = refs
        at = 0
        for part in queries:
            query[at:at + part.shape[0], :] = part[...]
            at += part.shape[0]

        def write(columns, block):
            result[:, columns] = block.astype(jnp.bfloat16)

        rest = attend(query, [key, key_beside], [value, value_beside], flags, write)
        sent = jnp.zeros_like(rest)
        for piece in range(3):
            part = rest.astype(jnp.bfloat16).astype(jnp.float32)
            sent = sent + (part if piece == 0 else pltpu.roll(part, piece * PIECE_LANES, 1))
            rest = rest - part
        result[:, query.shape[1]:] = sent.astype(jnp.bfloat16)


def merge(span, distances, own, own_sum, served, write):
    width = own.shape[1]
    sums = [own_sum[...]]
    for distance, ref in zip(distances, served):
        sent = ref[:, width:].astype(jnp.float32)
        joined = sent
        for piece in (1, 2):
            joined = joined + pltpu.roll(sent, LANES - piece * PIECE_LANES, 1)
        sums.append(jnp.where(span >= distance, joined, HIDDEN))
    top = functools.reduce(jnp.maximum, sums)
    shares = [jnp.exp2(one - top) for one in sums]
    over = 1.0 / sum(shares)
    shares = [share * over for share in shares]
    for head in range(width // HD):
        columns = head_columns(head)
        merged = own[:, columns] * shares[0][:, head:head + 1]
        for distance, share, ref in zip(distances, shares[1:], served):
            away = jnp.where(span >= distance, ref[:, columns].astype(jnp.float32), 0.0)
            merged = merged + away * share[:, head:head + 1]
        write(columns, merged.astype(jnp.bfloat16))


def streamed(weight, first, tiles, semaphores):
    count, _, tile = tiles.shape
    return [
        copied(weight.at[:, pl.ds(first + index * tile, tile)], tiles.at[index], semaphores.at[index])
        for index in range(count)
    ]


def fetch_kernel(askers, weight, *refs):
    tiles, semaphores = refs[-2:]
    span, _ = place_here()

    @pl.when(span > 1 if askers else span < 2)
    def _():
        for copy in streamed(weight, 0, tiles, semaphores):
            copy.wait()


def opening_kernel(ranks, distances, first, *refs):
    own, own_sum, *served = refs[:2 + len(distances)]
    weight, result, *scratch = refs[2 + len(distances):]
    rows = scratch[-1]
    place = place_here()

    @pl.when(jnp.logical_or(place[1] == 0, place[1] == ranks - 1))
    def _():
        tiles, copies = weight, [None] * weight.shape[0]
        if first:
            tiles, semaphores, _ = scratch
            copies = streamed(weight, first, tiles, semaphores)

        def write(columns, part):
            rows[:, columns] = part

        merge(place[0], distances, own, own_sum, served, write)
        tile = tiles.shape[2]
        for index, copy in enumerate(copies):
            if copy is not None:
                copy.wait()
            product = jnp.dot(rows[...], tiles[index], preferred_element_type=jnp.float32)
            result[:, index * tile:(index + 1) * tile] = product.astype(jnp.bfloat16)


def project_blocks(ranks, first, rank, step, attended, weight, up, down, tiles, semaphores):
    last = ranks - 1
    tile = tiles.shape[2]
    block = up.shape[0]
    copies = streamed(weight, first, tiles, semaphores)
    yield
    sends = rank <= step, rank >= last - step
    starts = [
        pl.multiple_of(jnp.clip(target, 0, last) * block, block) for target in (last - step + rank, step + rank - last)
    ]
    rows = [attended[pl.ds(start, block), :] for start in starts]
    for index, copy in enumerate(copies):
        copy.wait()
        there = slice(index * tile, (index + 1) * tile)

        @pl.when(jnp.logical_and(*sends))
        def _():
            both = jnp.dot(jnp.concatenate(rows, axis=0), tiles[index], preferred_element_type=jnp.float32)
            up[:, there] = both[:block].astype(jnp.bfloat16)
            down[:, there] = both[block:].astype(jnp.bfloat16)

        @pl.when(jnp.logical_not(jnp.logical_and(*sends)))
        def _():
            one = jnp.dot(
                jnp.where(sends[0], rows[0], rows[1]), tiles[index], preferred_element_type=jnp.float32
            ).astype(jnp.bfloat16)
            up[:, there] = one
            down[:, there] = one


def merged_blocks_kernel(ranks, distances, place, *refs):
    each = 2 + len(distances)
    parts, (weight, attended, *results) = (refs[:each], refs[each:2 * each]), refs[2 * each:]
    work = project_blocks(ranks, 0, place[1], 1, attended, weight, *results)
    next(work)
    for (start, size), (own, own_sum, *served) in zip(parts_of(place[1], ranks, attended.shape[0]), parts):
        there = pl.ds(start, size)

        def write(columns, part):
            attended[there, columns] = part

        merge(place[0], distances, own, own_sum, served, write)
    for _ in work:
        pass


def blocks_kernel(ranks, first, step, place, attended, weight, *results):
    for _ in project_blocks(ranks, first, place[1], step, attended, weight, *results):
        pass


def own_kernel(place, levels, attended, weight, gate_table, result, gate, tiles, gates, semaphores):
    block = result.shape[0]
    count, _, tile = tiles.shape
    level = levels[place[0]]
    above = pl.multiple_of(level // 8 * 8, 8)
    gate_copy = copied(gate_table.at[pl.ds(above, 8)], gates, semaphores.at[count])
    copies = streamed(weight, 0, tiles, semaphores)
    start = pl.multiple_of(place[1] * block, block)
    for index, copy in enumerate(copies):
        copy.wait()
        product = jnp.dot(attended[pl.ds(start, block), :], tiles[index], preferred_element_type=jnp.float32)
        result[:, index * tile:(index + 1) * tile] = product.astype(jnp.bfloat16)
    gate_copy.wait()
    gate[...] = gates[pl.ds(lax.rem(level, 8), 1), :]


def final_kernel(done, projected, gate, up, down, result, own, gated, semaphores):
    first, (block, columns) = done.shape[1], own.shape
    pieces = gated.shape[0]
    wide = columns // pieces
    own_copy = copied(projected.at[:, pl.ds(first, columns)], own, semaphores.at[0])
    sent = [copied(done, result.at[:, pl.ds(0, first)], semaphores.at[1])]
    own_copy.wait()
    for piece in range(pieces):
        there = slice(piece * wide, (piece + 1) * wide)
        summed = own[:, there].astype(jnp.float32) + up[:, there].astype(jnp.float32)
        summed = summed + down[:, there].astype(jnp.float32)
        gated[piece] = (summed * gate[:, first + piece * wide:first + (piece + 1) * wide]).astype(jnp.bfloat16)
        sent.append(copied(
            gated.at[piece], result.at[:, pl.ds(first + piece * wide, wide)], semaphores.at[2 + piece]
        ))
    for copy in sent:
        copy.wait()


def body(queries, keys, values, out_weight, gate_table, levels, visible):
    rows, width = queries.shape
    model = out_weight.shape[1]
    spans = lax.axis_size("span")
    ranks = lax.axis_size("tensor")
    span = lax.axis_index("span")
    rank = lax.axis_index("tensor")
    block = rows // ranks
    bf16, f32 = jnp.bfloat16, jnp.float32
    place = jnp.stack([span, rank]).astype(jnp.int32)
    third = (rows - block) // 48 * 16
    query_early, *query_late = pl.pallas_call(
        functools.partial(split_kernel, ranks),
        in_specs=[HBM],
        out_specs=[VMEM] * 3,
        out_shape=[jax.ShapeDtypeStruct((part, width), bf16) for part in (block, rows - block - third, third)],
        scratch_shapes=[pltpu.SemaphoreType.DMA((3,))],
        compiler_params=PARAMS,
        cost_estimate=taking(1.7),
        name="split",
    )(in_hbm(queries))
    distances = list(range(2, spans, 2))
    asked_early = [shifted(query_early, "span", -distance) for distance in distances]
    swap = [(i, i + 1 - 2 * (i % 2)) for i in range(spans)]
    key_beside = lax.ppermute(keys, "span", swap)
    value_beside = lax.ppermute(values, "span", swap)

    def after(value, *others):
        return lax.optimization_barrier((value, others))[0]

    def local(part, queries):
        size = (block, rows - block)[part]
        return pl.pallas_call(
            functools.partial(local_kernel, ranks, part),
            in_specs=[HBM, HBM, HBM, HBM, ANY, ANY],
            out_specs=[VMEM] * 3,
            out_shape=[
                jax.ShapeDtypeStruct((size, width), f32),
                jax.ShapeDtypeStruct((size, LANES), f32),
                jax.ShapeDtypeStruct(visible.shape, visible.dtype),
            ],
            scratch_shapes=[pltpu.VMEM((size, width), bf16)] + [pltpu.VMEM((rows, width), bf16)] * 4
            + [pltpu.SemaphoreType.DMA((6,))],
            compiler_params=PARAMS,
            cost_estimate=taking(4.0),
            name="local",
        )(in_hbm(visible), in_hbm(queries), in_hbm(keys), in_hbm(values), key_beside, value_beside)

    def served(asked, distance):
        return pl.pallas_call(
            functools.partial(served_kernel, distance, spans),
            in_specs=[VMEM] * (5 + len(asked)),
            out_specs=VMEM,
            out_shape=jax.ShapeDtypeStruct((sum(part.shape[0] for part in asked), width + LANES), bf16),
            scratch_shapes=[pltpu.VMEM((sum(part.shape[0] for part in asked), width), bf16)],
            compiler_params=PARAMS,
            cost_estimate=taking(3.3),
            name="served",
        )(seen, keys, values, key_beside, value_beside, *asked)

    *early, seen = local(0, queries)
    query_late = after(query_late, early)
    asked_early = after(asked_early, early)
    chunks = 2
    columns = model // chunks
    tiles = 4
    tile = columns // tiles
    last = ranks - 1
    weight = in_hbm(out_weight)

    tile_shape = (tiles, width, tile)
    streaming = dict(
        scratch_shapes=[pltpu.VMEM(tile_shape, bf16), pltpu.SemaphoreType.DMA((tiles,))],
        compiler_params=PARAMS,
        cost_estimate=taking(3.0),
    )

    def fetch(askers, weight, *before):
        return pl.pallas_call(
            functools.partial(fetch_kernel, askers),
            in_specs=[HBM] + [VMEM] * len(before),
            out_specs=VMEM,
            out_shape=jax.ShapeDtypeStruct(tile_shape, bf16),
            input_output_aliases={1: 0} if before else {},
            scratch_shapes=[pltpu.SemaphoreType.DMA((tiles,))],
            compiler_params=PARAMS,
            cost_estimate=taking(2.4),
            name="fetch",
        )(in_hbm(weight), *before)

    out_early = [served([q], d) for q, d in zip(asked_early, distances)]
    early += [shifted(o, "span", d) for o, d in zip(out_early, distances)]
    fetched = fetch(True, after(out_weight, out_early))
    query_late = [query_late[0], after(query_late[1], fetched)]
    asked_late = [[shifted(query, "span", -distance) for query in query_late] for distance in distances]
    fetched = fetch(False, out_weight, fetched)

    def opening(chunk, weight):
        scratch = streaming["scratch_shapes"] if chunk else []
        return pl.pallas_call(
            functools.partial(opening_kernel, ranks, distances, chunk * columns),
            in_specs=[VMEM] * (2 + len(distances)) + [HBM if chunk else VMEM],
            out_specs=VMEM,
            out_shape=jax.ShapeDtypeStruct((block, columns), bf16),
            scratch_shapes=scratch + [pltpu.VMEM((block, width), bf16)],
            compiler_params=PARAMS,
            cost_estimate=taking(3.4),
            name="opening",
        )(*early, in_hbm(weight) if chunk else fetched)

    ends = [(0, 1), (last, last - 1)]
    sent = opening(0, out_weight)
    arrived = [[lax.ppermute(sent, "tensor", ends)]]
    out_late = [served(q, d) for q, d in zip(after(asked_late, sent), distances)]
    for chunk in range(1, chunks):
        sent = opening(chunk, after(out_weight, out_late))
        arrived.append([lax.ppermute(sent, "tensor", ends)])
    *late, _ = local(1, after(queries, sent))
    late += [shifted(o, "span", d) for o, d in zip(out_late, distances)]

    attended_shape = jax.ShapeDtypeStruct((rows, width), bf16)
    block_shapes = [jax.ShapeDtypeStruct((block, columns), bf16)] * 2
    attended, *merged = pl.pallas_call(
        functools.partial(merged_blocks_kernel, ranks, distances),
        in_specs=[SMEM] + [VMEM] * (4 + 2 * len(distances)) + [HBM],
        out_specs=[VMEM] * 3,
        out_shape=[attended_shape] + block_shapes,
        name="merged_blocks",
        **streaming,
    )(place, *early, *late, weight)

    def blocks_of(step, chunk, attended):
        return pl.pallas_call(
            functools.partial(blocks_kernel, ranks, chunk * columns, step),
            in_specs=[SMEM, VMEM, HBM],
            out_specs=[VMEM] * 2,
            out_shape=block_shapes,
            name="blocks",
            **streaming,
        )(place, attended, weight)

    before = attended
    for step in range(1, last):
        for chunk in range(chunks):
            if step == 1 and chunk == 0:
                blocks = merged
            else:
                blocks = blocks_of(step, chunk, after(attended, before))
            comes, blocks = lax.optimization_barrier((arrived[chunk], blocks))
            if step == 1 and chunk == 0:
                down = (blocks[1].astype(f32) + comes[-1].astype(f32)).astype(bf16)
                up = (after(blocks[0], down).astype(f32) + comes[0].astype(f32)).astype(bf16)
            else:
                up = (blocks[0].astype(f32) + comes[0].astype(f32)).astype(bf16)
                down = (after(blocks[1], up).astype(f32) + comes[-1].astype(f32)).astype(bf16)
            before = (up, down)
            arrived[chunk] = [
                lax.ppermute(up, "tensor", [(i, i + 1) for i in range(step + 1)]),
                lax.ppermute(down, "tensor", [(last - i, last - i - 1) for i in range(step + 1)]),
            ]
    everything = chunks * tiles
    projected, gate = pl.pallas_call(
        own_kernel,
        in_specs=[SMEM, SMEM, VMEM, HBM, HBM],
        out_specs=[VMEM, VMEM],
        out_shape=[jax.ShapeDtypeStruct((block, model), bf16), jax.ShapeDtypeStruct((1, model), f32)],
        scratch_shapes=[
            pltpu.VMEM((everything, width, tile), bf16),
            pltpu.VMEM((8, model), f32),
            pltpu.SemaphoreType.DMA((everything + 1,)),
        ],
        compiler_params=PARAMS,
        cost_estimate=taking(5.0),
        name="own",
    )(place, levels, after(attended, before), weight, in_hbm(gate_table))

    finished = []
    for chunk in range(chunks - 1):
        there = slice(chunk * columns, (chunk + 1) * columns)
        summed = sum(part.astype(f32) for part in (projected[:, there], *arrived[chunk]))
        finished.append((summed * gate[:, there]).astype(bf16))
    pieces = 2
    return pl.pallas_call(
        final_kernel,
        in_specs=[ANY, ANY, VMEM, VMEM, VMEM],
        out_specs=HBM,
        out_shape=jax.ShapeDtypeStruct((block, model), bf16),
        scratch_shapes=[
            pltpu.VMEM((block, columns), bf16),
            pltpu.VMEM((pieces, block, columns // pieces), bf16),
            pltpu.SemaphoreType.DMA((2 + pieces,)),
        ],
        compiler_params=PARAMS,
        cost_estimate=taking(2.7),
        name="final",
    )(jnp.concatenate(finished, axis=1), projected, gate, *arrived[-1])


def solution(mesh):
    return jax.shard_map(
        body,
        mesh=mesh,
        in_specs=(
            P(("group", "span"), "tensor"),
            P(("group", "span"), "tensor"),
            P(("group", "span"), "tensor"),
            P("tensor", None),
            P(),
            P("group"),
            P("group", None),
        ),
        out_specs=P(("group", "span", "tensor"), None),
        check_vma=False,
    )
```

```python
import functools

import jax
import jax.numpy as jnp
from jax import lax
from jax.experimental import pallas as pl
from jax.experimental.pallas import tpu as pltpu
from jax.sharding import PartitionSpec as P

HD = 128
LANES = 128
HIDDEN = -1e30
LOG2E = 1.4426950408889634
PARAMS = pltpu.CompilerParams(vmem_limit_bytes=24 * 1024 * 1024)
SMEM = pl.BlockSpec(memory_space=pltpu.SMEM)
VMEM = pl.BlockSpec(memory_space=pltpu.VMEM)
ANY = pl.BlockSpec(memory_space=pl.ANY)
HBM = pl.BlockSpec(memory_space=pltpu.HBM)
PIECE_LANES = 32


def taking(microseconds):
    return pl.CostEstimate(flops=0, bytes_accessed=int(microseconds * 3.69e6), transcendentals=0)


def in_hbm(array):
    return pltpu.with_memory_space_constraint(array, pltpu.HBM)


def shifted(block, axis, distance):
    count = lax.axis_size(axis)
    return lax.ppermute(block, axis, [(i, i + distance) for i in range(count) if 0 <= i + distance < count])


def head_columns(head):
    return slice(head * HD, (head + 1) * HD)


def attend(query, keys, values, flags, write, arrive=None):
    rows, width = query.shape
    scale = LOG2E * HD ** (-0.5)
    lane = lax.broadcasted_iota(jnp.int32, (rows, LANES), 1)
    packed = jnp.zeros((rows, LANES), jnp.float32)

    def scored(head):
        columns = head_columns(head)
        return [
            lax.dot_general(
                query[:, columns], key[:, columns], (((1,), (1,)), ((), ())), preferred_element_type=jnp.float32
            )
            for key in keys
        ]

    heads = width // HD
    later = scored(0)
    if arrive is not None:
        arrive()
    for head in range(heads):
        columns = head_columns(head)
        scores, later = later, scored(head + 1) if head + 1 < heads else None
        tops = [jnp.max(block, axis=-1, keepdims=True) * scale for block in scores]
        top = functools.reduce(
            jnp.maximum, [one if flag is None else jnp.where(flag, one, HIDDEN) for one, flag in zip(tops, flags)]
        )
        joined = None
        for block, value, flag in zip(scores, values, flags):
            above = top if flag is None else jnp.where(flag, top, -HIDDEN)
            probs = jnp.exp2(block * scale - above).astype(jnp.bfloat16)
            beside = jnp.concatenate([value[:, columns], jnp.ones((value.shape[0], HD), jnp.bfloat16)], axis=1)
            part = jnp.dot(probs, beside, preferred_element_type=jnp.float32)
            joined = part if joined is None else joined + part
        product, total = joined[:, :HD], jnp.where(joined[:, HD:] > 0.0, joined[:, HD:], 1.0)
        write(columns, product / total)
        packed = jnp.where(lane == head, top + jnp.log2(total), packed)
    return packed


def seen_by(visible, asker, span):
    table = visible[...]
    row, column = (lax.broadcasted_iota(jnp.int32, table.shape, axis) for axis in (0, 1))
    here = jnp.logical_and(row == asker, column == span)
    return jnp.max(jnp.where(here, table, 0).astype(jnp.float32), axis=(0, 1), keepdims=True) > 0.0


def beside_of(span):
    return span + 1 - 2 * lax.rem(span, 2)


def place_here():
    return lax.axis_index("span"), lax.axis_index("tensor")


def copied(source, target, semaphore):
    copy = pltpu.make_async_copy(source, target, semaphore)
    copy.start()
    return copy


def parts_of(rank, ranks, rows):
    block = rows // ranks
    lower = rank < ranks // 2
    early = pl.multiple_of(jnp.where(lower, rows - block, 0), block)
    late = pl.multiple_of(jnp.where(lower, 0, block), block)
    return (early, block), (late, rows - block)


def split_kernel(ranks, query, *refs):
    *targets, semaphores = refs
    place = place_here()

    @pl.when(place[0] > 1)
    def _():
        (early, _), (late, _) = parts_of(place[1], ranks, query.shape[0])
        starts = (early, late, pl.multiple_of(late + targets[1].shape[0], 16))
        copies = [
            copied(query.at[pl.ds(start, target.shape[0])], target, semaphores.at[index])
            for index, (start, target) in enumerate(zip(starts, targets))
        ]
        for copy in copies:
            copy.wait()


def local_kernel(ranks, part, visible, query, key, value, key_beside, value_beside,
                 result, sums, seen, *scratch):
    query_, key_, value_, key_beside_, value_beside_, semaphores = scratch
    place = place_here()
    start, size = parts_of(place[1], ranks, query.shape[0])[part]
    copies = [
        copied(source, target, semaphores.at[index])
        for index, (source, target) in enumerate((
            (visible, seen), (query.at[pl.ds(start, size)], query_),
            (key, key_), (key_beside, key_beside_), (value, value_), (value_beside, value_beside_),
        ))
    ]
    for copy in copies[:4]:
        copy.wait()

    def arrive():
        for copy in copies[4:]:
            copy.wait()

    def write(columns, block):
        result[:, columns] = block

    flags = [None, seen_by(seen, place[0], beside_of(place[0]))]
    sums[...] = attend(query_, [key_, key_beside_], [value_, value_beside_], flags, write, arrive)


def served_kernel(distance, spans, visible, key, value, key_beside, value_beside, *refs):
    span, _ = place_here()

    @pl.when(span + distance < spans)
    def _():
        asker = jnp.minimum(span + distance, spans - 1)
        flags = [seen_by(visible, asker, span), seen_by(visible, asker, beside_of(span))]
        *queries, result, query = refs
        at = 0
        for part in queries:
            query[at:at + part.shape[0], :] = part[...]
            at += part.shape[0]

        def write(columns, block):
            result[:, columns] = block.astype(jnp.bfloat16)

        rest = attend(query, [key, key_beside], [value, value_beside], flags, write)
        sent = jnp.zeros_like(rest)
        for piece in range(3):
            part = rest.astype(jnp.bfloat16).astype(jnp.float32)
            sent = sent + (part if piece == 0 else pltpu.roll(part, piece * PIECE_LANES, 1))
            rest = rest - part
        result[:, query.shape[1]:] = sent.astype(jnp.bfloat16)


def merge(span, distances, own, own_sum, served, write):
    width = own.shape[1]
    sums = [own_sum[...]]
    for distance, ref in zip(distances, served):
        sent = ref[:, width:].astype(jnp.float32)
        joined = sent
        for piece in (1, 2):
            joined = joined + pltpu.roll(sent, LANES - piece * PIECE_LANES, 1)
        sums.append(jnp.where(span >= distance, joined, HIDDEN))
    top = functools.reduce(jnp.maximum, sums)
    shares = [jnp.exp2(one - top) for one in sums]
    over = 1.0 / sum(shares)
    shares = [share * over for share in shares]
    for head in range(width // HD):
        columns = head_columns(head)
        merged = own[:, columns] * shares[0][:, head:head + 1]
        for distance, share, ref in zip(distances, shares[1:], served):
            away = jnp.where(span >= distance, ref[:, columns].astype(jnp.float32), 0.0)
            merged = merged + away * share[:, head:head + 1]
        write(columns, merged.astype(jnp.bfloat16))


def streamed(weight, first, tiles, semaphores):
    count, _, tile = tiles.shape
    return [
        copied(weight.at[:, pl.ds(first + index * tile, tile)], tiles.at[index], semaphores.at[index])
        for index in range(count)
    ]


def fetch_kernel(weight, tiles, semaphores):
    for copy in streamed(weight, 0, tiles, semaphores):
        copy.wait()


def opening_kernel(ranks, distances, first, *refs):
    own, own_sum, *served = refs[:2 + len(distances)]
    weight, result, *scratch = refs[2 + len(distances):]
    rows = scratch[-1]
    place = place_here()

    @pl.when(jnp.logical_or(place[1] == 0, place[1] == ranks - 1))
    def _():
        tiles, copies = weight, [None] * weight.shape[0]
        if first:
            tiles, semaphores, _ = scratch
            copies = streamed(weight, first, tiles, semaphores)

        def write(columns, part):
            rows[:, columns] = part

        merge(place[0], distances, own, own_sum, served, write)
        tile = tiles.shape[2]
        for index, copy in enumerate(copies):
            if copy is not None:
                copy.wait()
            product = jnp.dot(rows[...], tiles[index], preferred_element_type=jnp.float32)
            result[:, index * tile:(index + 1) * tile] = product.astype(jnp.bfloat16)


def project_blocks(ranks, first, rank, step, attended, weight, up, down, tiles, semaphores):
    last = ranks - 1
    tile = tiles.shape[2]
    block = up.shape[0]
    copies = streamed(weight, first, tiles, semaphores)
    yield
    sends = rank <= step, rank >= last - step
    starts = [
        pl.multiple_of(jnp.clip(target, 0, last) * block, block) for target in (last - step + rank, step + rank - last)
    ]
    rows = [attended[pl.ds(start, block), :] for start in starts]
    for index, copy in enumerate(copies):
        copy.wait()
        there = slice(index * tile, (index + 1) * tile)

        @pl.when(jnp.logical_and(*sends))
        def _():
            both = jnp.dot(jnp.concatenate(rows, axis=0), tiles[index], preferred_element_type=jnp.float32)
            up[:, there] = both[:block].astype(jnp.bfloat16)
            down[:, there] = both[block:].astype(jnp.bfloat16)

        @pl.when(jnp.logical_not(jnp.logical_and(*sends)))
        def _():
            one = jnp.dot(
                jnp.where(sends[0], rows[0], rows[1]), tiles[index], preferred_element_type=jnp.float32
            ).astype(jnp.bfloat16)
            up[:, there] = one
            down[:, there] = one


def merged_blocks_kernel(ranks, distances, place, *refs):
    each = 2 + len(distances)
    parts, (weight, attended, *results) = (refs[:each], refs[each:2 * each]), refs[2 * each:]
    work = project_blocks(ranks, 0, place[1], 1, attended, weight, *results)
    next(work)
    for (start, size), (own, own_sum, *served) in zip(parts_of(place[1], ranks, attended.shape[0]), parts):
        there = pl.ds(start, size)

        def write(columns, part):
            attended[there, columns] = part

        merge(place[0], distances, own, own_sum, served, write)
    for _ in work:
        pass


def blocks_kernel(ranks, first, step, place, attended, weight, *results):
    for _ in project_blocks(ranks, first, place[1], step, attended, weight, *results):
        pass


def own_kernel(place, levels, attended, weight, gate_table, result, gate, tiles, gates, semaphores):
    block = result.shape[0]
    count, _, tile = tiles.shape
    level = levels[place[0]]
    above = pl.multiple_of(level // 8 * 8, 8)
    gate_copy = copied(gate_table.at[pl.ds(above, 8)], gates, semaphores.at[count])
    copies = streamed(weight, 0, tiles, semaphores)
    start = pl.multiple_of(place[1] * block, block)
    for index, copy in enumerate(copies):
        copy.wait()
        product = jnp.dot(attended[pl.ds(start, block), :], tiles[index], preferred_element_type=jnp.float32)
        result[:, index * tile:(index + 1) * tile] = product.astype(jnp.bfloat16)
    gate_copy.wait()
    gate[...] = gates[pl.ds(lax.rem(level, 8), 1), :]


def final_kernel(done, projected, gate, up, down, result, own, gated, semaphores):
    first, (block, columns) = done.shape[1], own.shape
    pieces = gated.shape[0]
    wide = columns // pieces
    own_copy = copied(projected.at[:, pl.ds(first, columns)], own, semaphores.at[0])
    sent = [copied(done, result.at[:, pl.ds(0, first)], semaphores.at[1])]
    own_copy.wait()
    for piece in range(pieces):
        there = slice(piece * wide, (piece + 1) * wide)
        summed = own[:, there].astype(jnp.float32) + up[:, there].astype(jnp.float32)
        summed = summed + down[:, there].astype(jnp.float32)
        gated[piece] = (summed * gate[:, first + piece * wide:first + (piece + 1) * wide]).astype(jnp.bfloat16)
        sent.append(copied(
            gated.at[piece], result.at[:, pl.ds(first + piece * wide, wide)], semaphores.at[2 + piece]
        ))
    for copy in sent:
        copy.wait()


def body(queries, keys, values, out_weight, gate_table, levels, visible):
    rows, width = queries.shape
    model = out_weight.shape[1]
    spans = lax.axis_size("span")
    ranks = lax.axis_size("tensor")
    span = lax.axis_index("span")
    rank = lax.axis_index("tensor")
    block = rows // ranks
    bf16, f32 = jnp.bfloat16, jnp.float32
    place = jnp.stack([span, rank]).astype(jnp.int32)
    third = (rows - block) // 48 * 16
    query_early, *query_late = pl.pallas_call(
        functools.partial(split_kernel, ranks),
        in_specs=[HBM],
        out_specs=[VMEM] * 3,
        out_shape=[jax.ShapeDtypeStruct((part, width), bf16) for part in (block, rows - block - third, third)],
        scratch_shapes=[pltpu.SemaphoreType.DMA((3,))],
        compiler_params=PARAMS,
        cost_estimate=taking(1.7),
        name="split",
    )(in_hbm(queries))
    distances = list(range(2, spans, 2))
    asked_early = [shifted(query_early, "span", -distance) for distance in distances]
    swap = [(i, i + 1 - 2 * (i % 2)) for i in range(spans)]
    key_beside = lax.ppermute(keys, "span", swap)
    value_beside = lax.ppermute(values, "span", swap)

    def after(value, *others):
        return lax.optimization_barrier((value, others))[0]

    def local(part, queries):
        size = (block, rows - block)[part]
        return pl.pallas_call(
            functools.partial(local_kernel, ranks, part),
            in_specs=[HBM, HBM, HBM, HBM, ANY, ANY],
            out_specs=[VMEM] * 3,
            out_shape=[
                jax.ShapeDtypeStruct((size, width), f32),
                jax.ShapeDtypeStruct((size, LANES), f32),
                jax.ShapeDtypeStruct(visible.shape, visible.dtype),
            ],
            scratch_shapes=[pltpu.VMEM((size, width), bf16)] + [pltpu.VMEM((rows, width), bf16)] * 4
            + [pltpu.SemaphoreType.DMA((6,))],
            compiler_params=PARAMS,
            cost_estimate=taking(4.0),
            name="local",
        )(in_hbm(visible), in_hbm(queries), in_hbm(keys), in_hbm(values), key_beside, value_beside)

    def served(asked, distance):
        return pl.pallas_call(
            functools.partial(served_kernel, distance, spans),
            in_specs=[VMEM] * (5 + len(asked)),
            out_specs=VMEM,
            out_shape=jax.ShapeDtypeStruct((sum(part.shape[0] for part in asked), width + LANES), bf16),
            scratch_shapes=[pltpu.VMEM((sum(part.shape[0] for part in asked), width), bf16)],
            compiler_params=PARAMS,
            cost_estimate=taking(3.3),
            name="served",
        )(seen, keys, values, key_beside, value_beside, *asked)

    *early, seen = local(0, queries)
    query_late = after(query_late, early)
    asked_early = after(asked_early, early)
    asked_late = [[shifted(query, "span", -distance) for query in query_late] for distance in distances]
    out_early = [served([q], d) for q, d in zip(asked_early, distances)]
    early += [shifted(o, "span", d) for o, d in zip(out_early, distances)]

    chunks = 2
    columns = model // chunks
    tiles = 4
    tile = columns // tiles
    last = ranks - 1
    weight = in_hbm(out_weight)

    tile_shape = (tiles, width, tile)
    streaming = dict(
        scratch_shapes=[pltpu.VMEM(tile_shape, bf16), pltpu.SemaphoreType.DMA((tiles,))],
        compiler_params=PARAMS,
        cost_estimate=taking(3.0),
    )
    fetched = pl.pallas_call(
        fetch_kernel,
        in_specs=[HBM],
        out_specs=VMEM,
        out_shape=jax.ShapeDtypeStruct(tile_shape, bf16),
        scratch_shapes=[pltpu.SemaphoreType.DMA((tiles,))],
        compiler_params=PARAMS,
        cost_estimate=taking(2.4),
        name="fetch",
    )(in_hbm(after(out_weight, out_early)))

    def opening(chunk, weight):
        scratch = streaming["scratch_shapes"] if chunk else []
        return pl.pallas_call(
            functools.partial(opening_kernel, ranks, distances, chunk * columns),
            in_specs=[VMEM] * (2 + len(distances)) + [HBM if chunk else VMEM],
            out_specs=VMEM,
            out_shape=jax.ShapeDtypeStruct((block, columns), bf16),
            scratch_shapes=scratch + [pltpu.VMEM((block, width), bf16)],
            compiler_params=PARAMS,
            cost_estimate=taking(3.4),
            name="opening",
        )(*early, in_hbm(weight) if chunk else fetched)

    ends = [(0, 1), (last, last - 1)]
    sent = opening(0, out_weight)
    arrived = [[lax.ppermute(sent, "tensor", ends)]]
    out_late = [served(q, d) for q, d in zip(after(asked_late, sent), distances)]
    for chunk in range(1, chunks):
        sent = opening(chunk, after(out_weight, out_late))
        arrived.append([lax.ppermute(sent, "tensor", ends)])
    *late, _ = local(1, after(queries, sent))
    late += [shifted(o, "span", d) for o, d in zip(out_late, distances)]

    attended_shape = jax.ShapeDtypeStruct((rows, width), bf16)
    block_shapes = [jax.ShapeDtypeStruct((block, columns), bf16)] * 2
    attended, *merged = pl.pallas_call(
        functools.partial(merged_blocks_kernel, ranks, distances),
        in_specs=[SMEM] + [VMEM] * (4 + 2 * len(distances)) + [HBM],
        out_specs=[VMEM] * 3,
        out_shape=[attended_shape] + block_shapes,
        name="merged_blocks",
        **streaming,
    )(place, *early, *late, weight)

    def blocks_of(step, chunk, attended):
        return pl.pallas_call(
            functools.partial(blocks_kernel, ranks, chunk * columns, step),
            in_specs=[SMEM, VMEM, HBM],
            out_specs=[VMEM] * 2,
            out_shape=block_shapes,
            name="blocks",
            **streaming,
        )(place, attended, weight)

    before = attended
    for step in range(1, last):
        for chunk in range(chunks):
            if step == 1 and chunk == 0:
                blocks = merged
            else:
                blocks = blocks_of(step, chunk, after(attended, before))
            comes, blocks = lax.optimization_barrier((arrived[chunk], blocks))
            up, down = [
                (mine.astype(f32) + come.astype(f32)).astype(bf16)
                for mine, come in zip(blocks, (comes[0], comes[-1]))
            ]
            before = (up, down)
            arrived[chunk] = [
                lax.ppermute(up, "tensor", [(i, i + 1) for i in range(step + 1)]),
                lax.ppermute(down, "tensor", [(last - i, last - i - 1) for i in range(step + 1)]),
            ]
    everything = chunks * tiles
    projected, gate = pl.pallas_call(
        own_kernel,
        in_specs=[SMEM, SMEM, VMEM, HBM, HBM],
        out_specs=[VMEM, VMEM],
        out_shape=[jax.ShapeDtypeStruct((block, model), bf16), jax.ShapeDtypeStruct((1, model), f32)],
        scratch_shapes=[
            pltpu.VMEM((everything, width, tile), bf16),
            pltpu.VMEM((8, model), f32),
            pltpu.SemaphoreType.DMA((everything + 1,)),
        ],
        compiler_params=PARAMS,
        cost_estimate=taking(5.0),
        name="own",
    )(place, levels, after(attended, before), weight, in_hbm(gate_table))

    finished = []
    for chunk in range(chunks - 1):
        there = slice(chunk * columns, (chunk + 1) * columns)
        summed = sum(part.astype(f32) for part in (projected[:, there], *arrived[chunk]))
        finished.append((summed * gate[:, there]).astype(bf16))
    pieces = 2
    return pl.pallas_call(
        final_kernel,
        in_specs=[ANY, ANY, VMEM, VMEM, VMEM],
        out_specs=HBM,
        out_shape=jax.ShapeDtypeStruct((block, model), bf16),
        scratch_shapes=[
            pltpu.VMEM((block, columns), bf16),
            pltpu.VMEM((pieces, block, columns // pieces), bf16),
            pltpu.SemaphoreType.DMA((2 + pieces,)),
        ],
        compiler_params=PARAMS,
        cost_estimate=taking(2.7),
        name="final",
    )(jnp.concatenate(finished, axis=1), projected, gate, *arrived[-1])


def solution(mesh):
    return jax.shard_map(
        body,
        mesh=mesh,
        in_specs=(
            P(("group", "span"), "tensor"),
            P(("group", "span"), "tensor"),
            P(("group", "span"), "tensor"),
            P("tensor", None),
            P(),
            P("group"),
            P("group", None),
        ),
        out_specs=P(("group", "span", "tensor"), None),
        check_vma=False,
    )
```
